32 devices in a mesh: energy: 8 (over y, x, core), slab: 4 (over z).
Axes of the slice: x: 2, y: 2, z: 4, core: 2. Of those that a mesh axis runs over, the one named last changes fastest.
Arguments:
- potential_old: float32 [64, 32, 128], P('slab', 'energy'), may hold values from -6 to 6
- charge: float32 [64, 32, 128], P('slab', 'energy'), may hold values from -6 to 6
- permittivity: float32 [64, 32, 128], P('slab', 'energy'), may hold values from 1 to 12
- owner_cell: int32 [16, 256], P('slab'), may hold values from 0 to 16383
- green_free: float32 [8, 16, 2, 256, 256], P('energy', 'slab')
- coupling: float32 [16, 2, 256, 256], P('slab'), may hold values from -0.25 to 0.25
- shifts: int32 [4], replicated, may hold values from 1 to 2, as said below
- occupation: float32 [4], replicated, may hold values from 0.1 to 3
- mode_tiles: float32 [4, 256, 256], replicated, may hold values from -6 to 6
Outputs:
- potential_new: float32 [64, 32, 128], P('slab', 'energy')
- self_energy: float32 [8, 16, 2, 256, 256], P('energy', 'slab')
The draws below stay inside these ranges and needn't reach their ends.
Inputs may be any that keep to these rules, and one draw needn't show every extreme that they name: `shifts`: every whole number from 1 to 2 is the shift of some mode.
All inputs are finite; a program needn't handle non-finite values.
Results may differ from the reference program's by a relative error of at most 0.00023.
Values sent between devices are 32-bit elements; how exact they have to be, the bound alone decides.
No kernel may reach another device: no remote copies, remote signals or barrier semaphores. Data moves between devices by JAX's collectives and lax.ppermute only.
A program may use at most 128 MiB of HBM per device.

```python
import math
import jax
import jax.numpy as jnp
from jax import lax

ORBITALS = 256
SLABS = 16
ENERGIES = 8
SLAB_CELLS = 4
CROSS = 32
DEPTH = 128
MODES = 4
SHIFT_MOST = 2


def draw_green_free(key, part):
    array_shape = (ENERGIES, SLABS, 2, ORBITALS, ORBITALS)
    jitter = jax.random.normal(key, array_shape, jnp.float32)
    identity_block = jnp.eye(ORBITALS, dtype=jnp.float32)
    diagonal = jnp.stack([0.75 * identity_block, -0.25 * identity_block])
    return diagonal + jitter * (0.3 / math.sqrt(ORBITALS))


def draw_shifts(key, part):
    leading = jax.random.permutation(jax.random.fold_in(key, 11), SHIFT_MOST).astype(jnp.int32) + 1
    trailing = jax.random.randint(jax.random.fold_in(key, 12), (MODES - SHIFT_MOST,), 1, SHIFT_MOST + 1).astype(jnp.int32)
    return jnp.concatenate([leading, trailing]).astype(jnp.int32)


def with_ends(array, key, low, top_value):
    spot = [jax.random.randint(jax.random.fold_in(key, axis), (), 0, length) for axis, length in enumerate(array.shape)]
    widest = array.shape.index(max(array.shape))
    next_to = spot[:widest] + [(spot[widest] + 1) % array.shape[widest]] + spot[widest + 1:]
    return array.at[tuple(spot)].set(low).at[tuple(next_to)].set(top_value)


def steps_of(own_key, extent, cuts, smallest, largest):
    def one(dim, blocks):
        steps = jax.random.uniform(jax.random.fold_in(jax.random.fold_in(own_key, 6), dim), (blocks,), jnp.float32, smallest / len(cuts), largest / len(cuts))
        return jnp.repeat(jnp.exp(steps), extent[dim] // blocks).reshape((-1,) + (1,) * (len(extent) - dim - 1))

    loudness = one(*cuts[0])
    for cut in cuts[1:]:
        loudness = loudness * one(*cut)
    return loudness


def gaussian(own_key, shape, width, reach, split=(), kind=jnp.bfloat16):
    array = jax.random.normal(own_key, shape, jnp.float32) * width
    if len(split) > 0:
        array = steps_of(own_key, shape, split, -0.22, 0.18) * array
    return jnp.clip(array, min=-reach, max=reach).astype(kind)


def setup_inputs(seed: int = 0) -> dict:
    streams_of = jax.random.split(jax.random.key(seed), 10)
    return {
        "potential_old": gaussian(streams_of[0], (SLABS * SLAB_CELLS, CROSS, DEPTH), 1.0, 6.0, ((0, 4), (1, 8)), jnp.float32),
        "charge": gaussian(streams_of[1], (SLABS * SLAB_CELLS, CROSS, DEPTH), 1.0, 6.0, ((0, 4), (1, 8)), jnp.float32),
        "permittivity": jnp.clip(jnp.exp(math.log(12.0) - 2.4849066 * jax.random.uniform(streams_of[2], (SLABS * SLAB_CELLS, CROSS, DEPTH), jnp.float32) ** steps_of(streams_of[2], (SLABS * SLAB_CELLS, CROSS, DEPTH), ((0, 4), (1, 8)), -0.2, 0.2)), 1.0, 12.0),
        "owner_cell": with_ends(jax.random.randint(streams_of[3], (SLABS, ORBITALS), 0, SLAB_CELLS * CROSS * DEPTH), jax.random.fold_in(streams_of[3], 1), 0, (SLAB_CELLS * CROSS * DEPTH) - 1).astype(jnp.int32),
        "green_free": draw_green_free(jax.random.fold_in(streams_of[9], 71), 0),
        "coupling": gaussian(streams_of[5], (SLABS, 2, ORBITALS, ORBITALS), (7 * ORBITALS // 4) ** -0.5, 0.25, ((0, 4),), jnp.float32),
        "shifts": draw_shifts(jax.random.fold_in(streams_of[9], 71), 0),
        "occupation": jnp.clip(jnp.exp(jax.random.uniform(streams_of[7], (MODES,), jnp.float32, math.log(0.1), math.log(3.0))), 0.1, 3.0),
        "mode_tiles": gaussian(streams_of[8], (MODES, ORBITALS, ORBITALS), 1.0, 6.0, (), jnp.float32),
    }


FULL_PRECISION = lax.Precision.HIGHEST


def complex_product(former, latter):
    real_part = jnp.matmul(former[..., 0, :, :], latter[..., 0, :, :], precision=FULL_PRECISION) - jnp.matmul(former[..., 1, :, :], latter[..., 1, :, :], precision=FULL_PRECISION)
    imag_part = jnp.matmul(former[..., 0, :, :], latter[..., 1, :, :], precision=FULL_PRECISION) + jnp.matmul(former[..., 1, :, :], latter[..., 0, :, :], precision=FULL_PRECISION)
    return jnp.stack([real_part, imag_part], axis=-3)


def flipped(matrix):
    return jnp.swapaxes(matrix, -1, -2)


def neighbour_windows():
    inner = slice(1, -1)
    return [(slice(2, None), inner, inner), (slice(None, -2), inner, inner),
            (inner, slice(2, None), inner), (inner, slice(None, -2), inner),
            (inner, inner, slice(2, None)), (inner, inner, slice(None, -2))]


def relaxed(padded_field, padded_perm, charge):
    centre = padded_perm[1:-1, 1:-1, 1:-1]
    numerator = charge
    denominator = jnp.zeros_like(charge)
    for window_cut in neighbour_windows():
        face_perm = 0.5 * (centre + padded_perm[window_cut])
        numerator = numerator + face_perm * padded_field[window_cut]
        denominator = denominator + face_perm
    return numerator / denominator


def reference(potential_old, charge, permittivity, owner_cell, green_free, coupling, shifts, occupation, mode_tiles):
    potential_new = relaxed(jnp.pad(potential_old, 1), jnp.pad(permittivity, 1), charge)
    flattened = potential_new.reshape(SLABS, SLAB_CELLS * CROSS * DEPTH)
    orbital_potential = jnp.take_along_axis(flattened, owner_cell.astype(jnp.int32), axis=1)

    def one_energy(free_blocks):
        linkage = complex_product(free_blocks, coupling)
        scaled = free_blocks * orbital_potential[:, None, None, :]
        source = free_blocks + complex_product(scaled, free_blocks)

        def advance(running, members):
            link_now, source_now = members
            updated = complex_product(complex_product(link_now, running), flipped(link_now)) + source_now
            return updated, updated

        start = jnp.zeros((2, ORBITALS, ORBITALS), jnp.float32)
        finished, chained = lax.scan(advance, start, (linkage, source))
        return chained

    greens = lax.map(one_energy, green_free)
    margin_zeros = jnp.zeros((SHIFT_MOST,) + greens.shape[1:], jnp.float32)
    padded_greens = jnp.concatenate([margin_zeros, greens, margin_zeros], axis=0)
    self_energy = jnp.zeros_like(greens)
    for member in range(MODES):
        offset = shifts[member].astype(jnp.int32)
        raised = lax.dynamic_slice_in_dim(padded_greens, (SHIFT_MOST + offset).astype(jnp.int32), ENERGIES, 0)
        lowered = lax.dynamic_slice_in_dim(padded_greens, (SHIFT_MOST - offset).astype(jnp.int32), ENERGIES, 0)
        mixed = occupation[member] * raised + (occupation[member] + 1.0) * lowered
        self_energy = self_energy + mode_tiles[member][None, None, None, :, :] * mixed
    return potential_new, self_energy
```

```python
import functools
import jax
import jax.numpy as jnp
from jax import lax
from jax.experimental import pallas as pl
from jax.experimental.pallas import tpu as pltpu
from jax.sharding import PartitionSpec as P

SHIFT_MOST = 2
VMEM_LIMIT = 56 * 1024 * 1024


def halves(value):
    high = value.astype(jnp.bfloat16)
    low = (value - high.astype(jnp.float32)).astype(jnp.bfloat16)
    return high, low


def left_form(block):
    forms = []
    for real, imag in zip(halves(block[0]), halves(block[1])):
        upper = jnp.concatenate([real, -imag], axis=1)
        lower = jnp.concatenate([imag, real], axis=1)
        forms.append(jnp.concatenate([upper, lower], axis=0))
    return forms


def right_form(block):
    return [
        jnp.concatenate([real, imag], axis=0)
        for real, imag in zip(halves(block[0]), halves(block[1]))
    ]


def right_form_flipped(block):
    return [
        jnp.concatenate([real, imag], axis=1)
        for real, imag in zip(halves(block[0]), halves(block[1]))
    ]


def three_passes(left, right, flipped):
    dims = (((1,), (1 if flipped else 0,)), ((), ()))
    dot = functools.partial(
        lax.dot_general, dimension_numbers=dims, preferred_element_type=jnp.float32
    )
    out = dot(left[0], right[0]) + (dot(left[0], right[1]) + dot(left[1], right[0]))
    width = out.shape[0] // 2
    return out[:width], out[width:]


def product(former, latter):
    return three_passes(left_form(former), right_form(latter), False)


def sandwich(link, inner):
    half_way = product(link, inner)
    return three_passes(left_form(half_way), right_form_flipped(link), True)


def added(first, second):
    return first[0] + second[0], first[1] + second[1]


def pair_of(ref, *where):
    return ref[(*where, 0)], ref[(*where, 1)]


def put(ref, value, *where):
    ref[(*where, 0)] = value[0]
    ref[(*where, 1)] = value[1]


def call(kernel, out_shapes, *operands, **more):
    return pl.pallas_call(
        kernel,
        out_shape=out_shapes,
        compiler_params=pltpu.CompilerParams(vmem_limit_bytes=VMEM_LIMIT),
        **more,
    )(*operands)


def shape(*dims):
    return jax.ShapeDtypeStruct(dims, jnp.float32)


def linkage_kernel(free, coupling, link, whole_map):
    count = free.shape[0]
    total = None
    for slab in range(count):
        now = product(pair_of(free, slab), pair_of(coupling, slab))
        put(link, now, slab)
        total = now if total is None else product(now, total)
    put(whole_map, total)


def source_of(free, potential, slab):
    block = pair_of(free, slab)
    row = potential[slab : slab + 1, :]
    scaled = (block[0] * row, block[1] * row)
    return added(block, product(scaled, block))


def source_kernel(free, link, potential, source, whole_source):
    count = free.shape[0]
    state = None
    for slab in range(count):
        now = source_of(free, potential, slab)
        put(source, now, slab)
        state = now if state is None else added(sandwich(pair_of(link, slab), state), now)
    put(whole_source, state)


def hop_kernel(whole_map, whole_source, carried, out):
    put(out, added(sandwich(pair_of(whole_map), pair_of(carried)), pair_of(whole_source)))


def neighbour_kernel(free_near, free_far, coupling, potential, link, source):
    potential_row = potential[0]
    for which, free in enumerate((free_near, free_far)):
        block = pair_of(free, 0)
        put(link, product(block, pair_of(coupling, 0)), which, 0)
        scaled = (block[0] * potential_row, block[1] * potential_row)
        put(source, added(block, product(scaled, block)), which, 0)


def own_greens_kernel(link, source, carried, greens, state):
    @pl.when(pl.program_id(0) == 0)
    def _():
        state[...] = carried[...]

    now = added(sandwich(pair_of(link, 0), pair_of(state)), pair_of(source, 0))
    put(state, now)
    put(greens, now, 0)


def mixing_kernel(link, source, near, far, own, weights, here, there, state):
    @pl.when(pl.program_id(0) == 0)
    def _():
        state[0] = near[...]
        state[1] = far[...]

    near_now = added(sandwich(pair_of(link, 0, 0), pair_of(state, 0)), pair_of(source, 0, 0))
    far_now = added(sandwich(pair_of(link, 1, 0), pair_of(state, 1)), pair_of(source, 1, 0))
    put(state, near_now, 0)
    put(state, far_now, 1)
    by_one, by_two = weights[0], weights[1]
    for part in range(2):
        here[0, part] = by_one * near_now[part] + by_two * far_now[part]
        there[0, part] = by_one * own[0, part] + by_two * near_now[part]


def relaxed(field, perm, charge, halos):
    numerator = charge
    denominator = jnp.zeros_like(charge)
    for dim in range(3):
        length = charge.shape[dim]
        before, after = halos[dim]
        for side in range(2):
            sides = []
            for which, array in enumerate((field, perm)):
                if side == 0:
                    kept = lax.slice_in_dim(array, 1, length, axis=dim)
                    parts = [kept, after[which]]
                else:
                    kept = lax.slice_in_dim(array, 0, length - 1, axis=dim)
                    parts = [before[which], kept]
                sides.append(jnp.concatenate(parts, axis=dim))
            face = 0.5 * (perm + sides[1])
            numerator = numerator + face * sides[0]
            denominator = denominator + face
    return numerator / denominator


def halo_planes(stacked, axis, dim):
    peers, length = lax.axis_size(axis), stacked.shape[dim]
    up = [(i, i + 1) for i in range(peers - 1)]
    down = [(j, i) for i, j in up]
    last = lax.slice_in_dim(stacked, length - 1, length, axis=dim)
    first = lax.slice_in_dim(stacked, 0, 1, axis=dim)
    return lax.ppermute(last, axis, up), lax.ppermute(first, axis, down)


def orbital_values(potential_new, owner_cell):
    slab_count, _ = owner_cell.shape
    cells, rows, depth = potential_new.shape
    cells = cells // slab_count
    cross = rows * lax.axis_size("energy")
    first = owner_cell // (cross * depth)
    second = (owner_cell // depth) % cross - lax.axis_index("energy") * rows
    third = owner_cell % depth
    mine = (second >= 0) & (second < rows)
    row = jnp.where(mine, first * rows + second, -1)
    table = potential_new.reshape(slab_count, 1, cells * rows, depth)
    row_ids = lax.broadcasted_iota(jnp.int32, (1, 1, cells * rows, 1), 2)
    lane_ids = lax.broadcasted_iota(jnp.int32, (1, 1, 1, depth), 3)
    hit = (row[:, :, None, None] == row_ids) & (third[:, :, None, None] == lane_ids)
    values = jnp.sum(jnp.where(hit, table, 0.0), axis=(2, 3))
    return lax.psum(values, "energy")


def per_device(
    potential_old,
    charge,
    permittivity,
    owner_cell,
    green_free,
    coupling,
    shifts,
    occupation,
    mode_tiles,
):
    energies, peers = lax.axis_size("energy"), lax.axis_size("slab")
    free = green_free[0]
    count, _, width, _ = free.shape

    near_pairs = [(e, e + 1 if e % 2 else e - 1) for e in range(energies)]
    far_pairs = [(e, e - 2 if e % 2 else e + 2) for e in range(energies)]
    near_pairs = [(a, b) for a, b in near_pairs if 0 <= b < energies]
    far_pairs = [(a, b) for a, b in far_pairs if 0 <= b < energies]
    twin_pairs = [(e, e ^ 1) for e in range(energies)]

    stacked = jnp.stack([potential_old, permittivity])
    slab_halo = halo_planes(stacked, "slab", 1)
    energy_halo = halo_planes(stacked, "energy", 2)
    edge = jnp.zeros((2, *charge.shape[:2], 1), jnp.float32)
    potential_new = relaxed(
        potential_old, permittivity, charge, (slab_halo, energy_halo, (edge, edge))
    )
    orbital_potential = orbital_values(potential_new, owner_cell)

    free_near = lax.ppermute(free, "energy", near_pairs)
    free_far = lax.ppermute(free, "energy", far_pairs)

    link, whole_map = call(
        linkage_kernel, (shape(count, 2, width, width), shape(2, width, width)), free, coupling
    )
    source, whole_source = call(
        source_kernel,
        (shape(count, 2, width, width), shape(2, width, width)),
        free,
        link,
        orbital_potential,
    )

    onward = [(i, i + 1) for i in range(peers - 1)]
    leaving = whole_source
    for _ in range(peers - 2):
        carried = lax.ppermute(leaving, "slab", onward)
        leaving = call(hop_kernel, shape(2, width, width), whole_map, whole_source, carried)

    def both(pairs):
        return [(a * peers + i, b * peers + j) for a, b in pairs for i, j in onward]

    carried = lax.ppermute(leaving, "slab", onward)
    carried_near = lax.ppermute(leaving, ("energy", "slab"), both(near_pairs))
    carried_far = lax.ppermute(leaving, ("energy", "slab"), both(far_pairs))

    block = pl.BlockSpec((1, 2, width, width), lambda s: (s, 0, 0, 0))
    two_blocks = pl.BlockSpec((2, 1, 2, width, width), lambda s: (0, s, 0, 0, 0))
    one_state = pl.BlockSpec((2, width, width), lambda s: (0, 0, 0))
    greens = call(
        own_greens_kernel,
        shape(count, 2, width, width),
        link,
        source,
        carried,
        grid=(count,),
        in_specs=[block, block, one_state],
        out_specs=block,
        scratch_shapes=[pltpu.VMEM((2, width, width), jnp.float32)],
    )
    link_beside, source_beside = call(
        neighbour_kernel,
        (shape(2, count, 2, width, width), shape(2, count, 2, width, width)),
        free_near,
        free_far,
        coupling,
        orbital_potential.reshape(count, 1, width),
        grid=(count,),
        in_specs=[block, block, block, pl.BlockSpec((1, 1, width), lambda s: (s, 0, 0))],
        out_specs=(two_blocks, two_blocks),
    )

    levels = jnp.arange(1, SHIFT_MOST + 1, dtype=jnp.int32)
    matches = (shifts[None, :] == levels[:, None]).astype(jnp.float32)
    lowered = (1 - lax.axis_index("energy") % 2).astype(jnp.float32)
    factors = matches * (occupation + lowered)[None, :]
    weights = jnp.sum(factors[:, :, None, None] * mode_tiles[None], axis=1)

    here, there = call(
        mixing_kernel,
        (shape(count, 2, width, width), shape(count, 2, width, width)),
        link_beside,
        source_beside,
        carried_near,
        carried_far,
        greens,
        weights,
        grid=(count,),
        in_specs=[two_blocks, two_blocks, one_state, one_state, block, one_state],
        out_specs=(block, block),
        scratch_shapes=[pltpu.VMEM((2, 2, width, width), jnp.float32)],
    )
    self_energy = here + lax.ppermute(there, "energy", twin_pairs)
    return potential_new, self_energy[None]


def solution(mesh):
    in_specs = (
        P("slab", "energy", None),
        P("slab", "energy", None),
        P("slab", "energy", None),
        P("slab", None),
        P("energy", "slab", None, None, None),
        P("slab", None, None, None),
        P(),
        P(),
        P(),
    )
    out_specs = (P("slab", "energy", None), P("energy", "slab", None, None, None))
    return jax.shard_map(
        per_device, mesh=mesh, in_specs=in_specs, out_specs=out_specs, check_vma=False
    )
```

```python
import functools
import jax
import jax.numpy as jnp
from jax import lax
from jax.experimental import pallas as pl
from jax.experimental.pallas import tpu as pltpu
from jax.sharding import PartitionSpec as P

VMEM_LIMIT = 56 * 1024 * 1024


def halves(value):
    high = value.astype(jnp.bfloat16)
    low = (value - high.astype(jnp.float32)).astype(jnp.bfloat16)
    return high, low


def left_form(block):
    forms = []
    for real, imag in zip(halves(block[0]), halves(block[1])):
        upper = jnp.concatenate([real, -imag], axis=1)
        lower = jnp.concatenate([imag, real], axis=1)
        forms.append(jnp.concatenate([upper, lower], axis=0))
    return forms


def right_form(block, axis=0):
    return [
        jnp.concatenate([real, imag], axis=axis)
        for real, imag in zip(halves(block[0]), halves(block[1]))
    ]


def three_passes(left, right, flipped):
    dims = (((1,), (1 if flipped else 0,)), ((), ()))
    dot = functools.partial(
        lax.dot_general, dimension_numbers=dims, preferred_element_type=jnp.float32
    )
    out = dot(left[0], right[0]) + (dot(left[0], right[1]) + dot(left[1], right[0]))
    width = out.shape[0] // 2
    return out[:width], out[width:]


def row_blocks(block, count=2):
    rows = block[0].shape[0] // count
    return [
        (block[0][i * rows : (i + 1) * rows], block[1][i * rows : (i + 1) * rows])
        for i in range(count)
    ]


def stacked_rows(blocks):
    return tuple(jnp.concatenate([b[part] for b in blocks], axis=0) for part in range(2))


def product(former, latter):
    right = right_form(latter)
    return stacked_rows(
        [three_passes(left_form(rows), right, False) for rows in row_blocks(former)]
    )


def sandwich(link, inner):
    right, outer = right_form(inner), right_form(link, 1)
    half_way = [three_passes(left_form(rows), right, False) for rows in row_blocks(link)]
    return stacked_rows([three_passes(left_form(rows), outer, True) for rows in half_way])


def added(first, second):
    return first[0] + second[0], first[1] + second[1]


def pair_of(ref, *where):
    return ref[(*where, 0)], ref[(*where, 1)]


def put(ref, value, *where):
    ref[(*where, 0)] = value[0]
    ref[(*where, 1)] = value[1]


def call(kernel, out_shapes, *operands, **more):
    return pl.pallas_call(
        kernel,
        out_shape=out_shapes,
        compiler_params=pltpu.CompilerParams(vmem_limit_bytes=VMEM_LIMIT),
        **more,
    )(*operands)


def shape(*dims):
    return jax.ShapeDtypeStruct(dims, jnp.float32)


def gather_kernel(rows, field, perm, charge, before, after, key, lane, out):
    total, depth = charge.shape
    count = key.shape[0]
    height = total // count
    row_ids = lax.broadcasted_iota(jnp.int32, (total, depth), 0) % rows
    lane_ids = lax.broadcasted_iota(jnp.int32, (total, depth), 1)

    def neighbours(inner, first, last):
        down = jnp.concatenate([first, inner[:-rows]], axis=0)
        up = jnp.concatenate([inner[rows:], last], axis=0)
        left = jnp.where(lane_ids == 0, 0.0, pltpu.roll(inner, 1, axis=1))
        right = jnp.where(lane_ids == depth - 1, 0.0, pltpu.roll(inner, depth - 1, axis=1))
        low = jnp.where(row_ids == 0, 0.0, pltpu.roll(inner, 1, axis=0))
        high = jnp.where(row_ids == rows - 1, 0.0, pltpu.roll(inner, total - 1, axis=0))
        return (down + up) + (left + right) + (low + high)

    first, last = (before[0], before[1]), (after[0], after[1])
    field_now, perm_now = field[...], perm[...]
    both = perm_now * field_now
    own = [
        charge[...],
        perm_now,
        neighbours(field_now, first[0], last[0]),
        neighbours(both, first[0] * first[1], last[0] * last[1]),
        neighbours(perm_now, first[1], last[1]),
    ]
    beside = [jnp.zeros_like(both), jnp.zeros_like(both), field_now, both, perm_now]
    kinds = len(own)
    places = lax.broadcasted_iota(jnp.int32, (2 * height, key.shape[2]), 0)
    for slab in range(count):
        cut = slice(slab * height, (slab + 1) * height)
        table = jnp.concatenate(
            [
                jnp.concatenate([t[cut] for t in own], axis=1),
                jnp.concatenate([t[cut] for t in beside], axis=1),
            ],
            axis=0,
        ).T
        high, rest = halves(table)
        middle = rest.astype(jnp.float32)
        lowest = ((table - high.astype(jnp.float32)) - middle).astype(jnp.bfloat16)
        hit = jnp.where(places == key[slab], 1.0, 0.0).astype(jnp.bfloat16)
        found = jnp.dot(
            jnp.concatenate([high, rest, lowest], axis=1),
            jnp.concatenate([hit, hit, hit], axis=0),
            preferred_element_type=jnp.float32,
        )
        depths = lax.broadcasted_iota(jnp.int32, (depth, key.shape[2]), 0)
        here = depths == lane[slab]
        for kind in range(kinds):
            part = found[kind * depth : (kind + 1) * depth]
            out[kind, slab : slab + 1, :] = jnp.sum(
                jnp.where(here, part, 0.0), axis=0, keepdims=True
            )


def potential_of(sums, slab):
    charge, perm, fields, both, perms = (sums[k, slab : slab + 1, :] for k in range(5))
    return (charge + 0.5 * (perm * fields + both)) / (3.0 * perm + 0.5 * perms)


def source_of(block, potential):
    scaled = (block[0] * potential, block[1] * potential)
    return added(block, product(scaled, block))


def linkage_kernel(free, coupling, link, whole_map):
    count = free.shape[0]
    links = []
    for slab in range(count):
        links.append(product(pair_of(free, slab), pair_of(coupling, slab)))
        put(link, links[-1], slab)
    while len(links) > 1:
        paired = [product(b, a) for a, b in zip(links[0::2], links[1::2])]
        links = paired + links[len(paired) * 2 :]
    put(whole_map, links[0])


def source_kernel(free, link, sums, source, whole_source):
    count = free.shape[0]
    state = None
    for slab in range(count):
        now = source_of(pair_of(free, slab), potential_of(sums, slab))
        put(source, now, slab)
        state = now if state is None else added(sandwich(pair_of(link, slab), state), now)
    put(whole_source, state)


def hop_kernel(whole_map, whole_source, carried, out):
    put(out, added(sandwich(pair_of(whole_map), pair_of(carried)), pair_of(whole_source)))


def beside_kernel(free, coupling, sums, link, source):
    for slab in range(free.shape[0]):
        block = pair_of(free, slab)
        put(link, product(block, pair_of(coupling, slab)), slab)
        put(source, source_of(block, potential_of(sums, slab)), slab)


def greens_kernel(link, source, carried, greens, state):
    @pl.when(pl.program_id(0) == 0)
    def _():
        state[...] = carried[...]

    now = added(sandwich(pair_of(link, 0), pair_of(state)), pair_of(source, 0))
    put(state, now)
    put(greens, now, 0)


def mixing_kernel(pick, link, source, carried, own, first, weights, here, there, state):
    @pl.when(pl.program_id(0) == 0)
    def _():
        state[...] = carried[...]

    second = added(sandwich(pair_of(link, 0), pair_of(state)), pair_of(source, 0))
    put(state, second)
    for part in range(2):
        first_now = first[0, part]
        here[0, part] = weights[0] * first_now + weights[1] * second[part]
        picked = jnp.where(pick[0] == 0, first_now, second[part])
        there[0, part] = weights[2] * own[0, part] + weights[3] * picked


def relaxed(field, perm, charge, halos):
    numerator = charge
    denominator = jnp.zeros_like(charge)
    for dim in range(3):
        length = charge.shape[dim]
        before, after = halos[dim]
        for side in range(2):
            sides = []
            for which, array in enumerate((field, perm)):
                if side == 0:
                    kept = lax.slice_in_dim(array, 1, length, axis=dim)
                    parts = [kept, after[which]]
                else:
                    kept = lax.slice_in_dim(array, 0, length - 1, axis=dim)
                    parts = [before[which], kept]
                sides.append(jnp.concatenate(parts, axis=dim))
            face = 0.5 * (perm + sides[1])
            numerator = numerator + face * sides[0]
            denominator = denominator + face
    return numerator / denominator


def halo_planes(stacked, axis, dim):
    peers, length = lax.axis_size(axis), stacked.shape[dim]
    up = [(i, i + 1) for i in range(peers - 1)]
    down = [(j, i) for i, j in up]
    last = lax.slice_in_dim(stacked, length - 1, length, axis=dim)
    first = lax.slice_in_dim(stacked, 0, 1, axis=dim)
    return lax.ppermute(last, axis, up), lax.ppermute(first, axis, down)


def orbital_sums(potential_old, permittivity, charge, slab_halo, owner_cell):
    slab_count, orbitals = owner_cell.shape
    cells, rows, depth = charge.shape
    cells = cells // slab_count
    cross = rows * lax.axis_size("energy")
    first = owner_cell // (cross * depth)
    second = (owner_cell // depth) % cross - lax.axis_index("energy") * rows
    third = owner_cell % depth
    mine = first * rows + second
    low = cells * rows + first * rows
    high = low + rows - 1
    key = jnp.where(second == -1, low, jnp.where(second == rows, high, -1))
    key = jnp.where((second >= 0) & (second < rows), mine, key)
    flat = [array.reshape(-1, depth) for array in (potential_old, permittivity, charge)]
    planes = [plane.reshape(2, rows, depth) for plane in slab_halo]
    sums = call(
        functools.partial(gather_kernel, rows),
        shape(5, slab_count, orbitals),
        *flat,
        *planes,
        key.reshape(slab_count, 1, orbitals),
        third.reshape(slab_count, 1, orbitals),
    )
    return lax.psum(sums, "energy")


def per_device(
    potential_old,
    charge,
    permittivity,
    owner_cell,
    green_free,
    coupling,
    shifts,
    occupation,
    mode_tiles,
):
    energies, peers = lax.axis_size("energy"), lax.axis_size("slab")
    mine = lax.axis_index("energy")
    free = green_free[0]
    count, _, width, _ = free.shape
    whole = shape(2, width, width)
    blocks = shape(count, 2, width, width)

    everyone = range(energies)
    relayed = energies == 8
    if relayed:
        first_pairs = [(e, e ^ 2) for e in everyone]
        second_pairs = [(2, 4), (3, 5), (4, 2), (5, 3)]
        relay_pairs = [(0, 4), (1, 5), (6, 2), (7, 3)]
        turned = (mine // 2) % 2
    else:
        first_pairs = [(e, e - 2) for e in everyone if e >= 2]
        second_pairs = [(e, e + 2) for e in everyone if e + 2 < energies]
        relay_pairs = None
        turned = jnp.zeros_like(mine)
    twin_pairs = [(e, e ^ 1) for e in everyone]

    stacked = jnp.stack([potential_old, permittivity])
    slab_halo = halo_planes(stacked, "slab", 1)
    sums = orbital_sums(potential_old, permittivity, charge, slab_halo, owner_cell)
    link, whole_map = call(linkage_kernel, (blocks, whole), free, coupling)

    stacked, free_out, sums = lax.optimization_barrier((stacked, free, sums))
    source, whole_source = call(source_kernel, (blocks, whole), free, link, sums)
    energy_halo = halo_planes(stacked, "energy", 2)
    edge = jnp.zeros((2, *charge.shape[:2], 1), jnp.float32)
    potential_new = relaxed(
        potential_old, permittivity, charge, (slab_halo, energy_halo, (edge, edge))
    )
    cuts = [free_out[: count // 2], free_out[count // 2 :]]
    free_first = [lax.ppermute(cut, "energy", first_pairs) for cut in cuts]
    if relayed:
        free_second = [lax.ppermute(cut, "energy", relay_pairs) for cut in free_first]
    else:
        free_second = [lax.ppermute(cut, "energy", second_pairs) for cut in cuts]

    onward = [(i, i + 1) for i in range(peers - 1)]
    leaving = whole_source
    for _ in range(peers - 2):
        carried = lax.ppermute(leaving, "slab", onward)
        leaving = call(hop_kernel, whole, whole_map, whole_source, carried)

    def both(pairs):
        return [(a * peers + i, b * peers + j) for a, b in pairs for i, j in onward]

    carried = lax.ppermute(leaving, "slab", onward)
    carried_first = lax.ppermute(leaving, ("energy", "slab"), both(first_pairs))
    carried_second = lax.ppermute(leaving, ("energy", "slab"), both(second_pairs))

    def beside(parts):
        made = []
        for index, part in enumerate(parts):
            cut = slice(index * count // 2, (index + 1) * count // 2)
            half = shape(count // 2, 2, width, width)
            made.append(call(beside_kernel, (half, half), part, coupling[cut], sums[:, cut]))
        return made

    beside_first, beside_second = beside(free_first), beside(free_second)

    block = pl.BlockSpec((1, 2, width, width), lambda s: (s, 0, 0, 0))
    one_state = pl.BlockSpec((2, width, width), lambda s: (0, 0, 0))
    state = pltpu.VMEM((2, width, width), jnp.float32)

    def greens_of(link, source, carried):
        return call(
            greens_kernel,
            shape(*link.shape),
            link,
            source,
            carried,
            grid=(link.shape[0],),
            in_specs=[block, block, one_state],
            out_specs=block,
            scratch_shapes=[state],
        )

    greens = greens_of(link, source, carried)
    greens_first = []
    for part in beside_first:
        greens_first.append(greens_of(*part, carried_first))
        carried_first = greens_first[-1][-1]

    odd = mine % 2
    distance = jnp.array([2, 2, 1, 1], jnp.int32)
    lowered = jnp.stack([turned, 1 - turned, 1 - odd, odd]).astype(jnp.float32)
    factors = (shifts[None, :] == distance[:, None]) * (occupation[None, :] + lowered[:, None])
    weights = jnp.sum(factors[:, :, None, None] * mode_tiles[None], axis=1)
    pick = jnp.reshape(turned ^ odd, (1,)).astype(jnp.int32)

    outputs = []
    half = count // 2
    own_block = [
        pl.BlockSpec((1, 2, width, width), lambda s, first=i * half: (first + s, 0, 0, 0))
        for i in range(2)
    ]
    for index, part in enumerate(beside_second):
        here, there, carried_second = call(
            mixing_kernel,
            (shape(half, 2, width, width), shape(half, 2, width, width), whole),
            pick,
            *part,
            carried_second,
            greens,
            greens_first[index],
            weights,
            grid=(half,),
            in_specs=[
                pl.BlockSpec(memory_space=pltpu.SMEM),
                block,
                block,
                one_state,
                own_block[index],
                block,
                pl.BlockSpec((4, width, width), lambda s: (0, 0, 0)),
            ],
            out_specs=(block, block, one_state),
        )
        outputs.append(here + lax.ppermute(there, "energy", twin_pairs))
    return potential_new, jnp.concatenate(outputs, axis=0)[None]


def solution(mesh):
    in_specs = (
        P("slab", "energy", None),
        P("slab", "energy", None),
        P("slab", "energy", None),
        P("slab", None),
        P("energy", "slab", None, None, None),
        P("slab", None, None, None),
        P(),
        P(),
        P(),
    )
    out_specs = (P("slab", "energy", None), P("energy", "slab", None, None, None))
    return jax.shard_map(
        per_device, mesh=mesh, in_specs=in_specs, out_specs=out_specs, check_vma=False
    )
```

```python
import functools
import jax
import jax.numpy as jnp
from jax import lax
from jax.experimental import pallas as pl
from jax.experimental.pallas import tpu as pltpu
from jax.sharding import PartitionSpec as P

MIB = 1024 * 1024


def halves(value):
    high = value.astype(jnp.bfloat16)
    low = (value - high.astype(jnp.float32)).astype(jnp.bfloat16)
    return high, low


def parts_of(block):
    real, imag = block
    return [halves(real), halves(imag), halves(0.5 * real + 0.5 * imag)]


def left_form(block):
    return [jnp.concatenate([high, high, low], axis=1) for high, low in parts_of(block)]


def right_form(block, axis=0):
    return [jnp.concatenate([high, low, high], axis=axis) for high, low in parts_of(block)]


def three_products(left, right, flipped):
    dims = (((1,), (1 if flipped else 0,)), ((), ()))
    by_real, by_imag, by_mean = (
        lax.dot_general(a, b, dimension_numbers=dims, preferred_element_type=jnp.float32)
        for a, b in zip(left, right)
    )
    return by_real - by_imag, 4.0 * (by_mean - 0.25 * by_real - 0.25 * by_imag)


def product(former, latter):
    return three_products(left_form(former), right_form(latter), False)


def sandwich(link, inner):
    half_way = three_products(left_form(link), right_form(inner), False)
    return three_products(left_form(half_way), right_form(link, 1), True)


def added(first, second):
    return first[0] + second[0], first[1] + second[1]


def pair_of(ref, *where):
    return ref[(*where, 0)], ref[(*where, 1)]


def put(ref, value, *where):
    ref[(*where, 0)] = value[0]
    ref[(*where, 1)] = value[1]


def call(kernel, room, out_shapes, *operands, **more):
    return pl.pallas_call(
        kernel,
        out_shape=out_shapes,
        compiler_params=pltpu.CompilerParams(vmem_limit_bytes=room * MIB),
        **more,
    )(*operands)


def shape(*dims):
    return jax.ShapeDtypeStruct(dims, jnp.float32)


def gather_kernel(rows, peers, mine, field, perm, charge, before, after, owner, out):
    total, depth = charge.shape
    count, orbitals = owner.shape
    height = total // count
    cross = rows * peers
    row_ids = lax.broadcasted_iota(jnp.int32, (total, depth), 0) % rows
    lane_ids = lax.broadcasted_iota(jnp.int32, (total, depth), 1)

    def neighbours(inner, first, last):
        down = jnp.concatenate([first, inner[:-rows]], axis=0)
        up = jnp.concatenate([inner[rows:], last], axis=0)
        left = jnp.where(lane_ids == 0, 0.0, pltpu.roll(inner, 1, axis=1))
        right = jnp.where(lane_ids == depth - 1, 0.0, pltpu.roll(inner, depth - 1, axis=1))
        low = jnp.where(row_ids == 0, 0.0, pltpu.roll(inner, 1, axis=0))
        high = jnp.where(row_ids == rows - 1, 0.0, pltpu.roll(inner, total - 1, axis=0))
        return (down + up) + (left + right) + (low + high)

    first, last = (before[0], before[1]), (after[0], after[1])
    field_now, perm_now = field[...], perm[...]
    both = perm_now * field_now
    own = [
        charge[...],
        perm_now,
        neighbours(field_now, first[0], last[0]),
        neighbours(both, first[0] * first[1], last[0] * last[1]),
        neighbours(perm_now, first[1], last[1]),
    ]
    beside = [jnp.zeros_like(both), jnp.zeros_like(both), field_now, both, perm_now]
    kinds = len(own)
    places = lax.broadcasted_iota(jnp.int32, (2 * height, orbitals), 0)
    depths = lax.broadcasted_iota(jnp.int32, (depth, orbitals), 0)
    first_row = mine[0] * rows
    step = 0
    for slab in range(count):
        cells = owner[slab : slab + 1, :]
        lane, line = cells % depth, cells // depth
        across, along = line % cross - first_row, line // cross * rows
        key = jnp.where(across == rows, height + along + rows - 1, -1)
        key = jnp.where(across == -1, height + along, key)
        key = jnp.where((across >= 0) & (across < rows), along + across, key)
        cut = slice(slab * height, (slab + 1) * height)
        table = jnp.concatenate(
            [
                jnp.concatenate([t[cut] for t in own], axis=1),
                jnp.concatenate([t[cut] for t in beside], axis=1),
            ],
            axis=0,
        ).T
        high, rest = halves(table)
        middle = rest.astype(jnp.float32)
        lowest = ((table - high.astype(jnp.float32)) - middle).astype(jnp.bfloat16)
        hit = jnp.where(places == key, 1.0, 0.0).astype(jnp.bfloat16)
        found = jnp.dot(
            jnp.concatenate([high, rest, lowest], axis=1),
            jnp.concatenate([hit, hit, hit], axis=0),
            preferred_element_type=jnp.float32,
        )
        for kind in range(kinds):
            part = found[kind * depth : (kind + 1) * depth]
            value = jnp.sum(jnp.where(depths == lane, part, 0.0), axis=0, keepdims=True)
            for piece in range(orbitals // depth):
                row = sums_row(kind, slab, count, orbitals // depth) + piece
                out[row : row + 1, :] = value[:, piece * depth : (piece + 1) * depth]
    start = kinds * count * (orbitals // depth)
    for array in (field, perm):
        for end in (0, rows - 1):
            out[start : start + total // rows, :] = array[pl.ds(end, total // rows, stride=rows), :]
            start += total // rows


def sums_row(kind, slab, count, pieces):
    return (kind * count + slab) * pieces


def potential_of(sums, slab, count, orbitals):
    pieces = orbitals // sums.shape[1]

    def value(kind):
        first = sums_row(kind, slab, count, pieces)
        return jnp.concatenate([sums[pl.ds(first + p, 1), :] for p in range(pieces)], axis=1)

    charge, perm, fields, both, perms = (value(kind) for kind in range(5))
    return (charge + 0.5 * (perm * fields + both)) / (3.0 * perm + 0.5 * perms)


def source_of(block, potential):
    scaled = (block[0] * potential, block[1] * potential)
    return added(block, product(scaled, block))


def linkage_kernel(free, coupling, link, whole_map):
    count = free.shape[0]
    links = []
    for slab in range(count):
        links.append(product(pair_of(free, slab), pair_of(coupling, slab)))
        put(link, links[-1], slab)
    while len(links) > 1:
        paired = [product(b, a) for a, b in zip(links[0::2], links[1::2])]
        links = paired + links[len(paired) * 2 :]
    put(whole_map, links[0])


def source_kernel(free, link, sums, source, whole_source):
    count = free.shape[0]
    state = None
    for slab in range(count):
        row = potential_of(sums, slab, count, free.shape[-1])
        now = source_of(pair_of(free, slab), row)
        put(source, now, slab)
        state = now if state is None else added(sandwich(pair_of(link, slab), state), now)
    put(whole_source, state)


def hop_kernel(whole_map, whole_source, carried, out):
    put(out, added(sandwich(pair_of(whole_map), pair_of(carried)), pair_of(whole_source)))


def beside_kernel(first, count, free, coupling, sums, link, source):
    block = pair_of(free, 0)
    put(link, product(block, pair_of(coupling, 0)), 0)
    row = potential_of(sums, first + pl.program_id(0), count, free.shape[-1])
    put(source, source_of(block, row), 0)


def greens_kernel(link, source, carried, greens, state):
    @pl.when(pl.program_id(0) == 0)
    def _():
        state[...] = carried[...]

    now = added(sandwich(pair_of(link, 0), pair_of(state)), pair_of(source, 0))
    put(state, now)
    put(greens, now, 0)


def mixing_kernel(pick, link, source, carried, own, first, weights, here, there, state):
    @pl.when(pl.program_id(0) == 0)
    def _():
        state[...] = carried[...]

    second = added(sandwich(pair_of(link, 0), pair_of(state)), pair_of(source, 0))
    put(state, second)
    for part in range(2):
        first_now = first[0, part]
        here[0, part] = weights[0] * first_now + weights[1] * second[part]
        picked = jnp.where(pick[0] == 0, first_now, second[part])
        there[0, part] = weights[2] * own[0, part] + weights[3] * picked


def relaxed(field, perm, charge, halos):
    numerator = charge
    denominator = jnp.zeros_like(charge)
    for dim in range(3):
        length = charge.shape[dim]
        before, after = halos[dim]
        for side in range(2):
            sides = []
            for which, array in enumerate((field, perm)):
                if side == 0:
                    kept = lax.slice_in_dim(array, 1, length, axis=dim)
                    parts = [kept, after[which]]
                else:
                    kept = lax.slice_in_dim(array, 0, length - 1, axis=dim)
                    parts = [before[which], kept]
                sides.append(jnp.concatenate(parts, axis=dim))
            face = 0.5 * (perm + sides[1])
            numerator = numerator + face * sides[0]
            denominator = denominator + face
    return numerator / denominator


def end_planes(array, dim):
    length = array.shape[dim]
    return (
        lax.slice_in_dim(array, 0, 1, axis=dim),
        lax.slice_in_dim(array, length - 1, length, axis=dim),
    )


def exchanged(payload, head):
    peers, mine = lax.axis_size("energy"), lax.axis_index("energy")
    assert peers & (peers - 1) == 0
    rest = payload[head:]
    before = after = jnp.zeros_like(rest)
    is_head = lax.broadcasted_iota(jnp.int32, payload.shape, 0) < head
    mask = 1
    while mask < peers:
        arrived = lax.ppermute(payload, "energy", [(e, e ^ mask) for e in range(peers)])
        before = jnp.where((mine ^ mask) == mine - 1, arrived[head:], before)
        after = jnp.where((mine ^ mask) == mine + 1, arrived[head:], after)
        payload = jnp.where(is_head, payload + arrived, payload)
        mask = 2 * mask + 1
    return payload, before, after


def per_device(
    potential_old,
    charge,
    permittivity,
    owner_cell,
    green_free,
    coupling,
    shifts,
    occupation,
    mode_tiles,
):
    energies, peers = lax.axis_size("energy"), lax.axis_size("slab")
    mine = lax.axis_index("energy")
    free = green_free[0]
    count, _, width, _ = free.shape
    whole = shape(2, width, width)
    blocks = shape(count, 2, width, width)

    everyone = range(energies)
    relayed = energies == 8
    if relayed:
        first_pairs = [(e, e ^ 2) for e in everyone]
        second_pairs = [(2, 4), (3, 5), (4, 2), (5, 3)]
        relay_pairs = [(0, 4), (1, 5), (6, 2), (7, 3)]
        turned = (mine // 2) % 2
    else:
        first_pairs = [(e, e - 2) for e in everyone if e >= 2]
        second_pairs = [(e, e + 2) for e in everyone if e + 2 < energies]
        relay_pairs = None
        turned = jnp.zeros_like(mine)
    twin_pairs = [(e, e ^ 1) for e in everyone]

    half = count // 2
    cuts = [free[:half], free[half:]]
    free_first = [lax.ppermute(cuts[0], "energy", first_pairs)]

    wire_up = [(i, i + 1) for i in range(peers - 1)]
    wire_down = [(j, i) for i, j in wire_up]
    stacked = jnp.stack([potential_old, permittivity])
    lower, upper = end_planes(stacked, 1)
    wire_before = lax.ppermute(upper, "slab", wire_up)
    wire_after = lax.ppermute(lower, "slab", wire_down)
    link, whole_map = call(linkage_kernel, 24, (blocks, whole), free, coupling)

    cells, rows, depth = charge.shape
    head = 5 * count * (width // depth)
    payload = call(
        functools.partial(gather_kernel, rows, energies),
        16,
        shape(head + 4 * cells, depth),
        jnp.reshape(mine, (1,)),
        *(array.reshape(-1, depth) for array in (potential_old, permittivity, charge)),
        wire_before.reshape(2, rows, depth),
        wire_after.reshape(2, rows, depth),
        owner_cell,
        in_specs=[pl.BlockSpec(memory_space=pltpu.SMEM)]
        + [pl.BlockSpec(memory_space=pltpu.VMEM)] * 6,
    )
    sums, ends_before, ends_after = exchanged(payload, head)

    cut, arrived, sums = lax.optimization_barrier((cuts[1], free_first[0], sums))
    free_first = [arrived, lax.ppermute(cut, "energy", first_pairs)]
    if relayed:
        free_second = [lax.ppermute(part, "energy", relay_pairs) for part in free_first]
    else:
        free_second = [lax.ppermute(part, "energy", second_pairs) for part in (cuts[0], cut)]
    source, whole_source = call(source_kernel, 24, (blocks, whole), free, link, sums)

    ends_before = ends_before.reshape(2, 2, cells, 1, depth)
    ends_after = ends_after.reshape(2, 2, cells, 1, depth)
    edge = jnp.zeros((2, cells, rows, 1), jnp.float32)
    halos = ((wire_before, wire_after), (ends_before[:, 1], ends_after[:, 0]), (edge, edge))
    potential_new = relaxed(potential_old, permittivity, charge, halos)

    leaving = whole_source
    for _ in range(peers - 2):
        carried = lax.ppermute(leaving, "slab", wire_up)
        leaving = call(hop_kernel, 12, whole, whole_map, whole_source, carried)

    def both(pairs):
        return [(a * peers + i, b * peers + j) for a, b in pairs for i, j in wire_up]

    carried = lax.ppermute(leaving, "slab", wire_up)
    carried_first = lax.ppermute(leaving, ("energy", "slab"), both(first_pairs))
    carried_second = lax.ppermute(leaving, ("energy", "slab"), both(second_pairs))

    block = pl.BlockSpec((1, 2, width, width), lambda s: (s, 0, 0, 0))
    one_state = pl.BlockSpec((2, width, width), lambda s: (0, 0, 0))
    own_block = [
        pl.BlockSpec((1, 2, width, width), lambda s, first=i * half: (first + s, 0, 0, 0))
        for i in range(2)
    ]

    def beside(parts):
        made = []
        for index, part in enumerate(parts):
            made.append(
                call(
                    functools.partial(beside_kernel, index * half, count),
                    16,
                    (shape(half, 2, width, width), shape(half, 2, width, width)),
                    part,
                    coupling,
                    sums,
                    grid=(half,),
                    in_specs=[block, own_block[index], pl.BlockSpec(sums.shape, lambda s: (0, 0))],
                    out_specs=(block, block),
                )
            )
        return made

    beside_first, beside_second = beside(free_first), beside(free_second)

    def greens_of(link, source, carried):
        return call(
            greens_kernel,
            16,
            (shape(*link.shape), whole),
            link,
            source,
            carried,
            grid=(link.shape[0],),
            in_specs=[block, block, one_state],
            out_specs=(block, one_state),
        )

    greens, _ = greens_of(link, source, carried)
    greens_first = []
    for part in beside_first:
        made, carried_first = greens_of(*part, carried_first)
        greens_first.append(made)

    odd = mine % 2
    distance = jnp.array([2, 2, 1, 1], jnp.int32)
    lowered = jnp.stack([turned, 1 - turned, 1 - odd, odd]).astype(jnp.float32)
    factors = (shifts[None, :] == distance[:, None]) * (occupation[None, :] + lowered[:, None])
    weights = jnp.sum(factors[:, :, None, None] * mode_tiles[None], axis=1)
    pick = jnp.reshape(turned ^ odd, (1,)).astype(jnp.int32)

    outputs = []
    for index, part in enumerate(beside_second):
        here, there, carried_second = call(
            mixing_kernel,
            20,
            (shape(half, 2, width, width), shape(half, 2, width, width), whole),
            pick,
            *part,
            carried_second,
            greens,
            greens_first[index],
            weights,
            grid=(half,),
            in_specs=[
                pl.BlockSpec(memory_space=pltpu.SMEM),
                block,
                block,
                one_state,
                own_block[index],
                block,
                pl.BlockSpec((4, width, width), lambda s: (0, 0, 0)),
            ],
            out_specs=(block, block, one_state),
        )
        outputs.append(here + lax.ppermute(there, "energy", twin_pairs))
    return potential_new, jnp.concatenate(outputs, axis=0)[None]


def solution(mesh):
    in_specs = (
        P("slab", "energy", None),
        P("slab", "energy", None),
        P("slab", "energy", None),
        P("slab", None),
        P("energy", "slab", None, None, None),
        P("slab", None, None, None),
        P(),
        P(),
        P(),
    )
    out_specs = (P("slab", "energy", None), P("energy", "slab", None, None, None))
    return jax.shard_map(
        per_device, mesh=mesh, in_specs=in_specs, out_specs=out_specs, check_vma=False
    )
```

```python
import functools
import math
import jax
import jax.numpy as jnp
from jax import lax
from jax.experimental import pallas as pl
from jax.experimental.pallas import tpu as pltpu
from jax.sharding import PartitionSpec as P

MIB = 1024 * 1024


def halves(value):
    high = value.astype(jnp.bfloat16)
    low = (value - high.astype(jnp.float32)).astype(jnp.bfloat16)
    return high, low


def parts_of(block):
    real, imag = block
    return [halves(real), halves(imag), halves(0.5 * real + 0.5 * imag)]


def left_form(block):
    return [jnp.concatenate([high, high, low], axis=1) for high, low in parts_of(block)]


def right_form(block, axis=0):
    return [jnp.concatenate([high, low, high], axis=axis) for high, low in parts_of(block)]


def three_products(left, right, flipped):
    dims = (((1,), (1 if flipped else 0,)), ((), ()))
    by_real, by_imag, by_mean = (
        lax.dot_general(a, b, dimension_numbers=dims, preferred_element_type=jnp.float32)
        for a, b in zip(left, right)
    )
    return by_real - by_imag, 4.0 * (by_mean - 0.25 * by_real - 0.25 * by_imag)


def product(former, latter):
    return three_products(left_form(former), right_form(latter), False)


def sandwich(link, inner):
    half_way = three_products(left_form(link), right_form(inner), False)
    return three_products(left_form(half_way), right_form(link, 1), True)


def added(first, second):
    return first[0] + second[0], first[1] + second[1]


def pair_of(ref, *where):
    return ref[(*where, 0)], ref[(*where, 1)]


def put(ref, value, *where):
    ref[(*where, 0)] = value[0]
    ref[(*where, 1)] = value[1]


def call(kernel, room, products, out_shapes, *operands, **more):
    flops = products * 9 * 2 * max(x.shape[-1] for x in operands) ** 3
    moved = sum(4 * math.prod(x.shape) for x in jax.tree.leaves((operands, out_shapes)))
    cost = pl.CostEstimate(flops=flops, bytes_accessed=moved, transcendentals=0)
    return pl.pallas_call(
        kernel,
        out_shape=out_shapes,
        cost_estimate=cost,
        compiler_params=pltpu.CompilerParams(vmem_limit_bytes=room * MIB),
        **more,
    )(*operands)


def shape(*dims):
    return jax.ShapeDtypeStruct(dims, jnp.float32)


def gather_kernel(rows, peers, mine, field, perm, charge, before, after, owner, out):
    total, depth = charge.shape
    count, orbitals = owner.shape
    height = total // count
    cross = rows * peers
    row_ids = lax.broadcasted_iota(jnp.int32, (total, depth), 0) % rows
    lane_ids = lax.broadcasted_iota(jnp.int32, (total, depth), 1)

    def neighbours(inner, first, last):
        down = jnp.concatenate([first, inner[:-rows]], axis=0)
        up = jnp.concatenate([inner[rows:], last], axis=0)
        left = jnp.where(lane_ids == 0, 0.0, pltpu.roll(inner, 1, axis=1))
        right = jnp.where(lane_ids == depth - 1, 0.0, pltpu.roll(inner, depth - 1, axis=1))
        low = jnp.where(row_ids == 0, 0.0, pltpu.roll(inner, 1, axis=0))
        high = jnp.where(row_ids == rows - 1, 0.0, pltpu.roll(inner, total - 1, axis=0))
        return (down + up) + (left + right) + (low + high)

    first, last = (before[0], before[1]), (after[0], after[1])
    field_now, perm_now = field[...], perm[...]
    both = perm_now * field_now
    own = [
        charge[...],
        perm_now,
        neighbours(field_now, first[0], last[0]),
        neighbours(both, first[0] * first[1], last[0] * last[1]),
        neighbours(perm_now, first[1], last[1]),
    ]
    beside = [jnp.zeros_like(both), jnp.zeros_like(both), field_now, both, perm_now]
    kinds = len(own)
    places = lax.broadcasted_iota(jnp.int32, (2 * height, orbitals), 0)
    depths = lax.broadcasted_iota(jnp.int32, (depth, orbitals), 0)
    first_row = mine[0] * rows
    step = 0
    for slab in range(count):
        cells = owner[slab : slab + 1, :]
        lane, line = cells % depth, cells // depth
        across, along = line % cross - first_row, line // cross * rows
        key = jnp.where(across == rows, height + along + rows - 1, -1)
        key = jnp.where(across == -1, height + along, key)
        key = jnp.where((across >= 0) & (across < rows), along + across, key)
        cut = slice(slab * height, (slab + 1) * height)
        table = jnp.concatenate(
            [
                jnp.concatenate([t[cut] for t in own], axis=1),
                jnp.concatenate([t[cut] for t in beside], axis=1),
            ],
            axis=0,
        ).T
        high, rest = halves(table)
        middle = rest.astype(jnp.float32)
        lowest = ((table - high.astype(jnp.float32)) - middle).astype(jnp.bfloat16)
        hit = jnp.where(places == key, 1.0, 0.0).astype(jnp.bfloat16)
        found = jnp.dot(
            jnp.concatenate([high, rest, lowest], axis=1),
            jnp.concatenate([hit, hit, hit], axis=0),
            preferred_element_type=jnp.float32,
        )
        for kind in range(kinds):
            part = found[kind * depth : (kind + 1) * depth]
            value = jnp.sum(jnp.where(depths == lane, part, 0.0), axis=0, keepdims=True)
            for piece in range(orbitals // depth):
                row = sums_row(kind, slab, count, orbitals // depth) + piece
                out[row : row + 1, :] = value[:, piece * depth : (piece + 1) * depth]
    start = kinds * count * (orbitals // depth)
    for array in (field, perm):
        for end in (0, rows - 1):
            out[start : start + total // rows, :] = array[pl.ds(end, total // rows, stride=rows), :]
            start += total // rows


def sums_row(kind, slab, count, pieces):
    return (kind * count + slab) * pieces


def potential_of(sums, slab, count, orbitals):
    pieces = orbitals // sums.shape[1]

    def value(kind):
        first = sums_row(kind, slab, count, pieces)
        return jnp.concatenate([sums[pl.ds(first + p, 1), :] for p in range(pieces)], axis=1)

    charge, perm, fields, both, perms = (value(kind) for kind in range(5))
    return (charge + 0.5 * (perm * fields + both)) / (3.0 * perm + 0.5 * perms)


def source_of(block, potential):
    scaled = (block[0] * potential, block[1] * potential)
    return added(block, product(scaled, block))


def linkage_kernel(free, coupling, link, whole_map):
    count = free.shape[0]
    links = []
    for slab in range(count):
        links.append(product(pair_of(free, slab), pair_of(coupling, slab)))
        put(link, links[-1], slab)
    while len(links) > 1:
        paired = [product(b, a) for a, b in zip(links[0::2], links[1::2])]
        links = paired + links[len(paired) * 2 :]
    put(whole_map, links[0])


def source_kernel(free, link, sums, source, whole_source):
    count = free.shape[0]
    state = None
    for slab in range(count):
        row = potential_of(sums, slab, count, free.shape[-1])
        now = source_of(pair_of(free, slab), row)
        put(source, now, slab)
        state = now if state is None else added(sandwich(pair_of(link, slab), state), now)
    put(whole_source, state)


def hop_kernel(whole_map, whole_source, carried, out):
    put(out, added(sandwich(pair_of(whole_map), pair_of(carried)), pair_of(whole_source)))


def beside_kernel(start, count, parts, *refs):
    frees, (coupling, sums, link, source) = refs[:parts], refs[parts:]
    slab = 0
    for free in frees:
        for place in range(free.shape[0]):
            block = pair_of(free, place)
            put(link, product(block, pair_of(coupling, slab)), slab)
            row = potential_of(sums, start + slab, count, free.shape[-1])
            put(source, source_of(block, row), slab)
            slab += 1


def greens_kernel(link, source, carried, greens, state):
    @pl.when(pl.program_id(0) == 0)
    def _():
        state[...] = carried[...]

    now = added(sandwich(pair_of(link, 0), pair_of(state)), pair_of(source, 0))
    put(state, now)
    put(greens, now, 0)


def mixing_kernel(pick, link, source, carried, own, second, weights, here, there, state):
    @pl.when(pl.program_id(0) == 0)
    def _():
        state[...] = carried[...]

    first = added(sandwich(pair_of(link, 0), pair_of(state)), pair_of(source, 0))
    put(state, first)
    for part in range(2):
        second_now = second[0, part]
        here[0, part] = weights[0] * first[part] + weights[1] * second_now
        picked = jnp.where(pick[0] == 0, first[part], second_now)
        there[0, part] = weights[2] * own[0, part] + weights[3] * picked


def relaxed(field, perm, charge, halos):
    numerator = charge
    denominator = jnp.zeros_like(charge)
    for dim in range(3):
        length = charge.shape[dim]
        before, after = halos[dim]
        for side in range(2):
            sides = []
            for which, array in enumerate((field, perm)):
                if side == 0:
                    kept = lax.slice_in_dim(array, 1, length, axis=dim)
                    parts = [kept, after[which]]
                else:
                    kept = lax.slice_in_dim(array, 0, length - 1, axis=dim)
                    parts = [before[which], kept]
                sides.append(jnp.concatenate(parts, axis=dim))
            face = 0.5 * (perm + sides[1])
            numerator = numerator + face * sides[0]
            denominator = denominator + face
    return numerator / denominator


def end_planes(array, dim):
    length = array.shape[dim]
    return (
        lax.slice_in_dim(array, 0, 1, axis=dim),
        lax.slice_in_dim(array, length - 1, length, axis=dim),
    )


def exchanged(payload, head):
    peers, mine = lax.axis_size("energy"), lax.axis_index("energy")
    assert peers & (peers - 1) == 0
    rest = payload[head:]
    before = after = jnp.zeros_like(rest)
    is_head = lax.broadcasted_iota(jnp.int32, payload.shape, 0) < head
    mask = 1
    while mask < peers:
        arrived = lax.ppermute(payload, "energy", [(e, e ^ mask) for e in range(peers)])
        before = jnp.where((mine ^ mask) == mine - 1, arrived[head:], before)
        after = jnp.where((mine ^ mask) == mine + 1, arrived[head:], after)
        payload = jnp.where(is_head, payload + arrived, payload)
        mask = 2 * mask + 1
    return payload, before, after


def per_device(
    potential_old,
    charge,
    permittivity,
    owner_cell,
    green_free,
    coupling,
    shifts,
    occupation,
    mode_tiles,
):
    energies, peers = lax.axis_size("energy"), lax.axis_size("slab")
    mine = lax.axis_index("energy")
    free = green_free[0]
    count, _, width, _ = free.shape
    whole = shape(2, width, width)
    blocks = shape(count, 2, width, width)

    everyone = range(energies)
    relayed = energies == 8
    if relayed:
        first_pairs = [(e, e ^ 2) for e in everyone]
        second_pairs = [(2, 4), (3, 5), (4, 2), (5, 3)]
        relay_pairs = [(0, 4), (1, 5), (6, 2), (7, 3)]
        turned = (mine // 2) % 2
    else:
        first_pairs = [(e, e - 2) for e in everyone if e >= 2]
        second_pairs = [(e, e + 2) for e in everyone if e + 2 < energies]
        relay_pairs = None
        turned = jnp.zeros_like(mine)
    twin_pairs = [(e, e ^ 1) for e in everyone]

    half = count // 2
    cuts = [free[:1], free[1:half], free[half:]]
    free_first = [lax.ppermute(cuts[0], "energy", first_pairs)]

    wire_up = [(i, i + 1) for i in range(peers - 1)]
    wire_down = [(j, i) for i, j in wire_up]
    stacked = jnp.stack([potential_old, permittivity])
    lower, upper = end_planes(stacked, 1)
    wire_before = lax.ppermute(upper, "slab", wire_up)
    wire_after = lax.ppermute(lower, "slab", wire_down)
    link, whole_map = call(linkage_kernel, 24, 2 * count - 1, (blocks, whole), free, coupling)

    wire_before, wire_after, link, whole_map = lax.optimization_barrier(
        (wire_before, wire_after, link, whole_map)
    )
    cells, rows, depth = charge.shape
    head = 5 * count * (width // depth)
    payload = call(
        functools.partial(gather_kernel, rows, energies),
        16,
        1,
        shape(head + 4 * cells, depth),
        jnp.reshape(mine, (1,)),
        *(array.reshape(-1, depth) for array in (potential_old, permittivity, charge)),
        wire_before.reshape(2, rows, depth),
        wire_after.reshape(2, rows, depth),
        owner_cell,
        in_specs=[pl.BlockSpec(memory_space=pltpu.SMEM)]
        + [pl.BlockSpec(memory_space=pltpu.VMEM)] * 6,
    )
    sums, ends_before, ends_after = exchanged(payload, head)

    first_arrived, middle, sums = lax.optimization_barrier((free_first[0], cuts[1], sums))
    free_first = [first_arrived, lax.ppermute(middle, "energy", first_pairs)]
    relay, relayed_cuts = (relay_pairs, free_first) if relayed else (second_pairs, cuts)
    free_second = [lax.ppermute(part, "energy", relay) for part in relayed_cuts[:2]]
    source, whole_source = call(source_kernel, 24, 3 * count - 2, (blocks, whole), free, link, sums)

    ends_before = ends_before.reshape(2, 2, cells, 1, depth)
    ends_after = ends_after.reshape(2, 2, cells, 1, depth)
    edge = jnp.zeros((2, cells, rows, 1), jnp.float32)
    halos = ((wire_before, wire_after), (ends_before[:, 1], ends_after[:, 0]), (edge, edge))
    potential_new = relaxed(potential_old, permittivity, charge, halos)

    odd = mine % 2
    distance = jnp.array([2, 2, 1, 1], jnp.int32)
    lowered = jnp.stack([turned, 1 - turned, 1 - odd, odd]).astype(jnp.float32)
    factors = (shifts[None, :] == distance[:, None]) * (occupation[None, :] + lowered[:, None])
    weights = jnp.sum(factors[:, :, None, None] * mode_tiles[None], axis=1)
    pick = jnp.reshape(turned ^ odd, (1,)).astype(jnp.int32)

    block = pl.BlockSpec((1, 2, width, width), lambda s: (s, 0, 0, 0))
    one_state = pl.BlockSpec((2, width, width), lambda s: (0, 0, 0))
    own_block = [
        pl.BlockSpec((1, 2, width, width), lambda s, first=i * half: (first + s, 0, 0, 0))
        for i in range(2)
    ]

    def beside(index, parts):
        made = shape(half, 2, width, width)
        whole_spec = pl.BlockSpec((half, 2, width, width), lambda s: (0, 0, 0, 0))
        return call(
            functools.partial(beside_kernel, index * half, count, len(parts)),
            24,
            2 * half,
            (made, made),
            *parts,
            coupling,
            sums,
            grid=(1,),
            in_specs=[pl.BlockSpec(part.shape, lambda s: (0, 0, 0, 0)) for part in parts]
            + [
                pl.BlockSpec((half, 2, width, width), lambda s: (index, 0, 0, 0)),
                pl.BlockSpec(sums.shape, lambda s: (0, 0)),
            ],
            out_specs=(whole_spec, whole_spec),
        )

    def greens_of(link, source, carried):
        return call(
            greens_kernel,
            16,
            2 * link.shape[0],
            (shape(*link.shape), whole),
            link,
            source,
            carried,
            grid=(link.shape[0],),
            in_specs=[block, block, one_state],
            out_specs=(block, one_state),
        )

    leaving = whole_source
    beside_first, beside_second = [None, None], [None, None]
    for hop in range(peers - 2):
        carried = lax.ppermute(leaving, "slab", wire_up)
        if hop == 0:
            free_first[1], last = lax.optimization_barrier((free_first[1], cuts[2]))
            free_first.append(lax.ppermute(last, "energy", first_pairs))
            carried, potential_new, weights, free_first[1], free_second[0] = (
                lax.optimization_barrier(
                    (carried, potential_new, weights, free_first[1], free_second[0])
                )
            )
        if hop == 1:
            beside_first[0] = beside(0, free_first[:2])
            carried, beside_first[0] = lax.optimization_barrier((carried, beside_first[0]))
        leaving = call(hop_kernel, 12, 2, whole, whole_map, whole_source, carried)

    def both(pairs):
        return [(a * peers + i, b * peers + j) for a, b in pairs for i, j in wire_up]

    carried = lax.ppermute(leaving, "slab", wire_up)
    carried_second = lax.ppermute(leaving, ("energy", "slab"), both(second_pairs))
    beside_second[0] = beside(0, free_second[:2])
    leaving, last = lax.optimization_barrier((leaving, free_first[2] if relayed else last))
    free_second.append(lax.ppermute(last, "energy", relay))
    beside_first[1] = beside(1, free_first[2:])
    carried, beside_first[1], beside_second[0] = lax.optimization_barrier(
        (carried, beside_first[1], beside_second[0])
    )
    carried_first = lax.ppermute(carried, "energy", first_pairs)
    greens, _ = greens_of(link, source, carried)
    beside_second[1] = beside(1, free_second[2:])
    carried_second, greens = lax.optimization_barrier((carried_second, greens))
    greens_second = []
    for part in beside_second:
        made, carried_second = greens_of(*part, carried_second)
        greens_second.append(made)
    carried_first, greens_second[0], beside_second[1] = lax.optimization_barrier(
        (carried_first, greens_second[0], beside_second[1])
    )

    outputs = []
    for index, part in enumerate(beside_first):
        here, there, carried_first = call(
            mixing_kernel,
            20,
            2 * half,
            (shape(half, 2, width, width), shape(half, 2, width, width), whole),
            pick,
            *part,
            carried_first,
            greens,
            greens_second[index],
            weights,
            grid=(half,),
            in_specs=[
                pl.BlockSpec(memory_space=pltpu.SMEM),
                block,
                block,
                one_state,
                own_block[index],
                block,
                pl.BlockSpec((4, width, width), lambda s: (0, 0, 0)),
            ],
            out_specs=(block, block, one_state),
        )
        if outputs:
            outputs[0], there = lax.optimization_barrier((outputs[0], there))
        outputs.append(here + lax.ppermute(there, "energy", twin_pairs))
    return potential_new, jnp.concatenate(outputs, axis=0)[None]


def solution(mesh):
    in_specs = (
        P("slab", "energy", None),
        P("slab", "energy", None),
        P("slab", "energy", None),
        P("slab", None),
        P("energy", "slab", None, None, None),
        P("slab", None, None, None),
        P(),
        P(),
        P(),
    )
    out_specs = (P("slab", "energy", None), P("energy", "slab", None, None, None))
    return jax.shard_map(
        per_device, mesh=mesh, in_specs=in_specs, out_specs=out_specs, check_vma=False
    )
```

```python
import functools
import math
import jax
import jax.numpy as jnp
from jax import lax
from jax.experimental import pallas as pl
from jax.experimental.pallas import tpu as pltpu
from jax.sharding import PartitionSpec as P

MIB = 1024 * 1024


def halves(value):
    high = value.astype(jnp.bfloat16)
    low = (value - high.astype(jnp.float32)).astype(jnp.bfloat16)
    return high, low


def parts_of(block):
    real, imag = block
    return [halves(real), halves(imag), halves(0.5 * real + 0.5 * imag)]


def left_form(block):
    return [jnp.concatenate([high, high, low], axis=1) for high, low in parts_of(block)]


def right_form(block, axis=0):
    return [jnp.concatenate([high, low, high], axis=axis) for high, low in parts_of(block)]


def three_products(left, right, flipped):
    dims = (((1,), (1 if flipped else 0,)), ((), ()))
    by_real, by_imag, by_mean = (
        lax.dot_general(a, b, dimension_numbers=dims, preferred_element_type=jnp.float32)
        for a, b in zip(left, right)
    )
    return by_real - by_imag, 4.0 * (by_mean - 0.25 * by_real - 0.25 * by_imag)


def product(former, latter):
    return three_products(left_form(former), right_form(latter), False)


def sandwich(link, inner):
    half_way = three_products(left_form(link), right_form(inner), False)
    return three_products(left_form(half_way), right_form(link, 1), True)


def added(first, second):
    return first[0] + second[0], first[1] + second[1]


def pair_of(ref, *where):
    return ref[(*where, 0)], ref[(*where, 1)]


def put(ref, value, *where):
    ref[(*where, 0)] = value[0]
    ref[(*where, 1)] = value[1]


def call(kernel, room, products, out_shapes, *operands, **more):
    flops = products * 9 * 2 * max(x.shape[-1] for x in operands) ** 3
    moved = sum(4 * math.prod(x.shape) for x in jax.tree.leaves((operands, out_shapes)))
    cost = pl.CostEstimate(flops=flops, bytes_accessed=moved, transcendentals=0)
    return pl.pallas_call(
        kernel,
        out_shape=out_shapes,
        cost_estimate=cost,
        compiler_params=pltpu.CompilerParams(vmem_limit_bytes=room * MIB),
        **more,
    )(*operands)


def shape(*dims):
    return jax.ShapeDtypeStruct(dims, jnp.float32)


def gather_kernel(rows, peers, mine, field, perm, charge, before, after, owner, out):
    total, depth = charge.shape
    count, orbitals = owner.shape
    height = total // count
    cross = rows * peers
    row_ids = lax.broadcasted_iota(jnp.int32, (total, depth), 0) % rows
    lane_ids = lax.broadcasted_iota(jnp.int32, (total, depth), 1)

    def neighbours(inner, first, last):
        down = jnp.concatenate([first, inner[:-rows]], axis=0)
        up = jnp.concatenate([inner[rows:], last], axis=0)
        left = jnp.where(lane_ids == 0, 0.0, pltpu.roll(inner, 1, axis=1))
        right = jnp.where(lane_ids == depth - 1, 0.0, pltpu.roll(inner, depth - 1, axis=1))
        low = jnp.where(row_ids == 0, 0.0, pltpu.roll(inner, 1, axis=0))
        high = jnp.where(row_ids == rows - 1, 0.0, pltpu.roll(inner, total - 1, axis=0))
        return (down + up) + (left + right) + (low + high)

    first, last = (before[0], before[1]), (after[0], after[1])
    field_now, perm_now = field[...], perm[...]
    both = perm_now * field_now
    own = [
        charge[...],
        perm_now,
        neighbours(field_now, first[0], last[0]),
        neighbours(both, first[0] * first[1], last[0] * last[1]),
        neighbours(perm_now, first[1], last[1]),
    ]
    beside = [jnp.zeros_like(both), jnp.zeros_like(both), field_now, both, perm_now]
    kinds = len(own)
    places = lax.broadcasted_iota(jnp.int32, (2 * height, orbitals), 0)
    depths = lax.broadcasted_iota(jnp.int32, (depth, orbitals), 0)
    first_row = mine[0] * rows
    step = 0
    for slab in range(count):
        cells = owner[slab : slab + 1, :]
        lane, line = cells % depth, cells // depth
        across, along = line % cross - first_row, line // cross * rows
        key = jnp.where(across == rows, height + along + rows - 1, -1)
        key = jnp.where(across == -1, height + along, key)
        key = jnp.where((across >= 0) & (across < rows), along + across, key)
        cut = slice(slab * height, (slab + 1) * height)
        table = jnp.concatenate(
            [
                jnp.concatenate([t[cut] for t in own], axis=1),
                jnp.concatenate([t[cut] for t in beside], axis=1),
            ],
            axis=0,
        ).T
        high, rest = halves(table)
        middle = rest.astype(jnp.float32)
        lowest = ((table - high.astype(jnp.float32)) - middle).astype(jnp.bfloat16)
        hit = jnp.where(places == key, 1.0, 0.0).astype(jnp.bfloat16)
        found = jnp.dot(
            jnp.concatenate([high, rest, lowest], axis=1),
            jnp.concatenate([hit, hit, hit], axis=0),
            preferred_element_type=jnp.float32,
        )
        for kind in range(kinds):
            part = found[kind * depth : (kind + 1) * depth]
            value = jnp.sum(jnp.where(depths == lane, part, 0.0), axis=0, keepdims=True)
            for piece in range(orbitals // depth):
                row = sums_row(kind, slab, count, orbitals // depth) + piece
                out[row : row + 1, :] = value[:, piece * depth : (piece + 1) * depth]
    start = kinds * count * (orbitals // depth)
    for array in (field, perm):
        for end in (0, rows - 1):
            out[start : start + total // rows, :] = array[pl.ds(end, total // rows, stride=rows), :]
            start += total // rows


def sums_row(kind, slab, count, pieces):
    return (kind * count + slab) * pieces


def potential_of(sums, slab, count, orbitals):
    pieces = orbitals // sums.shape[1]

    def value(kind):
        first = sums_row(kind, slab, count, pieces)
        return jnp.concatenate([sums[pl.ds(first + p, 1), :] for p in range(pieces)], axis=1)

    charge, perm, fields, both, perms = (value(kind) for kind in range(5))
    return (charge + 0.5 * (perm * fields + both)) / (3.0 * perm + 0.5 * perms)


def source_of(block, potential):
    scaled = (block[0] * potential, block[1] * potential)
    return added(block, product(scaled, block))


def copies(pairs, sems):
    made = [pltpu.make_async_copy(a, b, sems.at[i]) for i, (a, b) in enumerate(pairs)]
    for copy in made:
        copy.start()
    return made


def linkage_kernel(free_far, coupling_far, link_far, whole_map, free, coupling, link, here, gone):
    count = free.shape[0]
    pairs = []
    for slab in range(count):
        pairs.append((free_far.at[slab], free.at[slab]))
        pairs.append((coupling_far.at[slab], coupling.at[slab]))
    loads = copies(pairs, here)
    links = []
    for slab in range(count):
        if slab <= count // 2:
            for load in loads[2 * slab : 2 * slab + 2 if slab < count // 2 else None]:
                load.wait()
        links.append(product(pair_of(free, slab), pair_of(coupling, slab)))
        put(link, links[-1], slab)
    while len(links) > 1:
        paired = [product(b, a) for a, b in zip(links[0::2], links[1::2])]
        links = paired + links[len(paired) * 2 :]
    put(whole_map, links[0])
    for store in copies([(link.at[slab], link_far.at[slab]) for slab in range(count)], gone):
        store.wait()


def source_kernel(
    free_far, link_far, sums, source_far, whole_source, free, link, source, here, gone
):
    count = free.shape[0]
    pairs = [(free_far.at[slab], free.at[slab]) for slab in range(count)]
    pairs += [(link_far.at[slab], link.at[slab]) for slab in range(1, count)]
    loads = copies(pairs, here)
    state, stores = None, []
    for slab in range(count):
        if slab <= 1:
            for load in loads[slab : slab + 1 if slab == 0 else None]:
                load.wait()
        row = potential_of(sums, slab, count, free.shape[-1])
        now = source_of(pair_of(free, slab), row)
        put(source, now, slab)
        state = now if state is None else added(sandwich(pair_of(link, slab), state), now)
    put(whole_source, state)
    for store in copies([(source.at[slab], source_far.at[slab]) for slab in range(count)], gone):
        store.wait()


def hop_kernel(here, whole_map, whole_source, arrived, kept, out, kept_out):
    state = []
    for part in range(2):
        before = jnp.zeros_like(arrived[part]) if kept is None else kept[part]
        state.append(jnp.where(here[0] != 0, arrived[part], before))
    put(kept_out, state)
    put(out, added(sandwich(pair_of(whole_map), state), pair_of(whole_source)))


def first_hop_kernel(here, whole_map, whole_source, arrived, out, kept_out):
    hop_kernel(here, whole_map, whole_source, arrived, None, out, kept_out)


def beside_kernel(start, count, parts, *refs):
    frees, (coupling, sums, link, source) = refs[:parts], refs[parts:]
    slab = 0
    for free in frees:
        for place in range(free.shape[0]):
            block = pair_of(free, place)
            put(link, product(block, pair_of(coupling, slab)), slab)
            row = potential_of(sums, start + slab, count, free.shape[-1])
            put(source, source_of(block, row), slab)
            slab += 1


def greens_kernel(link, source, carried, greens, state):
    @pl.when(pl.program_id(0) == 0)
    def _():
        state[...] = carried[...]

    now = added(sandwich(pair_of(link, 0), pair_of(state)), pair_of(source, 0))
    put(state, now)
    put(greens, now, 0)


def mixing_kernel(pick, link, source, carried, own, second, weights, here, there, state):
    @pl.when(pl.program_id(0) == 0)
    def _():
        state[...] = carried[...]

    first = added(sandwich(pair_of(link, 0), pair_of(state)), pair_of(source, 0))
    put(state, first)
    for part in range(2):
        second_now = jnp.where(pick[1] != 0, second[0, part], 0.0)
        here[0, part] = weights[0] * first[part] + weights[1] * second_now
        picked = jnp.where(pick[0] == 0, first[part], second_now)
        there[0, part] = weights[2] * own[0, part] + weights[3] * picked


def relaxed(field, perm, charge, halos):
    numerator = charge
    denominator = jnp.zeros_like(charge)
    for dim in range(3):
        length = charge.shape[dim]
        before, after = halos[dim]
        for side in range(2):
            sides = []
            for which, array in enumerate((field, perm)):
                if side == 0:
                    kept = lax.slice_in_dim(array, 1, length, axis=dim)
                    parts = [kept, after[which]]
                else:
                    kept = lax.slice_in_dim(array, 0, length - 1, axis=dim)
                    parts = [before[which], kept]
                sides.append(jnp.concatenate(parts, axis=dim))
            face = 0.5 * (perm + sides[1])
            numerator = numerator + face * sides[0]
            denominator = denominator + face
    return numerator / denominator


def end_planes(array, dim):
    length = array.shape[dim]
    return (
        lax.slice_in_dim(array, 0, 1, axis=dim),
        lax.slice_in_dim(array, length - 1, length, axis=dim),
    )


def exchanged(payload, head, beside):
    peers, mine = lax.axis_size("energy"), lax.axis_index("energy")
    assert peers & (peers - 1) == 0
    rest = payload[head:]
    before = after = jnp.zeros_like(rest)
    is_head = lax.broadcasted_iota(jnp.int32, payload.shape, 0) < head
    mask = 1
    while mask < peers:
        if mask * 2 > peers // 2:
            payload, beside = lax.optimization_barrier((payload, beside))
        arrived = lax.ppermute(payload, "energy", [(e, e ^ mask) for e in range(peers)])
        before = jnp.where((mine ^ mask) == mine - 1, arrived[head:], before)
        after = jnp.where((mine ^ mask) == mine + 1, arrived[head:], after)
        payload = jnp.where(is_head, payload + arrived, payload)
        mask = 2 * mask + 1
    return payload, before, after, beside


def per_device(
    potential_old,
    charge,
    permittivity,
    owner_cell,
    green_free,
    coupling,
    shifts,
    occupation,
    mode_tiles,
):
    energies, peers = lax.axis_size("energy"), lax.axis_size("slab")
    mine = lax.axis_index("energy")
    free = green_free[0]
    count, _, width, _ = free.shape
    whole = shape(2, width, width)
    blocks = shape(count, 2, width, width)

    everyone = range(energies)
    relayed = energies == 8
    if relayed:
        first_pairs = [(e, e ^ 2) for e in everyone]
        second_pairs = [(2, 4), (3, 5), (4, 2), (5, 3)]
        relay_pairs = [(e, e ^ 4) for e in everyone]
        turned = (mine // 2) % 2
        has_second = jnp.where((mine >= 2) & (mine < 6), 1, 0)
    else:
        first_pairs = [(e, e - 2) for e in everyone if e >= 2]
        second_pairs = [(e, e + 2) for e in everyone if e + 2 < energies]
        relay_pairs = second_pairs
        turned = jnp.zeros_like(mine)
        has_second = jnp.ones_like(mine)
    twin_pairs = [(e, e ^ 1) for e in everyone]

    half = count // 2
    free_first = [lax.ppermute(free[:1], "energy", first_pairs)]

    place = lax.axis_index("slab")
    wire_up = [(i, i + 1) for i in range(peers - 1)]

    def swaps(start):
        pairs = [(i, i + 1) for i in range(start, peers - 1, 2)]
        return pairs + [(j, i) for i, j in pairs]

    stacked = jnp.stack([potential_old, permittivity])
    lower, upper = end_planes(stacked, 1)
    even = place % 2 == 0
    arrived = lax.ppermute(jnp.where(even, upper, lower), "slab", swaps(0))
    crossed = lax.ppermute(jnp.where(even, lower, upper), "slab", swaps(1))
    wire_before = jnp.where(even, crossed, arrived)
    wire_after = jnp.where(even, arrived, crossed)

    cells, rows, depth = charge.shape
    head = 5 * count * (width // depth)
    payload = call(
        functools.partial(gather_kernel, rows, energies),
        16,
        1,
        shape(head + 4 * cells, depth),
        jnp.reshape(mine, (1,)),
        *(array.reshape(-1, depth) for array in (potential_old, permittivity, charge)),
        wire_before.reshape(2, rows, depth),
        wire_after.reshape(2, rows, depth),
        owner_cell,
        in_specs=[pl.BlockSpec(memory_space=pltpu.SMEM)]
        + [pl.BlockSpec(memory_space=pltpu.VMEM)] * 6,
    )
    payload, *at_gather = lax.optimization_barrier((payload, free, coupling))
    far, near = pl.BlockSpec(memory_space=pl.ANY), pl.BlockSpec(memory_space=pltpu.VMEM)
    held = pltpu.VMEM((count, 2, width, width), jnp.float32)
    link, whole_map = call(
        linkage_kernel,
        56,
        2 * count - 1,
        (blocks, whole),
        *at_gather,
        in_specs=[far, far],
        out_specs=(far, near),
        scratch_shapes=[
            held,
            held,
            held,
            pltpu.SemaphoreType.DMA((2 * count,)),
            pltpu.SemaphoreType.DMA((count,)),
        ],
    )
    sums, ends_before, ends_after, (link, whole_map) = exchanged(payload, head, (link, whole_map))

    arrived, free_then, field, perm, sums = lax.optimization_barrier(
        (free_first[0], free, potential_old, permittivity, sums)
    )
    free_first = [arrived, lax.ppermute(free_then[1:2], "energy", first_pairs)]
    free_second = [lax.ppermute(arrived if relayed else free_then[:1], "energy", relay_pairs)]

    def sent_on(part):
        given = free_first[part] if relayed else free_then[part : part + 1]
        free_second.append(lax.ppermute(given, "energy", relay_pairs))

    def sent_after(part, *others):
        tied = lax.optimization_barrier((free_first[part - 1], free_then, *others))
        free_first[part - 1] = tied[0]
        cut = tied[1][part : part + 1]
        free_first.append(lax.ppermute(cut, "energy", first_pairs))
        return tied[2:]

    source, whole_source = call(
        source_kernel,
        56,
        3 * count - 2,
        (blocks, whole),
        free,
        link,
        sums,
        in_specs=[far, far, near],
        out_specs=(far, near),
        scratch_shapes=[
            held,
            held,
            held,
            pltpu.SemaphoreType.DMA((2 * count - 1,)),
            pltpu.SemaphoreType.DMA((count,)),
        ],
    )

    ends_before = ends_before.reshape(2, 2, cells, 1, depth)
    ends_after = ends_after.reshape(2, 2, cells, 1, depth)
    edge = jnp.zeros((2, cells, rows, 1), jnp.float32)
    halos = ((wire_before, wire_after), (ends_before[:, 1], ends_after[:, 0]), (edge, edge))
    potential_new = relaxed(field, perm, charge, halos)

    odd = mine % 2
    distance = jnp.array([2, 2, 1, 1], jnp.int32)
    lowered = jnp.stack([turned, 1 - turned, 1 - odd, odd]).astype(jnp.float32)
    factors = (shifts[None, :] == distance[:, None]) * (occupation[None, :] + lowered[:, None])
    weights = jnp.sum(factors[:, :, None, None] * mode_tiles[None], axis=1)
    pick = jnp.stack([turned ^ odd, has_second]).astype(jnp.int32)

    block = pl.BlockSpec((1, 2, width, width), lambda s: (s, 0, 0, 0))
    one_state = pl.BlockSpec((2, width, width), lambda s: (0, 0, 0))
    own_block = [
        pl.BlockSpec((1, 2, width, width), lambda s, first=i * half: (first + s, 0, 0, 0))
        for i in range(2)
    ]

    def beside(index, parts):
        made = shape(half, 2, width, width)
        whole_spec = pl.BlockSpec((half, 2, width, width), lambda s: (0, 0, 0, 0))
        return call(
            functools.partial(beside_kernel, index * half, count, len(parts)),
            24,
            2 * half,
            (made, made),
            *parts,
            coupling,
            sums,
            grid=(1,),
            in_specs=[pl.BlockSpec(part.shape, lambda s: (0, 0, 0, 0)) for part in parts]
            + [
                pl.BlockSpec((half, 2, width, width), lambda s: (index, 0, 0, 0)),
                pl.BlockSpec(sums.shape, lambda s: (0, 0)),
            ],
            out_specs=(whole_spec, whole_spec),
        )

    def greens_of(room, link, source, carried):
        return call(
            greens_kernel,
            room,
            2 * link.shape[0],
            (shape(*link.shape), whole),
            link,
            source,
            carried,
            grid=(link.shape[0],),
            in_specs=[block, block, one_state],
            out_specs=(block, one_state),
        )

    leaving, kept = whole_source, None
    beside_first, beside_second = [None, None], [None, None]
    flag = pl.BlockSpec(memory_space=pltpu.SMEM)
    for hop in range(1, peers - 1):
        arrived = lax.ppermute(leaving, "slab", swaps((hop - 1) % 2))
        if hop == 1:
            sent_on(1)
            sent_after(2)
            arrived, potential_new, weights, free_first[1], free_second[0] = (
                lax.optimization_barrier(
                    (arrived, potential_new, weights, free_first[1], free_second[0])
                )
            )
        if hop == 2:
            sent_on(2)
            sent_after(3)
            beside_first[0] = beside(0, free_first[:2])
            arrived, beside_first[0], free_first[2], free_second[1] = lax.optimization_barrier(
                (arrived, beside_first[0], free_first[2], free_second[1])
            )
        here = jnp.reshape(place == hop, (1,)).astype(jnp.int32)
        states = (arrived,) if kept is None else (arrived, kept)
        leaving, kept = call(
            first_hop_kernel if kept is None else hop_kernel,
            12,
            2,
            (whole, whole),
            here,
            whole_map,
            whole_source,
            *states,
            in_specs=[flag] + [near] * (2 + len(states)),
            out_specs=(near, near),
        )

    def both(pairs):
        return [(a * peers + i, b * peers + j) for a, b in pairs for i, j in wire_up]

    arrived = lax.ppermute(leaving, "slab", swaps((peers - 2) % 2))
    carried_second = lax.ppermute(leaving, ("energy", "slab"), both(second_pairs))
    beside_second[0] = beside(0, free_second[:2])
    sent_on(3)
    beside_first[1] = beside(1, free_first[2:])
    arrived, beside_first[1], beside_second[0], free_second[2] = lax.optimization_barrier(
        (arrived, beside_first[1], beside_second[0], free_second[2])
    )
    carried = jnp.where(place == peers - 1, arrived, kept)
    carried_first = lax.ppermute(carried, "energy", first_pairs)
    greens, _ = greens_of(56, link, source, carried)
    beside_second[1] = beside(1, free_second[2:])
    carried_second, greens = lax.optimization_barrier((carried_second, greens))
    greens_second = []
    for part in beside_second:
        made, carried_second = greens_of(16, *part, carried_second)
        greens_second.append(made)
    carried_first, greens_second[0] = lax.optimization_barrier((carried_first, greens_second[0]))

    outputs = []
    for index, part in enumerate(beside_first):
        here, there, carried_first = call(
            mixing_kernel,
            20,
            2 * half,
            (shape(half, 2, width, width), shape(half, 2, width, width), whole),
            pick,
            *part,
            carried_first,
            greens,
            greens_second[index],
            weights,
            grid=(half,),
            in_specs=[
                pl.BlockSpec(memory_space=pltpu.SMEM),
                block,
                block,
                one_state,
                own_block[index],
                block,
                pl.BlockSpec((4, width, width), lambda s: (0, 0, 0)),
            ],
            out_specs=(block, block, one_state),
        )
        if outputs:
            outputs[0], there = lax.optimization_barrier((outputs[0], there))
        outputs.append(here + lax.ppermute(there, "energy", twin_pairs))
    return potential_new, jnp.concatenate(outputs, axis=0)[None]


def solution(mesh):
    in_specs = (
        P("slab", "energy", None),
        P("slab", "energy", None),
        P("slab", "energy", None),
        P("slab", None),
        P("energy", "slab", None, None, None),
        P("slab", None, None, None),
        P(),
        P(),
        P(),
    )
    out_specs = (P("slab", "energy", None), P("energy", "slab", None, None, None))
    return jax.shard_map(
        per_device, mesh=mesh, in_specs=in_specs, out_specs=out_specs, check_vma=False
    )
```

```python
import functools
import math
import jax
import jax.numpy as jnp
from jax import lax
from jax.experimental import pallas as pl
from jax.experimental.pallas import tpu as pltpu
from jax.sharding import PartitionSpec as P

MIB = 1024 * 1024


def halves(value):
    high = value.astype(jnp.bfloat16)
    low = (value - high.astype(jnp.float32)).astype(jnp.bfloat16)
    return high, low


def parts_of(block):
    real, imag = block
    return [halves(real), halves(imag), halves(0.5 * real + 0.5 * imag)]


def left_form(block):
    return [jnp.concatenate([high, high, low], axis=1) for high, low in parts_of(block)]


def right_form(block, axis=0):
    return [jnp.concatenate([high, low, high], axis=axis) for high, low in parts_of(block)]


def three_products(left, right, flipped):
    dims = (((1,), (1 if flipped else 0,)), ((), ()))
    by_real, by_imag, by_mean = (
        lax.dot_general(a, b, dimension_numbers=dims, preferred_element_type=jnp.float32)
        for a, b in zip(left, right)
    )
    return by_real - by_imag, 4.0 * (by_mean - 0.25 * by_real - 0.25 * by_imag)


def product(former, latter):
    return three_products(left_form(former), right_form(latter), False)


def sandwich(link, inner):
    half_way = three_products(left_form(link), right_form(inner), False)
    return three_products(left_form(half_way), right_form(link, 1), True)


def added(first, second):
    return first[0] + second[0], first[1] + second[1]


def pair_of(ref, *where):
    return ref[(*where, 0)], ref[(*where, 1)]


def put(ref, value, *where):
    ref[(*where, 0)] = value[0]
    ref[(*where, 1)] = value[1]


def call(kernel, room, products, out_shapes, *operands, **more):
    flops = products * 9 * 2 * max(x.shape[-1] for x in operands) ** 3
    moved = sum(4 * math.prod(x.shape) for x in jax.tree.leaves((operands, out_shapes)))
    cost = pl.CostEstimate(flops=flops, bytes_accessed=moved, transcendentals=0)
    return pl.pallas_call(
        kernel,
        out_shape=out_shapes,
        cost_estimate=cost,
        compiler_params=pltpu.CompilerParams(vmem_limit_bytes=room * MIB),
        **more,
    )(*operands)


def shape(*dims):
    return jax.ShapeDtypeStruct(dims, jnp.float32)


def gather_kernel(rows, peers, mine, field, perm, charge, before, after, owner, out):
    total, depth = charge.shape
    count, orbitals = owner.shape
    height = total // count
    cross = rows * peers
    row_ids = lax.broadcasted_iota(jnp.int32, (total, depth), 0) % rows
    lane_ids = lax.broadcasted_iota(jnp.int32, (total, depth), 1)

    def neighbours(inner, first, last):
        down = jnp.concatenate([first, inner[:-rows]], axis=0)
        up = jnp.concatenate([inner[rows:], last], axis=0)
        left = jnp.where(lane_ids == 0, 0.0, pltpu.roll(inner, 1, axis=1))
        right = jnp.where(lane_ids == depth - 1, 0.0, pltpu.roll(inner, depth - 1, axis=1))
        low = jnp.where(row_ids == 0, 0.0, pltpu.roll(inner, 1, axis=0))
        high = jnp.where(row_ids == rows - 1, 0.0, pltpu.roll(inner, total - 1, axis=0))
        return (down + up) + (left + right) + (low + high)

    first, last = (before[0], before[1]), (after[0], after[1])
    field_now, perm_now = field[...], perm[...]
    both = perm_now * field_now
    own = [
        charge[...],
        perm_now,
        neighbours(field_now, first[0], last[0]),
        neighbours(both, first[0] * first[1], last[0] * last[1]),
        neighbours(perm_now, first[1], last[1]),
    ]
    beside = [jnp.zeros_like(both), jnp.zeros_like(both), field_now, both, perm_now]
    kinds = len(own)
    places = lax.broadcasted_iota(jnp.int32, (2 * height, orbitals), 0)
    depths = lax.broadcasted_iota(jnp.int32, (depth, orbitals), 0)
    first_row = mine[0] * rows
    step = 0
    for slab in range(count):
        cells = owner[slab : slab + 1, :]
        lane, line = cells % depth, cells // depth
        across, along = line % cross - first_row, line // cross * rows
        key = jnp.where(across == rows, height + along + rows - 1, -1)
        key = jnp.where(across == -1, height + along, key)
        key = jnp.where((across >= 0) & (across < rows), along + across, key)
        cut = slice(slab * height, (slab + 1) * height)
        table = jnp.concatenate(
            [
                jnp.concatenate([t[cut] for t in own], axis=1),
                jnp.concatenate([t[cut] for t in beside], axis=1),
            ],
            axis=0,
        ).T
        high, rest = halves(table)
        middle = rest.astype(jnp.float32)
        lowest = ((table - high.astype(jnp.float32)) - middle).astype(jnp.bfloat16)
        hit = jnp.where(places == key, 1.0, 0.0).astype(jnp.bfloat16)
        found = jnp.dot(
            jnp.concatenate([high, rest, lowest], axis=1),
            jnp.concatenate([hit, hit, hit], axis=0),
            preferred_element_type=jnp.float32,
        )
        for kind in range(kinds):
            part = found[kind * depth : (kind + 1) * depth]
            value = jnp.sum(jnp.where(depths == lane, part, 0.0), axis=0, keepdims=True)
            for piece in range(orbitals // depth):
                row = sums_row(kind, slab, count, orbitals // depth) + piece
                out[row : row + 1, :] = value[:, piece * depth : (piece + 1) * depth]
    start = kinds * count * (orbitals // depth)
    for array in (field, perm):
        for end in (0, rows - 1):
            out[start : start + total // rows, :] = array[pl.ds(end, total // rows, stride=rows), :]
            start += total // rows


def sums_row(kind, slab, count, pieces):
    return (kind * count + slab) * pieces


def potential_of(sums, slab, count, orbitals):
    pieces = orbitals // sums.shape[1]

    def value(kind):
        first = sums_row(kind, slab, count, pieces)
        return jnp.concatenate([sums[pl.ds(first + p, 1), :] for p in range(pieces)], axis=1)

    charge, perm, fields, both, perms = (value(kind) for kind in range(5))
    return (charge + 0.5 * (perm * fields + both)) / (3.0 * perm + 0.5 * perms)


def source_of(block, potential):
    scaled = (block[0] * potential, block[1] * potential)
    return added(block, product(scaled, block))


def copies(pairs, sems):
    made = [pltpu.make_async_copy(a, b, sems.at[i]) for i, (a, b) in enumerate(pairs)]
    for copy in made:
        copy.start()
    return made


def linkage_kernel(free_far, coupling_far, link_far, whole_map, free, coupling, link, here, gone):
    count = free.shape[0]
    pairs = []
    for slab in range(count):
        pairs.append((free_far.at[slab], free.at[slab]))
        pairs.append((coupling_far.at[slab], coupling.at[slab]))
    loads = copies(pairs, here)
    links, stores = [], []
    for slab in range(count):
        for load in loads[2 * slab : 2 * slab + 2]:
            load.wait()
        links.append(product(pair_of(free, slab), pair_of(coupling, slab)))
        put(link, links[-1], slab)
        stores += copies([(link.at[slab], link_far.at[slab])], gone.at[slab : slab + 1])
    while len(links) > 1:
        paired = [product(b, a) for a, b in zip(links[0::2], links[1::2])]
        links = paired + links[len(paired) * 2 :]
    put(whole_map, links[0])
    for store in stores:
        store.wait()


def source_kernel(
    free_far, link_far, sums, source_far, whole_source, free, link, source, here, gone
):
    count = free.shape[0]
    pairs = [(free_far.at[slab], free.at[slab]) for slab in range(count)]
    pairs += [(link_far.at[slab], link.at[slab]) for slab in range(1, count)]
    loads = copies(pairs, here)
    sources, stores = [], []
    for slab in range(count):
        loads[slab].wait()
        row = potential_of(sums, slab, count, free.shape[-1])
        sources.append(source_of(pair_of(free, slab), row))
        put(source, sources[-1], slab)
        stores += copies([(source.at[slab], source_far.at[slab])], gone.at[slab : slab + 1])
    for load in loads[count:]:
        load.wait()
    state = sources[0]
    for slab in range(1, count):
        state = added(sandwich(pair_of(link, slab), state), sources[slab])
    put(whole_source, state)
    for store in stores:
        store.wait()


def hop_kernel(whole_map, whole_source, carried, out):
    put(out, added(sandwich(pair_of(whole_map), pair_of(carried)), pair_of(whole_source)))


def beside_kernel(start, count, parts, *refs):
    frees, (coupling, sums, link, source) = refs[:parts], refs[parts:]
    slab = 0
    for free in frees:
        for place in range(free.shape[0]):
            block = pair_of(free, place)
            put(link, product(block, pair_of(coupling, slab)), slab)
            row = potential_of(sums, start + slab, count, free.shape[-1])
            put(source, source_of(block, row), slab)
            slab += 1


def greens_kernel(link, source, carried, greens, state):
    @pl.when(pl.program_id(0) == 0)
    def _():
        state[...] = carried[...]

    now = added(sandwich(pair_of(link, 0), pair_of(state)), pair_of(source, 0))
    put(state, now)
    put(greens, now, 0)


def mixing_kernel(pick, link, source, carried, own, second, weights, here, there, state):
    @pl.when(pl.program_id(0) == 0)
    def _():
        state[...] = carried[...]

    first = added(sandwich(pair_of(link, 0), pair_of(state)), pair_of(source, 0))
    put(state, first)
    for part in range(2):
        second_now = jnp.where(pick[1] != 0, second[0, part], 0.0)
        here[0, part] = weights[0] * first[part] + weights[1] * second_now
        picked = jnp.where(pick[0] == 0, first[part], second_now)
        there[0, part] = weights[2] * own[0, part] + weights[3] * picked


def relaxed(field, perm, charge, halos):
    numerator = charge
    denominator = jnp.zeros_like(charge)
    for dim in range(3):
        length = charge.shape[dim]
        before, after = halos[dim]
        for side in range(2):
            sides = []
            for which, array in enumerate((field, perm)):
                if side == 0:
                    kept = lax.slice_in_dim(array, 1, length, axis=dim)
                    parts = [kept, after[which]]
                else:
                    kept = lax.slice_in_dim(array, 0, length - 1, axis=dim)
                    parts = [before[which], kept]
                sides.append(jnp.concatenate(parts, axis=dim))
            face = 0.5 * (perm + sides[1])
            numerator = numerator + face * sides[0]
            denominator = denominator + face
    return numerator / denominator


def end_planes(array, dim):
    length = array.shape[dim]
    return (
        lax.slice_in_dim(array, 0, 1, axis=dim),
        lax.slice_in_dim(array, length - 1, length, axis=dim),
    )


def exchanged(payload, head, beside):
    peers, mine = lax.axis_size("energy"), lax.axis_index("energy")
    assert peers & (peers - 1) == 0
    rest = payload[head:]
    before = after = jnp.zeros_like(rest)
    is_head = lax.broadcasted_iota(jnp.int32, payload.shape, 0) < head
    mask = 1
    while mask < peers:
        if mask * 2 > peers // 2:
            payload, beside = lax.optimization_barrier((payload, beside))
        arrived = lax.ppermute(payload, "energy", [(e, e ^ mask) for e in range(peers)])
        before = jnp.where((mine ^ mask) == mine - 1, arrived[head:], before)
        after = jnp.where((mine ^ mask) == mine + 1, arrived[head:], after)
        payload = jnp.where(is_head, payload + arrived, payload)
        mask = 2 * mask + 1
    return payload, before, after, beside


def per_device(
    potential_old,
    charge,
    permittivity,
    owner_cell,
    green_free,
    coupling,
    shifts,
    occupation,
    mode_tiles,
):
    energies, peers = lax.axis_size("energy"), lax.axis_size("slab")
    mine = lax.axis_index("energy")
    free = green_free[0]
    count, _, width, _ = free.shape
    whole = shape(2, width, width)
    blocks = shape(count, 2, width, width)

    everyone = range(energies)
    relayed = energies == 8
    if relayed:
        first_pairs = [(e, e ^ 2) for e in everyone]
        second_pairs = [(2, 4), (3, 5), (4, 2), (5, 3)]
        relay_pairs = [(e, e ^ 4) for e in everyone]
        around_pairs = [(2, 6), (3, 7), (4, 0), (5, 1)]
        back_pairs = [(6, 4), (7, 5), (0, 2), (1, 3)]
        turned = (mine // 2) % 2
        has_second = jnp.where((mine >= 2) & (mine < 6), 1, 0)
    else:
        first_pairs = [(e, e - 2) for e in everyone if e >= 2]
        second_pairs = [(e, e + 2) for e in everyone if e + 2 < energies]
        relay_pairs = back_pairs = second_pairs
        turned = jnp.zeros_like(mine)
        has_second = jnp.ones_like(mine)
    twin_pairs = [(e, e ^ 1) for e in everyone]

    half = count // 2
    cuts = [free[slab : slab + 1] for slab in range(count)]
    free_first = [lax.ppermute(cuts[0], "energy", first_pairs)]

    place = lax.axis_index("slab")
    wire_up = [(i, i + 1) for i in range(peers - 1)]

    def swaps(start):
        pairs = [(i, i + 1) for i in range(start, peers - 1, 2)]
        return pairs + [(j, i) for i, j in pairs]

    stacked = jnp.stack([potential_old, permittivity])
    lower, upper = end_planes(stacked, 1)
    even = place % 2 == 0
    arrived = lax.ppermute(jnp.where(even, upper, lower), "slab", swaps(0))
    crossed = lax.ppermute(jnp.where(even, lower, upper), "slab", swaps(1))
    wire_before = jnp.where(even, crossed, arrived)
    wire_after = jnp.where(even, arrived, crossed)

    cells, rows, depth = charge.shape
    head = 5 * count * (width // depth)
    payload = call(
        functools.partial(gather_kernel, rows, energies),
        56,
        1,
        shape(head + 4 * cells, depth),
        jnp.reshape(mine, (1,)),
        *(array.reshape(-1, depth) for array in (potential_old, permittivity, charge)),
        wire_before.reshape(2, rows, depth),
        wire_after.reshape(2, rows, depth),
        owner_cell,
        in_specs=[pl.BlockSpec(memory_space=pltpu.SMEM)]
        + [pl.BlockSpec(memory_space=pltpu.VMEM)] * 6,
    )
    payload, *at_gather = lax.optimization_barrier((payload, free, coupling))
    far, near = pl.BlockSpec(memory_space=pl.ANY), pl.BlockSpec(memory_space=pltpu.VMEM)
    held = pltpu.VMEM((count, 2, width, width), jnp.float32)
    link, whole_map = call(
        linkage_kernel,
        56,
        2 * count - 1,
        (blocks, whole),
        *at_gather,
        in_specs=[far, far],
        out_specs=(far, near),
        scratch_shapes=[
            held,
            held,
            held,
            pltpu.SemaphoreType.DMA((2 * count,)),
            pltpu.SemaphoreType.DMA((count,)),
        ],
    )
    sums, ends_before, ends_after, (link, whole_map) = exchanged(payload, head, (link, whole_map))

    arrived, *cuts[1:], field, perm, sums = lax.optimization_barrier(
        (free_first[0], *cuts[1:], potential_old, permittivity, sums)
    )
    free_first = [arrived, lax.ppermute(cuts[1], "energy", first_pairs)]
    free_second = [lax.ppermute(arrived if relayed else cuts[0], "energy", relay_pairs)]
    around = lax.ppermute(cuts[-1], "energy", around_pairs) if relayed else cuts[-1]

    def sent_on(part):
        given = free_first[part] if relayed else cuts[part]
        free_second.append(lax.ppermute(given, "energy", relay_pairs))

    def sent_after(part):
        free_first[part - 1], cut = lax.optimization_barrier((free_first[part - 1], cuts[part]))
        free_first.append(lax.ppermute(cut, "energy", first_pairs))

    source, whole_source = call(
        source_kernel,
        56,
        3 * count - 2,
        (blocks, whole),
        free,
        link,
        sums,
        in_specs=[far, far, near],
        out_specs=(far, near),
        scratch_shapes=[
            held,
            held,
            held,
            pltpu.SemaphoreType.DMA((2 * count - 1,)),
            pltpu.SemaphoreType.DMA((count,)),
        ],
    )

    ends_before = ends_before.reshape(2, 2, cells, 1, depth)
    ends_after = ends_after.reshape(2, 2, cells, 1, depth)
    edge = jnp.zeros((2, cells, rows, 1), jnp.float32)
    halos = ((wire_before, wire_after), (ends_before[:, 1], ends_after[:, 0]), (edge, edge))
    potential_new = relaxed(field, perm, charge, halos)

    odd = mine % 2
    distance = jnp.array([2, 2, 1, 1], jnp.int32)
    lowered = jnp.stack([turned, 1 - turned, 1 - odd, odd]).astype(jnp.float32)
    factors = (shifts[None, :] == distance[:, None]) * (occupation[None, :] + lowered[:, None])
    weights = jnp.sum(factors[:, :, None, None] * mode_tiles[None], axis=1)
    pick = jnp.stack([turned ^ odd, has_second]).astype(jnp.int32)

    block = pl.BlockSpec((1, 2, width, width), lambda s: (s, 0, 0, 0))
    one_state = pl.BlockSpec((2, width, width), lambda s: (0, 0, 0))
    own_block = [
        pl.BlockSpec((1, 2, width, width), lambda s, first=i * half: (first + s, 0, 0, 0))
        for i in range(2)
    ]

    def beside(index, parts):
        made = shape(half, 2, width, width)
        whole_spec = pl.BlockSpec((half, 2, width, width), lambda s: (0, 0, 0, 0))
        return call(
            functools.partial(beside_kernel, index * half, count, len(parts)),
            24,
            2 * half,
            (made, made),
            *parts,
            coupling,
            sums,
            grid=(1,),
            in_specs=[pl.BlockSpec(part.shape, lambda s: (0, 0, 0, 0)) for part in parts]
            + [
                pl.BlockSpec((half, 2, width, width), lambda s: (index, 0, 0, 0)),
                pl.BlockSpec(sums.shape, lambda s: (0, 0)),
            ],
            out_specs=(whole_spec, whole_spec),
        )

    def greens_of(room, link, source, carried):
        return call(
            greens_kernel,
            room,
            2 * link.shape[0],
            (shape(*link.shape), whole),
            link,
            source,
            carried,
            grid=(link.shape[0],),
            in_specs=[block, block, one_state],
            out_specs=(block, one_state),
        )

    leaving = whole_source
    beside_first, beside_second = [None, None], [None, None]
    for hop in range(1, peers - 1):
        arrived = lax.ppermute(leaving, "slab", wire_up)
        if hop == 1:
            sent_on(1)
            sent_after(2)
            arrived, potential_new, weights, free_first[1], free_second[0], around = (
                lax.optimization_barrier(
                    (arrived, potential_new, weights, free_first[1], free_second[0], around)
                )
            )
        if hop == 2:
            sent_on(2)
            sent_after(3)
            beside_first[0] = beside(0, free_first[:2])
            arrived, beside_first[0], free_first[2], free_second[1] = lax.optimization_barrier(
                (arrived, beside_first[0], free_first[2], free_second[1])
            )
        leaving = call(hop_kernel, 12, 2, whole, whole_map, whole_source, arrived)

    def both(pairs):
        return [(a * peers + i, b * peers + j) for a, b in pairs for i, j in wire_up]

    carried = lax.ppermute(leaving, "slab", wire_up)
    carried_second = lax.ppermute(leaving, ("energy", "slab"), both(second_pairs))
    beside_second[0] = beside(0, free_second[:2])
    beside_first[1] = beside(1, free_first[2:])
    free_first[3], around = lax.optimization_barrier((free_first[3], around))
    free_second.append(lax.ppermute(around, "energy", back_pairs))
    carried, beside_first[1], beside_second[0], free_second[2] = lax.optimization_barrier(
        (carried, beside_first[1], beside_second[0], free_second[2])
    )
    carried_first = lax.ppermute(carried, "energy", first_pairs)
    carried, free_second[3] = lax.optimization_barrier((carried, free_second[3]))
    greens, _ = greens_of(56, link, source, carried)
    beside_second[1] = beside(1, free_second[2:])
    carried_second, greens = lax.optimization_barrier((carried_second, greens))
    greens_second = []
    for part in beside_second:
        made, carried_second = greens_of(16, *part, carried_second)
        greens_second.append(made)
    carried_first, greens_second[0] = lax.optimization_barrier((carried_first, greens_second[0]))

    outputs = []
    for index, part in enumerate(beside_first):
        here, there, carried_first = call(
            mixing_kernel,
            20,
            2 * half,
            (shape(half, 2, width, width), shape(half, 2, width, width), whole),
            pick,
            *part,
            carried_first,
            greens,
            greens_second[index],
            weights,
            grid=(half,),
            in_specs=[
                pl.BlockSpec(memory_space=pltpu.SMEM),
                block,
                block,
                one_state,
                own_block[index],
                block,
                pl.BlockSpec((4, width, width), lambda s: (0, 0, 0)),
            ],
            out_specs=(block, block, one_state),
        )
        if outputs:
            outputs[0], there = lax.optimization_barrier((outputs[0], there))
        outputs.append(here + lax.ppermute(there, "energy", twin_pairs))
    return potential_new, jnp.concatenate(outputs, axis=0)[None]


def solution(mesh):
    in_specs = (
        P("slab", "energy", None),
        P("slab", "energy", None),
        P("slab", "energy", None),
        P("slab", None),
        P("energy", "slab", None, None, None),
        P("slab", None, None, None),
        P(),
        P(),
        P(),
    )
    out_specs = (P("slab", "energy", None), P("energy", "slab", None, None, None))
    return jax.shard_map(
        per_device, mesh=mesh, in_specs=in_specs, out_specs=out_specs, check_vma=False
    )
```

```python
import functools
import math
import jax
import jax.numpy as jnp
from jax import lax
from jax.experimental import pallas as pl
from jax.experimental.pallas import tpu as pltpu
from jax.sharding import PartitionSpec as P

MIB = 1024 * 1024


def halves(value):
    high = value.astype(jnp.bfloat16)
    low = (value - high.astype(jnp.float32)).astype(jnp.bfloat16)
    return high, low


def parts_of(block):
    real, imag = block
    return [halves(real), halves(imag), halves(0.5 * real + 0.5 * imag)]


def left_form(block):
    return [jnp.concatenate([high, high, low], axis=1) for high, low in parts_of(block)]


def right_form(block, axis=0):
    return [jnp.concatenate([high, low, high], axis=axis) for high, low in parts_of(block)]


def three_products(left, right, flipped):
    dims = (((1,), (1 if flipped else 0,)), ((), ()))
    by_real, by_imag, by_mean = (
        lax.dot_general(a, b, dimension_numbers=dims, preferred_element_type=jnp.float32)
        for a, b in zip(left, right)
    )
    return by_real - by_imag, 4.0 * (by_mean - 0.25 * by_real - 0.25 * by_imag)


def product(former, latter):
    return three_products(left_form(former), right_form(latter), False)


def sandwich(link, inner):
    half_way = three_products(left_form(link), right_form(inner), False)
    return three_products(left_form(half_way), right_form(link, 1), True)


def added(first, second):
    return first[0] + second[0], first[1] + second[1]


def pair_of(ref, *where):
    return ref[(*where, 0)], ref[(*where, 1)]


def put(ref, value, *where):
    ref[(*where, 0)] = value[0]
    ref[(*where, 1)] = value[1]


def call(kernel, room, products, out_shapes, *operands, **more):
    flops = products * 9 * 2 * max(x.shape[-1] for x in operands) ** 3
    moved = sum(4 * math.prod(x.shape) for x in jax.tree.leaves((operands, out_shapes)))
    cost = pl.CostEstimate(flops=flops, bytes_accessed=moved, transcendentals=0)
    return pl.pallas_call(
        kernel,
        out_shape=out_shapes,
        cost_estimate=cost,
        compiler_params=pltpu.CompilerParams(vmem_limit_bytes=room * MIB),
        **more,
    )(*operands)


def shape(*dims):
    return jax.ShapeDtypeStruct(dims, jnp.float32)


def gather_kernel(rows, peers, mine, field, perm, charge, before, after, owner, out):
    total, depth = charge.shape
    count, orbitals = owner.shape
    height = total // count
    cross = rows * peers
    row_ids = lax.broadcasted_iota(jnp.int32, (total, depth), 0) % rows
    lane_ids = lax.broadcasted_iota(jnp.int32, (total, depth), 1)

    def neighbours(inner, first, last):
        down = jnp.concatenate([first, inner[:-rows]], axis=0)
        up = jnp.concatenate([inner[rows:], last], axis=0)
        left = jnp.where(lane_ids == 0, 0.0, pltpu.roll(inner, 1, axis=1))
        right = jnp.where(lane_ids == depth - 1, 0.0, pltpu.roll(inner, depth - 1, axis=1))
        low = jnp.where(row_ids == 0, 0.0, pltpu.roll(inner, 1, axis=0))
        high = jnp.where(row_ids == rows - 1, 0.0, pltpu.roll(inner, total - 1, axis=0))
        return (down + up) + (left + right) + (low + high)

    first, last = (before[0], before[1]), (after[0], after[1])
    field_now, perm_now = field[...], perm[...]
    both = perm_now * field_now
    own = [
        charge[...],
        perm_now,
        neighbours(field_now, first[0], last[0]),
        neighbours(both, first[0] * first[1], last[0] * last[1]),
        neighbours(perm_now, first[1], last[1]),
    ]
    beside = [jnp.zeros_like(both), jnp.zeros_like(both), field_now, both, perm_now]
    kinds = len(own)
    places = lax.broadcasted_iota(jnp.int32, (2 * height, orbitals), 0)
    depths = lax.broadcasted_iota(jnp.int32, (depth, orbitals), 0)
    first_row = mine[0] * rows
    step = 0
    for slab in range(count):
        cells = owner[slab : slab + 1, :]
        lane, line = cells % depth, cells // depth
        across, along = line % cross - first_row, line // cross * rows
        key = jnp.where(across == rows, height + along + rows - 1, -1)
        key = jnp.where(across == -1, height + along, key)
        key = jnp.where((across >= 0) & (across < rows), along + across, key)
        cut = slice(slab * height, (slab + 1) * height)
        table = jnp.concatenate(
            [
                jnp.concatenate([t[cut] for t in own], axis=1),
                jnp.concatenate([t[cut] for t in beside], axis=1),
            ],
            axis=0,
        ).T
        high, rest = halves(table)
        middle = rest.astype(jnp.float32)
        lowest = ((table - high.astype(jnp.float32)) - middle).astype(jnp.bfloat16)
        hit = jnp.where(places == key, 1.0, 0.0).astype(jnp.bfloat16)
        found = jnp.dot(
            jnp.concatenate([high, rest, lowest], axis=1),
            jnp.concatenate([hit, hit, hit], axis=0),
            preferred_element_type=jnp.float32,
        )
        for kind in range(kinds):
            part = found[kind * depth : (kind + 1) * depth]
            value = jnp.sum(jnp.where(depths == lane, part, 0.0), axis=0, keepdims=True)
            for piece in range(orbitals // depth):
                row = sums_row(kind, slab, count, orbitals // depth) + piece
                out[row : row + 1, :] = value[:, piece * depth : (piece + 1) * depth]
    start = kinds * count * (orbitals // depth)
    for array in (field, perm):
        for end in (0, rows - 1):
            out[start : start + total // rows, :] = array[pl.ds(end, total // rows, stride=rows), :]
            start += total // rows


def sums_row(kind, slab, count, pieces):
    return (kind * count + slab) * pieces


def potential_of(sums, slab, count, orbitals):
    pieces = orbitals // sums.shape[1]

    def value(kind):
        first = sums_row(kind, slab, count, pieces)
        return jnp.concatenate([sums[pl.ds(first + p, 1), :] for p in range(pieces)], axis=1)

    charge, perm, fields, both, perms = (value(kind) for kind in range(5))
    return (charge + 0.5 * (perm * fields + both)) / (3.0 * perm + 0.5 * perms)


def source_of(block, potential):
    scaled = (block[0] * potential, block[1] * potential)
    return added(block, product(scaled, block))


def own_kernel(free, coupling, sums, whole_map, whole_source):
    count = free.shape[0]
    links, state = [], None
    for slab in range(count):
        block = pair_of(free, slab)
        links.append(product(block, pair_of(coupling, slab)))
        source = source_of(block, potential_of(sums, slab, count, free.shape[-1]))
        state = source if state is None else added(sandwich(links[slab], state), source)
    put(whole_source, state)
    while len(links) > 1:
        paired = [product(b, a) for a, b in zip(links[0::2], links[1::2])]
        links = paired + links[len(paired) * 2 :]
    put(whole_map, links[0])


def hop_kernel(whole_map, whole_source, carried, out):
    put(out, added(sandwich(pair_of(whole_map), pair_of(carried)), pair_of(whole_source)))


def beside_kernel(start, count, parts, *refs):
    frees, (coupling, sums, link, source) = refs[:parts], refs[parts:]
    slab = 0
    for free in frees:
        for place in range(free.shape[0]):
            block = pair_of(free, place)
            put(link, product(block, pair_of(coupling, slab)), slab)
            row = potential_of(sums, start + slab, count, free.shape[-1])
            put(source, source_of(block, row), slab)
            slab += 1


def greens_kernel(link, source, carried, greens, state):
    @pl.when(pl.program_id(0) == 0)
    def _():
        state[...] = carried[...]

    now = added(sandwich(pair_of(link, 0), pair_of(state)), pair_of(source, 0))
    put(state, now)
    put(greens, now, 0)


def own_greens_kernel(count, free, coupling, sums, carried, greens, state):
    @pl.when(pl.program_id(0) == 0)
    def _():
        state[...] = carried[...]

    block = pair_of(free, 0)
    link = product(block, pair_of(coupling, 0))
    row = potential_of(sums, pl.program_id(0), count, free.shape[-1])
    now = added(sandwich(link, pair_of(state)), source_of(block, row))
    put(state, now)
    put(greens, now, 0)


def mixing_kernel(pick, link, source, carried, own, second, weights, here, there, state):
    @pl.when(pl.program_id(0) == 0)
    def _():
        state[...] = carried[...]

    first = added(sandwich(pair_of(link, 0), pair_of(state)), pair_of(source, 0))
    put(state, first)
    for part in range(2):
        second_now = jnp.where(pick[1] != 0, second[0, part], 0.0)
        here[0, part] = weights[0] * first[part] + weights[1] * second_now
        picked = jnp.where(pick[0] == 0, first[part], second_now)
        there[0, part] = weights[2] * own[0, part] + weights[3] * picked


def relaxed(field, perm, charge, halos):
    numerator = charge
    denominator = jnp.zeros_like(charge)
    for dim in range(3):
        length = charge.shape[dim]
        before, after = halos[dim]
        for side in range(2):
            sides = []
            for which, array in enumerate((field, perm)):
                if side == 0:
                    kept = lax.slice_in_dim(array, 1, length, axis=dim)
                    parts = [kept, after[which]]
                else:
                    kept = lax.slice_in_dim(array, 0, length - 1, axis=dim)
                    parts = [before[which], kept]
                sides.append(jnp.concatenate(parts, axis=dim))
            face = 0.5 * (perm + sides[1])
            numerator = numerator + face * sides[0]
            denominator = denominator + face
    return numerator / denominator


def end_planes(array, dim):
    length = array.shape[dim]
    return (
        lax.slice_in_dim(array, 0, 1, axis=dim),
        lax.slice_in_dim(array, length - 1, length, axis=dim),
    )


def exchanged(payload, head, early):
    peers, mine = lax.axis_size("energy"), lax.axis_index("energy")
    assert peers & (peers - 1) == 0
    rest = payload[head:]
    before = after = jnp.zeros_like(rest)
    is_head = lax.broadcasted_iota(jnp.int32, payload.shape, 0) < head
    mask = 1
    while mask < peers:
        if mask > 1:
            payload, early = lax.optimization_barrier((payload, early))
        arrived = lax.ppermute(payload, "energy", [(e, e ^ mask) for e in range(peers)])
        before = jnp.where((mine ^ mask) == mine - 1, arrived[head:], before)
        after = jnp.where((mine ^ mask) == mine + 1, arrived[head:], after)
        payload = jnp.where(is_head, payload + arrived, payload)
        mask = 2 * mask + 1
    return payload, before, after, early


def per_device(
    potential_old,
    charge,
    permittivity,
    owner_cell,
    green_free,
    coupling,
    shifts,
    occupation,
    mode_tiles,
):
    energies, peers = lax.axis_size("energy"), lax.axis_size("slab")
    mine = lax.axis_index("energy")
    free = green_free[0]
    count, _, width, _ = free.shape
    whole = shape(2, width, width)
    blocks = shape(count, 2, width, width)

    everyone = range(energies)
    relayed = energies == 8
    if relayed:
        first_pairs = [(e, e ^ 2) for e in everyone]
        second_pairs = [(2, 4), (3, 5), (4, 2), (5, 3)]
        relay_pairs = [(e, e ^ 4) for e in everyone]
        around_pairs = [(2, 6), (3, 7), (4, 0), (5, 1)]
        back_pairs = [(6, 4), (7, 5), (0, 2), (1, 3)]
        turned = (mine // 2) % 2
        has_second = jnp.where((mine >= 2) & (mine < 6), 1, 0)
    else:
        first_pairs = [(e, e - 2) for e in everyone if e >= 2]
        second_pairs = [(e, e + 2) for e in everyone if e + 2 < energies]
        relay_pairs = back_pairs = second_pairs
        turned = jnp.zeros_like(mine)
        has_second = jnp.ones_like(mine)
    twin_pairs = [(e, e ^ 1) for e in everyone]

    half = count // 2
    cuts = [free[slab : slab + 1] for slab in range(count)]
    free_first = [lax.ppermute(cuts[0], "energy", first_pairs)]

    place = lax.axis_index("slab")
    wire_up = [(i, i + 1) for i in range(peers - 1)]

    def swaps(start):
        pairs = [(i, i + 1) for i in range(start, peers - 1, 2)]
        return pairs + [(j, i) for i, j in pairs]

    cuts[0], stacked = lax.optimization_barrier(
        (cuts[0], jnp.stack([potential_old, permittivity]))
    )
    lower, upper = end_planes(stacked, 1)
    even = place % 2 == 0
    arrived = lax.ppermute(jnp.where(even, upper, lower), "slab", swaps(0))
    crossed = lax.ppermute(jnp.where(even, lower, upper), "slab", swaps(1))
    wire_before = jnp.where(even, crossed, arrived)
    wire_after = jnp.where(even, arrived, crossed)

    cells, rows, depth = charge.shape
    head = 5 * count * (width // depth)
    payload = call(
        functools.partial(gather_kernel, rows, energies),
        56,
        1,
        shape(head + 4 * cells, depth),
        jnp.reshape(mine, (1,)),
        *(array.reshape(-1, depth) for array in (potential_old, permittivity, charge)),
        wire_before.reshape(2, rows, depth),
        wire_after.reshape(2, rows, depth),
        owner_cell,
        in_specs=[pl.BlockSpec(memory_space=pltpu.SMEM)]
        + [pl.BlockSpec(memory_space=pltpu.VMEM)] * 6,
    )
    sums, ends_before, ends_after, free_first[0] = exchanged(payload, head, free_first[0])

    arrived, *cuts[1:], field, perm, sums = lax.optimization_barrier(
        (free_first[0], *cuts[1:], potential_old, permittivity, sums)
    )
    free_first = [arrived, lax.ppermute(cuts[1], "energy", first_pairs)]
    free_second = [lax.ppermute(arrived if relayed else cuts[0], "energy", relay_pairs)]
    around = lax.ppermute(cuts[-1], "energy", around_pairs) if relayed else cuts[-1]

    def sent_on(part):
        given = free_first[part] if relayed else cuts[part]
        free_second.append(lax.ppermute(given, "energy", relay_pairs))

    def sent_after(part):
        free_first[part - 1], cut = lax.optimization_barrier((free_first[part - 1], cuts[part]))
        free_first.append(lax.ppermute(cut, "energy", first_pairs))

    whole_map, whole_source = call(
        own_kernel,
        32,
        5 * count - 3,
        (whole, whole),
        free,
        coupling,
        sums,
    )

    ends_before = ends_before.reshape(2, 2, cells, 1, depth)
    ends_after = ends_after.reshape(2, 2, cells, 1, depth)
    edge = jnp.zeros((2, cells, rows, 1), jnp.float32)
    halos = ((wire_before, wire_after), (ends_before[:, 1], ends_after[:, 0]), (edge, edge))
    potential_new = relaxed(field, perm, charge, halos)

    odd = mine % 2
    distance = jnp.array([2, 2, 1, 1], jnp.int32)
    lowered = jnp.stack([turned, 1 - turned, 1 - odd, odd]).astype(jnp.float32)
    factors = (shifts[None, :] == distance[:, None]) * (occupation[None, :] + lowered[:, None])
    weights = jnp.sum(factors[:, :, None, None] * mode_tiles[None], axis=1)
    pick = jnp.stack([turned ^ odd, has_second]).astype(jnp.int32)

    block = pl.BlockSpec((1, 2, width, width), lambda s: (s, 0, 0, 0))
    one_state = pl.BlockSpec((2, width, width), lambda s: (0, 0, 0))
    own_block = [
        pl.BlockSpec((1, 2, width, width), lambda s, first=i * half: (first + s, 0, 0, 0))
        for i in range(2)
    ]

    def beside(index, parts):
        made = shape(half, 2, width, width)
        whole_spec = pl.BlockSpec((half, 2, width, width), lambda s: (0, 0, 0, 0))
        return call(
            functools.partial(beside_kernel, index * half, count, len(parts)),
            24,
            2 * half,
            (made, made),
            *parts,
            coupling,
            sums,
            grid=(1,),
            in_specs=[pl.BlockSpec(part.shape, lambda s: (0, 0, 0, 0)) for part in parts]
            + [
                pl.BlockSpec((half, 2, width, width), lambda s: (index, 0, 0, 0)),
                pl.BlockSpec(sums.shape, lambda s: (0, 0)),
            ],
            out_specs=(whole_spec, whole_spec),
        )

    def greens_of(room, link, source, carried):
        return call(
            greens_kernel,
            room,
            2 * link.shape[0],
            (shape(*link.shape), whole),
            link,
            source,
            carried,
            grid=(link.shape[0],),
            in_specs=[block, block, one_state],
            out_specs=(block, one_state),
        )

    leaving = whole_source
    beside_first, beside_second = [None, None], [None, None]
    for hop in range(1, peers - 1):
        arrived = lax.ppermute(leaving, "slab", wire_up)
        if hop == 1:
            sent_on(1)
            sent_after(2)
            arrived, potential_new, weights, free_first[1] = lax.optimization_barrier(
                (arrived, potential_new, weights, free_first[1])
            )
        if hop == 2:
            sent_on(2)
            sent_after(3)
            beside_first[0] = beside(0, free_first[:2])
            arrived, beside_first[0], free_first[2], free_second[0], around = (
                lax.optimization_barrier(
                    (arrived, beside_first[0], free_first[2], free_second[0], around)
                )
            )
        leaving = call(hop_kernel, 12, 2, whole, whole_map, whole_source, arrived)

    def both(pairs):
        return [(a * peers + i, b * peers + j) for a, b in pairs for i, j in wire_up]

    carried = lax.ppermute(leaving, "slab", wire_up)
    carried_second = lax.ppermute(leaving, ("energy", "slab"), both(second_pairs))
    beside_second[0] = beside(0, free_second[:2])
    beside_first[1] = beside(1, free_first[2:])
    free_first[3], around = lax.optimization_barrier((free_first[3], around))
    free_second.append(lax.ppermute(around, "energy", back_pairs))
    carried, beside_first[1], beside_second[0], free_second[2] = lax.optimization_barrier(
        (carried, beside_first[1], beside_second[0], free_second[2])
    )
    carried_first = lax.ppermute(carried, "energy", first_pairs)
    carried, free_second[3] = lax.optimization_barrier((carried, free_second[3]))
    greens, _ = call(
        functools.partial(own_greens_kernel, count),
        24,
        4 * count,
        (blocks, whole),
        free,
        coupling,
        sums,
        carried,
        grid=(count,),
        in_specs=[block, block, pl.BlockSpec(sums.shape, lambda s: (0, 0)), one_state],
        out_specs=(block, one_state),
    )
    beside_second[1] = beside(1, free_second[2:])
    carried_second, greens = lax.optimization_barrier((carried_second, greens))
    greens_second = []
    for part in beside_second:
        made, carried_second = greens_of(16, *part, carried_second)
        greens_second.append(made)
    carried_first, greens_second = lax.optimization_barrier((carried_first, greens_second))

    outputs = []
    for index, part in enumerate(beside_first):
        here, there, carried_first = call(
            mixing_kernel,
            20,
            2 * half,
            (shape(half, 2, width, width), shape(half, 2, width, width), whole),
            pick,
            *part,
            carried_first,
            greens,
            greens_second[index],
            weights,
            grid=(half,),
            in_specs=[
                pl.BlockSpec(memory_space=pltpu.SMEM),
                block,
                block,
                one_state,
                own_block[index],
                block,
                pl.BlockSpec((4, width, width), lambda s: (0, 0, 0)),
            ],
            out_specs=(block, block, one_state),
        )
        if outputs:
            outputs[0], there = lax.optimization_barrier((outputs[0], there))
        outputs.append(here + lax.ppermute(there, "energy", twin_pairs))
    return potential_new, jnp.concatenate(outputs, axis=0)[None]


def solution(mesh):
    in_specs = (
        P("slab", "energy", None),
        P("slab", "energy", None),
        P("slab", "energy", None),
        P("slab", None),
        P("energy", "slab", None, None, None),
        P("slab", None, None, None),
        P(),
        P(),
        P(),
    )
    out_specs = (P("slab", "energy", None), P("energy", "slab", None, None, None))
    return jax.shard_map(
        per_device, mesh=mesh, in_specs=in_specs, out_specs=out_specs, check_vma=False
    )
```

```python
import functools
import math
import jax
import jax.numpy as jnp
from jax import lax
from jax.experimental import pallas as pl
from jax.experimental.pallas import tpu as pltpu
from jax.sharding import PartitionSpec as P

MIB = 1024 * 1024


def halves(value):
    high = value.astype(jnp.bfloat16)
    low = (value - high.astype(jnp.float32)).astype(jnp.bfloat16)
    return high, low


def parts_of(block):
    real, imag = block
    return [halves(real), halves(imag), halves(0.5 * real + 0.5 * imag)]


def left_form(block):
    return [jnp.concatenate([high, high, low], axis=1) for high, low in parts_of(block)]


def right_form(block, axis=0):
    return [jnp.concatenate([high, low, high], axis=axis) for high, low in parts_of(block)]


def three_products(left, right, flipped):
    dims = (((1,), (1 if flipped else 0,)), ((), ()))
    by_real, by_imag, by_mean = (
        lax.dot_general(a, b, dimension_numbers=dims, preferred_element_type=jnp.float32)
        for a, b in zip(left, right)
    )
    return by_real - by_imag, 4.0 * (by_mean - 0.25 * by_real - 0.25 * by_imag)


def product(former, latter):
    return three_products(left_form(former), right_form(latter), False)


def sandwich(link, inner):
    half_way = three_products(left_form(link), right_form(inner), False)
    return three_products(left_form(half_way), right_form(link, 1), True)


def added(first, second):
    return first[0] + second[0], first[1] + second[1]


def pair_of(ref, *where):
    return ref[(*where, 0)], ref[(*where, 1)]


def put(ref, value, *where):
    ref[(*where, 0)] = value[0]
    ref[(*where, 1)] = value[1]


def call(kernel, room, products, out_shapes, *operands, **more):
    flops = products * 9 * 2 * max(x.shape[-1] for x in operands) ** 3
    moved = sum(4 * math.prod(x.shape) for x in jax.tree.leaves((operands, out_shapes)))
    cost = pl.CostEstimate(flops=flops, bytes_accessed=moved, transcendentals=0)
    return pl.pallas_call(
        kernel,
        out_shape=out_shapes,
        cost_estimate=cost,
        compiler_params=pltpu.CompilerParams(vmem_limit_bytes=room * MIB),
        **more,
    )(*operands)


def shape(*dims):
    return jax.ShapeDtypeStruct(dims, jnp.float32)


def gather_kernel(rows, peers, sizes, mine, field, perm, charge, before, after, owner, free, *refs):
    out, ends, *parts, sems = refs
    taken = []
    for index, part in enumerate(parts):
        cut = free.at[pl.ds(sum(sizes[:index]), sizes[index])]
        taken.append(pltpu.make_async_copy(cut, part, sems.at[index]))
        taken[-1].start()
    total, depth = charge.shape
    count, orbitals = owner.shape
    height = total // count
    cross = rows * peers
    row_ids = lax.broadcasted_iota(jnp.int32, (total, depth), 0) % rows
    lane_ids = lax.broadcasted_iota(jnp.int32, (total, depth), 1)

    def neighbours(inner, first, last):
        down = jnp.concatenate([first, inner[:-rows]], axis=0)
        up = jnp.concatenate([inner[rows:], last], axis=0)
        left = jnp.where(lane_ids == 0, 0.0, pltpu.roll(inner, 1, axis=1))
        right = jnp.where(lane_ids == depth - 1, 0.0, pltpu.roll(inner, depth - 1, axis=1))
        low = jnp.where(row_ids == 0, 0.0, pltpu.roll(inner, 1, axis=0))
        high = jnp.where(row_ids == rows - 1, 0.0, pltpu.roll(inner, total - 1, axis=0))
        return (down + up) + (left + right) + (low + high)

    first, last = (before[0], before[1]), (after[0], after[1])
    field_now, perm_now = field[...], perm[...]
    both = perm_now * field_now
    own = [
        charge[...],
        perm_now,
        neighbours(field_now, first[0], last[0]),
        neighbours(both, first[0] * first[1], last[0] * last[1]),
        neighbours(perm_now, first[1], last[1]),
    ]
    beside = [jnp.zeros_like(both), jnp.zeros_like(both), field_now, both, perm_now]
    kinds = len(own)
    places = lax.broadcasted_iota(jnp.int32, (2 * height, orbitals), 0)
    depths = lax.broadcasted_iota(jnp.int32, (depth, orbitals), 0)
    first_row = mine[0] * rows
    step = 0
    for slab in range(count):
        cells = owner[slab : slab + 1, :]
        lane, line = cells % depth, cells // depth
        across, along = line % cross - first_row, line // cross * rows
        key = jnp.where(across == rows, height + along + rows - 1, -1)
        key = jnp.where(across == -1, height + along, key)
        key = jnp.where((across >= 0) & (across < rows), along + across, key)
        cut = slice(slab * height, (slab + 1) * height)
        table = jnp.concatenate(
            [
                jnp.concatenate([t[cut] for t in own], axis=1),
                jnp.concatenate([t[cut] for t in beside], axis=1),
            ],
            axis=0,
        ).T
        high, rest = halves(table)
        middle = rest.astype(jnp.float32)
        lowest = ((table - high.astype(jnp.float32)) - middle).astype(jnp.bfloat16)
        hit = jnp.where(places == key, 1.0, 0.0).astype(jnp.bfloat16)
        found = jnp.dot(
            jnp.concatenate([high, rest, lowest], axis=1),
            jnp.concatenate([hit, hit, hit], axis=0),
            preferred_element_type=jnp.float32,
        )
        for kind in range(kinds):
            part = found[kind * depth : (kind + 1) * depth]
            value = jnp.sum(jnp.where(depths == lane, part, 0.0), axis=0, keepdims=True)
            for piece in range(orbitals // depth):
                row = sums_row(kind, slab, count, orbitals // depth) + piece
                out[row : row + 1, :] = value[:, piece * depth : (piece + 1) * depth]
    start = 0
    for array in (field, perm):
        for end in (0, rows - 1):
            ends[start : start + total // rows, :] = array[
                pl.ds(end, total // rows, stride=rows), :
            ]
            start += total // rows
    for copy in taken:
        copy.wait()


def sums_row(kind, slab, count, pieces):
    return (kind * count + slab) * pieces


def potential_of(sums, slab, count, orbitals):
    pieces = orbitals // sums.shape[1]

    def value(kind):
        first = sums_row(kind, slab, count, pieces)
        return jnp.concatenate([sums[pl.ds(first + p, 1), :] for p in range(pieces)], axis=1)

    charge, perm, fields, both, perms = (value(kind) for kind in range(5))
    return (charge + 0.5 * (perm * fields + both)) / (3.0 * perm + 0.5 * perms)


def source_of(block, potential):
    scaled = (block[0] * potential, block[1] * potential)
    return added(block, product(scaled, block))


def own_kernel(free, coupling, sums, whole_map, whole_source):
    count = free.shape[0]
    links, state = [], None
    for slab in range(count):
        block = pair_of(free, slab)
        links.append(product(block, pair_of(coupling, slab)))
        source = source_of(block, potential_of(sums, slab, count, free.shape[-1]))
        state = source if state is None else added(sandwich(links[slab], state), source)
    put(whole_source, state)
    while len(links) > 1:
        paired = [product(b, a) for a, b in zip(links[0::2], links[1::2])]
        links = paired + links[len(paired) * 2 :]
    put(whole_map, links[0])


def hop_kernel(whole_map, whole_source, carried, out):
    put(out, added(sandwich(pair_of(whole_map), pair_of(carried)), pair_of(whole_source)))


def beside_kernel(start, count, parts, *refs):
    frees, (coupling, sums, link, source) = refs[:parts], refs[parts:]
    slab = 0
    for free in frees:
        for place in range(free.shape[0]):
            block = pair_of(free, place)
            put(link, product(block, pair_of(coupling, slab)), slab)
            row = potential_of(sums, start + slab, count, free.shape[-1])
            put(source, source_of(block, row), slab)
            slab += 1


def greens_kernel(link, source, carried, greens, state):
    @pl.when(pl.program_id(0) == 0)
    def _():
        state[...] = carried[...]

    now = added(sandwich(pair_of(link, 0), pair_of(state)), pair_of(source, 0))
    put(state, now)
    put(greens, now, 0)


def own_greens_kernel(count, free, coupling, sums, carried, greens, state):
    @pl.when(pl.program_id(0) == 0)
    def _():
        state[...] = carried[...]

    block = pair_of(free, 0)
    link = product(block, pair_of(coupling, 0))
    row = potential_of(sums, pl.program_id(0), count, free.shape[-1])
    now = added(sandwich(link, pair_of(state)), source_of(block, row))
    put(state, now)
    put(greens, now, 0)


def mixing_kernel(pick, link, source, carried, own, second, weights, here, there, state):
    @pl.when(pl.program_id(0) == 0)
    def _():
        state[...] = carried[...]

    first = added(sandwich(pair_of(link, 0), pair_of(state)), pair_of(source, 0))
    put(state, first)
    for part in range(2):
        second_now = jnp.where(pick[1] != 0, second[0, part], 0.0)
        here[0, part] = weights[0] * first[part] + weights[1] * second_now
        picked = jnp.where(pick[0] == 0, first[part], second_now)
        there[0, part] = weights[2] * own[0, part] + weights[3] * picked


def relaxed(field, perm, charge, halos):
    numerator = charge
    denominator = jnp.zeros_like(charge)
    for dim in range(3):
        length = charge.shape[dim]
        before, after = halos[dim]
        for side in range(2):
            sides = []
            for which, array in enumerate((field, perm)):
                if side == 0:
                    kept = lax.slice_in_dim(array, 1, length, axis=dim)
                    parts = [kept, after[which]]
                else:
                    kept = lax.slice_in_dim(array, 0, length - 1, axis=dim)
                    parts = [before[which], kept]
                sides.append(jnp.concatenate(parts, axis=dim))
            face = 0.5 * (perm + sides[1])
            numerator = numerator + face * sides[0]
            denominator = denominator + face
    return numerator / denominator


def end_planes(array, dim):
    length = array.shape[dim]
    return (
        lax.slice_in_dim(array, 0, 1, axis=dim),
        lax.slice_in_dim(array, length - 1, length, axis=dim),
    )


def exchanged(sums, ends):
    peers = lax.axis_size("energy")
    assert peers >= 4 and peers & (peers - 1) == 0
    masks = [2, 1] + [1 << k for k in range(2, peers.bit_length() - 1)]
    rows, twin_ends = sums.shape[0], None
    first = None
    for mask in masks:
        given = jnp.concatenate([sums, ends]) if mask == 1 else sums
        arrived = lax.ppermute(given, "energy", [(e, e ^ mask) for e in range(peers)])
        if mask == 1:
            twin_ends = arrived[rows:]
        sums = sums + arrived[:rows]
        first = sums if first is None else first
    return sums, twin_ends, first


def per_device(
    potential_old,
    charge,
    permittivity,
    owner_cell,
    green_free,
    coupling,
    shifts,
    occupation,
    mode_tiles,
):
    energies, peers = lax.axis_size("energy"), lax.axis_size("slab")
    mine = lax.axis_index("energy")
    free = green_free[0]
    count, _, width, _ = free.shape
    whole = shape(2, width, width)
    blocks = shape(count, 2, width, width)

    everyone = range(energies)
    relayed = energies == 8
    if relayed:
        first_pairs = [(e, e ^ 2) for e in everyone]
        second_pairs = [(2, 4), (3, 5), (4, 2), (5, 3)]
        relay_pairs = [(e, e ^ 4) for e in everyone]
        around_pairs = [(2, 6), (3, 7), (4, 0), (5, 1)]
        back_pairs = [(6, 4), (7, 5), (0, 2), (1, 3)]
        turned = (mine // 2) % 2
        has_second = jnp.where((mine >= 2) & (mine < 6), 1, 0)
    else:
        first_pairs = [(e, e - 2) for e in everyone if e >= 2]
        second_pairs = [(e, e + 2) for e in everyone if e + 2 < energies]
        relay_pairs = back_pairs = second_pairs
        turned = jnp.zeros_like(mine)
        has_second = jnp.ones_like(mine)
    twin_pairs = [(e, e ^ 1) for e in everyone]

    half = count // 2
    sizes = (half,) + (1,) * (count - half)

    place = lax.axis_index("slab")
    wire_up = [(i, i + 1) for i in range(peers - 1)]

    def swaps(start):
        pairs = [(i, i + 1) for i in range(start, peers - 1, 2)]
        return pairs + [(j, i) for i, j in pairs]

    stacked = jnp.stack([potential_old, permittivity])
    lower, upper = end_planes(stacked, 1)
    even = place % 2 == 0
    arrived = lax.ppermute(jnp.where(even, upper, lower), "slab", swaps(0))
    crossed = lax.ppermute(jnp.where(even, lower, upper), "slab", swaps(1))
    wire_before = jnp.where(even, crossed, arrived)
    wire_after = jnp.where(even, arrived, crossed)

    cells, rows, depth = charge.shape
    far, near = pl.BlockSpec(memory_space=pl.ANY), pl.BlockSpec(memory_space=pltpu.VMEM)
    sums, ends, *cuts = call(
        functools.partial(gather_kernel, rows, energies, sizes),
        56,
        1,
        (
            shape(5 * count * (width // depth), depth),
            shape(4 * cells, depth),
            *(shape(size, 2, width, width) for size in sizes),
        ),
        jnp.reshape(mine, (1,)),
        *(array.reshape(-1, depth) for array in (potential_old, permittivity, charge)),
        wire_before.reshape(2, rows, depth),
        wire_after.reshape(2, rows, depth),
        owner_cell,
        free,
        in_specs=[pl.BlockSpec(memory_space=pltpu.SMEM)] + [near] * 6 + [far],
        out_specs=(near, near, *(far for _ in sizes)),
        scratch_shapes=[pltpu.SemaphoreType.DMA((len(sizes),))],
    )
    sums, twin_ends, crossed = exchanged(sums, ends)

    crossed, cuts[0] = lax.optimization_barrier((crossed, cuts[0]))
    free_first = [lax.ppermute(cuts[0], "energy", first_pairs)]
    sums, cuts[-1] = lax.optimization_barrier((sums, cuts[-1]))
    around = lax.ppermute(cuts[-1], "energy", around_pairs) if relayed else cuts[-1]
    free_second = []

    def sent_on(part):
        given = free_first[part] if relayed else cuts[part]
        free_second.append(lax.ppermute(given, "energy", relay_pairs))

    def sent_after(part):
        free_first[part - 1], cut = lax.optimization_barrier((free_first[part - 1], cuts[part]))
        free_first.append(lax.ppermute(cut, "energy", first_pairs))

    whole_map, whole_source = call(
        own_kernel,
        32,
        5 * count - 3,
        (whole, whole),
        free,
        coupling,
        sums,
    )

    whole_source, field, perm, ends, mode_tiles = lax.optimization_barrier(
        (whole_source, potential_old, permittivity, ends, mode_tiles)
    )
    beyond = [(e, e + 1) for e in range(1, energies - 1, 2)]
    other_ends = lax.ppermute(ends, "energy", beyond + [(b, a) for a, b in beyond])
    is_odd = mine % 2 == 1
    ends_before = jnp.where(is_odd, twin_ends, other_ends).reshape(2, 2, cells, 1, depth)
    ends_after = jnp.where(is_odd, other_ends, twin_ends).reshape(2, 2, cells, 1, depth)
    edge = jnp.zeros((2, cells, rows, 1), jnp.float32)
    halos = ((wire_before, wire_after), (ends_before[:, 1], ends_after[:, 0]), (edge, edge))
    potential_new = relaxed(field, perm, charge, halos)

    odd = mine % 2
    distance = jnp.array([2, 2, 1, 1], jnp.int32)
    lowered = jnp.stack([turned, 1 - turned, 1 - odd, odd]).astype(jnp.float32)
    factors = (shifts[None, :] == distance[:, None]) * (occupation[None, :] + lowered[:, None])
    weights = jnp.sum(factors[:, :, None, None] * mode_tiles[None], axis=1)
    pick = jnp.stack([turned ^ odd, has_second]).astype(jnp.int32)

    block = pl.BlockSpec((1, 2, width, width), lambda s: (s, 0, 0, 0))
    one_state = pl.BlockSpec((2, width, width), lambda s: (0, 0, 0))
    own_block = [
        pl.BlockSpec((1, 2, width, width), lambda s, first=i * half: (first + s, 0, 0, 0))
        for i in range(2)
    ]

    def beside(index, parts):
        made = shape(half, 2, width, width)
        whole_spec = pl.BlockSpec((half, 2, width, width), lambda s: (0, 0, 0, 0))
        return call(
            functools.partial(beside_kernel, index * half, count, len(parts)),
            24,
            2 * half,
            (made, made),
            *parts,
            coupling,
            sums,
            grid=(1,),
            in_specs=[pl.BlockSpec(part.shape, lambda s: (0, 0, 0, 0)) for part in parts]
            + [
                pl.BlockSpec((half, 2, width, width), lambda s: (index, 0, 0, 0)),
                pl.BlockSpec(sums.shape, lambda s: (0, 0)),
            ],
            out_specs=(whole_spec, whole_spec),
        )

    def greens_of(room, link, source, carried):
        return call(
            greens_kernel,
            room,
            2 * link.shape[0],
            (shape(*link.shape), whole),
            link,
            source,
            carried,
            grid=(link.shape[0],),
            in_specs=[block, block, one_state],
            out_specs=(block, one_state),
        )

    leaving = whole_source
    beside_first, beside_second = [None, None], [None, None]
    for hop in range(1, peers - 1):
        arrived = lax.ppermute(leaving, "slab", wire_up)
        if hop == 1:
            sent_on(0)
            sent_after(1)
            arrived, weights, free_first[0] = lax.optimization_barrier(
                (arrived, weights, free_first[0])
            )
        if hop == 2:
            sent_after(2)
            beside_first[0] = beside(0, free_first[:1])
            arrived, beside_first[0], free_first[1], around = lax.optimization_barrier(
                (arrived, beside_first[0], free_first[1], around)
            )
        leaving = call(hop_kernel, 12, 2, whole, whole_map, whole_source, arrived)

    def both(pairs):
        return [(a * peers + i, b * peers + j) for a, b in pairs for i, j in wire_up]

    carried = lax.ppermute(leaving, "slab", wire_up)
    carried_second = lax.ppermute(leaving, ("energy", "slab"), both(second_pairs))
    sent_on(1)
    beside_second[0] = beside(0, free_second[:1])
    beside_first[1] = beside(1, free_first[1:])
    free_first[2], around = lax.optimization_barrier((free_first[2], around))
    free_second.append(lax.ppermute(around, "energy", back_pairs))
    carried, beside_first[1], beside_second[0], potential_new = lax.optimization_barrier(
        (carried, beside_first[1], beside_second[0], potential_new)
    )
    carried_first = lax.ppermute(carried, "energy", first_pairs)
    carried, free_second[1], free_second[2] = lax.optimization_barrier(
        (carried, free_second[1], free_second[2])
    )
    greens, _ = call(
        functools.partial(own_greens_kernel, count),
        24,
        4 * count,
        (blocks, whole),
        free,
        coupling,
        sums,
        carried,
        grid=(count,),
        in_specs=[block, block, pl.BlockSpec(sums.shape, lambda s: (0, 0)), one_state],
        out_specs=(block, one_state),
    )
    beside_second[1] = beside(1, free_second[1:])
    carried_second, greens = lax.optimization_barrier((carried_second, greens))
    greens_second = []
    for part in beside_second:
        made, carried_second = greens_of(16, *part, carried_second)
        greens_second.append(made)
    carried_first, greens_second = lax.optimization_barrier((carried_first, greens_second))

    outputs = []
    for index, part in enumerate(beside_first):
        here, there, carried_first = call(
            mixing_kernel,
            20,
            2 * half,
            (shape(half, 2, width, width), shape(half, 2, width, width), whole),
            pick,
            *part,
            carried_first,
            greens,
            greens_second[index],
            weights,
            grid=(half,),
            in_specs=[
                pl.BlockSpec(memory_space=pltpu.SMEM),
                block,
                block,
                one_state,
                own_block[index],
                block,
                pl.BlockSpec((4, width, width), lambda s: (0, 0, 0)),
            ],
            out_specs=(block, block, one_state),
        )
        if outputs:
            outputs[0], there = lax.optimization_barrier((outputs[0], there))
        outputs.append(here + lax.ppermute(there, "energy", twin_pairs))
    return potential_new, jnp.concatenate(outputs, axis=0)[None]


def solution(mesh):
    in_specs = (
        P("slab", "energy", None),
        P("slab", "energy", None),
        P("slab", "energy", None),
        P("slab", None),
        P("energy", "slab", None, None, None),
        P("slab", None, None, None),
        P(),
        P(),
        P(),
    )
    out_specs = (P("slab", "energy", None), P("energy", "slab", None, None, None))
    return jax.shard_map(
        per_device, mesh=mesh, in_specs=in_specs, out_specs=out_specs, check_vma=False
    )
```

```python
import functools
import math
import jax
import jax.numpy as jnp
from jax import lax
from jax.experimental import pallas as pl
from jax.experimental.pallas import tpu as pltpu
from jax.sharding import PartitionSpec as P

MIB = 1024 * 1024


def halves(value):
    high = value.astype(jnp.bfloat16)
    low = (value - high.astype(jnp.float32)).astype(jnp.bfloat16)
    return high, low


def parts_of(block):
    real, imag = block
    return [halves(real), halves(imag), halves(0.5 * real + 0.5 * imag)]


def left_form(block):
    return [jnp.concatenate([high, high, low], axis=1) for high, low in parts_of(block)]


def right_form(block, axis=0):
    return [jnp.concatenate([high, low, high], axis=axis) for high, low in parts_of(block)]


def three_products(left, right, flipped):
    dims = (((1,), (1 if flipped else 0,)), ((), ()))
    by_real, by_imag, by_mean = (
        lax.dot_general(a, b, dimension_numbers=dims, preferred_element_type=jnp.float32)
        for a, b in zip(left, right)
    )
    return by_real - by_imag, 4.0 * (by_mean - 0.25 * by_real - 0.25 * by_imag)


def product(former, latter):
    return three_products(left_form(former), right_form(latter), False)


def sandwich(link, inner):
    half_way = three_products(left_form(link), right_form(inner), False)
    return three_products(left_form(half_way), right_form(link, 1), True)


def added(first, second):
    return first[0] + second[0], first[1] + second[1]


def pair_of(ref, *where):
    return ref[(*where, 0)], ref[(*where, 1)]


def put(ref, value, *where):
    ref[(*where, 0)] = value[0]
    ref[(*where, 1)] = value[1]


def call(kernel, room, products, out_shapes, *operands, **more):
    flops = products * 9 * 2 * max(x.shape[-1] for x in operands) ** 3
    moved = sum(4 * math.prod(x.shape) for x in jax.tree.leaves((operands, out_shapes)))
    cost = pl.CostEstimate(flops=flops, bytes_accessed=moved, transcendentals=0)
    return pl.pallas_call(
        kernel,
        out_shape=out_shapes,
        cost_estimate=cost,
        compiler_params=pltpu.CompilerParams(vmem_limit_bytes=room * MIB),
        **more,
    )(*operands)


def shape(*dims):
    return jax.ShapeDtypeStruct(dims, jnp.float32)


def gather_kernel(rows, peers, mine, field, perm, charge, before, after, owner, free, *refs):
    out, ends, *parts, held, here, gone = refs
    loads, stores = [], []
    for index in range(len(parts)):
        slab = free.at[index + 1 : index + 2]
        loads.append(
            pltpu.make_async_copy(slab, held.at[index : index + 1], here.at[index])
        )
        loads[-1].start()
    total, depth = charge.shape
    count, orbitals = owner.shape
    height = total // count
    cross = rows * peers
    row_ids = lax.broadcasted_iota(jnp.int32, (total, depth), 0) % rows
    lane_ids = lax.broadcasted_iota(jnp.int32, (total, depth), 1)

    def neighbours(inner, first, last):
        down = jnp.concatenate([first, inner[:-rows]], axis=0)
        up = jnp.concatenate([inner[rows:], last], axis=0)
        left = jnp.where(lane_ids == 0, 0.0, pltpu.roll(inner, 1, axis=1))
        right = jnp.where(lane_ids == depth - 1, 0.0, pltpu.roll(inner, depth - 1, axis=1))
        low = jnp.where(row_ids == 0, 0.0, pltpu.roll(inner, 1, axis=0))
        high = jnp.where(row_ids == rows - 1, 0.0, pltpu.roll(inner, total - 1, axis=0))
        return (down + up) + (left + right) + (low + high)

    first, last = (before[0], before[1]), (after[0], after[1])
    field_now, perm_now = field[...], perm[...]
    both = perm_now * field_now
    own = [
        charge[...],
        perm_now,
        neighbours(field_now, first[0], last[0]),
        neighbours(both, first[0] * first[1], last[0] * last[1]),
        neighbours(perm_now, first[1], last[1]),
    ]
    beside = [jnp.zeros_like(both), jnp.zeros_like(both), field_now, both, perm_now]
    kinds = len(own)
    places = lax.broadcasted_iota(jnp.int32, (2 * height, orbitals), 0)
    depths = lax.broadcasted_iota(jnp.int32, (depth, orbitals), 0)
    first_row = mine[0] * rows
    step = 0
    for slab in range(count):
        if slab == count // 2:
            for index, part in enumerate(parts):
                loads[index].wait()
                stores.append(
                    pltpu.make_async_copy(held.at[index : index + 1], part, gone.at[index])
                )
                stores[-1].start()
        cells = owner[slab : slab + 1, :]
        lane, line = cells % depth, cells // depth
        across, along = line % cross - first_row, line // cross * rows
        key = jnp.where(across == rows, height + along + rows - 1, -1)
        key = jnp.where(across == -1, height + along, key)
        key = jnp.where((across >= 0) & (across < rows), along + across, key)
        cut = slice(slab * height, (slab + 1) * height)
        table = jnp.concatenate(
            [
                jnp.concatenate([t[cut] for t in own], axis=1),
                jnp.concatenate([t[cut] for t in beside], axis=1),
            ],
            axis=0,
        ).T
        high, rest = halves(table)
        middle = rest.astype(jnp.float32)
        lowest = ((table - high.astype(jnp.float32)) - middle).astype(jnp.bfloat16)
        hit = jnp.where(places == key, 1.0, 0.0).astype(jnp.bfloat16)
        found = jnp.dot(
            jnp.concatenate([high, rest, lowest], axis=1),
            jnp.concatenate([hit, hit, hit], axis=0),
            preferred_element_type=jnp.float32,
        )
        for kind in range(kinds):
            part = found[kind * depth : (kind + 1) * depth]
            value = jnp.sum(jnp.where(depths == lane, part, 0.0), axis=0, keepdims=True)
            for piece in range(orbitals // depth):
                row = sums_row(kind, slab, count, orbitals // depth) + piece
                out[row : row + 1, :] = value[:, piece * depth : (piece + 1) * depth]
    start = 0
    for array in (field, perm):
        for end in (0, rows - 1):
            ends[start : start + total // rows, :] = array[
                pl.ds(end, total // rows, stride=rows), :
            ]
            start += total // rows
    for store in stores:
        store.wait()


def sums_row(kind, slab, count, pieces):
    return (kind * count + slab) * pieces


def potential_of(sums, slab, count, orbitals):
    pieces = orbitals // sums.shape[1]

    def value(kind):
        first = sums_row(kind, slab, count, pieces)
        return jnp.concatenate([sums[pl.ds(first + p, 1), :] for p in range(pieces)], axis=1)

    charge, perm, fields, both, perms = (value(kind) for kind in range(5))
    return (charge + 0.5 * (perm * fields + both)) / (3.0 * perm + 0.5 * perms)


def source_of(block, potential):
    scaled = (block[0] * potential, block[1] * potential)
    return added(block, product(scaled, block))


def own_kernel(free, coupling, sums, whole_map, whole_source):
    count = free.shape[0]
    links, state = [], None
    for slab in range(count):
        block = pair_of(free, slab)
        links.append(product(block, pair_of(coupling, slab)))
        source = source_of(block, potential_of(sums, slab, count, free.shape[-1]))
        state = source if state is None else added(sandwich(links[slab], state), source)
    put(whole_source, state)
    while len(links) > 1:
        paired = [product(b, a) for a, b in zip(links[0::2], links[1::2])]
        links = paired + links[len(paired) * 2 :]
    put(whole_map, links[0])


def hop_kernel(whole_map, whole_source, carried, out):
    put(out, added(sandwich(pair_of(whole_map), pair_of(carried)), pair_of(whole_source)))


def beside_kernel(start, count, parts, *refs):
    frees, (coupling, sums, link, source) = refs[:parts], refs[parts:]
    slab = 0
    for free in frees:
        for place in range(free.shape[0]):
            block = pair_of(free, place)
            put(link, product(block, pair_of(coupling, slab)), slab)
            row = potential_of(sums, start + slab, count, free.shape[-1])
            put(source, source_of(block, row), slab)
            slab += 1


def greens_kernel(link, source, carried, greens, state):
    @pl.when(pl.program_id(0) == 0)
    def _():
        state[...] = carried[...]

    now = added(sandwich(pair_of(link, 0), pair_of(state)), pair_of(source, 0))
    put(state, now)
    put(greens, now, 0)


def own_greens_kernel(count, free, coupling, sums, carried, greens, state):
    @pl.when(pl.program_id(0) == 0)
    def _():
        state[...] = carried[...]

    block = pair_of(free, 0)
    link = product(block, pair_of(coupling, 0))
    row = potential_of(sums, pl.program_id(0), count, free.shape[-1])
    now = added(sandwich(link, pair_of(state)), source_of(block, row))
    put(state, now)
    put(greens, now, 0)


def mixing_kernel(pick, link, source, carried, own, second, weights, here, there, state):
    @pl.when(pl.program_id(0) == 0)
    def _():
        state[...] = carried[...]

    first = added(sandwich(pair_of(link, 0), pair_of(state)), pair_of(source, 0))
    put(state, first)
    for part in range(2):
        second_now = jnp.where(pick[1] != 0, second[0, part], 0.0)
        here[0, part] = weights[0] * first[part] + weights[1] * second_now
        picked = jnp.where(pick[0] == 0, first[part], second_now)
        there[0, part] = weights[2] * own[0, part] + weights[3] * picked


def relaxed(field, perm, charge, halos):
    numerator = charge
    denominator = jnp.zeros_like(charge)
    for dim in range(3):
        length = charge.shape[dim]
        before, after = halos[dim]
        for side in range(2):
            sides = []
            for which, array in enumerate((field, perm)):
                if side == 0:
                    kept = lax.slice_in_dim(array, 1, length, axis=dim)
                    parts = [kept, after[which]]
                else:
                    kept = lax.slice_in_dim(array, 0, length - 1, axis=dim)
                    parts = [before[which], kept]
                sides.append(jnp.concatenate(parts, axis=dim))
            face = 0.5 * (perm + sides[1])
            numerator = numerator + face * sides[0]
            denominator = denominator + face
    return numerator / denominator


def end_planes(array, dim):
    length = array.shape[dim]
    return (
        lax.slice_in_dim(array, 0, 1, axis=dim),
        lax.slice_in_dim(array, length - 1, length, axis=dim),
    )


def exchanged(sums, ends, early):
    peers = lax.axis_size("energy")
    assert peers >= 4 and peers & (peers - 1) == 0
    masks = [2, 1] + [1 << k for k in range(2, peers.bit_length() - 1)]
    rows, twin_ends = sums.shape[0], None
    first = None
    sums, early = lax.optimization_barrier((sums, early))
    for mask in masks:
        given = jnp.concatenate([sums, ends]) if mask == 1 else sums
        arrived = lax.ppermute(given, "energy", [(e, e ^ mask) for e in range(peers)])
        if mask == 1:
            twin_ends = arrived[rows:]
        sums = sums + arrived[:rows]
        first = sums if first is None else first
    return sums, twin_ends, first, early


def per_device(
    potential_old,
    charge,
    permittivity,
    owner_cell,
    green_free,
    coupling,
    shifts,
    occupation,
    mode_tiles,
):
    energies, peers = lax.axis_size("energy"), lax.axis_size("slab")
    mine = lax.axis_index("energy")
    free = green_free[0]
    count, _, width, _ = free.shape
    whole = shape(2, width, width)
    blocks = shape(count, 2, width, width)

    everyone = range(energies)
    relayed = energies == 8
    if relayed:
        first_pairs = [(e, e ^ 2) for e in everyone]
        second_pairs = [(2, 4), (3, 5), (4, 2), (5, 3)]
        relay_pairs = [(e, e ^ 4) for e in everyone]
        turned = (mine // 2) % 2
        has_second = jnp.where((mine >= 2) & (mine < 6), 1, 0)
    else:
        first_pairs = [(e, e - 2) for e in everyone if e >= 2]
        second_pairs = [(e, e + 2) for e in everyone if e + 2 < energies]
        relay_pairs = second_pairs
        turned = jnp.zeros_like(mine)
        has_second = jnp.ones_like(mine)
    twin_pairs = [(e, e ^ 1) for e in everyone]

    half = count // 2
    one_slab = shape(1, 2, width, width)
    first_cut = free[:1]
    free_first = [lax.ppermute(first_cut, "energy", first_pairs)]

    place = lax.axis_index("slab")
    wire_up = [(i, i + 1) for i in range(peers - 1)]

    def swaps(start):
        pairs = [(i, i + 1) for i in range(start, peers - 1, 2)]
        return pairs + [(j, i) for i, j in pairs]

    first_cut, stacked = lax.optimization_barrier(
        (first_cut, jnp.stack([potential_old, permittivity]))
    )
    lower, upper = end_planes(stacked, 1)
    even = place % 2 == 0
    arrived = lax.ppermute(jnp.where(even, upper, lower), "slab", swaps(0))
    crossed = lax.ppermute(jnp.where(even, lower, upper), "slab", swaps(1))
    wire_before = jnp.where(even, crossed, arrived)
    wire_after = jnp.where(even, arrived, crossed)

    cells, rows, depth = charge.shape
    far, near = pl.BlockSpec(memory_space=pl.ANY), pl.BlockSpec(memory_space=pltpu.VMEM)
    sums, ends, *cuts = call(
        functools.partial(gather_kernel, rows, energies),
        56,
        1,
        (
            shape(5 * count * (width // depth), depth),
            shape(4 * cells, depth),
            *[one_slab] * (count - 1),
        ),
        jnp.reshape(mine, (1,)),
        *(array.reshape(-1, depth) for array in (potential_old, permittivity, charge)),
        wire_before.reshape(2, rows, depth),
        wire_after.reshape(2, rows, depth),
        owner_cell,
        free,
        in_specs=[pl.BlockSpec(memory_space=pltpu.SMEM)] + [near] * 6 + [far],
        out_specs=(near, near, *[far] * (count - 1)),
        scratch_shapes=[
            pltpu.VMEM((count - 1, 2, width, width), jnp.float32),
            pltpu.SemaphoreType.DMA((count - 1,)),
            pltpu.SemaphoreType.DMA((count - 1,)),
        ],
    )
    cuts = [first_cut, *cuts]
    sums, twin_ends, crossed, arrived = exchanged(sums, ends, free_first[0])

    crossed, cuts[1] = lax.optimization_barrier((crossed, cuts[1]))
    sums, arrived = lax.optimization_barrier((sums, arrived))
    free_first = [arrived, lax.ppermute(cuts[1], "energy", first_pairs)]
    free_second = []

    def sent_on(part):
        given = free_first[part] if relayed else cuts[part]
        free_second.append(lax.ppermute(given, "energy", relay_pairs))

    def sent_after(part):
        free_first[part - 1], cut = lax.optimization_barrier((free_first[part - 1], cuts[part]))
        free_first.append(lax.ppermute(cut, "energy", first_pairs))

    sent_on(0)
    whole_map, whole_source = call(
        own_kernel,
        32,
        5 * count - 3,
        (whole, whole),
        free,
        coupling,
        sums,
    )

    whole_source, field, perm, ends, mode_tiles = lax.optimization_barrier(
        (whole_source, potential_old, permittivity, ends, mode_tiles)
    )
    beyond = [(e, e + 1) for e in range(1, energies - 1, 2)]
    other_ends = lax.ppermute(ends, "energy", beyond + [(b, a) for a, b in beyond])
    is_odd = mine % 2 == 1
    ends_before = jnp.where(is_odd, twin_ends, other_ends).reshape(2, 2, cells, 1, depth)
    ends_after = jnp.where(is_odd, other_ends, twin_ends).reshape(2, 2, cells, 1, depth)
    edge = jnp.zeros((2, cells, rows, 1), jnp.float32)
    halos = ((wire_before, wire_after), (ends_before[:, 1], ends_after[:, 0]), (edge, edge))
    potential_new = relaxed(field, perm, charge, halos)

    odd = mine % 2
    distance = jnp.array([2, 2, 1, 1], jnp.int32)
    lowered = jnp.stack([turned, 1 - turned, 1 - odd, odd]).astype(jnp.float32)
    factors = (shifts[None, :] == distance[:, None]) * (occupation[None, :] + lowered[:, None])
    weights = jnp.sum(factors[:, :, None, None] * mode_tiles[None], axis=1)
    pick = jnp.stack([turned ^ odd, has_second]).astype(jnp.int32)

    block = pl.BlockSpec((1, 2, width, width), lambda s: (s, 0, 0, 0))
    one_state = pl.BlockSpec((2, width, width), lambda s: (0, 0, 0))
    own_block = [
        pl.BlockSpec((1, 2, width, width), lambda s, first=i * half: (first + s, 0, 0, 0))
        for i in range(2)
    ]

    def beside(index, parts):
        made = shape(half, 2, width, width)
        whole_spec = pl.BlockSpec((half, 2, width, width), lambda s: (0, 0, 0, 0))
        return call(
            functools.partial(beside_kernel, index * half, count, len(parts)),
            24,
            2 * half,
            (made, made),
            *parts,
            coupling,
            sums,
            grid=(1,),
            in_specs=[pl.BlockSpec(part.shape, lambda s: (0, 0, 0, 0)) for part in parts]
            + [
                pl.BlockSpec((half, 2, width, width), lambda s: (index, 0, 0, 0)),
                pl.BlockSpec(sums.shape, lambda s: (0, 0)),
            ],
            out_specs=(whole_spec, whole_spec),
        )

    def greens_of(room, link, source, carried):
        return call(
            greens_kernel,
            room,
            2 * link.shape[0],
            (shape(*link.shape), whole),
            link,
            source,
            carried,
            grid=(link.shape[0],),
            in_specs=[block, block, one_state],
            out_specs=(block, one_state),
        )

    leaving = whole_source
    beside_first, beside_second = [None, None], [None, None]
    for hop in range(1, peers - 1):
        arrived = lax.ppermute(leaving, "slab", wire_up)
        if hop == 1:
            sent_on(1)
            sent_after(2)
            arrived, weights, free_first[1] = lax.optimization_barrier(
                (arrived, weights, free_first[1])
            )
        if hop == 2:
            sent_on(2)
            sent_after(3)
            beside_first[0] = beside(0, free_first[:2])
            arrived, beside_first[0], free_first[2], *free_second[:2] = lax.optimization_barrier(
                (arrived, beside_first[0], free_first[2], *free_second[:2])
            )
        leaving = call(hop_kernel, 12, 2, whole, whole_map, whole_source, arrived)

    def both(pairs):
        return [(a * peers + i, b * peers + j) for a, b in pairs for i, j in wire_up]

    carried = lax.ppermute(leaving, "slab", wire_up)
    carried_second = lax.ppermute(leaving, ("energy", "slab"), both(second_pairs))
    sent_on(3)
    beside_second[0] = beside(0, free_second[:2])
    beside_first[1] = beside(1, free_first[2:])
    carried, beside_first[1], beside_second[0], potential_new, free_second[2] = (
        lax.optimization_barrier(
            (carried, beside_first[1], beside_second[0], potential_new, free_second[2])
        )
    )
    carried_first = lax.ppermute(carried, "energy", first_pairs)
    carried, free_second[3] = lax.optimization_barrier((carried, free_second[3]))
    greens, _ = call(
        functools.partial(own_greens_kernel, count),
        24,
        4 * count,
        (blocks, whole),
        free,
        coupling,
        sums,
        carried,
        grid=(count,),
        in_specs=[block, block, pl.BlockSpec(sums.shape, lambda s: (0, 0)), one_state],
        out_specs=(block, one_state),
    )
    beside_second[1] = beside(1, free_second[2:])
    carried_second, greens = lax.optimization_barrier((carried_second, greens))
    greens_second = []
    for part in beside_second:
        made, carried_second = greens_of(16, *part, carried_second)
        greens_second.append(made)
    carried_first, greens_second = lax.optimization_barrier((carried_first, greens_second))

    outputs = []
    for index, part in enumerate(beside_first):
        here, there, carried_first = call(
            mixing_kernel,
            20,
            2 * half,
            (shape(half, 2, width, width), shape(half, 2, width, width), whole),
            pick,
            *part,
            carried_first,
            greens,
            greens_second[index],
            weights,
            grid=(half,),
            in_specs=[
                pl.BlockSpec(memory_space=pltpu.SMEM),
                block,
                block,
                one_state,
                own_block[index],
                block,
                pl.BlockSpec((4, width, width), lambda s: (0, 0, 0)),
            ],
            out_specs=(block, block, one_state),
        )
        if outputs:
            outputs[0], there = lax.optimization_barrier((outputs[0], there))
        outputs.append(here + lax.ppermute(there, "energy", twin_pairs))
    return potential_new, jnp.concatenate(outputs, axis=0)[None]


def solution(mesh):
    in_specs = (
        P("slab", "energy", None),
        P("slab", "energy", None),
        P("slab", "energy", None),
        P("slab", None),
        P("energy", "slab", None, None, None),
        P("slab", None, None, None),
        P(),
        P(),
        P(),
    )
    out_specs = (P("slab", "energy", None), P("energy", "slab", None, None, None))
    return jax.shard_map(
        per_device, mesh=mesh, in_specs=in_specs, out_specs=out_specs, check_vma=False
    )
```

```python
import functools
import math
import jax
import jax.numpy as jnp
from jax import lax
from jax.experimental import pallas as pl
from jax.experimental.pallas import tpu as pltpu
from jax.sharding import PartitionSpec as P

MIB = 1024 * 1024


def halves(value):
    high = value.astype(jnp.bfloat16)
    low = (value - high.astype(jnp.float32)).astype(jnp.bfloat16)
    return high, low


def parts_of(block):
    real, imag = block
    return [halves(real), halves(imag), halves(0.5 * real + 0.5 * imag)]


def left_form(block):
    return [jnp.concatenate([high, high, low], axis=1) for high, low in parts_of(block)]


def right_form(block, axis=0):
    return [jnp.concatenate([high, low, high], axis=axis) for high, low in parts_of(block)]


def three_products(left, right, flipped):
    dims = (((1,), (1 if flipped else 0,)), ((), ()))
    by_real, by_imag, by_mean = (
        lax.dot_general(a, b, dimension_numbers=dims, preferred_element_type=jnp.float32)
        for a, b in zip(left, right)
    )
    return by_real - by_imag, 4.0 * (by_mean - 0.25 * by_real - 0.25 * by_imag)


def product(former, latter):
    return three_products(left_form(former), right_form(latter), False)


def sandwich(link, inner):
    half_way = three_products(left_form(link), right_form(inner), False)
    return three_products(left_form(half_way), right_form(link, 1), True)


def added(first, second):
    return first[0] + second[0], first[1] + second[1]


def pair_of(ref, *where):
    return ref[(*where, 0)], ref[(*where, 1)]


def put(ref, value, *where):
    ref[(*where, 0)] = value[0]
    ref[(*where, 1)] = value[1]


def call(kernel, room, products, out_shapes, *operands, **more):
    flops = products * 9 * 2 * max(x.shape[-1] for x in operands) ** 3
    moved = sum(4 * math.prod(x.shape) for x in jax.tree.leaves((operands, out_shapes)))
    cost = pl.CostEstimate(flops=flops, bytes_accessed=moved, transcendentals=0)
    return pl.pallas_call(
        kernel,
        out_shape=out_shapes,
        cost_estimate=cost,
        compiler_params=pltpu.CompilerParams(vmem_limit_bytes=room * MIB),
        **more,
    )(*operands)


def shape(*dims):
    return jax.ShapeDtypeStruct(dims, jnp.float32)


def gather_kernel(rows, peers, mine, field, perm, charge, before, after, owner, free, *refs):
    out, ends, *parts, held, here, gone = refs
    loads, stores = [], []
    for index in range(len(parts)):
        slab = free.at[index + 1 : index + 2]
        loads.append(
            pltpu.make_async_copy(slab, held.at[index : index + 1], here.at[index])
        )
        loads[-1].start()
    total, depth = charge.shape
    count, orbitals = owner.shape
    height = total // count
    cross = rows * peers
    row_ids = lax.broadcasted_iota(jnp.int32, (total, depth), 0) % rows
    lane_ids = lax.broadcasted_iota(jnp.int32, (total, depth), 1)

    def neighbours(inner, first, last):
        down = jnp.concatenate([first, inner[:-rows]], axis=0)
        up = jnp.concatenate([inner[rows:], last], axis=0)
        left = jnp.where(lane_ids == 0, 0.0, pltpu.roll(inner, 1, axis=1))
        right = jnp.where(lane_ids == depth - 1, 0.0, pltpu.roll(inner, depth - 1, axis=1))
        low = jnp.where(row_ids == 0, 0.0, pltpu.roll(inner, 1, axis=0))
        high = jnp.where(row_ids == rows - 1, 0.0, pltpu.roll(inner, total - 1, axis=0))
        return (down + up) + (left + right) + (low + high)

    first, last = (before[0], before[1]), (after[0], after[1])
    field_now, perm_now = field[...], perm[...]
    both = perm_now * field_now
    own = [
        charge[...],
        perm_now,
        neighbours(field_now, first[0], last[0]),
        neighbours(both, first[0] * first[1], last[0] * last[1]),
        neighbours(perm_now, first[1], last[1]),
    ]
    beside = [jnp.zeros_like(both), jnp.zeros_like(both), field_now, both, perm_now]
    kinds = len(own)
    places = lax.broadcasted_iota(jnp.int32, (2 * height, orbitals), 0)
    depths = lax.broadcasted_iota(jnp.int32, (depth, orbitals), 0)
    first_row = mine[0] * rows
    step = 0
    for slab in range(count):
        if slab == count // 2:
            for index, part in enumerate(parts):
                loads[index].wait()
                stores.append(
                    pltpu.make_async_copy(held.at[index : index + 1], part, gone.at[index])
                )
                stores[-1].start()
        cells = owner[slab : slab + 1, :]
        lane, line = cells % depth, cells // depth
        across, along = line % cross - first_row, line // cross * rows
        key = jnp.where(across == rows, height + along + rows - 1, -1)
        key = jnp.where(across == -1, height + along, key)
        key = jnp.where((across >= 0) & (across < rows), along + across, key)
        cut = slice(slab * height, (slab + 1) * height)
        table = jnp.concatenate(
            [
                jnp.concatenate([t[cut] for t in own], axis=1),
                jnp.concatenate([t[cut] for t in beside], axis=1),
            ],
            axis=0,
        ).T
        high, rest = halves(table)
        middle = rest.astype(jnp.float32)
        lowest = ((table - high.astype(jnp.float32)) - middle).astype(jnp.bfloat16)
        hit = jnp.where(places == key, 1.0, 0.0).astype(jnp.bfloat16)
        found = jnp.dot(
            jnp.concatenate([high, rest, lowest], axis=1),
            jnp.concatenate([hit, hit, hit], axis=0),
            preferred_element_type=jnp.float32,
        )
        for kind in range(kinds):
            part = found[kind * depth : (kind + 1) * depth]
            value = jnp.sum(jnp.where(depths == lane, part, 0.0), axis=0, keepdims=True)
            for piece in range(orbitals // depth):
                row = sums_row(kind, slab, count, orbitals // depth) + piece
                out[row : row + 1, :] = value[:, piece * depth : (piece + 1) * depth]
    start = 0
    for array in (field, perm):
        for end in (0, rows - 1):
            ends[start : start + total // rows, :] = array[
                pl.ds(end, total // rows, stride=rows), :
            ]
            start += total // rows
    for store in stores:
        store.wait()


def sums_row(kind, slab, count, pieces):
    return (kind * count + slab) * pieces


def potential_of(sums, slab, count, orbitals):
    pieces = orbitals // sums.shape[1]

    def value(kind):
        first = sums_row(kind, slab, count, pieces)
        return jnp.concatenate([sums[pl.ds(first + p, 1), :] for p in range(pieces)], axis=1)

    charge, perm, fields, both, perms = (value(kind) for kind in range(5))
    return (charge + 0.5 * (perm * fields + both)) / (3.0 * perm + 0.5 * perms)


def source_of(block, potential):
    scaled = (block[0] * potential, block[1] * potential)
    return added(block, product(scaled, block))


def own_kernel(free, coupling, sums, whole_map, whole_source):
    count = free.shape[0]
    links, state = [], None
    for slab in range(count):
        block = pair_of(free, slab)
        links.append(product(block, pair_of(coupling, slab)))
        source = source_of(block, potential_of(sums, slab, count, free.shape[-1]))
        state = source if state is None else added(sandwich(links[slab], state), source)
    put(whole_source, state)
    while len(links) > 1:
        paired = [product(b, a) for a, b in zip(links[0::2], links[1::2])]
        links = paired + links[len(paired) * 2 :]
    put(whole_map, links[0])


def hop_kernel(whole_map, whole_source, carried, out):
    put(out, added(sandwich(pair_of(whole_map), pair_of(carried)), pair_of(whole_source)))


def last_hop_kernel(odd, whole_map, whole_source, carried, before, out, onward):
    now = added(sandwich(pair_of(whole_map), pair_of(carried)), pair_of(whole_source))
    put(out, now)
    put(onward, [jnp.where(odd[0] != 0, before[part], now[part]) for part in range(2)])


def beside_kernel(start, count, parts, *refs):
    frees, (coupling, sums, link, source) = refs[:parts], refs[parts:]
    slab = 0
    for free in frees:
        for place in range(free.shape[0]):
            block = pair_of(free, place)
            put(link, product(block, pair_of(coupling, slab)), slab)
            row = potential_of(sums, start + slab, count, free.shape[-1])
            put(source, source_of(block, row), slab)
            slab += 1


def greens_kernel(link, source, carried, greens, state):
    @pl.when(pl.program_id(0) == 0)
    def _():
        state[...] = carried[...]

    now = added(sandwich(pair_of(link, 0), pair_of(state)), pair_of(source, 0))
    put(state, now)
    put(greens, now, 0)


def own_greens_kernel(count, free, coupling, sums, carried, greens, state):
    @pl.when(pl.program_id(0) == 0)
    def _():
        state[...] = carried[...]

    block = pair_of(free, 0)
    link = product(block, pair_of(coupling, 0))
    row = potential_of(sums, pl.program_id(0), count, free.shape[-1])
    now = added(sandwich(link, pair_of(state)), source_of(block, row))
    put(state, now)
    put(greens, now, 0)


def mixing_kernel(pick, link, source, carried, own, second, weights, here, there, state):
    @pl.when(pl.program_id(0) == 0)
    def _():
        state[...] = carried[...]

    first = added(sandwich(pair_of(link, 0), pair_of(state)), pair_of(source, 0))
    put(state, first)
    for part in range(2):
        second_now = jnp.where(pick[1] != 0, second[0, part], 0.0)
        here[0, part] = weights[0] * first[part] + weights[1] * second_now
        picked = jnp.where(pick[0] == 0, first[part], second_now)
        there[0, part] = weights[2] * own[0, part] + weights[3] * picked


def relaxed(field, perm, charge, halos):
    numerator = charge
    denominator = jnp.zeros_like(charge)
    for dim in range(3):
        length = charge.shape[dim]
        before, after = halos[dim]
        for side in range(2):
            sides = []
            for which, array in enumerate((field, perm)):
                if side == 0:
                    kept = lax.slice_in_dim(array, 1, length, axis=dim)
                    parts = [kept, after[which]]
                else:
                    kept = lax.slice_in_dim(array, 0, length - 1, axis=dim)
                    parts = [before[which], kept]
                sides.append(jnp.concatenate(parts, axis=dim))
            face = 0.5 * (perm + sides[1])
            numerator = numerator + face * sides[0]
            denominator = denominator + face
    return numerator / denominator


def end_planes(array, dim):
    length = array.shape[dim]
    return (
        lax.slice_in_dim(array, 0, 1, axis=dim),
        lax.slice_in_dim(array, length - 1, length, axis=dim),
    )


def exchanged(sums, ends, early):
    peers = lax.axis_size("energy")
    assert peers >= 4 and peers & (peers - 1) == 0
    masks = [2, 1] + [1 << k for k in range(2, peers.bit_length() - 1)]
    rows, twin_ends = sums.shape[0], None
    first = None
    sums, early = lax.optimization_barrier((sums, early))
    for mask in masks:
        given = jnp.concatenate([sums, ends]) if mask == 1 else sums
        arrived = lax.ppermute(given, "energy", [(e, e ^ mask) for e in range(peers)])
        if mask == 1:
            twin_ends = arrived[rows:]
        sums = sums + arrived[:rows]
        first = sums if first is None else first
    return sums, twin_ends, first, early


def per_device(
    potential_old,
    charge,
    permittivity,
    owner_cell,
    green_free,
    coupling,
    shifts,
    occupation,
    mode_tiles,
):
    energies, peers = lax.axis_size("energy"), lax.axis_size("slab")
    mine = lax.axis_index("energy")
    free = green_free[0]
    count, _, width, _ = free.shape
    whole = shape(2, width, width)
    blocks = shape(count, 2, width, width)

    everyone = range(energies)
    relayed = energies == 8
    if relayed:
        first_pairs = [(e, e ^ 2) for e in everyone]
        second_pairs = [(2, 4), (3, 5), (4, 2), (5, 3)]
        relay_pairs = [(e, e ^ 4) for e in everyone]
        turned = (mine // 2) % 2
        has_second = jnp.where((mine >= 2) & (mine < 6), 1, 0)
    else:
        first_pairs = [(e, e - 2) for e in everyone if e >= 2]
        second_pairs = [(e, e + 2) for e in everyone if e + 2 < energies]
        relay_pairs = second_pairs
        turned = jnp.zeros_like(mine)
        has_second = jnp.ones_like(mine)
    twin_pairs = [(e, e ^ 1) for e in everyone]

    half = count // 2
    one_slab = shape(1, 2, width, width)
    first_cut = free[:1]
    free_first = [lax.ppermute(first_cut, "energy", first_pairs)]

    place = lax.axis_index("slab")
    wire_up = [(i, i + 1) for i in range(peers - 1)]

    def swaps(start):
        pairs = [(i, i + 1) for i in range(start, peers - 1, 2)]
        return pairs + [(j, i) for i, j in pairs]

    first_cut, stacked = lax.optimization_barrier(
        (first_cut, jnp.stack([potential_old, permittivity]))
    )
    lower, upper = end_planes(stacked, 1)
    even = place % 2 == 0
    arrived = lax.ppermute(jnp.where(even, upper, lower), "slab", swaps(0))
    crossed = lax.ppermute(jnp.where(even, lower, upper), "slab", swaps(1))
    wire_before = jnp.where(even, crossed, arrived)
    wire_after = jnp.where(even, arrived, crossed)

    cells, rows, depth = charge.shape
    far, near = pl.BlockSpec(memory_space=pl.ANY), pl.BlockSpec(memory_space=pltpu.VMEM)
    sums, ends, *cuts = call(
        functools.partial(gather_kernel, rows, energies),
        56,
        1,
        (
            shape(5 * count * (width // depth), depth),
            shape(4 * cells, depth),
            *[one_slab] * (count - 1),
        ),
        jnp.reshape(mine, (1,)),
        *(array.reshape(-1, depth) for array in (potential_old, permittivity, charge)),
        wire_before.reshape(2, rows, depth),
        wire_after.reshape(2, rows, depth),
        owner_cell,
        free,
        in_specs=[pl.BlockSpec(memory_space=pltpu.SMEM)] + [near] * 6 + [far],
        out_specs=(near, near, *[far] * (count - 1)),
        scratch_shapes=[
            pltpu.VMEM((count - 1, 2, width, width), jnp.float32),
            pltpu.SemaphoreType.DMA((count - 1,)),
            pltpu.SemaphoreType.DMA((count - 1,)),
        ],
    )
    cuts = [first_cut, *cuts]
    sums, twin_ends, crossed, arrived = exchanged(sums, ends, free_first[0])

    crossed, cuts[1] = lax.optimization_barrier((crossed, cuts[1]))
    sums, arrived = lax.optimization_barrier((sums, arrived))
    free_first = [arrived, lax.ppermute(cuts[1], "energy", first_pairs)]
    free_second = []

    def sent_on(part):
        given = free_first[part] if relayed else cuts[part]
        free_second.append(lax.ppermute(given, "energy", relay_pairs))

    def sent_after(part):
        free_first[part - 1], cut = lax.optimization_barrier((free_first[part - 1], cuts[part]))
        free_first.append(lax.ppermute(cut, "energy", first_pairs))

    sent_on(0)
    whole_map, whole_source = call(
        own_kernel,
        32,
        5 * count - 3,
        (whole, whole),
        free,
        coupling,
        sums,
    )

    whole_source, mode_tiles = lax.optimization_barrier((whole_source, mode_tiles))
    odd = mine % 2
    distance = jnp.array([2, 2, 1, 1], jnp.int32)
    lowered = jnp.stack([turned, 1 - turned, 1 - odd, odd]).astype(jnp.float32)
    factors = (shifts[None, :] == distance[:, None]) * (occupation[None, :] + lowered[:, None])
    weights = jnp.sum(factors[:, :, None, None] * mode_tiles[None], axis=1)
    pick = jnp.stack([turned ^ odd, has_second]).astype(jnp.int32)

    block = pl.BlockSpec((1, 2, width, width), lambda s: (s, 0, 0, 0))
    one_state = pl.BlockSpec((2, width, width), lambda s: (0, 0, 0))
    own_block = [
        pl.BlockSpec((1, 2, width, width), lambda s, first=i * half: (first + s, 0, 0, 0))
        for i in range(2)
    ]

    def beside(index, parts):
        made = shape(half, 2, width, width)
        whole_spec = pl.BlockSpec((half, 2, width, width), lambda s: (0, 0, 0, 0))
        return call(
            functools.partial(beside_kernel, index * half, count, len(parts)),
            24,
            2 * half,
            (made, made),
            *parts,
            coupling,
            sums,
            grid=(1,),
            in_specs=[pl.BlockSpec(part.shape, lambda s: (0, 0, 0, 0)) for part in parts]
            + [
                pl.BlockSpec((half, 2, width, width), lambda s: (index, 0, 0, 0)),
                pl.BlockSpec(sums.shape, lambda s: (0, 0)),
            ],
            out_specs=(whole_spec, whole_spec),
        )

    def greens_of(room, link, source, carried):
        return call(
            greens_kernel,
            room,
            2 * link.shape[0],
            (shape(*link.shape), whole),
            link,
            source,
            carried,
            grid=(link.shape[0],),
            in_specs=[block, block, one_state],
            out_specs=(block, one_state),
        )

    assert peers % 2 == 0
    leaving, previous, before = whole_source, None, None
    beside_first, beside_second = [None, None], [None, None]
    for hop in range(1, peers - 1):
        arrived = lax.ppermute(leaving, "slab", swaps((hop - 1) % 2))
        if hop == 1:
            sent_on(1)
            sent_after(2)
            arrived, weights, free_first[1] = lax.optimization_barrier(
                (arrived, weights, free_first[1])
            )
        if hop == 2:
            sent_on(2)
            sent_after(3)
            beside_first[0] = beside(0, free_first[:2])
            arrived, beside_first[0], free_first[2], *free_second[:2] = lax.optimization_barrier(
                (arrived, beside_first[0], free_first[2], *free_second[:2])
            )
        previous, before = arrived, leaving
        if hop < peers - 2:
            leaving = call(hop_kernel, 12, 2, whole, whole_map, whole_source, arrived)
    leaving, onward = call(
        last_hop_kernel,
        12,
        2,
        (whole, whole),
        jnp.reshape(place % 2, (1,)),
        whole_map,
        whole_source,
        previous,
        before,
        in_specs=[pl.BlockSpec(memory_space=pltpu.SMEM)] + [near] * 4,
        out_specs=(near, near),
    )

    def both(pairs):
        return [(a * peers + i, b * peers + j) for a, b in pairs for i, j in wire_up]

    arrived = lax.ppermute(leaving, "slab", swaps((peers - 2) % 2))
    carried_second = lax.ppermute(onward, ("energy", "slab"), both(second_pairs))
    sent_on(3)
    beside_second[0] = beside(0, free_second[:2])
    beside_first[1] = beside(1, free_first[2:])
    arrived, beside_first[1], beside_second[0], free_second[2] = lax.optimization_barrier(
        (arrived, beside_first[1], beside_second[0], free_second[2])
    )
    carried = jnp.where(place % 2 == 1, arrived, previous)
    carried_first = lax.ppermute(carried, "energy", first_pairs)
    greens, _ = call(
        functools.partial(own_greens_kernel, count),
        24,
        4 * count,
        (blocks, whole),
        free,
        coupling,
        sums,
        carried,
        grid=(count,),
        in_specs=[block, block, pl.BlockSpec(sums.shape, lambda s: (0, 0)), one_state],
        out_specs=(block, one_state),
    )
    carried_second, greens, free_second[3], ends, field, perm = lax.optimization_barrier(
        (carried_second, greens, free_second[3], ends, potential_old, permittivity)
    )

    beyond = [(e, e + 1) for e in range(1, energies - 1, 2)]
    other_ends = lax.ppermute(ends, "energy", beyond + [(b, a) for a, b in beyond])
    ends_before = jnp.where(odd == 1, twin_ends, other_ends).reshape(2, 2, cells, 1, depth)
    ends_after = jnp.where(odd == 1, other_ends, twin_ends).reshape(2, 2, cells, 1, depth)
    edge = jnp.zeros((2, cells, rows, 1), jnp.float32)
    halos = ((wire_before, wire_after), (ends_before[:, 1], ends_after[:, 0]), (edge, edge))
    potential_new = relaxed(field, perm, charge, halos)

    beside_second[1] = beside(1, free_second[2:])
    greens_second = []
    for part in beside_second:
        made, carried_second = greens_of(16, *part, carried_second)
        greens_second.append(made)
    carried_first, greens_second, potential_new = lax.optimization_barrier(
        (carried_first, greens_second, potential_new)
    )

    outputs = []
    for index, part in enumerate(beside_first):
        here, there, carried_first = call(
            mixing_kernel,
            20,
            2 * half,
            (shape(half, 2, width, width), shape(half, 2, width, width), whole),
            pick,
            *part,
            carried_first,
            greens,
            greens_second[index],
            weights,
            grid=(half,),
            in_specs=[
                pl.BlockSpec(memory_space=pltpu.SMEM),
                block,
                block,
                one_state,
                own_block[index],
                block,
                pl.BlockSpec((4, width, width), lambda s: (0, 0, 0)),
            ],
            out_specs=(block, block, one_state),
        )
        if outputs:
            outputs[0], there = lax.optimization_barrier((outputs[0], there))
        outputs.append(here + lax.ppermute(there, "energy", twin_pairs))
    return potential_new, jnp.concatenate(outputs, axis=0)[None]


def solution(mesh):
    in_specs = (
        P("slab", "energy", None),
        P("slab", "energy", None),
        P("slab", "energy", None),
        P("slab", None),
        P("energy", "slab", None, None, None),
        P("slab", None, None, None),
        P(),
        P(),
        P(),
    )
    out_specs = (P("slab", "energy", None), P("energy", "slab", None, None, None))
    return jax.shard_map(
        per_device, mesh=mesh, in_specs=in_specs, out_specs=out_specs, check_vma=False
    )
```

```python
import functools
import math
import jax
import jax.numpy as jnp
from jax import lax
from jax.experimental import pallas as pl
from jax.experimental.pallas import tpu as pltpu
from jax.sharding import PartitionSpec as P

MIB = 1024 * 1024


def halves(value):
    high = value.astype(jnp.bfloat16)
    low = (value - high.astype(jnp.float32)).astype(jnp.bfloat16)
    return high, low


def parts_of(block):
    real, imag = block
    return [halves(real), halves(imag), halves(0.5 * real + 0.5 * imag)]


def left_form(block):
    return [jnp.concatenate([high, high, low], axis=1) for high, low in parts_of(block)]


def right_form(block, axis=0):
    return [jnp.concatenate([high, low, high], axis=axis) for high, low in parts_of(block)]


def three_products(left, right, flipped):
    dims = (((1,), (1 if flipped else 0,)), ((), ()))
    by_real, by_imag, by_mean = (
        lax.dot_general(a, b, dimension_numbers=dims, preferred_element_type=jnp.float32)
        for a, b in zip(left, right)
    )
    return by_real - by_imag, 4.0 * (by_mean - 0.25 * by_real - 0.25 * by_imag)


def product(former, latter):
    return three_products(left_form(former), right_form(latter), False)


def sandwich(link, inner):
    half_way = three_products(left_form(link), right_form(inner), False)
    return three_products(left_form(half_way), right_form(link, 1), True)


def added(first, second):
    return first[0] + second[0], first[1] + second[1]


def pair_of(ref, *where):
    return ref[(*where, 0)], ref[(*where, 1)]


def put(ref, value, *where):
    ref[(*where, 0)] = value[0]
    ref[(*where, 1)] = value[1]


def call(kernel, room, products, out_shapes, *operands, **more):
    flops = products * 9 * 2 * max(x.shape[-1] for x in operands) ** 3
    moved = sum(4 * math.prod(x.shape) for x in jax.tree.leaves((operands, out_shapes)))
    cost = pl.CostEstimate(flops=flops, bytes_accessed=moved, transcendentals=0)
    return pl.pallas_call(
        kernel,
        out_shape=out_shapes,
        cost_estimate=cost,
        compiler_params=pltpu.CompilerParams(vmem_limit_bytes=room * MIB),
        **more,
    )(*operands)


def shape(*dims):
    return jax.ShapeDtypeStruct(dims, jnp.float32)


def gather_kernel(rows, peers, mine, field, perm, charge, before, after, owner, free, *refs):
    out, ends, *parts, held, here, gone = refs
    loads, stores = [], []
    for index in range(len(parts)):
        slab = free.at[index + 1 : index + 2]
        loads.append(
            pltpu.make_async_copy(slab, held.at[index : index + 1], here.at[index])
        )
        loads[-1].start()
    total, depth = charge.shape
    count, orbitals = owner.shape
    height = total // count
    cross = rows * peers
    row_ids = lax.broadcasted_iota(jnp.int32, (total, depth), 0) % rows
    lane_ids = lax.broadcasted_iota(jnp.int32, (total, depth), 1)

    def neighbours(inner, first, last):
        down = jnp.concatenate([first, inner[:-rows]], axis=0)
        up = jnp.concatenate([inner[rows:], last], axis=0)
        left = jnp.where(lane_ids == 0, 0.0, pltpu.roll(inner, 1, axis=1))
        right = jnp.where(lane_ids == depth - 1, 0.0, pltpu.roll(inner, depth - 1, axis=1))
        low = jnp.where(row_ids == 0, 0.0, pltpu.roll(inner, 1, axis=0))
        high = jnp.where(row_ids == rows - 1, 0.0, pltpu.roll(inner, total - 1, axis=0))
        return (down + up) + (left + right) + (low + high)

    first, last = (before[0], before[1]), (after[0], after[1])
    field_now, perm_now = field[...], perm[...]
    both = perm_now * field_now
    own = [
        charge[...],
        perm_now,
        neighbours(field_now, first[0], last[0]),
        neighbours(both, first[0] * first[1], last[0] * last[1]),
        neighbours(perm_now, first[1], last[1]),
    ]
    beside = [jnp.zeros_like(both), jnp.zeros_like(both), field_now, both, perm_now]
    kinds = len(own)
    places = lax.broadcasted_iota(jnp.int32, (2 * height, orbitals), 0)
    depths = lax.broadcasted_iota(jnp.int32, (depth, orbitals), 0)
    first_row = mine[0] * rows
    step = 0
    for slab in range(count):
        if slab == count // 2:
            for index, part in enumerate(parts):
                loads[index].wait()
                stores.append(
                    pltpu.make_async_copy(held.at[index : index + 1], part, gone.at[index])
                )
                stores[-1].start()
        cells = owner[slab : slab + 1, :]
        lane, line = cells % depth, cells // depth
        across, along = line % cross - first_row, line // cross * rows
        key = jnp.where(across == rows, height + along + rows - 1, -1)
        key = jnp.where(across == -1, height + along, key)
        key = jnp.where((across >= 0) & (across < rows), along + across, key)
        cut = slice(slab * height, (slab + 1) * height)
        table = jnp.concatenate(
            [
                jnp.concatenate([t[cut] for t in own], axis=1),
                jnp.concatenate([t[cut] for t in beside], axis=1),
            ],
            axis=0,
        ).T
        high, rest = halves(table)
        middle = rest.astype(jnp.float32)
        lowest = ((table - high.astype(jnp.float32)) - middle).astype(jnp.bfloat16)
        hit = jnp.where(places == key, 1.0, 0.0).astype(jnp.bfloat16)
        found = jnp.dot(
            jnp.concatenate([high, rest, lowest], axis=1),
            jnp.concatenate([hit, hit, hit], axis=0),
            preferred_element_type=jnp.float32,
        )
        for kind in range(kinds):
            part = found[kind * depth : (kind + 1) * depth]
            value = jnp.sum(jnp.where(depths == lane, part, 0.0), axis=0, keepdims=True)
            for piece in range(orbitals // depth):
                row = sums_row(kind, slab, count, orbitals // depth) + piece
                out[row : row + 1, :] = value[:, piece * depth : (piece + 1) * depth]
    start = 0
    for array in (field, perm):
        for end in (0, rows - 1):
            ends[start : start + total // rows, :] = array[
                pl.ds(end, total // rows, stride=rows), :
            ]
            start += total // rows
    for store in stores:
        store.wait()


def sums_row(kind, slab, count, pieces):
    return (kind * count + slab) * pieces


def potential_of(sums, slab, count, orbitals):
    pieces = orbitals // sums.shape[1]

    def value(kind):
        first = sums_row(kind, slab, count, pieces)
        return jnp.concatenate([sums[pl.ds(first + p, 1), :] for p in range(pieces)], axis=1)

    charge, perm, fields, both, perms = (value(kind) for kind in range(5))
    return (charge + 0.5 * (perm * fields + both)) / (3.0 * perm + 0.5 * perms)


def source_of(block, potential):
    scaled = (block[0] * potential, block[1] * potential)
    return added(block, product(scaled, block))


def own_kernel(free, coupling, sums, whole_map, whole_source):
    count = free.shape[0]
    links, state = [], None
    for slab in range(count):
        block = pair_of(free, slab)
        links.append(product(block, pair_of(coupling, slab)))
        source = source_of(block, potential_of(sums, slab, count, free.shape[-1]))
        state = source if state is None else added(sandwich(links[slab], state), source)
    put(whole_source, state)
    while len(links) > 1:
        paired = [product(b, a) for a, b in zip(links[0::2], links[1::2])]
        links = paired + links[len(paired) * 2 :]
    put(whole_map, links[0])


def hop_kernel(whole_map, whole_source, carried, out):
    put(out, added(sandwich(pair_of(whole_map), pair_of(carried)), pair_of(whole_source)))


def last_hop_kernel(odd, whole_map, whole_source, carried, before, out, onward):
    now = added(sandwich(pair_of(whole_map), pair_of(carried)), pair_of(whole_source))
    put(out, now)
    put(onward, [jnp.where(odd[0] != 0, before[part], now[part]) for part in range(2)])


def beside_kernel(start, count, parts, *refs):
    frees, (coupling, sums, link, source) = refs[:parts], refs[parts:]
    slab = 0
    for free in frees:
        for place in range(free.shape[0]):
            block = pair_of(free, place)
            put(link, product(block, pair_of(coupling, slab)), slab)
            row = potential_of(sums, start + slab, count, free.shape[-1])
            put(source, source_of(block, row), slab)
            slab += 1


def greens_kernel(link, source, carried, greens, state):
    @pl.when(pl.program_id(0) == 0)
    def _():
        state[...] = carried[...]

    now = added(sandwich(pair_of(link, 0), pair_of(state)), pair_of(source, 0))
    put(state, now)
    put(greens, now, 0)


def own_greens_kernel(count, free, coupling, sums, carried, greens, state):
    @pl.when(pl.program_id(0) == 0)
    def _():
        state[...] = carried[...]

    block = pair_of(free, 0)
    link = product(block, pair_of(coupling, 0))
    row = potential_of(sums, pl.program_id(0), count, free.shape[-1])
    now = added(sandwich(link, pair_of(state)), source_of(block, row))
    put(state, now)
    put(greens, now, 0)


def mixing_kernel(pick, link, source, carried, own, second, weights, here, there, state):
    @pl.when(pl.program_id(0) == 0)
    def _():
        state[...] = carried[...]

    first = added(sandwich(pair_of(link, 0), pair_of(state)), pair_of(source, 0))
    put(state, first)
    for part in range(2):
        second_now = jnp.where(pick[1] != 0, second[0, part], 0.0)
        here[0, part] = weights[0] * first[part] + weights[1] * second_now
        picked = jnp.where(pick[0] == 0, first[part], second_now)
        there[0, part] = weights[2] * own[0, part] + weights[3] * picked


def relaxed(field, perm, charge, halos):
    numerator = charge
    denominator = jnp.zeros_like(charge)
    for dim in range(3):
        length = charge.shape[dim]
        before, after = halos[dim]
        for side in range(2):
            sides = []
            for which, array in enumerate((field, perm)):
                if side == 0:
                    kept = lax.slice_in_dim(array, 1, length, axis=dim)
                    parts = [kept, after[which]]
                else:
                    kept = lax.slice_in_dim(array, 0, length - 1, axis=dim)
                    parts = [before[which], kept]
                sides.append(jnp.concatenate(parts, axis=dim))
            face = 0.5 * (perm + sides[1])
            numerator = numerator + face * sides[0]
            denominator = denominator + face
    return numerator / denominator


def end_planes(array, dim):
    length = array.shape[dim]
    return (
        lax.slice_in_dim(array, 0, 1, axis=dim),
        lax.slice_in_dim(array, length - 1, length, axis=dim),
    )


def exchanged(sums, ends, early):
    peers = lax.axis_size("energy")
    assert peers >= 4 and peers & (peers - 1) == 0
    masks = [2, 1] + [1 << k for k in range(2, peers.bit_length() - 1)]
    rows, twin_ends = sums.shape[0], None
    first = None
    sums, early = lax.optimization_barrier((sums, early))
    for mask in masks:
        given = jnp.concatenate([sums, ends]) if mask == 1 else sums
        arrived = lax.ppermute(given, "energy", [(e, e ^ mask) for e in range(peers)])
        if mask == 1:
            twin_ends = arrived[rows:]
        sums = sums + arrived[:rows]
        first = sums if first is None else first
    return sums, twin_ends, first, early


def per_device(
    potential_old,
    charge,
    permittivity,
    owner_cell,
    green_free,
    coupling,
    shifts,
    occupation,
    mode_tiles,
):
    energies, peers = lax.axis_size("energy"), lax.axis_size("slab")
    mine = lax.axis_index("energy")
    free = green_free[0]
    count, _, width, _ = free.shape
    whole = shape(2, width, width)
    blocks = shape(count, 2, width, width)

    everyone = range(energies)
    relayed = energies == 8
    if relayed:
        first_pairs = [(e, e ^ 2) for e in everyone]
        second_pairs = [(2, 4), (3, 5), (4, 2), (5, 3)]
        relay_pairs = [(e, e ^ 4) for e in everyone]
        turned = (mine // 2) % 2
        has_second = jnp.where((mine >= 2) & (mine < 6), 1, 0)
    else:
        first_pairs = [(e, e - 2) for e in everyone if e >= 2]
        second_pairs = [(e, e + 2) for e in everyone if e + 2 < energies]
        relay_pairs = second_pairs
        turned = jnp.zeros_like(mine)
        has_second = jnp.ones_like(mine)
    twin_pairs = [(e, e ^ 1) for e in everyone]

    half = count // 2
    one_slab = shape(1, 2, width, width)
    first_cut = free[:1]
    free_first = [lax.ppermute(first_cut, "energy", first_pairs)]

    place = lax.axis_index("slab")
    wire_up = [(i, i + 1) for i in range(peers - 1)]

    def swaps(start):
        pairs = [(i, i + 1) for i in range(start, peers - 1, 2)]
        return pairs + [(j, i) for i, j in pairs]

    first_cut, stacked = lax.optimization_barrier(
        (first_cut, jnp.stack([potential_old, permittivity]))
    )
    lower, upper = end_planes(stacked, 1)
    even = place % 2 == 0
    arrived = lax.ppermute(jnp.where(even, upper, lower), "slab", swaps(0))
    crossed = lax.ppermute(jnp.where(even, lower, upper), "slab", swaps(1))
    wire_before = jnp.where(even, crossed, arrived)
    wire_after = jnp.where(even, arrived, crossed)

    cells, rows, depth = charge.shape
    far, near = pl.BlockSpec(memory_space=pl.ANY), pl.BlockSpec(memory_space=pltpu.VMEM)
    sums, ends, *cuts = call(
        functools.partial(gather_kernel, rows, energies),
        56,
        1,
        (
            shape(5 * count * (width // depth), depth),
            shape(4 * cells, depth),
            *[one_slab] * (count - 1),
        ),
        jnp.reshape(mine, (1,)),
        *(array.reshape(-1, depth) for array in (potential_old, permittivity, charge)),
        wire_before.reshape(2, rows, depth),
        wire_after.reshape(2, rows, depth),
        owner_cell,
        free,
        in_specs=[pl.BlockSpec(memory_space=pltpu.SMEM)] + [near] * 6 + [far],
        out_specs=(near, near, *[far] * (count - 1)),
        scratch_shapes=[
            pltpu.VMEM((count - 1, 2, width, width), jnp.float32),
            pltpu.SemaphoreType.DMA((count - 1,)),
            pltpu.SemaphoreType.DMA((count - 1,)),
        ],
    )
    cuts = [first_cut, *cuts]
    sums, twin_ends, crossed, arrived = exchanged(sums, ends, free_first[0])

    crossed, cuts[1] = lax.optimization_barrier((crossed, cuts[1]))
    sums, arrived = lax.optimization_barrier((sums, arrived))
    free_first = [arrived, lax.ppermute(cuts[1], "energy", first_pairs)]
    free_second = []

    def sent_on(part):
        given = free_first[part] if relayed else cuts[part]
        free_second.append(lax.ppermute(given, "energy", relay_pairs))

    def sent_after(part):
        free_first[part - 1], cut = lax.optimization_barrier((free_first[part - 1], cuts[part]))
        free_first.append(lax.ppermute(cut, "energy", first_pairs))

    sent_on(0)
    whole_map, whole_source = call(
        own_kernel,
        32,
        5 * count - 3,
        (whole, whole),
        free,
        coupling,
        sums,
    )

    whole_source, mode_tiles = lax.optimization_barrier((whole_source, mode_tiles))
    odd = mine % 2
    distance = jnp.array([2, 2, 1, 1], jnp.int32)
    lowered = jnp.stack([turned, 1 - turned, 1 - odd, odd]).astype(jnp.float32)
    factors = (shifts[None, :] == distance[:, None]) * (occupation[None, :] + lowered[:, None])
    weights = jnp.sum(factors[:, :, None, None] * mode_tiles[None], axis=1)
    pick = jnp.stack([turned ^ odd, has_second]).astype(jnp.int32)

    block = pl.BlockSpec((1, 2, width, width), lambda s: (s, 0, 0, 0))
    one_state = pl.BlockSpec((2, width, width), lambda s: (0, 0, 0))
    own_block = [
        pl.BlockSpec((1, 2, width, width), lambda s, first=i * half: (first + s, 0, 0, 0))
        for i in range(2)
    ]

    def beside(index, parts):
        made = shape(half, 2, width, width)
        whole_spec = pl.BlockSpec((half, 2, width, width), lambda s: (0, 0, 0, 0))
        return call(
            functools.partial(beside_kernel, index * half, count, len(parts)),
            24,
            2 * half,
            (made, made),
            *parts,
            coupling,
            sums,
            grid=(1,),
            in_specs=[pl.BlockSpec(part.shape, lambda s: (0, 0, 0, 0)) for part in parts]
            + [
                pl.BlockSpec((half, 2, width, width), lambda s: (index, 0, 0, 0)),
                pl.BlockSpec(sums.shape, lambda s: (0, 0)),
            ],
            out_specs=(whole_spec, whole_spec),
        )

    def greens_of(room, link, source, carried):
        return call(
            greens_kernel,
            room,
            2 * link.shape[0],
            (shape(*link.shape), whole),
            link,
            source,
            carried,
            grid=(link.shape[0],),
            in_specs=[block, block, one_state],
            out_specs=(block, one_state),
        )

    assert peers % 2 == 0
    leaving, previous, before = whole_source, None, None
    beside_first, beside_second = [None, None], [None, None]
    for hop in range(1, peers - 1):
        arrived = lax.ppermute(leaving, "slab", swaps((hop - 1) % 2))
        if hop == 1:
            sent_on(1)
            sent_after(2)
            beside_first[0] = beside(0, free_first[:2])
            arrived, weights, beside_first[0] = lax.optimization_barrier(
                (arrived, weights, beside_first[0])
            )
        if hop == 2:
            sent_on(2)
            sent_after(3)
            arrived, free_first[2], *free_second[:2] = lax.optimization_barrier(
                (arrived, free_first[2], *free_second[:2])
            )
        previous, before = arrived, leaving
        if hop < peers - 2:
            leaving = call(hop_kernel, 12, 2, whole, whole_map, whole_source, arrived)
    leaving, onward = call(
        last_hop_kernel,
        12,
        2,
        (whole, whole),
        jnp.reshape(place % 2, (1,)),
        whole_map,
        whole_source,
        previous,
        before,
        in_specs=[pl.BlockSpec(memory_space=pltpu.SMEM)] + [near] * 4,
        out_specs=(near, near),
    )

    def both(pairs):
        return [(a * peers + i, b * peers + j) for a, b in pairs for i, j in wire_up]

    arrived = lax.ppermute(leaving, "slab", swaps((peers - 2) % 2))
    carried_second = lax.ppermute(onward, ("energy", "slab"), both(second_pairs))
    sent_on(3)
    beside_second[0] = beside(0, free_second[:2])
    beside_first[1] = beside(1, free_first[2:])
    arrived, beside_first[1], beside_second[0], free_second[2] = lax.optimization_barrier(
        (arrived, beside_first[1], beside_second[0], free_second[2])
    )
    carried = jnp.where(place % 2 == 1, arrived, previous)
    carried_first = lax.ppermute(carried, "energy", first_pairs)
    greens, _ = call(
        functools.partial(own_greens_kernel, count),
        24,
        4 * count,
        (blocks, whole),
        free,
        coupling,
        sums,
        carried,
        grid=(count,),
        in_specs=[block, block, pl.BlockSpec(sums.shape, lambda s: (0, 0)), one_state],
        out_specs=(block, one_state),
    )
    carried_second, greens, free_second[3], ends, field, perm = lax.optimization_barrier(
        (carried_second, greens, free_second[3], ends, potential_old, permittivity)
    )

    beyond = [(e, e + 1) for e in range(1, energies - 1, 2)]
    other_ends = lax.ppermute(ends, "energy", beyond + [(b, a) for a, b in beyond])
    ends_before = jnp.where(odd == 1, twin_ends, other_ends).reshape(2, 2, cells, 1, depth)
    ends_after = jnp.where(odd == 1, other_ends, twin_ends).reshape(2, 2, cells, 1, depth)
    edge = jnp.zeros((2, cells, rows, 1), jnp.float32)
    halos = ((wire_before, wire_after), (ends_before[:, 1], ends_after[:, 0]), (edge, edge))
    potential_new = relaxed(field, perm, charge, halos)

    greens_second = [None, None]
    greens_second[0], carried_second = greens_of(16, *beside_second[0], carried_second)
    beside_second[1] = beside(1, free_second[2:])
    greens_second[1], _ = greens_of(16, *beside_second[1], carried_second)
    carried_first, greens_second, potential_new = lax.optimization_barrier(
        (carried_first, greens_second, potential_new)
    )

    outputs = []
    for index, part in enumerate(beside_first):
        here, there, carried_first = call(
            mixing_kernel,
            20,
            2 * half,
            (shape(half, 2, width, width), shape(half, 2, width, width), whole),
            pick,
            *part,
            carried_first,
            greens,
            greens_second[index],
            weights,
            grid=(half,),
            in_specs=[
                pl.BlockSpec(memory_space=pltpu.SMEM),
                block,
                block,
                one_state,
                own_block[index],
                block,
                pl.BlockSpec((4, width, width), lambda s: (0, 0, 0)),
            ],
            out_specs=(block, block, one_state),
        )
        if outputs:
            outputs[0], there = lax.optimization_barrier((outputs[0], there))
        outputs.append(here + lax.ppermute(there, "energy", twin_pairs))
    return potential_new, jnp.concatenate(outputs, axis=0)[None]


def solution(mesh):
    in_specs = (
        P("slab", "energy", None),
        P("slab", "energy", None),
        P("slab", "energy", None),
        P("slab", None),
        P("energy", "slab", None, None, None),
        P("slab", None, None, None),
        P(),
        P(),
        P(),
    )
    out_specs = (P("slab", "energy", None), P("energy", "slab", None, None, None))
    return jax.shard_map(
        per_device, mesh=mesh, in_specs=in_specs, out_specs=out_specs, check_vma=False
    )
```

```python
import functools
import math
import jax
import jax.numpy as jnp
from jax import lax
from jax.experimental import pallas as pl
from jax.experimental.pallas import tpu as pltpu
from jax.sharding import PartitionSpec as P

MIB = 1024 * 1024


def halves(value):
    high = value.astype(jnp.bfloat16)
    low = (value - high.astype(jnp.float32)).astype(jnp.bfloat16)
    return high, low


def parts_of(block):
    real, imag = block
    return [halves(real), halves(imag), halves(0.5 * real + 0.5 * imag)]


def left_form(block):
    return [jnp.concatenate([high, high, low], axis=1) for high, low in parts_of(block)]


def right_form(block, axis=0):
    return [jnp.concatenate([high, low, high], axis=axis) for high, low in parts_of(block)]


def three_products(left, right, flipped):
    dims = (((1,), (1 if flipped else 0,)), ((), ()))
    by_real, by_imag, by_mean = (
        lax.dot_general(a, b, dimension_numbers=dims, preferred_element_type=jnp.float32)
        for a, b in zip(left, right)
    )
    return by_real - by_imag, 4.0 * (by_mean - 0.25 * by_real - 0.25 * by_imag)


def product(former, latter):
    return three_products(left_form(former), right_form(latter), False)


def sandwich(link, inner):
    half_way = three_products(left_form(link), right_form(inner), False)
    return three_products(left_form(half_way), right_form(link, 1), True)


def added(first, second):
    return first[0] + second[0], first[1] + second[1]


def pair_of(ref, *where):
    return ref[(*where, 0)], ref[(*where, 1)]


def put(ref, value, *where):
    ref[(*where, 0)] = value[0]
    ref[(*where, 1)] = value[1]


def call(kernel, room, products, out_shapes, *operands, **more):
    flops = products * 9 * 2 * max(x.shape[-1] for x in operands) ** 3
    moved = sum(4 * math.prod(x.shape) for x in jax.tree.leaves((operands, out_shapes)))
    cost = pl.CostEstimate(flops=flops, bytes_accessed=moved, transcendentals=0)
    return pl.pallas_call(
        kernel,
        out_shape=out_shapes,
        cost_estimate=cost,
        compiler_params=pltpu.CompilerParams(vmem_limit_bytes=room * MIB),
        **more,
    )(*operands)


def shape(*dims):
    return jax.ShapeDtypeStruct(dims, jnp.float32)


def gather_kernel(rows, peers, mine, field, perm, charge, before, after, owner, free, *refs):
    out, ends, *parts, held, here, gone = refs
    loads, stores = [], []
    for index in range(len(parts)):
        slab = free.at[index + 1 : index + 2]
        loads.append(
            pltpu.make_async_copy(slab, held.at[index : index + 1], here.at[index])
        )
        loads[-1].start()
    total, depth = charge.shape
    count, orbitals = owner.shape
    height = total // count
    cross = rows * peers
    row_ids = lax.broadcasted_iota(jnp.int32, (total, depth), 0) % rows
    lane_ids = lax.broadcasted_iota(jnp.int32, (total, depth), 1)

    def neighbours(inner, first, last):
        down = jnp.concatenate([first, inner[:-rows]], axis=0)
        up = jnp.concatenate([inner[rows:], last], axis=0)
        left = jnp.where(lane_ids == 0, 0.0, pltpu.roll(inner, 1, axis=1))
        right = jnp.where(lane_ids == depth - 1, 0.0, pltpu.roll(inner, depth - 1, axis=1))
        low = jnp.where(row_ids == 0, 0.0, pltpu.roll(inner, 1, axis=0))
        high = jnp.where(row_ids == rows - 1, 0.0, pltpu.roll(inner, total - 1, axis=0))
        return (down + up) + (left + right) + (low + high)

    first, last = (before[0], before[1]), (after[0], after[1])
    field_now, perm_now = field[...], perm[...]
    both = perm_now * field_now
    own = [
        charge[...],
        perm_now,
        neighbours(field_now, first[0], last[0]),
        neighbours(both, first[0] * first[1], last[0] * last[1]),
        neighbours(perm_now, first[1], last[1]),
    ]
    beside = [jnp.zeros_like(both), jnp.zeros_like(both), field_now, both, perm_now]
    kinds = len(own)
    places = lax.broadcasted_iota(jnp.int32, (2 * height, orbitals), 0)
    depths = lax.broadcasted_iota(jnp.int32, (depth, orbitals), 0)
    first_row = mine[0] * rows
    step = 0
    for slab in range(count):
        if slab == count // 2:
            for index, part in enumerate(parts):
                loads[index].wait()
                stores.append(
                    pltpu.make_async_copy(held.at[index : index + 1], part, gone.at[index])
                )
                stores[-1].start()
        cells = owner[slab : slab + 1, :]
        lane, line = cells % depth, cells // depth
        across, along = line % cross - first_row, line // cross * rows
        key = jnp.where(across == rows, height + along + rows - 1, -1)
        key = jnp.where(across == -1, height + along, key)
        key = jnp.where((across >= 0) & (across < rows), along + across, key)
        cut = slice(slab * height, (slab + 1) * height)
        table = jnp.concatenate(
            [
                jnp.concatenate([t[cut] for t in own], axis=1),
                jnp.concatenate([t[cut] for t in beside], axis=1),
            ],
            axis=0,
        ).T
        high, rest = halves(table)
        middle = rest.astype(jnp.float32)
        lowest = ((table - high.astype(jnp.float32)) - middle).astype(jnp.bfloat16)
        hit = jnp.where(places == key, 1.0, 0.0).astype(jnp.bfloat16)
        found = jnp.dot(
            jnp.concatenate([high, rest, lowest], axis=1),
            jnp.concatenate([hit, hit, hit], axis=0),
            preferred_element_type=jnp.float32,
        )
        for kind in range(kinds):
            part = found[kind * depth : (kind + 1) * depth]
            value = jnp.sum(jnp.where(depths == lane, part, 0.0), axis=0, keepdims=True)
            for piece in range(orbitals // depth):
                row = sums_row(kind, slab, count, orbitals // depth) + piece
                out[row : row + 1, :] = value[:, piece * depth : (piece + 1) * depth]
    start = 0
    for array in (field, perm):
        for end in (0, rows - 1):
            ends[start : start + total // rows, :] = array[
                pl.ds(end, total // rows, stride=rows), :
            ]
            start += total // rows
    for store in stores:
        store.wait()


def sums_row(kind, slab, count, pieces):
    return (kind * count + slab) * pieces


def potential_of(sums, slab, count, orbitals):
    pieces = orbitals // sums.shape[1]

    def value(kind):
        first = sums_row(kind, slab, count, pieces)
        return jnp.concatenate([sums[pl.ds(first + p, 1), :] for p in range(pieces)], axis=1)

    charge, perm, fields, both, perms = (value(kind) for kind in range(5))
    return (charge + 0.5 * (perm * fields + both)) / (3.0 * perm + 0.5 * perms)


def source_of(block, potential):
    scaled = (block[0] * potential, block[1] * potential)
    return added(block, product(scaled, block))


def own_kernel(free, coupling, sums, whole_map, whole_source):
    count = free.shape[0]
    links, state = [], None
    for slab in range(count):
        block = pair_of(free, slab)
        links.append(product(block, pair_of(coupling, slab)))
        source = source_of(block, potential_of(sums, slab, count, free.shape[-1]))
        state = source if state is None else added(sandwich(links[slab], state), source)
    put(whole_source, state)
    while len(links) > 1:
        paired = [product(b, a) for a, b in zip(links[0::2], links[1::2])]
        links = paired + links[len(paired) * 2 :]
    put(whole_map, links[0])


def hop_kernel(whole_map, whole_source, carried, out):
    put(out, added(sandwich(pair_of(whole_map), pair_of(carried)), pair_of(whole_source)))


def last_hop_kernel(odd, whole_map, whole_source, carried, before, out, onward):
    now = added(sandwich(pair_of(whole_map), pair_of(carried)), pair_of(whole_source))
    put(out, now)
    put(onward, [jnp.where(odd[0] != 0, before[part], now[part]) for part in range(2)])


def beside_kernel(start, count, parts, *refs):
    frees, (coupling, sums, link, source) = refs[:parts], refs[parts:]
    slab = 0
    for free in frees:
        for place in range(free.shape[0]):
            block = pair_of(free, place)
            put(link, product(block, pair_of(coupling, slab)), slab)
            row = potential_of(sums, start + slab, count, free.shape[-1])
            put(source, source_of(block, row), slab)
            slab += 1


def greens_kernel(link, source, carried, greens, state):
    @pl.when(pl.program_id(0) == 0)
    def _():
        state[...] = carried[...]

    now = added(sandwich(pair_of(link, 0), pair_of(state)), pair_of(source, 0))
    put(state, now)
    put(greens, now, 0)


def own_greens_kernel(count, free, coupling, sums, carried, greens, state):
    @pl.when(pl.program_id(0) == 0)
    def _():
        state[...] = carried[...]

    block = pair_of(free, 0)
    link = product(block, pair_of(coupling, 0))
    row = potential_of(sums, pl.program_id(0), count, free.shape[-1])
    now = added(sandwich(link, pair_of(state)), source_of(block, row))
    put(state, now)
    put(greens, now, 0)


def mixing_kernel(pick, link, source, carried, own, second, weights, here, there, state):
    @pl.when(pl.program_id(0) == 0)
    def _():
        state[...] = carried[...]

    first = added(sandwich(pair_of(link, 0), pair_of(state)), pair_of(source, 0))
    put(state, first)
    for part in range(2):
        second_now = jnp.where(pick[1] != 0, second[0, part], 0.0)
        here[0, part] = weights[0] * first[part] + weights[1] * second_now
        picked = jnp.where(pick[0] == 0, first[part], second_now)
        there[0, part] = weights[2] * own[0, part] + weights[3] * picked


def relaxed(field, perm, charge, halos):
    numerator = charge
    denominator = jnp.zeros_like(charge)
    for dim in range(3):
        length = charge.shape[dim]
        before, after = halos[dim]
        for side in range(2):
            sides = []
            for which, array in enumerate((field, perm)):
                if side == 0:
                    kept = lax.slice_in_dim(array, 1, length, axis=dim)
                    parts = [kept, after[which]]
                else:
                    kept = lax.slice_in_dim(array, 0, length - 1, axis=dim)
                    parts = [before[which], kept]
                sides.append(jnp.concatenate(parts, axis=dim))
            face = 0.5 * (perm + sides[1])
            numerator = numerator + face * sides[0]
            denominator = denominator + face
    return numerator / denominator


def end_planes(array, dim):
    length = array.shape[dim]
    return (
        lax.slice_in_dim(array, 0, 1, axis=dim),
        lax.slice_in_dim(array, length - 1, length, axis=dim),
    )


def exchanged(sums, ends, early, crossing):
    peers = lax.axis_size("energy")
    assert peers >= 4 and peers & (peers - 1) == 0
    masks = [1 << k for k in range(1, peers.bit_length() - 1)] + [1]
    rows = sums.shape[0]
    sums, early = lax.optimization_barrier((sums, early))
    for index, mask in enumerate(masks):
        given = jnp.concatenate([sums, ends]) if mask == 1 else sums
        arrived = lax.ppermute(given, "energy", [(e, e ^ mask) for e in range(peers)])
        if mask == 1:
            twin_ends = arrived[rows:]
        sums = sums + arrived[:rows]
        if mask != 1:
            sums = crossing(sums, early, index)
    return sums, twin_ends


def per_device(
    potential_old,
    charge,
    permittivity,
    owner_cell,
    green_free,
    coupling,
    shifts,
    occupation,
    mode_tiles,
):
    energies, peers = lax.axis_size("energy"), lax.axis_size("slab")
    mine = lax.axis_index("energy")
    free = green_free[0]
    count, _, width, _ = free.shape
    whole = shape(2, width, width)
    blocks = shape(count, 2, width, width)

    everyone = range(energies)
    relayed = energies == 8
    if relayed:
        first_pairs = [(e, e ^ 2) for e in everyone]
        second_pairs = [(2, 4), (3, 5), (4, 2), (5, 3)]
        relay_pairs = [(e, e ^ 4) for e in everyone]
        turned = (mine // 2) % 2
        has_second = jnp.where((mine >= 2) & (mine < 6), 1, 0)
    else:
        first_pairs = [(e, e - 2) for e in everyone if e >= 2]
        second_pairs = [(e, e + 2) for e in everyone if e + 2 < energies]
        relay_pairs = second_pairs
        turned = jnp.zeros_like(mine)
        has_second = jnp.ones_like(mine)
    twin_pairs = [(e, e ^ 1) for e in everyone]

    half = count // 2
    one_slab = shape(1, 2, width, width)
    first_cut = free[:1]
    free_first = [lax.ppermute(first_cut, "energy", first_pairs)]

    place = lax.axis_index("slab")
    wire_up = [(i, i + 1) for i in range(peers - 1)]

    def swaps(start):
        pairs = [(i, i + 1) for i in range(start, peers - 1, 2)]
        return pairs + [(j, i) for i, j in pairs]

    first_cut, stacked = lax.optimization_barrier(
        (first_cut, jnp.stack([potential_old, permittivity]))
    )
    lower, upper = end_planes(stacked, 1)
    even = place % 2 == 0
    arrived = lax.ppermute(jnp.where(even, upper, lower), "slab", swaps(0))
    crossed = lax.ppermute(jnp.where(even, lower, upper), "slab", swaps(1))
    wire_before = jnp.where(even, crossed, arrived)
    wire_after = jnp.where(even, arrived, crossed)

    cells, rows, depth = charge.shape
    far, near = pl.BlockSpec(memory_space=pl.ANY), pl.BlockSpec(memory_space=pltpu.VMEM)
    sums, ends, *cuts = call(
        functools.partial(gather_kernel, rows, energies),
        56,
        1,
        (
            shape(5 * count * (width // depth), depth),
            shape(4 * cells, depth),
            *[one_slab] * (count - 1),
        ),
        jnp.reshape(mine, (1,)),
        *(array.reshape(-1, depth) for array in (potential_old, permittivity, charge)),
        wire_before.reshape(2, rows, depth),
        wire_after.reshape(2, rows, depth),
        owner_cell,
        free,
        in_specs=[pl.BlockSpec(memory_space=pltpu.SMEM)] + [near] * 6 + [far],
        out_specs=(near, near, *[far] * (count - 1)),
        scratch_shapes=[
            pltpu.VMEM((count - 1, 2, width, width), jnp.float32),
            pltpu.SemaphoreType.DMA((count - 1,)),
            pltpu.SemaphoreType.DMA((count - 1,)),
        ],
    )
    cuts = [first_cut, *cuts]
    free_first, free_second = free_first[:1], []

    def crossing(sums, early, index):
        if index == 0:
            sums, cuts[1] = lax.optimization_barrier((sums, cuts[1]))
            free_first.append(lax.ppermute(cuts[1], "energy", first_pairs))
        if index == 1:
            sums, free_first[0] = lax.optimization_barrier((sums, early))
            sent_on(0)
        return sums

    def sent_on(part):
        given = free_first[part] if relayed else cuts[part]
        free_second.append(lax.ppermute(given, "energy", relay_pairs))

    def sent_after(part):
        free_first[part - 1], cut = lax.optimization_barrier((free_first[part - 1], cuts[part]))
        free_first.append(lax.ppermute(cut, "energy", first_pairs))

    sums, twin_ends = exchanged(sums, ends, free_first[0], crossing)

    whole_map, whole_source = call(
        own_kernel,
        32,
        5 * count - 3,
        (whole, whole),
        free,
        coupling,
        sums,
    )

    whole_source, mode_tiles = lax.optimization_barrier((whole_source, mode_tiles))
    odd = mine % 2
    distance = jnp.array([2, 2, 1, 1], jnp.int32)
    lowered = jnp.stack([turned, 1 - turned, 1 - odd, odd]).astype(jnp.float32)
    factors = (shifts[None, :] == distance[:, None]) * (occupation[None, :] + lowered[:, None])
    weights = jnp.sum(factors[:, :, None, None] * mode_tiles[None], axis=1)
    pick = jnp.stack([turned ^ odd, has_second]).astype(jnp.int32)

    block = pl.BlockSpec((1, 2, width, width), lambda s: (s, 0, 0, 0))
    one_state = pl.BlockSpec((2, width, width), lambda s: (0, 0, 0))
    own_block = [
        pl.BlockSpec((1, 2, width, width), lambda s, first=i * half: (first + s, 0, 0, 0))
        for i in range(2)
    ]

    def beside(index, parts):
        made = shape(half, 2, width, width)
        whole_spec = pl.BlockSpec((half, 2, width, width), lambda s: (0, 0, 0, 0))
        return call(
            functools.partial(beside_kernel, index * half, count, len(parts)),
            24,
            2 * half,
            (made, made),
            *parts,
            coupling,
            sums,
            grid=(1,),
            in_specs=[pl.BlockSpec(part.shape, lambda s: (0, 0, 0, 0)) for part in parts]
            + [
                pl.BlockSpec((half, 2, width, width), lambda s: (index, 0, 0, 0)),
                pl.BlockSpec(sums.shape, lambda s: (0, 0)),
            ],
            out_specs=(whole_spec, whole_spec),
        )

    def greens_of(room, link, source, carried):
        return call(
            greens_kernel,
            room,
            2 * link.shape[0],
            (shape(*link.shape), whole),
            link,
            source,
            carried,
            grid=(link.shape[0],),
            in_specs=[block, block, one_state],
            out_specs=(block, one_state),
        )

    assert peers % 2 == 0
    leaving, previous, before = whole_source, None, None
    beside_first, beside_second = [None, None], [None, None]
    for hop in range(1, peers - 1):
        arrived = lax.ppermute(leaving, "slab", swaps((hop - 1) % 2))
        if hop == 1:
            sent_on(1)
            sent_after(2)
            arrived, weights, free_first[1], free_second[0] = lax.optimization_barrier(
                (arrived, weights, free_first[1], free_second[0])
            )
        if hop == 2:
            sent_on(2)
            sent_after(3)
            beside_first[0] = beside(0, free_first[:2])
            arrived, beside_first[0], free_first[2], free_second[1] = lax.optimization_barrier(
                (arrived, beside_first[0], free_first[2], free_second[1])
            )
        previous, before = arrived, leaving
        if hop < peers - 2:
            leaving = call(hop_kernel, 12, 2, whole, whole_map, whole_source, arrived)
    leaving, onward = call(
        last_hop_kernel,
        12,
        2,
        (whole, whole),
        jnp.reshape(place % 2, (1,)),
        whole_map,
        whole_source,
        previous,
        before,
        in_specs=[pl.BlockSpec(memory_space=pltpu.SMEM)] + [near] * 4,
        out_specs=(near, near),
    )

    def both(pairs):
        return [(a * peers + i, b * peers + j) for a, b in pairs for i, j in wire_up]

    arrived = lax.ppermute(leaving, "slab", swaps((peers - 2) % 2))
    carried_second = lax.ppermute(onward, ("energy", "slab"), both(second_pairs))
    sent_on(3)
    beside_second[0] = beside(0, free_second[:2])
    beside_first[1] = beside(1, free_first[2:])
    arrived, beside_first[1], beside_second[0], free_second[2] = lax.optimization_barrier(
        (arrived, beside_first[1], beside_second[0], free_second[2])
    )
    carried = jnp.where(place % 2 == 1, arrived, previous)
    carried_first = lax.ppermute(carried, "energy", first_pairs)
    greens, _ = call(
        functools.partial(own_greens_kernel, count),
        24,
        4 * count,
        (blocks, whole),
        free,
        coupling,
        sums,
        carried,
        grid=(count,),
        in_specs=[block, block, pl.BlockSpec(sums.shape, lambda s: (0, 0)), one_state],
        out_specs=(block, one_state),
    )
    carried_second, greens, free_second[3], ends, field, perm = lax.optimization_barrier(
        (carried_second, greens, free_second[3], ends, potential_old, permittivity)
    )

    beyond = [(e, e + 1) for e in range(1, energies - 1, 2)]
    other_ends = lax.ppermute(ends, "energy", beyond + [(b, a) for a, b in beyond])
    ends_before = jnp.where(odd == 1, twin_ends, other_ends).reshape(2, 2, cells, 1, depth)
    ends_after = jnp.where(odd == 1, other_ends, twin_ends).reshape(2, 2, cells, 1, depth)
    edge = jnp.zeros((2, cells, rows, 1), jnp.float32)
    halos = ((wire_before, wire_after), (ends_before[:, 1], ends_after[:, 0]), (edge, edge))
    potential_new = relaxed(field, perm, charge, halos)

    greens_second = [None, None]
    greens_second[0], carried_second = greens_of(16, *beside_second[0], carried_second)
    beside_second[1] = beside(1, free_second[2:])
    greens_second[1], _ = greens_of(16, *beside_second[1], carried_second)
    carried_first, greens_second, potential_new = lax.optimization_barrier(
        (carried_first, greens_second, potential_new)
    )

    outputs = []
    for index, part in enumerate(beside_first):
        here, there, carried_first = call(
            mixing_kernel,
            20,
            2 * half,
            (shape(half, 2, width, width), shape(half, 2, width, width), whole),
            pick,
            *part,
            carried_first,
            greens,
            greens_second[index],
            weights,
            grid=(half,),
            in_specs=[
                pl.BlockSpec(memory_space=pltpu.SMEM),
                block,
                block,
                one_state,
                own_block[index],
                block,
                pl.BlockSpec((4, width, width), lambda s: (0, 0, 0)),
            ],
            out_specs=(block, block, one_state),
        )
        if outputs:
            outputs[0], there = lax.optimization_barrier((outputs[0], there))
        outputs.append(here + lax.ppermute(there, "energy", twin_pairs))
    return potential_new, jnp.concatenate(outputs, axis=0)[None]


def solution(mesh):
    in_specs = (
        P("slab", "energy", None),
        P("slab", "energy", None),
        P("slab", "energy", None),
        P("slab", None),
        P("energy", "slab", None, None, None),
        P("slab", None, None, None),
        P(),
        P(),
        P(),
    )
    out_specs = (P("slab", "energy", None), P("energy", "slab", None, None, None))
    return jax.shard_map(
        per_device, mesh=mesh, in_specs=in_specs, out_specs=out_specs, check_vma=False
    )
```

```python
import functools
import math
import jax
import jax.numpy as jnp
from jax import lax
from jax.experimental import pallas as pl
from jax.experimental.pallas import tpu as pltpu
from jax.sharding import PartitionSpec as P

MIB = 1024 * 1024


def halves(value):
    high = value.astype(jnp.bfloat16)
    low = (value - high.astype(jnp.float32)).astype(jnp.bfloat16)
    return high, low


def parts_of(block):
    real, imag = block
    return [halves(real), halves(imag), halves(0.5 * real + 0.5 * imag)]


def left_form(block):
    return [jnp.concatenate([high, high, low], axis=1) for high, low in parts_of(block)]


def right_form(block, axis=0):
    return [jnp.concatenate([high, low, high], axis=axis) for high, low in parts_of(block)]


def three_products(left, right, flipped):
    dims = (((1,), (1 if flipped else 0,)), ((), ()))
    by_real, by_imag, by_mean = (
        lax.dot_general(a, b, dimension_numbers=dims, preferred_element_type=jnp.float32)
        for a, b in zip(left, right)
    )
    return by_real - by_imag, 4.0 * (by_mean - 0.25 * by_real - 0.25 * by_imag)


def product(former, latter):
    return three_products(left_form(former), right_form(latter), False)


def sandwich(link, inner):
    half_way = three_products(left_form(link), right_form(inner), False)
    return three_products(left_form(half_way), right_form(link, 1), True)


def added(first, second):
    return first[0] + second[0], first[1] + second[1]


def pair_of(ref, *where):
    return ref[(*where, 0)], ref[(*where, 1)]


def put(ref, value, *where):
    ref[(*where, 0)] = value[0]
    ref[(*where, 1)] = value[1]


def call(kernel, room, products, out_shapes, *operands, **more):
    flops = products * 9 * 2 * max(x.shape[-1] for x in operands) ** 3
    moved = sum(4 * math.prod(x.shape) for x in jax.tree.leaves((operands, out_shapes)))
    cost = pl.CostEstimate(flops=flops, bytes_accessed=moved, transcendentals=0)
    return pl.pallas_call(
        kernel,
        out_shape=out_shapes,
        cost_estimate=cost,
        compiler_params=pltpu.CompilerParams(vmem_limit_bytes=room * MIB),
        **more,
    )(*operands)


def shape(*dims):
    return jax.ShapeDtypeStruct(dims, jnp.float32)


def gather_kernel(rows, peers, mine, field, perm, charge, before, after, owner, free, *refs):
    out, ends, *parts, held, here, gone = refs
    loads, stores = [], []
    for index in range(len(parts)):
        slab = free.at[index + 1 : index + 2]
        loads.append(
            pltpu.make_async_copy(slab, held.at[index : index + 1], here.at[index])
        )
        loads[-1].start()
    total, depth = charge.shape
    count, orbitals = owner.shape
    height = total // count
    cross = rows * peers
    row_ids = lax.broadcasted_iota(jnp.int32, (total, depth), 0) % rows
    lane_ids = lax.broadcasted_iota(jnp.int32, (total, depth), 1)

    def neighbours(inner, first, last):
        down = jnp.concatenate([first, inner[:-rows]], axis=0)
        up = jnp.concatenate([inner[rows:], last], axis=0)
        left = jnp.where(lane_ids == 0, 0.0, pltpu.roll(inner, 1, axis=1))
        right = jnp.where(lane_ids == depth - 1, 0.0, pltpu.roll(inner, depth - 1, axis=1))
        low = jnp.where(row_ids == 0, 0.0, pltpu.roll(inner, 1, axis=0))
        high = jnp.where(row_ids == rows - 1, 0.0, pltpu.roll(inner, total - 1, axis=0))
        return (down + up) + (left + right) + (low + high)

    first, last = (before[0], before[1]), (after[0], after[1])
    field_now, perm_now = field[...], perm[...]
    both = perm_now * field_now
    own = [
        charge[...],
        perm_now,
        neighbours(field_now, first[0], last[0]),
        neighbours(both, first[0] * first[1], last[0] * last[1]),
        neighbours(perm_now, first[1], last[1]),
    ]
    beside = [jnp.zeros_like(both), jnp.zeros_like(both), field_now, both, perm_now]
    kinds = len(own)
    places = lax.broadcasted_iota(jnp.int32, (2 * height, orbitals), 0)
    depths = lax.broadcasted_iota(jnp.int32, (depth, orbitals), 0)
    first_row = mine[0] * rows
    step = 0
    for slab in range(count):
        if slab == count // 2:
            for index, part in enumerate(parts):
                loads[index].wait()
                stores.append(
                    pltpu.make_async_copy(held.at[index : index + 1], part, gone.at[index])
                )
                stores[-1].start()
        cells = owner[slab : slab + 1, :]
        lane, line = cells % depth, cells // depth
        across, along = line % cross - first_row, line // cross * rows
        key = jnp.where(across == rows, height + along + rows - 1, -1)
        key = jnp.where(across == -1, height + along, key)
        key = jnp.where((across >= 0) & (across < rows), along + across, key)
        cut = slice(slab * height, (slab + 1) * height)
        table = jnp.concatenate(
            [
                jnp.concatenate([t[cut] for t in own], axis=1),
                jnp.concatenate([t[cut] for t in beside], axis=1),
            ],
            axis=0,
        ).T
        high, rest = halves(table)
        middle = rest.astype(jnp.float32)
        lowest = ((table - high.astype(jnp.float32)) - middle).astype(jnp.bfloat16)
        hit = jnp.where(places == key, 1.0, 0.0).astype(jnp.bfloat16)
        found = jnp.dot(
            jnp.concatenate([high, rest, lowest], axis=1),
            jnp.concatenate([hit, hit, hit], axis=0),
            preferred_element_type=jnp.float32,
        )
        for kind in range(kinds):
            part = found[kind * depth : (kind + 1) * depth]
            value = jnp.sum(jnp.where(depths == lane, part, 0.0), axis=0, keepdims=True)
            for piece in range(orbitals // depth):
                row = sums_row(kind, slab, count, orbitals // depth) + piece
                out[row : row + 1, :] = value[:, piece * depth : (piece + 1) * depth]
    start = 0
    for array in (field, perm):
        for end in (0, rows - 1):
            ends[start : start + total // rows, :] = array[
                pl.ds(end, total // rows, stride=rows), :
            ]
            start += total // rows
    for store in stores:
        store.wait()


def sums_row(kind, slab, count, pieces):
    return (kind * count + slab) * pieces


def potential_of(sums, slab, count, orbitals):
    pieces = orbitals // sums.shape[1]

    def value(kind):
        first = sums_row(kind, slab, count, pieces)
        return jnp.concatenate([sums[pl.ds(first + p, 1), :] for p in range(pieces)], axis=1)

    charge, perm, fields, both, perms = (value(kind) for kind in range(5))
    return (charge + 0.5 * (perm * fields + both)) / (3.0 * perm + 0.5 * perms)


def source_of(block, potential):
    scaled = (block[0] * potential, block[1] * potential)
    return added(block, product(scaled, block))


def own_kernel(free, coupling, sums, whole_map, whole_source):
    count = free.shape[0]
    links, state = [], None
    for slab in range(count):
        block = pair_of(free, slab)
        links.append(product(block, pair_of(coupling, slab)))
        source = source_of(block, potential_of(sums, slab, count, free.shape[-1]))
        state = source if state is None else added(sandwich(links[slab], state), source)
    put(whole_source, state)
    while len(links) > 1:
        paired = [product(b, a) for a, b in zip(links[0::2], links[1::2])]
        links = paired + links[len(paired) * 2 :]
    put(whole_map, links[0])


def hop_kernel(whole_map, whole_source, carried, out):
    put(out, added(sandwich(pair_of(whole_map), pair_of(carried)), pair_of(whole_source)))


def last_hop_kernel(odd, whole_map, whole_source, carried, before, out, onward):
    now = added(sandwich(pair_of(whole_map), pair_of(carried)), pair_of(whole_source))
    put(out, now)
    put(onward, [jnp.where(odd[0] != 0, before[part], now[part]) for part in range(2)])


def beside_kernel(start, count, parts, *refs):
    frees, (coupling, sums, link, source) = refs[:parts], refs[parts:]
    slab = 0
    for free in frees:
        for place in range(free.shape[0]):
            block = pair_of(free, place)
            put(link, product(block, pair_of(coupling, slab)), slab)
            row = potential_of(sums, start + slab, count, free.shape[-1])
            put(source, source_of(block, row), slab)
            slab += 1


def greens_kernel(link, source, carried, greens, state):
    @pl.when(pl.program_id(0) == 0)
    def _():
        state[...] = carried[...]

    now = added(sandwich(pair_of(link, 0), pair_of(state)), pair_of(source, 0))
    put(state, now)
    put(greens, now, 0)


def own_greens_kernel(count, free, coupling, sums, carried, greens, state):
    @pl.when(pl.program_id(0) == 0)
    def _():
        state[...] = carried[...]

    block = pair_of(free, 0)
    link = product(block, pair_of(coupling, 0))
    row = potential_of(sums, pl.program_id(0), count, free.shape[-1])
    now = added(sandwich(link, pair_of(state)), source_of(block, row))
    put(state, now)
    put(greens, now, 0)


def mixing_kernel(pick, link, source, carried, own, second, weights, here, there, state):
    @pl.when(pl.program_id(0) == 0)
    def _():
        state[...] = carried[...]

    first = added(sandwich(pair_of(link, 0), pair_of(state)), pair_of(source, 0))
    put(state, first)
    for part in range(2):
        second_now = jnp.where(pick[1] != 0, second[0, part], 0.0)
        here[0, part] = weights[0] * first[part] + weights[1] * second_now
        picked = jnp.where(pick[0] == 0, first[part], second_now)
        there[0, part] = weights[2] * own[0, part] + weights[3] * picked


def relaxed(field, perm, charge, halos):
    numerator = charge
    denominator = jnp.zeros_like(charge)
    for dim in range(3):
        length = charge.shape[dim]
        before, after = halos[dim]
        for side in range(2):
            sides = []
            for which, array in enumerate((field, perm)):
                if side == 0:
                    kept = lax.slice_in_dim(array, 1, length, axis=dim)
                    parts = [kept, after[which]]
                else:
                    kept = lax.slice_in_dim(array, 0, length - 1, axis=dim)
                    parts = [before[which], kept]
                sides.append(jnp.concatenate(parts, axis=dim))
            face = 0.5 * (perm + sides[1])
            numerator = numerator + face * sides[0]
            denominator = denominator + face
    return numerator / denominator


def end_planes(array, dim):
    length = array.shape[dim]
    return (
        lax.slice_in_dim(array, 0, 1, axis=dim),
        lax.slice_in_dim(array, length - 1, length, axis=dim),
    )


def exchanged(sums, ends, early):
    peers = lax.axis_size("energy")
    assert peers >= 4 and peers & (peers - 1) == 0
    masks = [2, 1] + [1 << k for k in range(2, peers.bit_length() - 1)]
    rows, twin_ends = sums.shape[0], None
    first = None
    sums, early = lax.optimization_barrier((sums, early))
    for mask in masks:
        given = jnp.concatenate([sums, ends]) if mask == 1 else sums
        arrived = lax.ppermute(given, "energy", [(e, e ^ mask) for e in range(peers)])
        if mask == 1:
            twin_ends = arrived[rows:]
        sums = sums + arrived[:rows]
        first = sums if first is None else first
    return sums, twin_ends, first, early


def per_device(
    potential_old,
    charge,
    permittivity,
    owner_cell,
    green_free,
    coupling,
    shifts,
    occupation,
    mode_tiles,
):
    energies, peers = lax.axis_size("energy"), lax.axis_size("slab")
    mine = lax.axis_index("energy")
    free = green_free[0]
    count, _, width, _ = free.shape
    whole = shape(2, width, width)
    blocks = shape(count, 2, width, width)

    everyone = range(energies)
    relayed = energies == 8
    if relayed:
        first_pairs = [(e, e ^ 2) for e in everyone]
        second_pairs = [(2, 4), (3, 5), (4, 2), (5, 3)]
        relay_pairs = [(e, e ^ 4) for e in everyone]
        turned = (mine // 2) % 2
        has_second = jnp.where((mine >= 2) & (mine < 6), 1, 0)
    else:
        first_pairs = [(e, e - 2) for e in everyone if e >= 2]
        second_pairs = [(e, e + 2) for e in everyone if e + 2 < energies]
        relay_pairs = second_pairs
        turned = jnp.zeros_like(mine)
        has_second = jnp.ones_like(mine)
    twin_pairs = [(e, e ^ 1) for e in everyone]

    half = count // 2
    one_slab = shape(1, 2, width, width)
    first_cut = free[:1]
    free_first = [lax.ppermute(first_cut, "energy", first_pairs)]

    place = lax.axis_index("slab")
    wire_up = [(i, i + 1) for i in range(peers - 1)]

    def swaps(start):
        pairs = [(i, i + 1) for i in range(start, peers - 1, 2)]
        return pairs + [(j, i) for i, j in pairs]

    first_cut, stacked = lax.optimization_barrier(
        (first_cut, jnp.stack([potential_old, permittivity]))
    )
    lower, upper = end_planes(stacked, 1)
    even = place % 2 == 0
    arrived = lax.ppermute(jnp.where(even, upper, lower), "slab", swaps(0))
    crossed = lax.ppermute(jnp.where(even, lower, upper), "slab", swaps(1))
    wire_before = jnp.where(even, crossed, arrived)
    wire_after = jnp.where(even, arrived, crossed)

    cells, rows, depth = charge.shape
    far, near = pl.BlockSpec(memory_space=pl.ANY), pl.BlockSpec(memory_space=pltpu.VMEM)
    sums, ends, *cuts = call(
        functools.partial(gather_kernel, rows, energies),
        56,
        1,
        (
            shape(5 * count * (width // depth), depth),
            shape(4 * cells, depth),
            *[one_slab] * (count - 1),
        ),
        jnp.reshape(mine, (1,)),
        *(array.reshape(-1, depth) for array in (potential_old, permittivity, charge)),
        wire_before.reshape(2, rows, depth),
        wire_after.reshape(2, rows, depth),
        owner_cell,
        free,
        in_specs=[pl.BlockSpec(memory_space=pltpu.SMEM)] + [near] * 6 + [far],
        out_specs=(near, near, *[far] * (count - 1)),
        scratch_shapes=[
            pltpu.VMEM((count - 1, 2, width, width), jnp.float32),
            pltpu.SemaphoreType.DMA((count - 1,)),
            pltpu.SemaphoreType.DMA((count - 1,)),
        ],
    )
    cuts = [first_cut, *cuts]
    sums, twin_ends, crossed, arrived = exchanged(sums, ends, free_first[0])

    crossed, cuts[1] = lax.optimization_barrier((crossed, cuts[1]))
    sums, arrived = lax.optimization_barrier((sums, arrived))
    free_first = [arrived, lax.ppermute(cuts[1], "energy", first_pairs)]
    free_second = []

    def sent_on(part):
        given = free_first[part] if relayed else cuts[part]
        free_second.append(lax.ppermute(given, "energy", relay_pairs))

    def sent_after(part):
        free_first[part - 1], cut = lax.optimization_barrier((free_first[part - 1], cuts[part]))
        free_first.append(lax.ppermute(cut, "energy", first_pairs))

    whole_map, whole_source = call(
        own_kernel,
        32,
        5 * count - 3,
        (whole, whole),
        free,
        coupling,
        sums,
    )

    whole_source, mode_tiles = lax.optimization_barrier((whole_source, mode_tiles))
    odd = mine % 2
    distance = jnp.array([2, 2, 1, 1], jnp.int32)
    lowered = jnp.stack([turned, 1 - turned, 1 - odd, odd]).astype(jnp.float32)
    factors = (shifts[None, :] == distance[:, None]) * (occupation[None, :] + lowered[:, None])
    weights = jnp.sum(factors[:, :, None, None] * mode_tiles[None], axis=1)
    pick = jnp.stack([turned ^ odd, has_second]).astype(jnp.int32)

    block = pl.BlockSpec((1, 2, width, width), lambda s: (s, 0, 0, 0))
    one_state = pl.BlockSpec((2, width, width), lambda s: (0, 0, 0))
    own_block = [
        pl.BlockSpec((1, 2, width, width), lambda s, first=i * half: (first + s, 0, 0, 0))
        for i in range(2)
    ]

    def beside(index, parts):
        made = shape(half, 2, width, width)
        whole_spec = pl.BlockSpec((half, 2, width, width), lambda s: (0, 0, 0, 0))
        return call(
            functools.partial(beside_kernel, index * half, count, len(parts)),
            24,
            2 * half,
            (made, made),
            *parts,
            coupling,
            sums,
            grid=(1,),
            in_specs=[pl.BlockSpec(part.shape, lambda s: (0, 0, 0, 0)) for part in parts]
            + [
                pl.BlockSpec((half, 2, width, width), lambda s: (index, 0, 0, 0)),
                pl.BlockSpec(sums.shape, lambda s: (0, 0)),
            ],
            out_specs=(whole_spec, whole_spec),
        )

    def greens_of(room, link, source, carried):
        return call(
            greens_kernel,
            room,
            2 * link.shape[0],
            (shape(*link.shape), whole),
            link,
            source,
            carried,
            grid=(link.shape[0],),
            in_specs=[block, block, one_state],
            out_specs=(block, one_state),
        )

    assert peers % 2 == 0
    leaving, previous, before = whole_source, None, None
    beside_first, beside_second = [None, None], [None, None]
    for hop in range(1, peers - 1):
        arrived = lax.ppermute(leaving, "slab", swaps((hop - 1) % 2))
        if hop == 1:
            if relayed:
                begins = (mine >= 2) & (mine < 6)
                given = jnp.where(begins, cuts[-1], free_first[0])
                free_second.append(lax.ppermute(given, "energy", relay_pairs))
            else:
                sent_on(0)
            sent_on(1)
            sent_after(2)
            arrived, weights, free_first[1] = lax.optimization_barrier(
                (arrived, weights, free_first[1])
            )
        if hop == 2:
            sent_on(2)
            sent_after(3)
            free_first[:3] = lax.optimization_barrier(free_first[:3])
            beside_first[0] = beside(0, free_first[:2])
            arrived, beside_first[0], free_first[2], *free_second[:2] = lax.optimization_barrier(
                (arrived, beside_first[0], free_first[2], *free_second[:2])
            )
        previous, before = arrived, leaving
        if hop < peers - 2:
            leaving = call(hop_kernel, 12, 2, whole, whole_map, whole_source, arrived)
    leaving, onward = call(
        last_hop_kernel,
        12,
        2,
        (whole, whole),
        jnp.reshape(place % 2, (1,)),
        whole_map,
        whole_source,
        previous,
        before,
        in_specs=[pl.BlockSpec(memory_space=pltpu.SMEM)] + [near] * 4,
        out_specs=(near, near),
    )

    def both(pairs):
        return [(a * peers + i, b * peers + j) for a, b in pairs for i, j in wire_up]

    arrived = lax.ppermute(leaving, "slab", swaps((peers - 2) % 2))
    carried_second = lax.ppermute(onward, ("energy", "slab"), both(second_pairs))
    free_first[3], around = lax.optimization_barrier(
        (free_first[3], free_second[0] if relayed else cuts[-1])
    )
    free_second.append(lax.ppermute(around, "energy", first_pairs if relayed else second_pairs))
    beside_second[0] = beside(0, free_second[:2])
    beside_first[1] = beside(1, free_first[2:])
    arrived, beside_first[1], beside_second[0], free_second[2] = lax.optimization_barrier(
        (arrived, beside_first[1], beside_second[0], free_second[2])
    )
    carried = jnp.where(place % 2 == 1, arrived, previous)
    carried_first = lax.ppermute(carried, "energy", first_pairs)
    greens, _ = call(
        functools.partial(own_greens_kernel, count),
        24,
        4 * count,
        (blocks, whole),
        free,
        coupling,
        sums,
        carried,
        grid=(count,),
        in_specs=[block, block, pl.BlockSpec(sums.shape, lambda s: (0, 0)), one_state],
        out_specs=(block, one_state),
    )
    carried_second, greens, free_second[3], ends, field, perm = lax.optimization_barrier(
        (carried_second, greens, free_second[3], ends, potential_old, permittivity)
    )

    beyond = [(e, e + 1) for e in range(1, energies - 1, 2)]
    other_ends = lax.ppermute(ends, "energy", beyond + [(b, a) for a, b in beyond])
    ends_before = jnp.where(odd == 1, twin_ends, other_ends).reshape(2, 2, cells, 1, depth)
    ends_after = jnp.where(odd == 1, other_ends, twin_ends).reshape(2, 2, cells, 1, depth)
    edge = jnp.zeros((2, cells, rows, 1), jnp.float32)
    halos = ((wire_before, wire_after), (ends_before[:, 1], ends_after[:, 0]), (edge, edge))
    potential_new = relaxed(field, perm, charge, halos)


    beside_second[1] = beside(1, free_second[2:])
    greens_second = []
    for part in beside_second:
        made, carried_second = greens_of(16, *part, carried_second)
        greens_second.append(made)
    carried_first, greens_second, potential_new = lax.optimization_barrier(
        (carried_first, greens_second, potential_new)
    )

    outputs = []
    for index, part in enumerate(beside_first):
        here, there, carried_first = call(
            mixing_kernel,
            20,
            2 * half,
            (shape(half, 2, width, width), shape(half, 2, width, width), whole),
            pick,
            *part,
            carried_first,
            greens,
            greens_second[index],
            weights,
            grid=(half,),
            in_specs=[
                pl.BlockSpec(memory_space=pltpu.SMEM),
                block,
                block,
                one_state,
                own_block[index],
                block,
                pl.BlockSpec((4, width, width), lambda s: (0, 0, 0)),
            ],
            out_specs=(block, block, one_state),
        )
        if outputs:
            outputs[0], there = lax.optimization_barrier((outputs[0], there))
        outputs.append(here + lax.ppermute(there, "energy", twin_pairs))
    return potential_new, jnp.concatenate(outputs, axis=0)[None]


def solution(mesh):
    in_specs = (
        P("slab", "energy", None),
        P("slab", "energy", None),
        P("slab", "energy", None),
        P("slab", None),
        P("energy", "slab", None, None, None),
        P("slab", None, None, None),
        P(),
        P(),
        P(),
    )
    out_specs = (P("slab", "energy", None), P("energy", "slab", None, None, None))
    return jax.shard_map(
        per_device, mesh=mesh, in_specs=in_specs, out_specs=out_specs, check_vma=False
    )
```

```python
import functools
import math
import jax
import jax.numpy as jnp
from jax import lax
from jax.experimental import pallas as pl
from jax.experimental.pallas import tpu as pltpu
from jax.sharding import PartitionSpec as P

MIB = 1024 * 1024


def halves(value):
    high = value.astype(jnp.bfloat16)
    low = (value - high.astype(jnp.float32)).astype(jnp.bfloat16)
    return high, low


def parts_of(block):
    real, imag = block
    return [halves(real), halves(imag), halves(0.5 * real + 0.5 * imag)]


def left_form(block):
    return [jnp.concatenate([high, high, low], axis=1) for high, low in parts_of(block)]


def right_form(block, axis=0):
    return [jnp.concatenate([high, low, high], axis=axis) for high, low in parts_of(block)]


def three_products(left, right, flipped):
    dims = (((1,), (1 if flipped else 0,)), ((), ()))
    by_real, by_imag, by_mean = (
        lax.dot_general(a, b, dimension_numbers=dims, preferred_element_type=jnp.float32)
        for a, b in zip(left, right)
    )
    return by_real - by_imag, 4.0 * (by_mean - 0.25 * by_real - 0.25 * by_imag)


def product(former, latter):
    return three_products(left_form(former), right_form(latter), False)


def sandwich(link, inner):
    half_way = three_products(left_form(link), right_form(inner), False)
    return three_products(left_form(half_way), right_form(link, 1), True)


def added(first, second):
    return first[0] + second[0], first[1] + second[1]


def pair_of(ref, *where):
    return ref[(*where, 0)], ref[(*where, 1)]


def put(ref, value, *where):
    ref[(*where, 0)] = value[0]
    ref[(*where, 1)] = value[1]


def call(kernel, room, products, out_shapes, *operands, **more):
    flops = products * 9 * 2 * max(x.shape[-1] for x in operands) ** 3
    moved = sum(4 * math.prod(x.shape) for x in jax.tree.leaves((operands, out_shapes)))
    cost = pl.CostEstimate(flops=flops, bytes_accessed=moved, transcendentals=0)
    return pl.pallas_call(
        kernel,
        out_shape=out_shapes,
        cost_estimate=cost,
        compiler_params=pltpu.CompilerParams(vmem_limit_bytes=room * MIB),
        **more,
    )(*operands)


def shape(*dims):
    return jax.ShapeDtypeStruct(dims, jnp.float32)


def gather_kernel(rows, peers, mine, field, perm, charge, before, after, owner, free, *refs):
    out, ends, *parts, held, here, gone = refs
    loads, stores = [], []
    for index in range(len(parts)):
        slab = free.at[index + 1 : index + 2]
        loads.append(
            pltpu.make_async_copy(slab, held.at[index : index + 1], here.at[index])
        )
        loads[-1].start()
    total, depth = charge.shape
    count, orbitals = owner.shape
    height = total // count
    cross = rows * peers
    row_ids = lax.broadcasted_iota(jnp.int32, (total, depth), 0) % rows
    lane_ids = lax.broadcasted_iota(jnp.int32, (total, depth), 1)

    def neighbours(inner, first, last):
        down = jnp.concatenate([first, inner[:-rows]], axis=0)
        up = jnp.concatenate([inner[rows:], last], axis=0)
        left = jnp.where(lane_ids == 0, 0.0, pltpu.roll(inner, 1, axis=1))
        right = jnp.where(lane_ids == depth - 1, 0.0, pltpu.roll(inner, depth - 1, axis=1))
        low = jnp.where(row_ids == 0, 0.0, pltpu.roll(inner, 1, axis=0))
        high = jnp.where(row_ids == rows - 1, 0.0, pltpu.roll(inner, total - 1, axis=0))
        return (down + up) + (left + right) + (low + high)

    first, last = (before[0], before[1]), (after[0], after[1])
    field_now, perm_now = field[...], perm[...]
    both = perm_now * field_now
    own = [
        charge[...],
        perm_now,
        neighbours(field_now, first[0], last[0]),
        neighbours(both, first[0] * first[1], last[0] * last[1]),
        neighbours(perm_now, first[1], last[1]),
    ]
    beside = [jnp.zeros_like(both), jnp.zeros_like(both), field_now, both, perm_now]
    kinds = len(own)
    places = lax.broadcasted_iota(jnp.int32, (2 * height, orbitals), 0)
    depths = lax.broadcasted_iota(jnp.int32, (depth, orbitals), 0)
    first_row = mine[0] * rows
    step = 0
    for slab in range(count):
        if slab == count // 2:
            for index, part in enumerate(parts):
                loads[index].wait()
                stores.append(
                    pltpu.make_async_copy(held.at[index : index + 1], part, gone.at[index])
                )
                stores[-1].start()
        cells = owner[slab : slab + 1, :]
        lane, line = cells % depth, cells // depth
        across, along = line % cross - first_row, line // cross * rows
        key = jnp.where(across == rows, height + along + rows - 1, -1)
        key = jnp.where(across == -1, height + along, key)
        key = jnp.where((across >= 0) & (across < rows), along + across, key)
        cut = slice(slab * height, (slab + 1) * height)
        table = jnp.concatenate(
            [
                jnp.concatenate([t[cut] for t in own], axis=1),
                jnp.concatenate([t[cut] for t in beside], axis=1),
            ],
            axis=0,
        ).T
        high, rest = halves(table)
        middle = rest.astype(jnp.float32)
        lowest = ((table - high.astype(jnp.float32)) - middle).astype(jnp.bfloat16)
        hit = jnp.where(places == key, 1.0, 0.0).astype(jnp.bfloat16)
        found = jnp.dot(
            jnp.concatenate([high, rest, lowest], axis=1),
            jnp.concatenate([hit, hit, hit], axis=0),
            preferred_element_type=jnp.float32,
        )
        for kind in range(kinds):
            part = found[kind * depth : (kind + 1) * depth]
            value = jnp.sum(jnp.where(depths == lane, part, 0.0), axis=0, keepdims=True)
            for piece in range(orbitals // depth):
                row = sums_row(kind, slab, count, orbitals // depth) + piece
                out[row : row + 1, :] = value[:, piece * depth : (piece + 1) * depth]
    start = 0
    for array in (field, perm):
        for end in (0, rows - 1):
            ends[start : start + total // rows, :] = array[
                pl.ds(end, total // rows, stride=rows), :
            ]
            start += total // rows
    for store in stores:
        store.wait()


def sums_row(kind, slab, count, pieces):
    return (kind * count + slab) * pieces


def potential_of(sums, slab, count, orbitals):
    pieces = orbitals // sums.shape[1]

    def value(kind):
        first = sums_row(kind, slab, count, pieces)
        return jnp.concatenate([sums[pl.ds(first + p, 1), :] for p in range(pieces)], axis=1)

    charge, perm, fields, both, perms = (value(kind) for kind in range(5))
    return (charge + 0.5 * (perm * fields + both)) / (3.0 * perm + 0.5 * perms)


def source_of(block, potential):
    scaled = (block[0] * potential, block[1] * potential)
    return added(block, product(scaled, block))


def own_kernel(free, coupling, sums, whole_map, whole_source):
    count = free.shape[0]
    links, state = [], None
    for slab in range(count):
        block = pair_of(free, slab)
        links.append(product(block, pair_of(coupling, slab)))
        source = source_of(block, potential_of(sums, slab, count, free.shape[-1]))
        state = source if state is None else added(sandwich(links[slab], state), source)
    put(whole_source, state)
    while len(links) > 1:
        paired = [product(b, a) for a, b in zip(links[0::2], links[1::2])]
        links = paired + links[len(paired) * 2 :]
    put(whole_map, links[0])


def hop_kernel(whole_map, whole_source, carried, out):
    put(out, added(sandwich(pair_of(whole_map), pair_of(carried)), pair_of(whole_source)))


def last_hop_kernel(odd, whole_map, whole_source, carried, before, out, onward):
    now = added(sandwich(pair_of(whole_map), pair_of(carried)), pair_of(whole_source))
    put(out, now)
    put(onward, [jnp.where(odd[0] != 0, before[part], now[part]) for part in range(2)])


def beside_kernel(start, count, parts, *refs):
    frees, (coupling, sums, link, source) = refs[:parts], refs[parts:]
    slab = 0
    for free in frees:
        for place in range(free.shape[0]):
            block = pair_of(free, place)
            put(link, product(block, pair_of(coupling, slab)), slab)
            row = potential_of(sums, start + slab, count, free.shape[-1])
            put(source, source_of(block, row), slab)
            slab += 1


def greens_kernel(link, source, carried, greens, state):
    @pl.when(pl.program_id(0) == 0)
    def _():
        state[...] = carried[...]

    now = added(sandwich(pair_of(link, 0), pair_of(state)), pair_of(source, 0))
    put(state, now)
    put(greens, now, 0)


def own_greens_kernel(count, free, coupling, sums, carried, greens, state):
    @pl.when(pl.program_id(0) == 0)
    def _():
        state[...] = carried[...]

    block = pair_of(free, 0)
    link = product(block, pair_of(coupling, 0))
    row = potential_of(sums, pl.program_id(0), count, free.shape[-1])
    now = added(sandwich(link, pair_of(state)), source_of(block, row))
    put(state, now)
    put(greens, now, 0)


def mixing_kernel(pick, link, source, carried, own, second, weights, here, there, state):
    @pl.when(pl.program_id(0) == 0)
    def _():
        state[...] = carried[...]

    first = added(sandwich(pair_of(link, 0), pair_of(state)), pair_of(source, 0))
    put(state, first)
    for part in range(2):
        second_now = jnp.where(pick[1] != 0, second[0, part], 0.0)
        here[0, part] = weights[0] * first[part] + weights[1] * second_now
        picked = jnp.where(pick[0] == 0, first[part], second_now)
        there[0, part] = weights[2] * own[0, part] + weights[3] * picked


def relaxed(field, perm, charge, halos):
    numerator = charge
    denominator = jnp.zeros_like(charge)
    for dim in range(3):
        length = charge.shape[dim]
        before, after = halos[dim]
        for side in range(2):
            sides = []
            for which, array in enumerate((field, perm)):
                if side == 0:
                    kept = lax.slice_in_dim(array, 1, length, axis=dim)
                    parts = [kept, after[which]]
                else:
                    kept = lax.slice_in_dim(array, 0, length - 1, axis=dim)
                    parts = [before[which], kept]
                sides.append(jnp.concatenate(parts, axis=dim))
            face = 0.5 * (perm + sides[1])
            numerator = numerator + face * sides[0]
            denominator = denominator + face
    return numerator / denominator


def end_planes(array, dim):
    length = array.shape[dim]
    return (
        lax.slice_in_dim(array, 0, 1, axis=dim),
        lax.slice_in_dim(array, length - 1, length, axis=dim),
    )


def exchanged(sums, ends, early):
    peers = lax.axis_size("energy")
    assert peers >= 4 and peers & (peers - 1) == 0
    masks = [2, 1] + [1 << k for k in range(2, peers.bit_length() - 1)]
    rows, twin_ends = sums.shape[0], None
    first = None
    sums, early = lax.optimization_barrier((sums, early))
    for mask in masks:
        given = jnp.concatenate([sums, ends]) if mask == 1 else sums
        arrived = lax.ppermute(given, "energy", [(e, e ^ mask) for e in range(peers)])
        if mask == 1:
            twin_ends = arrived[rows:]
        sums = sums + arrived[:rows]
        first = sums if first is None else first
    return sums, twin_ends, first, early


def per_device(
    potential_old,
    charge,
    permittivity,
    owner_cell,
    green_free,
    coupling,
    shifts,
    occupation,
    mode_tiles,
):
    energies, peers = lax.axis_size("energy"), lax.axis_size("slab")
    mine = lax.axis_index("energy")
    free = green_free[0]
    count, _, width, _ = free.shape
    whole = shape(2, width, width)
    blocks = shape(count, 2, width, width)

    everyone = range(energies)
    relayed = energies == 8
    if relayed:
        first_pairs = [(e, e ^ 2) for e in everyone]
        second_pairs = [(2, 4), (3, 5), (4, 2), (5, 3)]
        relay_pairs = [(e, e ^ 4) for e in everyone]
        turned = (mine // 2) % 2
        has_second = jnp.where((mine >= 2) & (mine < 6), 1, 0)
    else:
        first_pairs = [(e, e - 2) for e in everyone if e >= 2]
        second_pairs = [(e, e + 2) for e in everyone if e + 2 < energies]
        relay_pairs = second_pairs
        turned = jnp.zeros_like(mine)
        has_second = jnp.ones_like(mine)
    twin_pairs = [(e, e ^ 1) for e in everyone]

    half = count // 2
    one_slab = shape(1, 2, width, width)
    first_cut = free[:1]
    free_first = [lax.ppermute(first_cut, "energy", first_pairs)]

    place = lax.axis_index("slab")
    wire_up = [(i, i + 1) for i in range(peers - 1)]

    def swaps(start):
        pairs = [(i, i + 1) for i in range(start, peers - 1, 2)]
        return pairs + [(j, i) for i, j in pairs]

    first_cut, stacked = lax.optimization_barrier(
        (first_cut, jnp.stack([potential_old, permittivity]))
    )
    lower, upper = end_planes(stacked, 1)
    even = place % 2 == 0
    arrived = lax.ppermute(jnp.where(even, upper, lower), "slab", swaps(0))
    crossed = lax.ppermute(jnp.where(even, lower, upper), "slab", swaps(1))
    wire_before = jnp.where(even, crossed, arrived)
    wire_after = jnp.where(even, arrived, crossed)

    cells, rows, depth = charge.shape
    far, near = pl.BlockSpec(memory_space=pl.ANY), pl.BlockSpec(memory_space=pltpu.VMEM)
    sums, ends, *cuts = call(
        functools.partial(gather_kernel, rows, energies),
        56,
        1,
        (
            shape(5 * count * (width // depth), depth),
            shape(4 * cells, depth),
            *[one_slab] * (count - 1),
        ),
        jnp.reshape(mine, (1,)),
        *(array.reshape(-1, depth) for array in (potential_old, permittivity, charge)),
        wire_before.reshape(2, rows, depth),
        wire_after.reshape(2, rows, depth),
        owner_cell,
        free,
        in_specs=[pl.BlockSpec(memory_space=pltpu.SMEM)] + [near] * 6 + [far],
        out_specs=(near, near, *[far] * (count - 1)),
        scratch_shapes=[
            pltpu.VMEM((count - 1, 2, width, width), jnp.float32),
            pltpu.SemaphoreType.DMA((count - 1,)),
            pltpu.SemaphoreType.DMA((count - 1,)),
        ],
    )
    cuts = [first_cut, *cuts]
    sums, twin_ends, crossed, arrived = exchanged(sums, ends, free_first[0])

    crossed, cuts[1] = lax.optimization_barrier((crossed, cuts[1]))
    sums, arrived = lax.optimization_barrier((sums, arrived))
    free_first = [arrived, lax.ppermute(cuts[1], "energy", first_pairs)]
    free_second = []

    def sent_on(part):
        given = free_first[part] if relayed else cuts[part]
        free_second.append(lax.ppermute(given, "energy", relay_pairs))

    def sent_after(part):
        free_first[part - 1], cut = lax.optimization_barrier((free_first[part - 1], cuts[part]))
        free_first.append(lax.ppermute(cut, "energy", first_pairs))

    sent_on(0)
    whole_map, whole_source = call(
        own_kernel,
        32,
        5 * count - 3,
        (whole, whole),
        free,
        coupling,
        sums,
    )

    whole_source, mode_tiles = lax.optimization_barrier((whole_source, mode_tiles))
    odd = mine % 2
    distance = jnp.array([2, 2, 1, 1], jnp.int32)
    lowered = jnp.stack([turned, 1 - turned, 1 - odd, odd]).astype(jnp.float32)
    factors = (shifts[None, :] == distance[:, None]) * (occupation[None, :] + lowered[:, None])
    weights = jnp.sum(factors[:, :, None, None] * mode_tiles[None], axis=1)
    pick = jnp.stack([turned ^ odd, has_second]).astype(jnp.int32)

    block = pl.BlockSpec((1, 2, width, width), lambda s: (s, 0, 0, 0))
    one_state = pl.BlockSpec((2, width, width), lambda s: (0, 0, 0))
    own_block = [
        pl.BlockSpec((1, 2, width, width), lambda s, first=i * half: (first + s, 0, 0, 0))
        for i in range(2)
    ]

    def beside(index, parts):
        made = shape(half, 2, width, width)
        whole_spec = pl.BlockSpec((half, 2, width, width), lambda s: (0, 0, 0, 0))
        return call(
            functools.partial(beside_kernel, index * half, count, len(parts)),
            24,
            2 * half,
            (made, made),
            *parts,
            coupling,
            sums,
            grid=(1,),
            in_specs=[pl.BlockSpec(part.shape, lambda s: (0, 0, 0, 0)) for part in parts]
            + [
                pl.BlockSpec((half, 2, width, width), lambda s: (index, 0, 0, 0)),
                pl.BlockSpec(sums.shape, lambda s: (0, 0)),
            ],
            out_specs=(whole_spec, whole_spec),
        )

    def greens_of(room, link, source, carried):
        return call(
            greens_kernel,
            room,
            2 * link.shape[0],
            (shape(*link.shape), whole),
            link,
            source,
            carried,
            grid=(link.shape[0],),
            in_specs=[block, block, one_state],
            out_specs=(block, one_state),
        )

    assert peers % 2 == 0
    leaving, previous, before = whole_source, None, None
    beside_first, beside_second = [None, None], [None, None]
    for hop in range(1, peers - 1):
        arrived = lax.ppermute(leaving, "slab", swaps((hop - 1) % 2))
        if hop == 1:
            sent_on(1)
            sent_after(2)
            arrived, weights, free_first[1] = lax.optimization_barrier(
                (arrived, weights, free_first[1])
            )
        if hop == 2:
            sent_on(2)
            sent_after(3)
            beside_first[0] = beside(0, free_first[:2])
            arrived, beside_first[0], free_first[2], *free_second[:2] = lax.optimization_barrier(
                (arrived, beside_first[0], free_first[2], *free_second[:2])
            )
        previous, before = arrived, leaving
        if hop < peers - 2:
            leaving = call(hop_kernel, 12, 2, whole, whole_map, whole_source, arrived)
    leaving, onward = call(
        last_hop_kernel,
        12,
        2,
        (whole, whole),
        jnp.reshape(place % 2, (1,)),
        whole_map,
        whole_source,
        previous,
        before,
        in_specs=[pl.BlockSpec(memory_space=pltpu.SMEM)] + [near] * 4,
        out_specs=(near, near),
    )

    def both(pairs):
        return [(a * peers + i, b * peers + j) for a, b in pairs for i, j in wire_up]

    arrived = lax.ppermute(leaving, "slab", swaps((peers - 2) % 2))
    carried_second = lax.ppermute(onward, ("energy", "slab"), both(second_pairs))
    sent_on(3)
    beside_second[0] = beside(0, free_second[:2])
    beside_first[1] = beside(1, free_first[2:])
    arrived, beside_first[1], beside_second[0], free_second[2] = lax.optimization_barrier(
        (arrived, beside_first[1], beside_second[0], free_second[2])
    )
    carried = jnp.where(place % 2 == 1, arrived, previous)
    carried_first = lax.ppermute(carried, "energy", first_pairs)
    greens, _ = call(
        functools.partial(own_greens_kernel, count),
        24,
        4 * count,
        (blocks, whole),
        free,
        coupling,
        sums,
        carried,
        grid=(count,),
        in_specs=[block, block, pl.BlockSpec(sums.shape, lambda s: (0, 0)), one_state],
        out_specs=(block, one_state),
    )
    greens, ends, field, perm = lax.optimization_barrier(
        (greens, ends, potential_old, permittivity)
    )

    beyond = [(e, e + 1) for e in range(1, energies - 1, 2)]
    other_ends = lax.ppermute(ends, "energy", beyond + [(b, a) for a, b in beyond])
    carried_second, other_ends, free_second[3] = lax.optimization_barrier(
        (carried_second, other_ends, free_second[3])
    )
    ends_before = jnp.where(odd == 1, twin_ends, other_ends).reshape(2, 2, cells, 1, depth)
    ends_after = jnp.where(odd == 1, other_ends, twin_ends).reshape(2, 2, cells, 1, depth)
    edge = jnp.zeros((2, cells, rows, 1), jnp.float32)
    halos = ((wire_before, wire_after), (ends_before[:, 1], ends_after[:, 0]), (edge, edge))
    potential_new = relaxed(field, perm, charge, halos)

    beside_second[1] = beside(1, free_second[2:])
    greens_second = []
    for part in beside_second:
        made, carried_second = greens_of(16, *part, carried_second)
        greens_second.append(made)
    carried_first, greens_second, potential_new = lax.optimization_barrier(
        (carried_first, greens_second, potential_new)
    )

    outputs = []
    for index, part in enumerate(beside_first):
        here, there, carried_first = call(
            mixing_kernel,
            20,
            2 * half,
            (shape(half, 2, width, width), shape(half, 2, width, width), whole),
            pick,
            *part,
            carried_first,
            greens,
            greens_second[index],
            weights,
            grid=(half,),
            in_specs=[
                pl.BlockSpec(memory_space=pltpu.SMEM),
                block,
                block,
                one_state,
                own_block[index],
                block,
                pl.BlockSpec((4, width, width), lambda s: (0, 0, 0)),
            ],
            out_specs=(block, block, one_state),
        )
        if outputs:
            outputs[0], there = lax.optimization_barrier((outputs[0], there))
        outputs.append(here + lax.ppermute(there, "energy", twin_pairs))
    return potential_new, jnp.concatenate(outputs, axis=0)[None]


def solution(mesh):
    in_specs = (
        P("slab", "energy", None),
        P("slab", "energy", None),
        P("slab", "energy", None),
        P("slab", None),
        P("energy", "slab", None, None, None),
        P("slab", None, None, None),
        P(),
        P(),
        P(),
    )
    out_specs = (P("slab", "energy", None), P("energy", "slab", None, None, None))
    return jax.shard_map(
        per_device, mesh=mesh, in_specs=in_specs, out_specs=out_specs, check_vma=False
    )
```

```python
import functools
import math
import jax
import jax.numpy as jnp
from jax import lax
from jax.experimental import pallas as pl
from jax.experimental.pallas import tpu as pltpu
from jax.sharding import PartitionSpec as P

MIB = 1024 * 1024


def halves(value):
    high = value.astype(jnp.bfloat16)
    low = (value - high.astype(jnp.float32)).astype(jnp.bfloat16)
    return high, low


def parts_of(block):
    real, imag = block
    return [halves(real), halves(imag), halves(0.5 * real + 0.5 * imag)]


def left_form(block):
    return [jnp.concatenate([high, high, low], axis=1) for high, low in parts_of(block)]


def right_form(block, axis=0):
    return [jnp.concatenate([high, low, high], axis=axis) for high, low in parts_of(block)]


def three_products(left, right, flipped):
    dims = (((1,), (1 if flipped else 0,)), ((), ()))
    by_real, by_imag, by_mean = (
        lax.dot_general(a, b, dimension_numbers=dims, preferred_element_type=jnp.float32)
        for a, b in zip(left, right)
    )
    return by_real - by_imag, 4.0 * (by_mean - 0.25 * by_real - 0.25 * by_imag)


def product(former, latter):
    return three_products(left_form(former), right_form(latter), False)


def sandwich(link, inner):
    half_way = three_products(left_form(link), right_form(inner), False)
    return three_products(left_form(half_way), right_form(link, 1), True)


def added(first, second):
    return first[0] + second[0], first[1] + second[1]


def pair_of(ref, *where):
    return ref[(*where, 0)], ref[(*where, 1)]


def put(ref, value, *where):
    ref[(*where, 0)] = value[0]
    ref[(*where, 1)] = value[1]


def call(kernel, room, products, out_shapes, *operands, **more):
    flops = products * 9 * 2 * max(x.shape[-1] for x in operands) ** 3
    moved = sum(4 * math.prod(x.shape) for x in jax.tree.leaves((operands, out_shapes)))
    cost = pl.CostEstimate(flops=flops, bytes_accessed=moved, transcendentals=0)
    return pl.pallas_call(
        kernel,
        out_shape=out_shapes,
        cost_estimate=cost,
        compiler_params=pltpu.CompilerParams(vmem_limit_bytes=room * MIB),
        **more,
    )(*operands)


def shape(*dims):
    return jax.ShapeDtypeStruct(dims, jnp.float32)


def gather_kernel(rows, peers, mine, field, perm, charge, before, after, owner, free, *refs):
    out, ends, *parts, held, here, gone = refs
    loads, stores = [], []
    for index in range(len(parts)):
        slab = free.at[index + 1 : index + 2]
        loads.append(
            pltpu.make_async_copy(slab, held.at[index : index + 1], here.at[index])
        )
        loads[-1].start()
    total, depth = charge.shape
    count, orbitals = owner.shape
    height = total // count
    cross = rows * peers
    row_ids = lax.broadcasted_iota(jnp.int32, (total, depth), 0) % rows
    lane_ids = lax.broadcasted_iota(jnp.int32, (total, depth), 1)

    def neighbours(inner, first, last):
        down = jnp.concatenate([first, inner[:-rows]], axis=0)
        up = jnp.concatenate([inner[rows:], last], axis=0)
        left = jnp.where(lane_ids == 0, 0.0, pltpu.roll(inner, 1, axis=1))
        right = jnp.where(lane_ids == depth - 1, 0.0, pltpu.roll(inner, depth - 1, axis=1))
        low = jnp.where(row_ids == 0, 0.0, pltpu.roll(inner, 1, axis=0))
        high = jnp.where(row_ids == rows - 1, 0.0, pltpu.roll(inner, total - 1, axis=0))
        return (down + up) + (left + right) + (low + high)

    first, last = (before[0], before[1]), (after[0], after[1])
    field_now, perm_now = field[...], perm[...]
    both = perm_now * field_now
    own = [
        charge[...],
        perm_now,
        neighbours(field_now, first[0], last[0]),
        neighbours(both, first[0] * first[1], last[0] * last[1]),
        neighbours(perm_now, first[1], last[1]),
    ]
    beside = [jnp.zeros_like(both), jnp.zeros_like(both), field_now, both, perm_now]
    kinds = len(own)
    places = lax.broadcasted_iota(jnp.int32, (2 * height, orbitals), 0)
    depths = lax.broadcasted_iota(jnp.int32, (depth, orbitals), 0)
    first_row = mine[0] * rows
    step = 0
    for slab in range(count):
        if slab == count // 2:
            for index, part in enumerate(parts):
                loads[index].wait()
                stores.append(
                    pltpu.make_async_copy(held.at[index : index + 1], part, gone.at[index])
                )
                stores[-1].start()
        cells = owner[slab : slab + 1, :]
        lane, line = cells % depth, cells // depth
        across, along = line % cross - first_row, line // cross * rows
        key = jnp.where(across == rows, height + along + rows - 1, -1)
        key = jnp.where(across == -1, height + along, key)
        key = jnp.where((across >= 0) & (across < rows), along + across, key)
        cut = slice(slab * height, (slab + 1) * height)
        table = jnp.concatenate(
            [
                jnp.concatenate([t[cut] for t in own], axis=1),
                jnp.concatenate([t[cut] for t in beside], axis=1),
            ],
            axis=0,
        ).T
        high, rest = halves(table)
        middle = rest.astype(jnp.float32)
        lowest = ((table - high.astype(jnp.float32)) - middle).astype(jnp.bfloat16)
        hit = jnp.where(places == key, 1.0, 0.0).astype(jnp.bfloat16)
        found = jnp.dot(
            jnp.concatenate([high, rest, lowest], axis=1),
            jnp.concatenate([hit, hit, hit], axis=0),
            preferred_element_type=jnp.float32,
        )
        for kind in range(kinds):
            part = found[kind * depth : (kind + 1) * depth]
            value = jnp.sum(jnp.where(depths == lane, part, 0.0), axis=0, keepdims=True)
            for piece in range(orbitals // depth):
                row = sums_row(kind, slab, count, orbitals // depth) + piece
                out[row : row + 1, :] = value[:, piece * depth : (piece + 1) * depth]
    start = 0
    for array in (field, perm):
        for end in (0, rows - 1):
            ends[start : start + total // rows, :] = array[
                pl.ds(end, total // rows, stride=rows), :
            ]
            start += total // rows
    for store in stores:
        store.wait()


def sums_row(kind, slab, count, pieces):
    return (kind * count + slab) * pieces


def potential_of(sums, slab, count, orbitals):
    pieces = orbitals // sums.shape[1]

    def value(kind):
        first = sums_row(kind, slab, count, pieces)
        return jnp.concatenate([sums[pl.ds(first + p, 1), :] for p in range(pieces)], axis=1)

    charge, perm, fields, both, perms = (value(kind) for kind in range(5))
    return (charge + 0.5 * (perm * fields + both)) / (3.0 * perm + 0.5 * perms)


def source_of(block, potential):
    scaled = (block[0] * potential, block[1] * potential)
    return added(block, product(scaled, block))


def own_kernel(free, coupling, sums, whole_map, whole_source):
    count = free.shape[0]
    links, state = [], None
    for slab in range(count):
        block = pair_of(free, slab)
        links.append(product(block, pair_of(coupling, slab)))
        source = source_of(block, potential_of(sums, slab, count, free.shape[-1]))
        state = source if state is None else added(sandwich(links[slab], state), source)
    put(whole_source, state)
    while len(links) > 1:
        paired = [product(b, a) for a, b in zip(links[0::2], links[1::2])]
        links = paired + links[len(paired) * 2 :]
    put(whole_map, links[0])


def hop_kernel(whole_map, whole_source, carried, out):
    put(out, added(sandwich(pair_of(whole_map), pair_of(carried)), pair_of(whole_source)))


def last_hop_kernel(odd, whole_map, whole_source, carried, before, out, onward):
    now = added(sandwich(pair_of(whole_map), pair_of(carried)), pair_of(whole_source))
    put(out, now)
    put(onward, [jnp.where(odd[0] != 0, before[part], now[part]) for part in range(2)])


def beside_kernel(start, count, parts, *refs):
    frees, (coupling, sums, link, source) = refs[:parts], refs[parts:]
    slab = 0
    for free in frees:
        for place in range(free.shape[0]):
            block = pair_of(free, place)
            put(link, product(block, pair_of(coupling, slab)), slab)
            row = potential_of(sums, start + slab, count, free.shape[-1])
            put(source, source_of(block, row), slab)
            slab += 1


def greens_kernel(link, source, carried, greens, state):
    @pl.when(pl.program_id(0) == 0)
    def _():
        state[...] = carried[...]

    now = added(sandwich(pair_of(link, 0), pair_of(state)), pair_of(source, 0))
    put(state, now)
    put(greens, now, 0)


def own_greens_kernel(count, free, coupling, sums, carried, greens, state):
    @pl.when(pl.program_id(0) == 0)
    def _():
        state[...] = carried[...]

    block = pair_of(free, 0)
    link = product(block, pair_of(coupling, 0))
    row = potential_of(sums, pl.program_id(0), count, free.shape[-1])
    now = added(sandwich(link, pair_of(state)), source_of(block, row))
    put(state, now)
    put(greens, now, 0)


def mixing_kernel(pick, link, source, carried, own, second, weights, here, there, state):
    @pl.when(pl.program_id(0) == 0)
    def _():
        state[...] = carried[...]

    first = added(sandwich(pair_of(link, 0), pair_of(state)), pair_of(source, 0))
    put(state, first)
    for part in range(2):
        second_now = jnp.where(pick[1] != 0, second[0, part], 0.0)
        here[0, part] = weights[0] * first[part] + weights[1] * second_now
        picked = jnp.where(pick[0] == 0, first[part], second_now)
        there[0, part] = weights[2] * own[0, part] + weights[3] * picked


def relaxed(field, perm, charge, halos):
    numerator = charge
    denominator = jnp.zeros_like(charge)
    for dim in range(3):
        length = charge.shape[dim]
        before, after = halos[dim]
        for side in range(2):
            sides = []
            for which, array in enumerate((field, perm)):
                if side == 0:
                    kept = lax.slice_in_dim(array, 1, length, axis=dim)
                    parts = [kept, after[which]]
                else:
                    kept = lax.slice_in_dim(array, 0, length - 1, axis=dim)
                    parts = [before[which], kept]
                sides.append(jnp.concatenate(parts, axis=dim))
            face = 0.5 * (perm + sides[1])
            numerator = numerator + face * sides[0]
            denominator = denominator + face
    return numerator / denominator


def end_planes(array, dim):
    length = array.shape[dim]
    return (
        lax.slice_in_dim(array, 0, 1, axis=dim),
        lax.slice_in_dim(array, length - 1, length, axis=dim),
    )


def exchanged(sums, ends, early):
    peers = lax.axis_size("energy")
    assert peers >= 4 and peers & (peers - 1) == 0
    masks = [2, 1] + [1 << k for k in range(2, peers.bit_length() - 1)]
    rows, twin_ends = sums.shape[0], None
    first = None
    sums, early = lax.optimization_barrier((sums, early))
    for mask in masks:
        given = jnp.concatenate([sums, ends]) if mask == 1 else sums
        arrived = lax.ppermute(given, "energy", [(e, e ^ mask) for e in range(peers)])
        if mask == 1:
            twin_ends = arrived[rows:]
        sums = sums + arrived[:rows]
        first = sums if first is None else first
    return sums, twin_ends, first, early


def per_device(
    potential_old,
    charge,
    permittivity,
    owner_cell,
    green_free,
    coupling,
    shifts,
    occupation,
    mode_tiles,
):
    energies, peers = lax.axis_size("energy"), lax.axis_size("slab")
    mine = lax.axis_index("energy")
    free = green_free[0]
    count, _, width, _ = free.shape
    whole = shape(2, width, width)
    blocks = shape(count, 2, width, width)

    everyone = range(energies)
    relayed = energies == 8
    if relayed:
        first_pairs = [(e, e ^ 2) for e in everyone]
        second_pairs = [(2, 4), (3, 5), (4, 2), (5, 3)]
        relay_pairs = [(e, e ^ 4) for e in everyone]
        turned = (mine // 2) % 2
        has_second = jnp.where((mine >= 2) & (mine < 6), 1, 0)
    else:
        first_pairs = [(e, e - 2) for e in everyone if e >= 2]
        second_pairs = [(e, e + 2) for e in everyone if e + 2 < energies]
        relay_pairs = second_pairs
        turned = jnp.zeros_like(mine)
        has_second = jnp.ones_like(mine)
    twin_pairs = [(e, e ^ 1) for e in everyone]

    half = count // 2
    one_slab = shape(1, 2, width, width)
    first_cut = free[:1]
    free_first = [lax.ppermute(first_cut, "energy", first_pairs)]

    place = lax.axis_index("slab")
    wire_up = [(i, i + 1) for i in range(peers - 1)]

    def swaps(start):
        pairs = [(i, i + 1) for i in range(start, peers - 1, 2)]
        return pairs + [(j, i) for i, j in pairs]

    first_cut, stacked = lax.optimization_barrier(
        (first_cut, jnp.stack([potential_old, permittivity]))
    )
    lower, upper = end_planes(stacked, 1)
    even = place % 2 == 0
    arrived = lax.ppermute(jnp.where(even, upper, lower), "slab", swaps(0))
    crossed = lax.ppermute(jnp.where(even, lower, upper), "slab", swaps(1))
    wire_before = jnp.where(even, crossed, arrived)
    wire_after = jnp.where(even, arrived, crossed)

    cells, rows, depth = charge.shape
    far, near = pl.BlockSpec(memory_space=pl.ANY), pl.BlockSpec(memory_space=pltpu.VMEM)
    sums, ends, *cuts = call(
        functools.partial(gather_kernel, rows, energies),
        56,
        1,
        (
            shape(5 * count * (width // depth), depth),
            shape(4 * cells, depth),
            *[one_slab] * (count - 1),
        ),
        jnp.reshape(mine, (1,)),
        *(array.reshape(-1, depth) for array in (potential_old, permittivity, charge)),
        wire_before.reshape(2, rows, depth),
        wire_after.reshape(2, rows, depth),
        owner_cell,
        free,
        in_specs=[pl.BlockSpec(memory_space=pltpu.SMEM)] + [near] * 6 + [far],
        out_specs=(near, near, *[far] * (count - 1)),
        scratch_shapes=[
            pltpu.VMEM((count - 1, 2, width, width), jnp.float32),
            pltpu.SemaphoreType.DMA((count - 1,)),
            pltpu.SemaphoreType.DMA((count - 1,)),
        ],
    )
    cuts = [first_cut, *cuts]
    sums, twin_ends, crossed, arrived = exchanged(sums, ends, free_first[0])

    crossed, cuts[1] = lax.optimization_barrier((crossed, cuts[1]))
    sums, arrived = lax.optimization_barrier((sums, arrived))
    free_first = [arrived, lax.ppermute(cuts[1], "energy", first_pairs)]
    free_second = []

    def sent_on(part):
        given = free_first[part] if relayed else cuts[part]
        free_second.append(lax.ppermute(given, "energy", relay_pairs))

    def sent_after(part):
        free_first[part - 1], cut = lax.optimization_barrier((free_first[part - 1], cuts[part]))
        free_first.append(lax.ppermute(cut, "energy", first_pairs))

    sent_on(0)
    whole_map, whole_source = call(
        own_kernel,
        32,
        5 * count - 3,
        (whole, whole),
        free,
        coupling,
        sums,
    )

    whole_source, mode_tiles = lax.optimization_barrier((whole_source, mode_tiles))
    odd = mine % 2
    distance = jnp.array([2, 2, 1, 1], jnp.int32)
    lowered = jnp.stack([turned, 1 - turned, 1 - odd, odd]).astype(jnp.float32)
    factors = (shifts[None, :] == distance[:, None]) * (occupation[None, :] + lowered[:, None])
    weights = jnp.sum(factors[:, :, None, None] * mode_tiles[None], axis=1)
    pick = jnp.stack([turned ^ odd, has_second]).astype(jnp.int32)

    block = pl.BlockSpec((1, 2, width, width), lambda s: (s, 0, 0, 0))
    one_state = pl.BlockSpec((2, width, width), lambda s: (0, 0, 0))
    own_block = [
        pl.BlockSpec((1, 2, width, width), lambda s, first=i * half: (first + s, 0, 0, 0))
        for i in range(2)
    ]

    def beside(index, parts):
        made = shape(half, 2, width, width)
        whole_spec = pl.BlockSpec((half, 2, width, width), lambda s: (0, 0, 0, 0))
        return call(
            functools.partial(beside_kernel, index * half, count, len(parts)),
            24,
            2 * half,
            (made, made),
            *parts,
            coupling,
            sums,
            grid=(1,),
            in_specs=[pl.BlockSpec(part.shape, lambda s: (0, 0, 0, 0)) for part in parts]
            + [
                pl.BlockSpec((half, 2, width, width), lambda s: (index, 0, 0, 0)),
                pl.BlockSpec(sums.shape, lambda s: (0, 0)),
            ],
            out_specs=(whole_spec, whole_spec),
        )

    def greens_of(room, link, source, carried):
        return call(
            greens_kernel,
            room,
            2 * link.shape[0],
            (shape(*link.shape), whole),
            link,
            source,
            carried,
            grid=(link.shape[0],),
            in_specs=[block, block, one_state],
            out_specs=(block, one_state),
        )

    assert peers % 2 == 0
    leaving, previous, before = whole_source, None, None
    beside_first, beside_second = [None, None], [None, None]
    for hop in range(1, peers - 1):
        arrived = lax.ppermute(leaving, "slab", swaps((hop - 1) % 2))
        if hop == 1:
            sent_on(1)
            sent_after(2)
            arrived, weights, free_first[1] = lax.optimization_barrier(
                (arrived, weights, free_first[1])
            )
        if hop == 2:
            sent_on(2)
            sent_after(3)
            beside_first[0] = beside(0, free_first[:2])
            arrived, beside_first[0], free_first[2], *free_second[:2] = lax.optimization_barrier(
                (arrived, beside_first[0], free_first[2], *free_second[:2])
            )
        previous, before = arrived, leaving
        if hop < peers - 2:
            leaving = call(hop_kernel, 12, 2, whole, whole_map, whole_source, arrived)
    leaving, onward = call(
        last_hop_kernel,
        12,
        2,
        (whole, whole),
        jnp.reshape(place % 2, (1,)),
        whole_map,
        whole_source,
        previous,
        before,
        in_specs=[pl.BlockSpec(memory_space=pltpu.SMEM)] + [near] * 4,
        out_specs=(near, near),
    )

    def both(pairs):
        return [(a * peers + i, b * peers + j) for a, b in pairs for i, j in wire_up]

    arrived = lax.ppermute(leaving, "slab", swaps((peers - 2) % 2))
    carried_second = lax.ppermute(onward, ("energy", "slab"), both(second_pairs))
    beside_second[0] = beside(0, free_second[:2])
    beside_first[1] = beside(1, free_first[2:])
    arrived, beside_first[1], beside_second[0], free_second[2] = lax.optimization_barrier(
        (arrived, beside_first[1], beside_second[0], free_second[2])
    )
    carried = jnp.where(place % 2 == 1, arrived, previous)
    carried_first = lax.ppermute(carried, "energy", first_pairs)
    carried, free_first[3] = lax.optimization_barrier((carried, free_first[3]))
    sent_on(3)
    greens, _ = call(
        functools.partial(own_greens_kernel, count),
        24,
        4 * count,
        (blocks, whole),
        free,
        coupling,
        sums,
        carried,
        grid=(count,),
        in_specs=[block, block, pl.BlockSpec(sums.shape, lambda s: (0, 0)), one_state],
        out_specs=(block, one_state),
    )
    greens, ends, field, perm = lax.optimization_barrier(
        (greens, ends, potential_old, permittivity)
    )

    beyond = [(e, e + 1) for e in range(1, energies - 1, 2)]
    other_ends = lax.ppermute(ends, "energy", beyond + [(b, a) for a, b in beyond])
    carried_second, other_ends, free_second[3] = lax.optimization_barrier(
        (carried_second, other_ends, free_second[3])
    )
    ends_before = jnp.where(odd == 1, twin_ends, other_ends).reshape(2, 2, cells, 1, depth)
    ends_after = jnp.where(odd == 1, other_ends, twin_ends).reshape(2, 2, cells, 1, depth)
    edge = jnp.zeros((2, cells, rows, 1), jnp.float32)
    halos = ((wire_before, wire_after), (ends_before[:, 1], ends_after[:, 0]), (edge, edge))
    potential_new = relaxed(field, perm, charge, halos)

    beside_second[1] = beside(1, free_second[2:])
    greens_second = []
    for part in beside_second:
        made, carried_second = greens_of(16, *part, carried_second)
        greens_second.append(made)
    carried_first, greens_second, potential_new = lax.optimization_barrier(
        (carried_first, greens_second, potential_new)
    )

    outputs = []
    for index, part in enumerate(beside_first):
        here, there, carried_first = call(
            mixing_kernel,
            20,
            2 * half,
            (shape(half, 2, width, width), shape(half, 2, width, width), whole),
            pick,
            *part,
            carried_first,
            greens,
            greens_second[index],
            weights,
            grid=(half,),
            in_specs=[
                pl.BlockSpec(memory_space=pltpu.SMEM),
                block,
                block,
                one_state,
                own_block[index],
                block,
                pl.BlockSpec((4, width, width), lambda s: (0, 0, 0)),
            ],
            out_specs=(block, block, one_state),
        )
        if outputs:
            outputs[0], there = lax.optimization_barrier((outputs[0], there))
        outputs.append(here + lax.ppermute(there, "energy", twin_pairs))
    return potential_new, jnp.concatenate(outputs, axis=0)[None]


def solution(mesh):
    in_specs = (
        P("slab", "energy", None),
        P("slab", "energy", None),
        P("slab", "energy", None),
        P("slab", None),
        P("energy", "slab", None, None, None),
        P("slab", None, None, None),
        P(),
        P(),
        P(),
    )
    out_specs = (P("slab", "energy", None), P("energy", "slab", None, None, None))
    return jax.shard_map(
        per_device, mesh=mesh, in_specs=in_specs, out_specs=out_specs, check_vma=False
    )
```

```python
import functools
import math
import jax
import jax.numpy as jnp
from jax import lax
from jax.experimental import pallas as pl
from jax.experimental.pallas import tpu as pltpu
from jax.sharding import PartitionSpec as P

MIB = 1024 * 1024


def halves(value):
    high = value.astype(jnp.bfloat16)
    low = (value - high.astype(jnp.float32)).astype(jnp.bfloat16)
    return high, low


def parts_of(block):
    real, imag = block
    return [halves(real), halves(imag), halves(0.5 * real + 0.5 * imag)]


def left_form(block):
    return [jnp.concatenate([high, high, low], axis=1) for high, low in parts_of(block)]


def right_form(block, axis=0):
    return [jnp.concatenate([high, low, high], axis=axis) for high, low in parts_of(block)]


def three_products(left, right, flipped):
    dims = (((1,), (1 if flipped else 0,)), ((), ()))
    by_real, by_imag, by_mean = (
        lax.dot_general(a, b, dimension_numbers=dims, preferred_element_type=jnp.float32)
        for a, b in zip(left, right)
    )
    return by_real - by_imag, 4.0 * (by_mean - 0.25 * by_real - 0.25 * by_imag)


def product(former, latter):
    return three_products(left_form(former), right_form(latter), False)


def sandwich(link, inner):
    half_way = three_products(left_form(link), right_form(inner), False)
    return three_products(left_form(half_way), right_form(link, 1), True)


def added(first, second):
    return first[0] + second[0], first[1] + second[1]


def pair_of(ref, *where):
    return ref[(*where, 0)], ref[(*where, 1)]


def put(ref, value, *where):
    ref[(*where, 0)] = value[0]
    ref[(*where, 1)] = value[1]


def call(kernel, room, products, out_shapes, *operands, **more):
    flops = products * 9 * 2 * max(x.shape[-1] for x in operands) ** 3
    moved = sum(4 * math.prod(x.shape) for x in jax.tree.leaves((operands, out_shapes)))
    cost = pl.CostEstimate(flops=flops, bytes_accessed=moved, transcendentals=0)
    return pl.pallas_call(
        kernel,
        out_shape=out_shapes,
        cost_estimate=cost,
        compiler_params=pltpu.CompilerParams(vmem_limit_bytes=room * MIB),
        **more,
    )(*operands)


def shape(*dims):
    return jax.ShapeDtypeStruct(dims, jnp.float32)


def gather_kernel(rows, peers, mine, field, perm, charge, before, after, owner, free, *refs):
    out, *parts, held, here, gone = refs
    loads, stores = [], []
    for index in range(len(parts)):
        slab = free.at[index + 1 : index + 2]
        loads.append(
            pltpu.make_async_copy(slab, held.at[index : index + 1], here.at[index])
        )
        loads[-1].start()
    total, depth = charge.shape
    count, orbitals = owner.shape
    height = total // count
    cross = rows * peers
    row_ids = lax.broadcasted_iota(jnp.int32, (total, depth), 0) % rows
    lane_ids = lax.broadcasted_iota(jnp.int32, (total, depth), 1)

    def neighbours(inner, first, last):
        down = jnp.concatenate([first, inner[:-rows]], axis=0)
        up = jnp.concatenate([inner[rows:], last], axis=0)
        left = jnp.where(lane_ids == 0, 0.0, pltpu.roll(inner, 1, axis=1))
        right = jnp.where(lane_ids == depth - 1, 0.0, pltpu.roll(inner, depth - 1, axis=1))
        low = jnp.where(row_ids == 0, 0.0, pltpu.roll(inner, 1, axis=0))
        high = jnp.where(row_ids == rows - 1, 0.0, pltpu.roll(inner, total - 1, axis=0))
        return (down + up) + (left + right) + (low + high)

    first, last = (before[0], before[1]), (after[0], after[1])
    field_now, perm_now = field[...], perm[...]
    both = perm_now * field_now
    own = [
        charge[...],
        perm_now,
        neighbours(field_now, first[0], last[0]),
        neighbours(both, first[0] * first[1], last[0] * last[1]),
        neighbours(perm_now, first[1], last[1]),
    ]
    beside = [jnp.zeros_like(both), jnp.zeros_like(both), field_now, both, perm_now]
    kinds = len(own)
    places = lax.broadcasted_iota(jnp.int32, (2 * height, orbitals), 0)
    depths = lax.broadcasted_iota(jnp.int32, (depth, orbitals), 0)
    first_row = mine[0] * rows
    step = 0
    for slab in range(count):
        if slab == count // 2:
            for index, part in enumerate(parts):
                loads[index].wait()
                stores.append(
                    pltpu.make_async_copy(held.at[index : index + 1], part, gone.at[index])
                )
                stores[-1].start()
        cells = owner[slab : slab + 1, :]
        lane, line = cells % depth, cells // depth
        across, along = line % cross - first_row, line // cross * rows
        key = jnp.where(across == rows, height + along + rows - 1, -1)
        key = jnp.where(across == -1, height + along, key)
        key = jnp.where((across >= 0) & (across < rows), along + across, key)
        cut = slice(slab * height, (slab + 1) * height)
        table = jnp.concatenate(
            [
                jnp.concatenate([t[cut] for t in own], axis=1),
                jnp.concatenate([t[cut] for t in beside], axis=1),
            ],
            axis=0,
        ).T
        high, rest = halves(table)
        middle = rest.astype(jnp.float32)
        lowest = ((table - high.astype(jnp.float32)) - middle).astype(jnp.bfloat16)
        hit = jnp.where(places == key, 1.0, 0.0).astype(jnp.bfloat16)
        found = jnp.dot(
            jnp.concatenate([high, rest, lowest], axis=1),
            jnp.concatenate([hit, hit, hit], axis=0),
            preferred_element_type=jnp.float32,
        )
        for kind in range(kinds):
            part = found[kind * depth : (kind + 1) * depth]
            value = jnp.sum(jnp.where(depths == lane, part, 0.0), axis=0, keepdims=True)
            for piece in range(orbitals // depth):
                row = sums_row(kind, slab, count, orbitals // depth) + piece
                out[row : row + 1, :] = value[:, piece * depth : (piece + 1) * depth]
    start = kinds * count * (orbitals // depth)
    for array in (field, perm):
        for end in (0, rows - 1):
            out[start : start + total // rows, :] = array[pl.ds(end, total // rows, stride=rows), :]
            start += total // rows
    for store in stores:
        store.wait()


def sums_row(kind, slab, count, pieces):
    return (kind * count + slab) * pieces


def potential_of(sums, slab, count, orbitals):
    pieces = orbitals // sums.shape[1]

    def value(kind):
        first = sums_row(kind, slab, count, pieces)
        return jnp.concatenate([sums[pl.ds(first + p, 1), :] for p in range(pieces)], axis=1)

    charge, perm, fields, both, perms = (value(kind) for kind in range(5))
    return (charge + 0.5 * (perm * fields + both)) / (3.0 * perm + 0.5 * perms)


def source_of(block, potential):
    scaled = (block[0] * potential, block[1] * potential)
    return added(block, product(scaled, block))


def own_kernel(free, coupling, sums, whole_map, whole_source):
    count = free.shape[0]
    links, state = [], None
    for slab in range(count):
        block = pair_of(free, slab)
        links.append(product(block, pair_of(coupling, slab)))
        source = source_of(block, potential_of(sums, slab, count, free.shape[-1]))
        state = source if state is None else added(sandwich(links[slab], state), source)
    put(whole_source, state)
    while len(links) > 1:
        paired = [product(b, a) for a, b in zip(links[0::2], links[1::2])]
        links = paired + links[len(paired) * 2 :]
    put(whole_map, links[0])


def hop_kernel(whole_map, whole_source, carried, out):
    put(out, added(sandwich(pair_of(whole_map), pair_of(carried)), pair_of(whole_source)))


def last_hop_kernel(odd, whole_map, whole_source, carried, before, out, onward):
    now = added(sandwich(pair_of(whole_map), pair_of(carried)), pair_of(whole_source))
    put(out, now)
    put(onward, [jnp.where(odd[0] != 0, before[part], now[part]) for part in range(2)])


def beside_kernel(start, count, parts, *refs):
    frees, (coupling, sums, link, source) = refs[:parts], refs[parts:]
    slab = 0
    for free in frees:
        for place in range(free.shape[0]):
            block = pair_of(free, place)
            put(link, product(block, pair_of(coupling, slab)), slab)
            row = potential_of(sums, start + slab, count, free.shape[-1])
            put(source, source_of(block, row), slab)
            slab += 1


def greens_kernel(link, source, carried, greens, state):
    @pl.when(pl.program_id(0) == 0)
    def _():
        state[...] = carried[...]

    now = added(sandwich(pair_of(link, 0), pair_of(state)), pair_of(source, 0))
    put(state, now)
    put(greens, now, 0)


def own_greens_kernel(count, free, coupling, sums, carried, greens, state):
    @pl.when(pl.program_id(0) == 0)
    def _():
        state[...] = carried[...]

    block = pair_of(free, 0)
    link = product(block, pair_of(coupling, 0))
    row = potential_of(sums, pl.program_id(0), count, free.shape[-1])
    now = added(sandwich(link, pair_of(state)), source_of(block, row))
    put(state, now)
    put(greens, now, 0)


def mixing_kernel(pick, link, source, carried, own, second, weights, here, there, state):
    @pl.when(pl.program_id(0) == 0)
    def _():
        state[...] = carried[...]

    first = added(sandwich(pair_of(link, 0), pair_of(state)), pair_of(source, 0))
    put(state, first)
    for part in range(2):
        second_now = jnp.where(pick[1] != 0, second[0, part], 0.0)
        here[0, part] = weights[0] * first[part] + weights[1] * second_now
        picked = jnp.where(pick[0] == 0, first[part], second_now)
        there[0, part] = weights[2] * own[0, part] + weights[3] * picked


def relaxed(field, perm, charge, halos):
    numerator = charge
    denominator = jnp.zeros_like(charge)
    for dim in range(3):
        length = charge.shape[dim]
        before, after = halos[dim]
        for side in range(2):
            sides = []
            for which, array in enumerate((field, perm)):
                if side == 0:
                    kept = lax.slice_in_dim(array, 1, length, axis=dim)
                    parts = [kept, after[which]]
                else:
                    kept = lax.slice_in_dim(array, 0, length - 1, axis=dim)
                    parts = [before[which], kept]
                sides.append(jnp.concatenate(parts, axis=dim))
            face = 0.5 * (perm + sides[1])
            numerator = numerator + face * sides[0]
            denominator = denominator + face
    return numerator / denominator


def end_planes(array, dim):
    length = array.shape[dim]
    return (
        lax.slice_in_dim(array, 0, 1, axis=dim),
        lax.slice_in_dim(array, length - 1, length, axis=dim),
    )


def exchanged(payload, head, early):
    peers, mine = lax.axis_size("energy"), lax.axis_index("energy")
    assert peers >= 4 and peers & (peers - 1) == 0
    masks = [(1 << k) - 1 for k in range(2, peers.bit_length())] + [1]
    rest = payload[head:]
    before = after = jnp.zeros_like(rest)
    is_head = lax.broadcasted_iota(jnp.int32, payload.shape, 0) < head
    payload, early = lax.optimization_barrier((payload, early))
    for mask in masks:
        arrived = lax.ppermute(payload, "energy", [(e, e ^ mask) for e in range(peers)])
        before = jnp.where((mine ^ mask) == mine - 1, arrived[head:], before)
        after = jnp.where((mine ^ mask) == mine + 1, arrived[head:], after)
        payload = jnp.where(is_head, payload + arrived, payload)
        if mask != 1:
            crossed = payload
    return payload, before, after, crossed, early


def per_device(
    potential_old,
    charge,
    permittivity,
    owner_cell,
    green_free,
    coupling,
    shifts,
    occupation,
    mode_tiles,
):
    energies, peers = lax.axis_size("energy"), lax.axis_size("slab")
    mine = lax.axis_index("energy")
    free = green_free[0]
    count, _, width, _ = free.shape
    whole = shape(2, width, width)
    blocks = shape(count, 2, width, width)

    everyone = range(energies)
    relayed = energies == 8
    if relayed:
        first_pairs = [(e, e ^ 2) for e in everyone]
        second_pairs = [(2, 4), (3, 5), (4, 2), (5, 3)]
        relay_pairs = [(e, e ^ 4) for e in everyone]
        turned = (mine // 2) % 2
        has_second = jnp.where((mine >= 2) & (mine < 6), 1, 0)
    else:
        first_pairs = [(e, e - 2) for e in everyone if e >= 2]
        second_pairs = [(e, e + 2) for e in everyone if e + 2 < energies]
        relay_pairs = second_pairs
        turned = jnp.zeros_like(mine)
        has_second = jnp.ones_like(mine)
    twin_pairs = [(e, e ^ 1) for e in everyone]

    half = count // 2
    one_slab = shape(1, 2, width, width)
    first_cut = free[:1]
    free_first = [lax.ppermute(first_cut, "energy", first_pairs)]

    place = lax.axis_index("slab")
    wire_up = [(i, i + 1) for i in range(peers - 1)]

    def swaps(start):
        pairs = [(i, i + 1) for i in range(start, peers - 1, 2)]
        return pairs + [(j, i) for i, j in pairs]

    first_cut, stacked = lax.optimization_barrier(
        (first_cut, jnp.stack([potential_old, permittivity]))
    )
    lower, upper = end_planes(stacked, 1)
    even = place % 2 == 0
    arrived = lax.ppermute(jnp.where(even, upper, lower), "slab", swaps(0))
    crossed = lax.ppermute(jnp.where(even, lower, upper), "slab", swaps(1))
    wire_before = jnp.where(even, crossed, arrived)
    wire_after = jnp.where(even, arrived, crossed)

    cells, rows, depth = charge.shape
    far, near = pl.BlockSpec(memory_space=pl.ANY), pl.BlockSpec(memory_space=pltpu.VMEM)
    head = 5 * count * (width // depth)
    payload, *cuts = call(
        functools.partial(gather_kernel, rows, energies),
        56,
        1,
        (
            shape(head + 4 * cells, depth),
            *[one_slab] * (count - 1),
        ),
        jnp.reshape(mine, (1,)),
        *(array.reshape(-1, depth) for array in (potential_old, permittivity, charge)),
        wire_before.reshape(2, rows, depth),
        wire_after.reshape(2, rows, depth),
        owner_cell,
        free,
        in_specs=[pl.BlockSpec(memory_space=pltpu.SMEM)] + [near] * 6 + [far],
        out_specs=(near, *[far] * (count - 1)),
        scratch_shapes=[
            pltpu.VMEM((count - 1, 2, width, width), jnp.float32),
            pltpu.SemaphoreType.DMA((count - 1,)),
            pltpu.SemaphoreType.DMA((count - 1,)),
        ],
    )
    cuts = [first_cut, *cuts]
    sums, ends_before, ends_after, crossed, arrived = exchanged(payload, head, free_first[0])

    crossed, cuts[1] = lax.optimization_barrier((crossed, cuts[1]))
    sums, arrived = lax.optimization_barrier((sums, arrived))
    free_first = [arrived, lax.ppermute(cuts[1], "energy", first_pairs)]
    free_second = []

    def sent_on(part):
        given = free_first[part] if relayed else cuts[part]
        free_second.append(lax.ppermute(given, "energy", relay_pairs))

    def sent_after(part):
        free_first[part - 1], cut = lax.optimization_barrier((free_first[part - 1], cuts[part]))
        free_first.append(lax.ppermute(cut, "energy", first_pairs))

    sent_on(0)
    whole_map, whole_source = call(
        own_kernel,
        32,
        5 * count - 3,
        (whole, whole),
        free,
        coupling,
        sums,
    )

    whole_source, mode_tiles, field, perm, ends_before, ends_after = lax.optimization_barrier(
        (whole_source, mode_tiles, potential_old, permittivity, ends_before, ends_after)
    )
    ends_before = ends_before.reshape(2, 2, cells, 1, depth)
    ends_after = ends_after.reshape(2, 2, cells, 1, depth)
    edge = jnp.zeros((2, cells, rows, 1), jnp.float32)
    halos = ((wire_before, wire_after), (ends_before[:, 1], ends_after[:, 0]), (edge, edge))
    potential_new = relaxed(field, perm, charge, halos)

    odd = mine % 2
    distance = jnp.array([2, 2, 1, 1], jnp.int32)
    lowered = jnp.stack([turned, 1 - turned, 1 - odd, odd]).astype(jnp.float32)
    factors = (shifts[None, :] == distance[:, None]) * (occupation[None, :] + lowered[:, None])
    weights = jnp.sum(factors[:, :, None, None] * mode_tiles[None], axis=1)
    pick = jnp.stack([turned ^ odd, has_second]).astype(jnp.int32)

    block = pl.BlockSpec((1, 2, width, width), lambda s: (s, 0, 0, 0))
    one_state = pl.BlockSpec((2, width, width), lambda s: (0, 0, 0))
    own_block = [
        pl.BlockSpec((1, 2, width, width), lambda s, first=i * half: (first + s, 0, 0, 0))
        for i in range(2)
    ]

    def beside(index, parts):
        made = shape(half, 2, width, width)
        whole_spec = pl.BlockSpec((half, 2, width, width), lambda s: (0, 0, 0, 0))
        return call(
            functools.partial(beside_kernel, index * half, count, len(parts)),
            24,
            2 * half,
            (made, made),
            *parts,
            coupling,
            sums,
            grid=(1,),
            in_specs=[pl.BlockSpec(part.shape, lambda s: (0, 0, 0, 0)) for part in parts]
            + [
                pl.BlockSpec((half, 2, width, width), lambda s: (index, 0, 0, 0)),
                pl.BlockSpec(sums.shape, lambda s: (0, 0)),
            ],
            out_specs=(whole_spec, whole_spec),
        )

    def greens_of(room, link, source, carried):
        return call(
            greens_kernel,
            room,
            2 * link.shape[0],
            (shape(*link.shape), whole),
            link,
            source,
            carried,
            grid=(link.shape[0],),
            in_specs=[block, block, one_state],
            out_specs=(block, one_state),
        )

    assert peers % 2 == 0
    leaving, previous, before = whole_source, None, None
    beside_first, beside_second = [None, None], [None, None]
    for hop in range(1, peers - 1):
        arrived = lax.ppermute(leaving, "slab", swaps((hop - 1) % 2))
        if hop == 1:
            sent_on(1)
            sent_after(2)
            arrived, weights, free_first[1], potential_new = lax.optimization_barrier(
                (arrived, weights, free_first[1], potential_new)
            )
        if hop == 2:
            sent_on(2)
            sent_after(3)
            beside_first[0] = beside(0, free_first[:2])
            arrived, beside_first[0], free_first[2], *free_second[:2] = lax.optimization_barrier(
                (arrived, beside_first[0], free_first[2], *free_second[:2])
            )
        previous, before = arrived, leaving
        if hop < peers - 2:
            leaving = call(hop_kernel, 12, 2, whole, whole_map, whole_source, arrived)
    leaving, onward = call(
        last_hop_kernel,
        12,
        2,
        (whole, whole),
        jnp.reshape(place % 2, (1,)),
        whole_map,
        whole_source,
        previous,
        before,
        in_specs=[pl.BlockSpec(memory_space=pltpu.SMEM)] + [near] * 4,
        out_specs=(near, near),
    )

    def both(pairs):
        return [(a * peers + i, b * peers + j) for a, b in pairs for i, j in wire_up]

    arrived = lax.ppermute(leaving, "slab", swaps((peers - 2) % 2))
    carried_second = lax.ppermute(onward, ("energy", "slab"), both(second_pairs))
    sent_on(3)
    beside_second[0] = beside(0, free_second[:2])
    beside_first[1] = beside(1, free_first[2:])
    arrived, beside_first[1], beside_second[0], free_second[2] = lax.optimization_barrier(
        (arrived, beside_first[1], beside_second[0], free_second[2])
    )
    carried = jnp.where(place % 2 == 1, arrived, previous)
    carried_first = lax.ppermute(carried, "energy", first_pairs)
    greens, _ = call(
        functools.partial(own_greens_kernel, count),
        24,
        4 * count,
        (blocks, whole),
        free,
        coupling,
        sums,
        carried,
        grid=(count,),
        in_specs=[block, block, pl.BlockSpec(sums.shape, lambda s: (0, 0)), one_state],
        out_specs=(block, one_state),
    )
    carried_second, greens, free_second[3] = lax.optimization_barrier(
        (carried_second, greens, free_second[3])
    )

    beside_second[1] = beside(1, free_second[2:])
    greens_second = []
    for part in beside_second:
        made, carried_second = greens_of(16, *part, carried_second)
        greens_second.append(made)
    carried_first, greens_second = lax.optimization_barrier((carried_first, greens_second))

    outputs = []
    for index, part in enumerate(beside_first):
        here, there, carried_first = call(
            mixing_kernel,
            20,
            2 * half,
            (shape(half, 2, width, width), shape(half, 2, width, width), whole),
            pick,
            *part,
            carried_first,
            greens,
            greens_second[index],
            weights,
            grid=(half,),
            in_specs=[
                pl.BlockSpec(memory_space=pltpu.SMEM),
                block,
                block,
                one_state,
                own_block[index],
                block,
                pl.BlockSpec((4, width, width), lambda s: (0, 0, 0)),
            ],
            out_specs=(block, block, one_state),
        )
        if outputs:
            outputs[0], there = lax.optimization_barrier((outputs[0], there))
        outputs.append(here + lax.ppermute(there, "energy", twin_pairs))
    return potential_new, jnp.concatenate(outputs, axis=0)[None]


def solution(mesh):
    in_specs = (
        P("slab", "energy", None),
        P("slab", "energy", None),
        P("slab", "energy", None),
        P("slab", None),
        P("energy", "slab", None, None, None),
        P("slab", None, None, None),
        P(),
        P(),
        P(),
    )
    out_specs = (P("slab", "energy", None), P("energy", "slab", None, None, None))
    return jax.shard_map(
        per_device, mesh=mesh, in_specs=in_specs, out_specs=out_specs, check_vma=False
    )
```

```python
import functools
import math
import jax
import jax.numpy as jnp
from jax import lax
from jax.experimental import pallas as pl
from jax.experimental.pallas import tpu as pltpu
from jax.sharding import PartitionSpec as P

MIB = 1024 * 1024


def halves(value):
    high = value.astype(jnp.bfloat16)
    low = (value - high.astype(jnp.float32)).astype(jnp.bfloat16)
    return high, low


def parts_of(block):
    real, imag = block
    return [halves(real), halves(imag), halves(0.5 * real + 0.5 * imag)]


def left_form(block):
    return [jnp.concatenate([high, high, low], axis=1) for high, low in parts_of(block)]


def right_form(block, axis=0):
    return [jnp.concatenate([high, low, high], axis=axis) for high, low in parts_of(block)]


def three_products(left, right, flipped):
    dims = (((1,), (1 if flipped else 0,)), ((), ()))
    by_real, by_imag, by_mean = (
        lax.dot_general(a, b, dimension_numbers=dims, preferred_element_type=jnp.float32)
        for a, b in zip(left, right)
    )
    return by_real - by_imag, 4.0 * (by_mean - 0.25 * by_real - 0.25 * by_imag)


def product(former, latter):
    return three_products(left_form(former), right_form(latter), False)


def sandwich(link, inner):
    half_way = three_products(left_form(link), right_form(inner), False)
    return three_products(left_form(half_way), right_form(link, 1), True)


def added(first, second):
    return first[0] + second[0], first[1] + second[1]


def pair_of(ref, *where):
    return ref[(*where, 0)], ref[(*where, 1)]


def put(ref, value, *where):
    ref[(*where, 0)] = value[0]
    ref[(*where, 1)] = value[1]


def call(kernel, room, products, out_shapes, *operands, **more):
    flops = products * 9 * 2 * max(x.shape[-1] for x in operands) ** 3
    moved = sum(4 * math.prod(x.shape) for x in jax.tree.leaves((operands, out_shapes)))
    cost = pl.CostEstimate(flops=flops, bytes_accessed=moved, transcendentals=0)
    return pl.pallas_call(
        kernel,
        out_shape=out_shapes,
        cost_estimate=cost,
        compiler_params=pltpu.CompilerParams(vmem_limit_bytes=room * MIB),
        **more,
    )(*operands)


def shape(*dims):
    return jax.ShapeDtypeStruct(dims, jnp.float32)


def gather_kernel(rows, peers, mine, field, perm, charge, before, after, owner, free, *refs):
    out, ends, *parts, held, here, gone = refs
    loads, stores = [], []
    for index in range(len(parts)):
        slab = free.at[index + 1 : index + 2]
        loads.append(
            pltpu.make_async_copy(slab, held.at[index : index + 1], here.at[index])
        )
        loads[-1].start()
    total, depth = charge.shape
    count, orbitals = owner.shape
    height = total // count
    cross = rows * peers
    row_ids = lax.broadcasted_iota(jnp.int32, (total, depth), 0) % rows
    lane_ids = lax.broadcasted_iota(jnp.int32, (total, depth), 1)

    def neighbours(inner, first, last):
        down = jnp.concatenate([first, inner[:-rows]], axis=0)
        up = jnp.concatenate([inner[rows:], last], axis=0)
        left = jnp.where(lane_ids == 0, 0.0, pltpu.roll(inner, 1, axis=1))
        right = jnp.where(lane_ids == depth - 1, 0.0, pltpu.roll(inner, depth - 1, axis=1))
        low = jnp.where(row_ids == 0, 0.0, pltpu.roll(inner, 1, axis=0))
        high = jnp.where(row_ids == rows - 1, 0.0, pltpu.roll(inner, total - 1, axis=0))
        return (down + up) + (left + right) + (low + high)

    first, last = (before[0], before[1]), (after[0], after[1])
    field_now, perm_now = field[...], perm[...]
    both = perm_now * field_now
    own = [
        charge[...],
        perm_now,
        neighbours(field_now, first[0], last[0]),
        neighbours(both, first[0] * first[1], last[0] * last[1]),
        neighbours(perm_now, first[1], last[1]),
    ]
    beside = [jnp.zeros_like(both), jnp.zeros_like(both), field_now, both, perm_now]
    kinds = len(own)
    places = lax.broadcasted_iota(jnp.int32, (2 * height, orbitals), 0)
    depths = lax.broadcasted_iota(jnp.int32, (depth, orbitals), 0)
    first_row = mine[0] * rows
    step = 0
    for slab in range(count):
        if slab == count // 2:
            for index, part in enumerate(parts):
                loads[index].wait()
                stores.append(
                    pltpu.make_async_copy(held.at[index : index + 1], part, gone.at[index])
                )
                stores[-1].start()
        cells = owner[slab : slab + 1, :]
        lane, line = cells % depth, cells // depth
        across, along = line % cross - first_row, line // cross * rows
        key = jnp.where(across == rows, height + along + rows - 1, -1)
        key = jnp.where(across == -1, height + along, key)
        key = jnp.where((across >= 0) & (across < rows), along + across, key)
        cut = slice(slab * height, (slab + 1) * height)
        table = jnp.concatenate(
            [
                jnp.concatenate([t[cut] for t in own], axis=1),
                jnp.concatenate([t[cut] for t in beside], axis=1),
            ],
            axis=0,
        ).T
        high, rest = halves(table)
        middle = rest.astype(jnp.float32)
        lowest = ((table - high.astype(jnp.float32)) - middle).astype(jnp.bfloat16)
        hit = jnp.where(places == key, 1.0, 0.0).astype(jnp.bfloat16)
        found = jnp.dot(
            jnp.concatenate([high, rest, lowest], axis=1),
            jnp.concatenate([hit, hit, hit], axis=0),
            preferred_element_type=jnp.float32,
        )
        for kind in range(kinds):
            part = found[kind * depth : (kind + 1) * depth]
            value = jnp.sum(jnp.where(depths == lane, part, 0.0), axis=0, keepdims=True)
            for piece in range(orbitals // depth):
                row = sums_row(kind, slab, count, orbitals // depth) + piece
                out[row : row + 1, :] = value[:, piece * depth : (piece + 1) * depth]
    start = 0
    for array in (field, perm):
        for end in (0, rows - 1):
            ends[start : start + total // rows, :] = array[
                pl.ds(end, total // rows, stride=rows), :
            ]
            start += total // rows
    for store in stores:
        store.wait()


def sums_row(kind, slab, count, pieces):
    return (kind * count + slab) * pieces


def potential_of(sums, slab, count, orbitals):
    pieces = orbitals // sums.shape[1]

    def value(kind):
        first = sums_row(kind, slab, count, pieces)
        return jnp.concatenate([sums[pl.ds(first + p, 1), :] for p in range(pieces)], axis=1)

    charge, perm, fields, both, perms = (value(kind) for kind in range(5))
    return (charge + 0.5 * (perm * fields + both)) / (3.0 * perm + 0.5 * perms)


def source_of(block, potential):
    scaled = (block[0] * potential, block[1] * potential)
    return added(block, product(scaled, block))


def own_kernel(free, coupling, sums, whole_map, whole_source):
    count = free.shape[0]
    links, state = [], None
    for slab in range(count):
        block = pair_of(free, slab)
        links.append(product(block, pair_of(coupling, slab)))
        source = source_of(block, potential_of(sums, slab, count, free.shape[-1]))
        state = source if state is None else added(sandwich(links[slab], state), source)
    put(whole_source, state)
    while len(links) > 1:
        paired = [product(b, a) for a, b in zip(links[0::2], links[1::2])]
        links = paired + links[len(paired) * 2 :]
    put(whole_map, links[0])


def hop_kernel(whole_map, whole_source, carried, out):
    put(out, added(sandwich(pair_of(whole_map), pair_of(carried)), pair_of(whole_source)))


def last_hop_kernel(odd, whole_map, whole_source, carried, before, out, onward):
    now = added(sandwich(pair_of(whole_map), pair_of(carried)), pair_of(whole_source))
    put(out, now)
    put(onward, [jnp.where(odd[0] != 0, before[part], now[part]) for part in range(2)])


def beside_kernel(start, count, parts, *refs):
    frees, (coupling, sums, link, source) = refs[:parts], refs[parts:]
    slab = 0
    for free in frees:
        for place in range(free.shape[0]):
            block = pair_of(free, place)
            put(link, product(block, pair_of(coupling, slab)), slab)
            row = potential_of(sums, start + slab, count, free.shape[-1])
            put(source, source_of(block, row), slab)
            slab += 1


def greens_kernel(link, source, carried, greens, state):
    @pl.when(pl.program_id(0) == 0)
    def _():
        state[...] = carried[...]

    now = added(sandwich(pair_of(link, 0), pair_of(state)), pair_of(source, 0))
    put(state, now)
    put(greens, now, 0)


def own_greens_kernel(count, free, coupling, sums, carried, greens, state):
    @pl.when(pl.program_id(0) == 0)
    def _():
        state[...] = carried[...]

    block = pair_of(free, 0)
    link = product(block, pair_of(coupling, 0))
    row = potential_of(sums, pl.program_id(0), count, free.shape[-1])
    now = added(sandwich(link, pair_of(state)), source_of(block, row))
    put(state, now)
    put(greens, now, 0)


def mixing_kernel(pick, link, source, carried, own, second, weights, here, there, state):
    @pl.when(pl.program_id(0) == 0)
    def _():
        state[...] = carried[...]

    first = added(sandwich(pair_of(link, 0), pair_of(state)), pair_of(source, 0))
    put(state, first)
    for part in range(2):
        second_now = jnp.where(pick[1] != 0, second[0, part], 0.0)
        here[0, part] = weights[0] * first[part] + weights[1] * second_now
        picked = jnp.where(pick[0] == 0, first[part], second_now)
        there[0, part] = weights[2] * own[0, part] + weights[3] * picked


def relaxed(field, perm, charge, halos):
    numerator = charge
    denominator = jnp.zeros_like(charge)
    for dim in range(3):
        length = charge.shape[dim]
        before, after = halos[dim]
        for side in range(2):
            sides = []
            for which, array in enumerate((field, perm)):
                if side == 0:
                    kept = lax.slice_in_dim(array, 1, length, axis=dim)
                    parts = [kept, after[which]]
                else:
                    kept = lax.slice_in_dim(array, 0, length - 1, axis=dim)
                    parts = [before[which], kept]
                sides.append(jnp.concatenate(parts, axis=dim))
            face = 0.5 * (perm + sides[1])
            numerator = numerator + face * sides[0]
            denominator = denominator + face
    return numerator / denominator


def end_planes(array, dim):
    length = array.shape[dim]
    return (
        lax.slice_in_dim(array, 0, 1, axis=dim),
        lax.slice_in_dim(array, length - 1, length, axis=dim),
    )


def exchanged(sums, ends, early):
    peers = lax.axis_size("energy")
    assert peers >= 4 and peers & (peers - 1) == 0
    masks = [2, 1] + [1 << k for k in range(2, peers.bit_length() - 1)]
    rows, twin_ends = sums.shape[0], None
    first = None
    sums, early = lax.optimization_barrier((sums, early))
    for mask in masks:
        given = jnp.concatenate([sums, ends]) if mask == 1 else sums
        arrived = lax.ppermute(given, "energy", [(e, e ^ mask) for e in range(peers)])
        if mask == 1:
            twin_ends = arrived[rows:]
        sums = sums + arrived[:rows]
        first = sums if first is None else first
    return sums, twin_ends, first, early


def per_device(
    potential_old,
    charge,
    permittivity,
    owner_cell,
    green_free,
    coupling,
    shifts,
    occupation,
    mode_tiles,
):
    energies, peers = lax.axis_size("energy"), lax.axis_size("slab")
    mine = lax.axis_index("energy")
    free = green_free[0]
    count, _, width, _ = free.shape
    whole = shape(2, width, width)
    blocks = shape(count, 2, width, width)

    everyone = range(energies)
    relayed = energies == 8
    if relayed:
        first_pairs = [(e, e ^ 2) for e in everyone]
        second_pairs = [(2, 4), (3, 5), (4, 2), (5, 3)]
        relay_pairs = [(e, e ^ 4) for e in everyone]
        turned = (mine // 2) % 2
        has_second = jnp.where((mine >= 2) & (mine < 6), 1, 0)
    else:
        first_pairs = [(e, e - 2) for e in everyone if e >= 2]
        second_pairs = [(e, e + 2) for e in everyone if e + 2 < energies]
        relay_pairs = second_pairs
        turned = jnp.zeros_like(mine)
        has_second = jnp.ones_like(mine)
    twin_pairs = [(e, e ^ 1) for e in everyone]

    half = count // 2
    one_slab = shape(1, 2, width, width)
    first_cut = free[:1]
    free_first = [lax.ppermute(first_cut, "energy", first_pairs)]

    place = lax.axis_index("slab")
    wire_up = [(i, i + 1) for i in range(peers - 1)]

    def swaps(start):
        pairs = [(i, i + 1) for i in range(start, peers - 1, 2)]
        return pairs + [(j, i) for i, j in pairs]

    first_cut, stacked = lax.optimization_barrier(
        (first_cut, jnp.stack([potential_old, permittivity]))
    )
    lower, upper = end_planes(stacked, 1)
    even = place % 2 == 0
    arrived = lax.ppermute(jnp.where(even, upper, lower), "slab", swaps(0))
    crossed = lax.ppermute(jnp.where(even, lower, upper), "slab", swaps(1))
    wire_before = jnp.where(even, crossed, arrived)
    wire_after = jnp.where(even, arrived, crossed)

    cells, rows, depth = charge.shape
    own_ends = jnp.concatenate(
        [array[:, end] for array in (potential_old, permittivity) for end in (0, rows - 1)]
    )
    beyond = [(e, e + 1) for e in range(1, energies - 1, 2)]
    other_ends = lax.ppermute(own_ends, "energy", beyond + [(b, a) for a, b in beyond])
    far, near = pl.BlockSpec(memory_space=pl.ANY), pl.BlockSpec(memory_space=pltpu.VMEM)
    sums, ends, *cuts = call(
        functools.partial(gather_kernel, rows, energies),
        56,
        1,
        (
            shape(5 * count * (width // depth), depth),
            shape(4 * cells, depth),
            *[one_slab] * (count - 1),
        ),
        jnp.reshape(mine, (1,)),
        *(array.reshape(-1, depth) for array in (potential_old, permittivity, charge)),
        wire_before.reshape(2, rows, depth),
        wire_after.reshape(2, rows, depth),
        owner_cell,
        free,
        in_specs=[pl.BlockSpec(memory_space=pltpu.SMEM)] + [near] * 6 + [far],
        out_specs=(near, near, *[far] * (count - 1)),
        scratch_shapes=[
            pltpu.VMEM((count - 1, 2, width, width), jnp.float32),
            pltpu.SemaphoreType.DMA((count - 1,)),
            pltpu.SemaphoreType.DMA((count - 1,)),
        ],
    )
    cuts = [first_cut, *cuts]
    sums, twin_ends, crossed, (arrived, other_ends) = exchanged(
        sums, ends, (free_first[0], other_ends)
    )

    crossed, cuts[1] = lax.optimization_barrier((crossed, cuts[1]))
    sums, arrived = lax.optimization_barrier((sums, arrived))
    free_first = [arrived, lax.ppermute(cuts[1], "energy", first_pairs)]
    free_second = []

    def sent_on(part):
        given = free_first[part] if relayed else cuts[part]
        free_second.append(lax.ppermute(given, "energy", relay_pairs))

    def sent_after(part):
        free_first[part - 1], cut = lax.optimization_barrier((free_first[part - 1], cuts[part]))
        free_first.append(lax.ppermute(cut, "energy", first_pairs))

    sent_on(0)
    whole_map, whole_source = call(
        own_kernel,
        32,
        5 * count - 3,
        (whole, whole),
        free,
        coupling,
        sums,
    )

    whole_source, mode_tiles = lax.optimization_barrier((whole_source, mode_tiles))
    odd = mine % 2
    distance = jnp.array([2, 2, 1, 1], jnp.int32)
    lowered = jnp.stack([turned, 1 - turned, 1 - odd, odd]).astype(jnp.float32)
    factors = (shifts[None, :] == distance[:, None]) * (occupation[None, :] + lowered[:, None])
    weights = jnp.sum(factors[:, :, None, None] * mode_tiles[None], axis=1)
    pick = jnp.stack([turned ^ odd, has_second]).astype(jnp.int32)

    block = pl.BlockSpec((1, 2, width, width), lambda s: (s, 0, 0, 0))
    one_state = pl.BlockSpec((2, width, width), lambda s: (0, 0, 0))
    own_block = [
        pl.BlockSpec((1, 2, width, width), lambda s, first=i * half: (first + s, 0, 0, 0))
        for i in range(2)
    ]

    def beside(index, parts):
        made = shape(half, 2, width, width)
        whole_spec = pl.BlockSpec((half, 2, width, width), lambda s: (0, 0, 0, 0))
        return call(
            functools.partial(beside_kernel, index * half, count, len(parts)),
            24,
            2 * half,
            (made, made),
            *parts,
            coupling,
            sums,
            grid=(1,),
            in_specs=[pl.BlockSpec(part.shape, lambda s: (0, 0, 0, 0)) for part in parts]
            + [
                pl.BlockSpec((half, 2, width, width), lambda s: (index, 0, 0, 0)),
                pl.BlockSpec(sums.shape, lambda s: (0, 0)),
            ],
            out_specs=(whole_spec, whole_spec),
        )

    def greens_of(room, link, source, carried):
        return call(
            greens_kernel,
            room,
            2 * link.shape[0],
            (shape(*link.shape), whole),
            link,
            source,
            carried,
            grid=(link.shape[0],),
            in_specs=[block, block, one_state],
            out_specs=(block, one_state),
        )

    assert peers % 2 == 0
    leaving, previous, before = whole_source, None, None
    beside_first, beside_second = [None, None], [None, None]
    for hop in range(1, peers - 1):
        arrived = lax.ppermute(leaving, "slab", swaps((hop - 1) % 2))
        if hop == 1:
            sent_on(1)
            sent_after(2)
            arrived, weights, free_first[1] = lax.optimization_barrier(
                (arrived, weights, free_first[1])
            )
        if hop == 2:
            sent_on(2)
            sent_after(3)
            free_first[:3] = lax.optimization_barrier(free_first[:3])
            beside_first[0] = beside(0, free_first[:2])
            arrived, beside_first[0], free_first[2], *free_second[:2] = lax.optimization_barrier(
                (arrived, beside_first[0], free_first[2], *free_second[:2])
            )
        previous, before = arrived, leaving
        if hop < peers - 2:
            leaving = call(hop_kernel, 12, 2, whole, whole_map, whole_source, arrived)
    leaving, onward = call(
        last_hop_kernel,
        12,
        2,
        (whole, whole),
        jnp.reshape(place % 2, (1,)),
        whole_map,
        whole_source,
        previous,
        before,
        in_specs=[pl.BlockSpec(memory_space=pltpu.SMEM)] + [near] * 4,
        out_specs=(near, near),
    )

    def both(pairs):
        return [(a * peers + i, b * peers + j) for a, b in pairs for i, j in wire_up]

    arrived = lax.ppermute(leaving, "slab", swaps((peers - 2) % 2))
    carried_second = lax.ppermute(onward, ("energy", "slab"), both(second_pairs))
    sent_on(3)
    beside_second[0] = beside(0, free_second[:2])
    beside_first[1] = beside(1, free_first[2:])
    arrived, beside_first[1], beside_second[0], free_second[2] = lax.optimization_barrier(
        (arrived, beside_first[1], beside_second[0], free_second[2])
    )
    carried = jnp.where(place % 2 == 1, arrived, previous)
    carried_first = lax.ppermute(carried, "energy", first_pairs)
    greens, _ = call(
        functools.partial(own_greens_kernel, count),
        24,
        4 * count,
        (blocks, whole),
        free,
        coupling,
        sums,
        carried,
        grid=(count,),
        in_specs=[block, block, pl.BlockSpec(sums.shape, lambda s: (0, 0)), one_state],
        out_specs=(block, one_state),
    )
    carried_second, greens, free_second[3], field, perm = lax.optimization_barrier(
        (carried_second, greens, free_second[3], potential_old, permittivity)
    )

    ends_before = jnp.where(odd == 1, twin_ends, other_ends).reshape(2, 2, cells, 1, depth)
    ends_after = jnp.where(odd == 1, other_ends, twin_ends).reshape(2, 2, cells, 1, depth)
    edge = jnp.zeros((2, cells, rows, 1), jnp.float32)
    halos = ((wire_before, wire_after), (ends_before[:, 1], ends_after[:, 0]), (edge, edge))
    potential_new = relaxed(field, perm, charge, halos)

    beside_second[1] = beside(1, free_second[2:])
    greens_second = []
    for part in beside_second:
        made, carried_second = greens_of(16, *part, carried_second)
        greens_second.append(made)
    carried_first, greens_second, potential_new = lax.optimization_barrier(
        (carried_first, greens_second, potential_new)
    )

    outputs = []
    for index, part in enumerate(beside_first):
        here, there, carried_first = call(
            mixing_kernel,
            20,
            2 * half,
            (shape(half, 2, width, width), shape(half, 2, width, width), whole),
            pick,
            *part,
            carried_first,
            greens,
            greens_second[index],
            weights,
            grid=(half,),
            in_specs=[
                pl.BlockSpec(memory_space=pltpu.SMEM),
                block,
                block,
                one_state,
                own_block[index],
                block,
                pl.BlockSpec((4, width, width), lambda s: (0, 0, 0)),
            ],
            out_specs=(block, block, one_state),
        )
        if outputs:
            outputs[0], there = lax.optimization_barrier((outputs[0], there))
        outputs.append(here + lax.ppermute(there, "energy", twin_pairs))
    return potential_new, jnp.concatenate(outputs, axis=0)[None]


def solution(mesh):
    in_specs = (
        P("slab", "energy", None),
        P("slab", "energy", None),
        P("slab", "energy", None),
        P("slab", None),
        P("energy", "slab", None, None, None),
        P("slab", None, None, None),
        P(),
        P(),
        P(),
    )
    out_specs = (P("slab", "energy", None), P("energy", "slab", None, None, None))
    return jax.shard_map(
        per_device, mesh=mesh, in_specs=in_specs, out_specs=out_specs, check_vma=False
    )
```

```python
import functools
import math
import jax
import jax.numpy as jnp
from jax import lax
from jax.experimental import pallas as pl
from jax.experimental.pallas import tpu as pltpu
from jax.sharding import PartitionSpec as P

MIB = 1024 * 1024


def halves(value):
    high = value.astype(jnp.bfloat16)
    low = (value - high.astype(jnp.float32)).astype(jnp.bfloat16)
    return high, low


def parts_of(block):
    real, imag = block
    return [halves(real), halves(imag), halves(0.5 * real + 0.5 * imag)]


def left_form(block):
    return [jnp.concatenate([high, high, low], axis=1) for high, low in parts_of(block)]


def right_form(block, axis=0):
    return [jnp.concatenate([high, low, high], axis=axis) for high, low in parts_of(block)]


def three_products(left, right, flipped):
    dims = (((1,), (1 if flipped else 0,)), ((), ()))
    by_real, by_imag, by_mean = (
        lax.dot_general(a, b, dimension_numbers=dims, preferred_element_type=jnp.float32)
        for a, b in zip(left, right)
    )
    return by_real - by_imag, 4.0 * (by_mean - 0.25 * by_real - 0.25 * by_imag)


def product(former, latter):
    return three_products(left_form(former), right_form(latter), False)


def sandwich(link, inner):
    half_way = three_products(left_form(link), right_form(inner), False)
    return three_products(left_form(half_way), right_form(link, 1), True)


def added(first, second):
    return first[0] + second[0], first[1] + second[1]


def pair_of(ref, *where):
    return ref[(*where, 0)], ref[(*where, 1)]


def put(ref, value, *where):
    ref[(*where, 0)] = value[0]
    ref[(*where, 1)] = value[1]


def call(kernel, room, products, out_shapes, *operands, **more):
    flops = products * 9 * 2 * max(x.shape[-1] for x in operands) ** 3
    moved = sum(4 * math.prod(x.shape) for x in jax.tree.leaves((operands, out_shapes)))
    cost = pl.CostEstimate(flops=flops, bytes_accessed=moved, transcendentals=0)
    return pl.pallas_call(
        kernel,
        out_shape=out_shapes,
        cost_estimate=cost,
        compiler_params=pltpu.CompilerParams(vmem_limit_bytes=room * MIB),
        **more,
    )(*operands)


def shape(*dims):
    return jax.ShapeDtypeStruct(dims, jnp.float32)


def gather_kernel(rows, peers, mine, field, perm, charge, before, after, owner, free, *refs):
    out, ends, *parts, held, here, gone = refs
    loads, stores = [], []
    for index in range(len(parts)):
        slab = free.at[index + 1 : index + 2]
        loads.append(
            pltpu.make_async_copy(slab, held.at[index : index + 1], here.at[index])
        )
        loads[-1].start()
    total, depth = charge.shape
    count, orbitals = owner.shape
    height = total // count
    cross = rows * peers
    row_ids = lax.broadcasted_iota(jnp.int32, (total, depth), 0) % rows
    lane_ids = lax.broadcasted_iota(jnp.int32, (total, depth), 1)

    def neighbours(inner, first, last):
        down = jnp.concatenate([first, inner[:-rows]], axis=0)
        up = jnp.concatenate([inner[rows:], last], axis=0)
        left = jnp.where(lane_ids == 0, 0.0, pltpu.roll(inner, 1, axis=1))
        right = jnp.where(lane_ids == depth - 1, 0.0, pltpu.roll(inner, depth - 1, axis=1))
        low = jnp.where(row_ids == 0, 0.0, pltpu.roll(inner, 1, axis=0))
        high = jnp.where(row_ids == rows - 1, 0.0, pltpu.roll(inner, total - 1, axis=0))
        return (down + up) + (left + right) + (low + high)

    first, last = (before[0], before[1]), (after[0], after[1])
    field_now, perm_now = field[...], perm[...]
    both = perm_now * field_now
    own = [
        charge[...],
        perm_now,
        neighbours(field_now, first[0], last[0]),
        neighbours(both, first[0] * first[1], last[0] * last[1]),
        neighbours(perm_now, first[1], last[1]),
    ]
    beside = [jnp.zeros_like(both), jnp.zeros_like(both), field_now, both, perm_now]
    kinds = len(own)
    places = lax.broadcasted_iota(jnp.int32, (2 * height, orbitals), 0)
    depths = lax.broadcasted_iota(jnp.int32, (depth, orbitals), 0)
    first_row = mine[0] * rows
    step = 0
    for slab in range(count):
        if slab == count // 2:
            for index, part in enumerate(parts):
                loads[index].wait()
                stores.append(
                    pltpu.make_async_copy(held.at[index : index + 1], part, gone.at[index])
                )
                stores[-1].start()
        cells = owner[slab : slab + 1, :]
        lane, line = cells % depth, cells // depth
        across, along = line % cross - first_row, line // cross * rows
        key = jnp.where(across == rows, height + along + rows - 1, -1)
        key = jnp.where(across == -1, height + along, key)
        key = jnp.where((across >= 0) & (across < rows), along + across, key)
        cut = slice(slab * height, (slab + 1) * height)
        table = jnp.concatenate(
            [
                jnp.concatenate([t[cut] for t in own], axis=1),
                jnp.concatenate([t[cut] for t in beside], axis=1),
            ],
            axis=0,
        ).T
        high, rest = halves(table)
        middle = rest.astype(jnp.float32)
        lowest = ((table - high.astype(jnp.float32)) - middle).astype(jnp.bfloat16)
        hit = jnp.where(places == key, 1.0, 0.0).astype(jnp.bfloat16)
        found = jnp.dot(
            jnp.concatenate([high, rest, lowest], axis=1),
            jnp.concatenate([hit, hit, hit], axis=0),
            preferred_element_type=jnp.float32,
        )
        for kind in range(kinds):
            part = found[kind * depth : (kind + 1) * depth]
            value = jnp.sum(jnp.where(depths == lane, part, 0.0), axis=0, keepdims=True)
            for piece in range(orbitals // depth):
                row = sums_row(kind, slab, count, orbitals // depth) + piece
                out[row : row + 1, :] = value[:, piece * depth : (piece + 1) * depth]
    start = 0
    for array in (field, perm):
        for end in (0, rows - 1):
            ends[start : start + total // rows, :] = array[
                pl.ds(end, total // rows, stride=rows), :
            ]
            start += total // rows
    for store in stores:
        store.wait()


def sums_row(kind, slab, count, pieces):
    return (kind * count + slab) * pieces


def potential_of(sums, slab, count, orbitals):
    pieces = orbitals // sums.shape[1]

    def value(kind):
        first = sums_row(kind, slab, count, pieces)
        return jnp.concatenate([sums[pl.ds(first + p, 1), :] for p in range(pieces)], axis=1)

    charge, perm, fields, both, perms = (value(kind) for kind in range(5))
    return (charge + 0.5 * (perm * fields + both)) / (3.0 * perm + 0.5 * perms)


def source_of(block, potential):
    scaled = (block[0] * potential, block[1] * potential)
    return added(block, product(scaled, block))


def own_kernel(free, coupling, sums, whole_map, whole_source):
    count = free.shape[0]
    links, state = [], None
    for slab in range(count):
        block = pair_of(free, slab)
        links.append(product(block, pair_of(coupling, slab)))
        source = source_of(block, potential_of(sums, slab, count, free.shape[-1]))
        state = source if state is None else added(sandwich(links[slab], state), source)
    put(whole_source, state)
    while len(links) > 1:
        paired = [product(b, a) for a, b in zip(links[0::2], links[1::2])]
        links = paired + links[len(paired) * 2 :]
    put(whole_map, links[0])


def hop_kernel(whole_map, whole_source, carried, out):
    put(out, added(sandwich(pair_of(whole_map), pair_of(carried)), pair_of(whole_source)))


def last_hop_kernel(odd, whole_map, whole_source, carried, before, out, onward):
    now = added(sandwich(pair_of(whole_map), pair_of(carried)), pair_of(whole_source))
    put(out, now)
    put(onward, [jnp.where(odd[0] != 0, before[part], now[part]) for part in range(2)])


def beside_kernel(start, count, parts, *refs):
    frees, (coupling, sums, link, source) = refs[:parts], refs[parts:]
    slab = 0
    for free in frees:
        for place in range(free.shape[0]):
            block = pair_of(free, place)
            put(link, product(block, pair_of(coupling, slab)), slab)
            row = potential_of(sums, start + slab, count, free.shape[-1])
            put(source, source_of(block, row), slab)
            slab += 1


def greens_kernel(link, source, carried, greens, state):
    @pl.when(pl.program_id(0) == 0)
    def _():
        state[...] = carried[...]

    now = added(sandwich(pair_of(link, 0), pair_of(state)), pair_of(source, 0))
    put(state, now)
    put(greens, now, 0)


def own_greens_kernel(count, free, coupling, sums, carried, greens, state):
    @pl.when(pl.program_id(0) == 0)
    def _():
        state[...] = carried[...]

    block = pair_of(free, 0)
    link = product(block, pair_of(coupling, 0))
    row = potential_of(sums, pl.program_id(0), count, free.shape[-1])
    now = added(sandwich(link, pair_of(state)), source_of(block, row))
    put(state, now)
    put(greens, now, 0)


def mixing_kernel(pick, link, source, carried, own, second, weights, here, there, state):
    @pl.when(pl.program_id(0) == 0)
    def _():
        state[...] = carried[...]

    first = added(sandwich(pair_of(link, 0), pair_of(state)), pair_of(source, 0))
    put(state, first)
    for part in range(2):
        second_now = jnp.where(pick[1] != 0, second[0, part], 0.0)
        here[0, part] = weights[0] * first[part] + weights[1] * second_now
        picked = jnp.where(pick[0] == 0, first[part], second_now)
        there[0, part] = weights[2] * own[0, part] + weights[3] * picked


def relaxed(field, perm, charge, halos):
    numerator = charge
    denominator = jnp.zeros_like(charge)
    for dim in range(3):
        length = charge.shape[dim]
        before, after = halos[dim]
        for side in range(2):
            sides = []
            for which, array in enumerate((field, perm)):
                if side == 0:
                    kept = lax.slice_in_dim(array, 1, length, axis=dim)
                    parts = [kept, after[which]]
                else:
                    kept = lax.slice_in_dim(array, 0, length - 1, axis=dim)
                    parts = [before[which], kept]
                sides.append(jnp.concatenate(parts, axis=dim))
            face = 0.5 * (perm + sides[1])
            numerator = numerator + face * sides[0]
            denominator = denominator + face
    return numerator / denominator


def end_planes(array, dim):
    length = array.shape[dim]
    return (
        lax.slice_in_dim(array, 0, 1, axis=dim),
        lax.slice_in_dim(array, length - 1, length, axis=dim),
    )


def exchanged(sums, ends, other_ends, early):
    peers = lax.axis_size("energy")
    assert peers >= 4 and peers & (peers - 1) == 0
    masks = [2, 1] + [1 << k for k in range(2, peers.bit_length() - 1)]
    rows, twin_ends = sums.shape[0], None
    first = None
    sums, early = lax.optimization_barrier((sums, early))
    for mask in masks:
        if mask == 4:
            sums, other_ends = lax.optimization_barrier((sums, other_ends))
        given = jnp.concatenate([sums, ends]) if mask == 1 else sums
        arrived = lax.ppermute(given, "energy", [(e, e ^ mask) for e in range(peers)])
        if mask == 1:
            twin_ends = arrived[rows:]
        sums = sums + arrived[:rows]
        first = sums if first is None else first
    return sums, twin_ends, other_ends, first, early


def per_device(
    potential_old,
    charge,
    permittivity,
    owner_cell,
    green_free,
    coupling,
    shifts,
    occupation,
    mode_tiles,
):
    energies, peers = lax.axis_size("energy"), lax.axis_size("slab")
    mine = lax.axis_index("energy")
    free = green_free[0]
    count, _, width, _ = free.shape
    whole = shape(2, width, width)
    blocks = shape(count, 2, width, width)

    everyone = range(energies)
    relayed = energies == 8
    if relayed:
        first_pairs = [(e, e ^ 2) for e in everyone]
        second_pairs = [(2, 4), (3, 5), (4, 2), (5, 3)]
        relay_pairs = [(e, e ^ 4) for e in everyone]
        turned = (mine // 2) % 2
        has_second = jnp.where((mine >= 2) & (mine < 6), 1, 0)
    else:
        first_pairs = [(e, e - 2) for e in everyone if e >= 2]
        second_pairs = [(e, e + 2) for e in everyone if e + 2 < energies]
        relay_pairs = second_pairs
        turned = jnp.zeros_like(mine)
        has_second = jnp.ones_like(mine)
    twin_pairs = [(e, e ^ 1) for e in everyone]

    half = count // 2
    one_slab = shape(1, 2, width, width)
    first_cut = free[:1]
    free_first = [lax.ppermute(first_cut, "energy", first_pairs)]

    place = lax.axis_index("slab")
    wire_up = [(i, i + 1) for i in range(peers - 1)]

    def swaps(start):
        pairs = [(i, i + 1) for i in range(start, peers - 1, 2)]
        return pairs + [(j, i) for i, j in pairs]

    first_cut, stacked = lax.optimization_barrier(
        (first_cut, jnp.stack([potential_old, permittivity]))
    )
    lower, upper = end_planes(stacked, 1)
    even = place % 2 == 0
    arrived = lax.ppermute(jnp.where(even, upper, lower), "slab", swaps(0))
    crossed = lax.ppermute(jnp.where(even, lower, upper), "slab", swaps(1))
    wire_before = jnp.where(even, crossed, arrived)
    wire_after = jnp.where(even, arrived, crossed)

    cells, rows, depth = charge.shape
    far, near = pl.BlockSpec(memory_space=pl.ANY), pl.BlockSpec(memory_space=pltpu.VMEM)
    sums, ends, *cuts = call(
        functools.partial(gather_kernel, rows, energies),
        56,
        1,
        (
            shape(5 * count * (width // depth), depth),
            shape(4 * cells, depth),
            *[one_slab] * (count - 1),
        ),
        jnp.reshape(mine, (1,)),
        *(array.reshape(-1, depth) for array in (potential_old, permittivity, charge)),
        wire_before.reshape(2, rows, depth),
        wire_after.reshape(2, rows, depth),
        owner_cell,
        free,
        in_specs=[pl.BlockSpec(memory_space=pltpu.SMEM)] + [near] * 6 + [far],
        out_specs=(near, near, *[far] * (count - 1)),
        scratch_shapes=[
            pltpu.VMEM((count - 1, 2, width, width), jnp.float32),
            pltpu.SemaphoreType.DMA((count - 1,)),
            pltpu.SemaphoreType.DMA((count - 1,)),
        ],
    )
    cuts = [first_cut, *cuts]
    beyond = [(e, e + 1) for e in range(1, energies - 1, 2)]
    other_ends = lax.ppermute(ends, "energy", beyond + [(b, a) for a, b in beyond])
    sums, twin_ends, other_ends, crossed, arrived = exchanged(
        sums, ends, other_ends, free_first[0]
    )

    crossed, cuts[1] = lax.optimization_barrier((crossed, cuts[1]))
    sums, arrived = lax.optimization_barrier((sums, arrived))
    free_first = [arrived, lax.ppermute(cuts[1], "energy", first_pairs)]
    free_second = []

    def sent_on(part):
        given = free_first[part] if relayed else cuts[part]
        free_second.append(lax.ppermute(given, "energy", relay_pairs))

    def sent_after(part):
        free_first[part - 1], cut = lax.optimization_barrier((free_first[part - 1], cuts[part]))
        free_first.append(lax.ppermute(cut, "energy", first_pairs))

    sent_on(0)
    whole_map, whole_source = call(
        own_kernel,
        32,
        5 * count - 3,
        (whole, whole),
        free,
        coupling,
        sums,
    )

    whole_source, mode_tiles = lax.optimization_barrier((whole_source, mode_tiles))
    odd = mine % 2
    distance = jnp.array([2, 2, 1, 1], jnp.int32)
    lowered = jnp.stack([turned, 1 - turned, 1 - odd, odd]).astype(jnp.float32)
    factors = (shifts[None, :] == distance[:, None]) * (occupation[None, :] + lowered[:, None])
    weights = jnp.sum(factors[:, :, None, None] * mode_tiles[None], axis=1)
    pick = jnp.stack([turned ^ odd, has_second]).astype(jnp.int32)

    block = pl.BlockSpec((1, 2, width, width), lambda s: (s, 0, 0, 0))
    one_state = pl.BlockSpec((2, width, width), lambda s: (0, 0, 0))
    own_block = [
        pl.BlockSpec((1, 2, width, width), lambda s, first=i * half: (first + s, 0, 0, 0))
        for i in range(2)
    ]

    def beside(index, parts):
        made = shape(half, 2, width, width)
        whole_spec = pl.BlockSpec((half, 2, width, width), lambda s: (0, 0, 0, 0))
        return call(
            functools.partial(beside_kernel, index * half, count, len(parts)),
            24,
            2 * half,
            (made, made),
            *parts,
            coupling,
            sums,
            grid=(1,),
            in_specs=[pl.BlockSpec(part.shape, lambda s: (0, 0, 0, 0)) for part in parts]
            + [
                pl.BlockSpec((half, 2, width, width), lambda s: (index, 0, 0, 0)),
                pl.BlockSpec(sums.shape, lambda s: (0, 0)),
            ],
            out_specs=(whole_spec, whole_spec),
        )

    def greens_of(room, link, source, carried):
        return call(
            greens_kernel,
            room,
            2 * link.shape[0],
            (shape(*link.shape), whole),
            link,
            source,
            carried,
            grid=(link.shape[0],),
            in_specs=[block, block, one_state],
            out_specs=(block, one_state),
        )

    assert peers % 2 == 0
    leaving, previous, before = whole_source, None, None
    beside_first, beside_second = [None, None], [None, None]
    for hop in range(1, peers - 1):
        arrived = lax.ppermute(leaving, "slab", swaps((hop - 1) % 2))
        if hop == 1:
            sent_on(1)
            sent_after(2)
            arrived, weights, free_first[1] = lax.optimization_barrier(
                (arrived, weights, free_first[1])
            )
        if hop == 2:
            sent_on(2)
            sent_after(3)
            free_first[:3] = lax.optimization_barrier(free_first[:3])
            beside_first[0] = beside(0, free_first[:2])
            arrived, beside_first[0], free_first[2], *free_second[:2] = lax.optimization_barrier(
                (arrived, beside_first[0], free_first[2], *free_second[:2])
            )
        previous, before = arrived, leaving
        if hop < peers - 2:
            leaving = call(hop_kernel, 12, 2, whole, whole_map, whole_source, arrived)
    leaving, onward = call(
        last_hop_kernel,
        12,
        2,
        (whole, whole),
        jnp.reshape(place % 2, (1,)),
        whole_map,
        whole_source,
        previous,
        before,
        in_specs=[pl.BlockSpec(memory_space=pltpu.SMEM)] + [near] * 4,
        out_specs=(near, near),
    )

    def both(pairs):
        return [(a * peers + i, b * peers + j) for a, b in pairs for i, j in wire_up]

    arrived = lax.ppermute(leaving, "slab", swaps((peers - 2) % 2))
    carried_second = lax.ppermute(onward, ("energy", "slab"), both(second_pairs))
    sent_on(3)
    beside_second[0] = beside(0, free_second[:2])
    beside_first[1] = beside(1, free_first[2:])
    arrived, beside_first[1], beside_second[0], free_second[2] = lax.optimization_barrier(
        (arrived, beside_first[1], beside_second[0], free_second[2])
    )
    carried = jnp.where(place % 2 == 1, arrived, previous)
    carried_first = lax.ppermute(carried, "energy", first_pairs)
    greens, _ = call(
        functools.partial(own_greens_kernel, count),
        24,
        4 * count,
        (blocks, whole),
        free,
        coupling,
        sums,
        carried,
        grid=(count,),
        in_specs=[block, block, pl.BlockSpec(sums.shape, lambda s: (0, 0)), one_state],
        out_specs=(block, one_state),
    )
    carried_second, greens, free_second[3], field, perm = lax.optimization_barrier(
        (carried_second, greens, free_second[3], potential_old, permittivity)
    )

    ends_before = jnp.where(odd == 1, twin_ends, other_ends).reshape(2, 2, cells, 1, depth)
    ends_after = jnp.where(odd == 1, other_ends, twin_ends).reshape(2, 2, cells, 1, depth)
    edge = jnp.zeros((2, cells, rows, 1), jnp.float32)
    halos = ((wire_before, wire_after), (ends_before[:, 1], ends_after[:, 0]), (edge, edge))
    potential_new = relaxed(field, perm, charge, halos)

    beside_second[1] = beside(1, free_second[2:])
    greens_second = []
    for part in beside_second:
        made, carried_second = greens_of(16, *part, carried_second)
        greens_second.append(made)
    carried_first, greens_second, potential_new = lax.optimization_barrier(
        (carried_first, greens_second, potential_new)
    )

    outputs = []
    for index, part in enumerate(beside_first):
        here, there, carried_first = call(
            mixing_kernel,
            20,
            2 * half,
            (shape(half, 2, width, width), shape(half, 2, width, width), whole),
            pick,
            *part,
            carried_first,
            greens,
            greens_second[index],
            weights,
            grid=(half,),
            in_specs=[
                pl.BlockSpec(memory_space=pltpu.SMEM),
                block,
                block,
                one_state,
                own_block[index],
                block,
                pl.BlockSpec((4, width, width), lambda s: (0, 0, 0)),
            ],
            out_specs=(block, block, one_state),
        )
        if outputs:
            outputs[0], there = lax.optimization_barrier((outputs[0], there))
        outputs.append(here + lax.ppermute(there, "energy", twin_pairs))
    return potential_new, jnp.concatenate(outputs, axis=0)[None]


def solution(mesh):
    in_specs = (
        P("slab", "energy", None),
        P("slab", "energy", None),
        P("slab", "energy", None),
        P("slab", None),
        P("energy", "slab", None, None, None),
        P("slab", None, None, None),
        P(),
        P(),
        P(),
    )
    out_specs = (P("slab", "energy", None), P("energy", "slab", None, None, None))
    return jax.shard_map(
        per_device, mesh=mesh, in_specs=in_specs, out_specs=out_specs, check_vma=False
    )
```

```python
import functools
import math
import jax
import jax.numpy as jnp
from jax import lax
from jax.experimental import pallas as pl
from jax.experimental.pallas import tpu as pltpu
from jax.sharding import PartitionSpec as P

MIB = 1024 * 1024


def halves(value):
    high = value.astype(jnp.bfloat16)
    low = (value - high.astype(jnp.float32)).astype(jnp.bfloat16)
    return high, low


def parts_of(block):
    real, imag = block
    return [halves(real), halves(imag), halves(0.5 * real + 0.5 * imag)]


def left_form(block):
    return [jnp.concatenate([high, high, low], axis=1) for high, low in parts_of(block)]


def right_form(block, axis=0):
    return [jnp.concatenate([high, low, high], axis=axis) for high, low in parts_of(block)]


def three_products(left, right, flipped):
    dims = (((1,), (1 if flipped else 0,)), ((), ()))
    by_real, by_imag, by_mean = (
        lax.dot_general(a, b, dimension_numbers=dims, preferred_element_type=jnp.float32)
        for a, b in zip(left, right)
    )
    return by_real - by_imag, 4.0 * (by_mean - 0.25 * by_real - 0.25 * by_imag)


def product(former, latter):
    return three_products(left_form(former), right_form(latter), False)


def sandwich(link, inner):
    half_way = three_products(left_form(link), right_form(inner), False)
    return three_products(left_form(half_way), right_form(link, 1), True)


def added(first, second):
    return first[0] + second[0], first[1] + second[1]


def pair_of(ref, *where):
    return ref[(*where, 0)], ref[(*where, 1)]


def put(ref, value, *where):
    ref[(*where, 0)] = value[0]
    ref[(*where, 1)] = value[1]


def call(kernel, room, products, out_shapes, *operands, **more):
    flops = products * 9 * 2 * max(x.shape[-1] for x in operands) ** 3
    moved = sum(4 * math.prod(x.shape) for x in jax.tree.leaves((operands, out_shapes)))
    cost = pl.CostEstimate(flops=flops, bytes_accessed=moved, transcendentals=0)
    return pl.pallas_call(
        kernel,
        out_shape=out_shapes,
        cost_estimate=cost,
        compiler_params=pltpu.CompilerParams(vmem_limit_bytes=room * MIB),
        **more,
    )(*operands)


def shape(*dims):
    return jax.ShapeDtypeStruct(dims, jnp.float32)


def gather_kernel(rows, peers, mine, field, perm, charge, before, after, owner, free, *refs):
    out, ends, *parts, held, here, gone = refs
    loads, stores = [], []
    for index in range(len(parts)):
        slab = free.at[index + 1 : index + 2]
        loads.append(
            pltpu.make_async_copy(slab, held.at[index : index + 1], here.at[index])
        )
        loads[-1].start()
    total, depth = charge.shape
    count, orbitals = owner.shape
    height = total // count
    cross = rows * peers
    row_ids = lax.broadcasted_iota(jnp.int32, (total, depth), 0) % rows
    lane_ids = lax.broadcasted_iota(jnp.int32, (total, depth), 1)

    def neighbours(inner, first, last):
        down = jnp.concatenate([first, inner[:-rows]], axis=0)
        up = jnp.concatenate([inner[rows:], last], axis=0)
        left = jnp.where(lane_ids == 0, 0.0, pltpu.roll(inner, 1, axis=1))
        right = jnp.where(lane_ids == depth - 1, 0.0, pltpu.roll(inner, depth - 1, axis=1))
        low = jnp.where(row_ids == 0, 0.0, pltpu.roll(inner, 1, axis=0))
        high = jnp.where(row_ids == rows - 1, 0.0, pltpu.roll(inner, total - 1, axis=0))
        return (down + up) + (left + right) + (low + high)

    first, last = (before[0], before[1]), (after[0], after[1])
    field_now, perm_now = field[...], perm[...]
    both = perm_now * field_now
    own = [
        charge[...],
        perm_now,
        neighbours(field_now, first[0], last[0]),
        neighbours(both, first[0] * first[1], last[0] * last[1]),
        neighbours(perm_now, first[1], last[1]),
    ]
    beside = [jnp.zeros_like(both), jnp.zeros_like(both), field_now, both, perm_now]
    kinds = len(own)
    places = lax.broadcasted_iota(jnp.int32, (2 * height, orbitals), 0)
    depths = lax.broadcasted_iota(jnp.int32, (depth, orbitals), 0)
    first_row = mine[0] * rows
    step = 0
    for slab in range(count):
        if slab == count // 2:
            for index, part in enumerate(parts):
                loads[index].wait()
                stores.append(
                    pltpu.make_async_copy(held.at[index : index + 1], part, gone.at[index])
                )
                stores[-1].start()
        cells = owner[slab : slab + 1, :]
        lane, line = cells % depth, cells // depth
        across, along = line % cross - first_row, line // cross * rows
        key = jnp.where(across == rows, height + along + rows - 1, -1)
        key = jnp.where(across == -1, height + along, key)
        key = jnp.where((across >= 0) & (across < rows), along + across, key)
        cut = slice(slab * height, (slab + 1) * height)
        table = jnp.concatenate(
            [
                jnp.concatenate([t[cut] for t in own], axis=1),
                jnp.concatenate([t[cut] for t in beside], axis=1),
            ],
            axis=0,
        ).T
        high, rest = halves(table)
        middle = rest.astype(jnp.float32)
        lowest = ((table - high.astype(jnp.float32)) - middle).astype(jnp.bfloat16)
        hit = jnp.where(places == key, 1.0, 0.0).astype(jnp.bfloat16)
        found = jnp.dot(
            jnp.concatenate([high, rest, lowest], axis=1),
            jnp.concatenate([hit, hit, hit], axis=0),
            preferred_element_type=jnp.float32,
        )
        for kind in range(kinds):
            part = found[kind * depth : (kind + 1) * depth]
            value = jnp.sum(jnp.where(depths == lane, part, 0.0), axis=0, keepdims=True)
            for piece in range(orbitals // depth):
                row = sums_row(kind, slab, count, orbitals // depth) + piece
                out[row : row + 1, :] = value[:, piece * depth : (piece + 1) * depth]
    start = 0
    for array in (field, perm):
        for end in (0, rows - 1):
            ends[start : start + total // rows, :] = array[
                pl.ds(end, total // rows, stride=rows), :
            ]
            start += total // rows
    for store in stores:
        store.wait()


def sums_row(kind, slab, count, pieces):
    return (kind * count + slab) * pieces


def potential_of(sums, slab, count, orbitals):
    pieces = orbitals // sums.shape[1]

    def value(kind):
        first = sums_row(kind, slab, count, pieces)
        return jnp.concatenate([sums[pl.ds(first + p, 1), :] for p in range(pieces)], axis=1)

    charge, perm, fields, both, perms = (value(kind) for kind in range(5))
    return (charge + 0.5 * (perm * fields + both)) / (3.0 * perm + 0.5 * perms)


def source_of(block, potential):
    scaled = (block[0] * potential, block[1] * potential)
    return added(block, product(scaled, block))


def own_kernel(free, coupling, sums, whole_map, whole_source):
    count = free.shape[0]
    links, state = [], None
    for slab in range(count):
        block = pair_of(free, slab)
        links.append(product(block, pair_of(coupling, slab)))
        source = source_of(block, potential_of(sums, slab, count, free.shape[-1]))
        state = source if state is None else added(sandwich(links[slab], state), source)
    put(whole_source, state)
    while len(links) > 1:
        paired = [product(b, a) for a, b in zip(links[0::2], links[1::2])]
        links = paired + links[len(paired) * 2 :]
    put(whole_map, links[0])


def hop_kernel(whole_map, whole_source, carried, out):
    put(out, added(sandwich(pair_of(whole_map), pair_of(carried)), pair_of(whole_source)))


def last_hop_kernel(odd, whole_map, whole_source, carried, before, out, onward):
    now = added(sandwich(pair_of(whole_map), pair_of(carried)), pair_of(whole_source))
    put(out, now)
    put(onward, [jnp.where(odd[0] != 0, before[part], now[part]) for part in range(2)])


def beside_kernel(start, count, parts, *refs):
    frees, (coupling, sums, link, source) = refs[:parts], refs[parts:]
    slab = 0
    for free in frees:
        for place in range(free.shape[0]):
            block = pair_of(free, place)
            put(link, product(block, pair_of(coupling, slab)), slab)
            row = potential_of(sums, start + slab, count, free.shape[-1])
            put(source, source_of(block, row), slab)
            slab += 1


def greens_kernel(link, source, carried, greens, state):
    @pl.when(pl.program_id(0) == 0)
    def _():
        state[...] = carried[...]

    now = added(sandwich(pair_of(link, 0), pair_of(state)), pair_of(source, 0))
    put(state, now)
    put(greens, now, 0)


def own_greens_kernel(count, free, coupling, sums, carried, greens, state):
    @pl.when(pl.program_id(0) == 0)
    def _():
        state[...] = carried[...]

    block = pair_of(free, 0)
    link = product(block, pair_of(coupling, 0))
    row = potential_of(sums, pl.program_id(0), count, free.shape[-1])
    now = added(sandwich(link, pair_of(state)), source_of(block, row))
    put(state, now)
    put(greens, now, 0)


def mixing_kernel(pick, link, source, carried, own, second, weights, here, there, state):
    @pl.when(pl.program_id(0) == 0)
    def _():
        state[...] = carried[...]

    first = added(sandwich(pair_of(link, 0), pair_of(state)), pair_of(source, 0))
    put(state, first)
    for part in range(2):
        second_now = jnp.where(pick[1] != 0, second[0, part], 0.0)
        here[0, part] = weights[0] * first[part] + weights[1] * second_now
        picked = jnp.where(pick[0] == 0, first[part], second_now)
        there[0, part] = weights[2] * own[0, part] + weights[3] * picked


def relaxed(field, perm, charge, halos):
    numerator = charge
    denominator = jnp.zeros_like(charge)
    for dim in range(3):
        length = charge.shape[dim]
        before, after = halos[dim]
        for side in range(2):
            sides = []
            for which, array in enumerate((field, perm)):
                if side == 0:
                    kept = lax.slice_in_dim(array, 1, length, axis=dim)
                    parts = [kept, after[which]]
                else:
                    kept = lax.slice_in_dim(array, 0, length - 1, axis=dim)
                    parts = [before[which], kept]
                sides.append(jnp.concatenate(parts, axis=dim))
            face = 0.5 * (perm + sides[1])
            numerator = numerator + face * sides[0]
            denominator = denominator + face
    return numerator / denominator


def end_planes(array, dim):
    length = array.shape[dim]
    return (
        lax.slice_in_dim(array, 0, 1, axis=dim),
        lax.slice_in_dim(array, length - 1, length, axis=dim),
    )


def exchanged(sums, ends, early):
    peers = lax.axis_size("energy")
    assert peers >= 4 and peers & (peers - 1) == 0
    masks = [2, 1] + [1 << k for k in range(2, peers.bit_length() - 1)]
    rows, twin_ends = sums.shape[0], None
    first = None
    sums, early = lax.optimization_barrier((sums, early))
    for mask in masks:
        given = jnp.concatenate([sums, ends]) if mask == 1 else sums
        arrived = lax.ppermute(given, "energy", [(e, e ^ mask) for e in range(peers)])
        if mask == 1:
            twin_ends = arrived[rows:]
        sums = sums + arrived[:rows]
        first = arrived if first is None else first
    return sums, twin_ends, first, early


def per_device(
    potential_old,
    charge,
    permittivity,
    owner_cell,
    green_free,
    coupling,
    shifts,
    occupation,
    mode_tiles,
):
    energies, peers = lax.axis_size("energy"), lax.axis_size("slab")
    mine = lax.axis_index("energy")
    free = green_free[0]
    count, _, width, _ = free.shape
    whole = shape(2, width, width)
    blocks = shape(count, 2, width, width)

    everyone = range(energies)
    relayed = energies == 8
    if relayed:
        first_pairs = [(e, e ^ 2) for e in everyone]
        second_pairs = [(2, 4), (3, 5), (4, 2), (5, 3)]
        relay_pairs = [(e, e ^ 4) for e in everyone]
        turned = (mine // 2) % 2
        has_second = jnp.where((mine >= 2) & (mine < 6), 1, 0)
    else:
        first_pairs = [(e, e - 2) for e in everyone if e >= 2]
        second_pairs = [(e, e + 2) for e in everyone if e + 2 < energies]
        relay_pairs = second_pairs
        turned = jnp.zeros_like(mine)
        has_second = jnp.ones_like(mine)
    twin_pairs = [(e, e ^ 1) for e in everyone]

    half = count // 2
    one_slab = shape(1, 2, width, width)
    first_cut = free[:1]
    free_first = [lax.ppermute(first_cut, "energy", first_pairs)]

    place = lax.axis_index("slab")
    wire_up = [(i, i + 1) for i in range(peers - 1)]

    def swaps(start):
        pairs = [(i, i + 1) for i in range(start, peers - 1, 2)]
        return pairs + [(j, i) for i, j in pairs]

    first_cut, stacked = lax.optimization_barrier(
        (first_cut, jnp.stack([potential_old, permittivity]))
    )
    lower, upper = end_planes(stacked, 1)
    even = place % 2 == 0
    arrived = lax.ppermute(jnp.where(even, upper, lower), "slab", swaps(0))
    crossed = lax.ppermute(jnp.where(even, lower, upper), "slab", swaps(1))
    wire_before = jnp.where(even, crossed, arrived)
    wire_after = jnp.where(even, arrived, crossed)

    cells, rows, depth = charge.shape
    beyond = [(e, e + 1) for e in range(1, energies - 1, 2)]
    other_ends = lax.ppermute(stacked, "energy", beyond + [(b, a) for a, b in beyond])
    far, near = pl.BlockSpec(memory_space=pl.ANY), pl.BlockSpec(memory_space=pltpu.VMEM)
    sums, ends, *cuts = call(
        functools.partial(gather_kernel, rows, energies),
        56,
        1,
        (
            shape(5 * count * (width // depth), depth),
            shape(4 * cells, depth),
            *[one_slab] * (count - 1),
        ),
        jnp.reshape(mine, (1,)),
        *(array.reshape(-1, depth) for array in (potential_old, permittivity, charge)),
        wire_before.reshape(2, rows, depth),
        wire_after.reshape(2, rows, depth),
        owner_cell,
        free,
        in_specs=[pl.BlockSpec(memory_space=pltpu.SMEM)] + [near] * 6 + [far],
        out_specs=(near, near, *[far] * (count - 1)),
        scratch_shapes=[
            pltpu.VMEM((count - 1, 2, width, width), jnp.float32),
            pltpu.SemaphoreType.DMA((count - 1,)),
            pltpu.SemaphoreType.DMA((count - 1,)),
        ],
    )
    cuts = [first_cut, *cuts]
    sums, twin_ends, crossed, (arrived, other_ends) = exchanged(
        sums, ends, (free_first[0], other_ends)
    )

    crossed, cuts[1] = lax.optimization_barrier((crossed, cuts[1]))
    sums, arrived = lax.optimization_barrier((sums, arrived))
    free_first = [arrived, lax.ppermute(cuts[1], "energy", first_pairs)]
    free_second = []

    def sent_on(part):
        given = free_first[part] if relayed else cuts[part]
        free_second.append(lax.ppermute(given, "energy", relay_pairs))

    def sent_after(part):
        free_first[part - 1], cut = lax.optimization_barrier((free_first[part - 1], cuts[part]))
        free_first.append(lax.ppermute(cut, "energy", first_pairs))

    sent_on(0)
    whole_map, whole_source = call(
        own_kernel,
        32,
        5 * count - 3,
        (whole, whole),
        free,
        coupling,
        sums,
    )

    whole_source, mode_tiles = lax.optimization_barrier((whole_source, mode_tiles))
    odd = mine % 2
    distance = jnp.array([2, 2, 1, 1], jnp.int32)
    lowered = jnp.stack([turned, 1 - turned, 1 - odd, odd]).astype(jnp.float32)
    factors = (shifts[None, :] == distance[:, None]) * (occupation[None, :] + lowered[:, None])
    weights = jnp.sum(factors[:, :, None, None] * mode_tiles[None], axis=1)
    pick = jnp.stack([turned ^ odd, has_second]).astype(jnp.int32)

    block = pl.BlockSpec((1, 2, width, width), lambda s: (s, 0, 0, 0))
    one_state = pl.BlockSpec((2, width, width), lambda s: (0, 0, 0))
    own_block = [
        pl.BlockSpec((1, 2, width, width), lambda s, first=i * half: (first + s, 0, 0, 0))
        for i in range(2)
    ]

    def beside(index, parts):
        made = shape(half, 2, width, width)
        whole_spec = pl.BlockSpec((half, 2, width, width), lambda s: (0, 0, 0, 0))
        return call(
            functools.partial(beside_kernel, index * half, count, len(parts)),
            24,
            2 * half,
            (made, made),
            *parts,
            coupling,
            sums,
            grid=(1,),
            in_specs=[pl.BlockSpec(part.shape, lambda s: (0, 0, 0, 0)) for part in parts]
            + [
                pl.BlockSpec((half, 2, width, width), lambda s: (index, 0, 0, 0)),
                pl.BlockSpec(sums.shape, lambda s: (0, 0)),
            ],
            out_specs=(whole_spec, whole_spec),
        )

    def greens_of(room, link, source, carried):
        return call(
            greens_kernel,
            room,
            2 * link.shape[0],
            (shape(*link.shape), whole),
            link,
            source,
            carried,
            grid=(link.shape[0],),
            in_specs=[block, block, one_state],
            out_specs=(block, one_state),
        )

    assert peers % 2 == 0
    leaving, previous, before = whole_source, None, None
    beside_first, beside_second = [None, None], [None, None]
    for hop in range(1, peers - 1):
        arrived = lax.ppermute(leaving, "slab", swaps((hop - 1) % 2))
        if hop == 1:
            sent_on(1)
            sent_after(2)
            arrived, weights, free_first[1] = lax.optimization_barrier(
                (arrived, weights, free_first[1])
            )
        if hop == 2:
            sent_on(2)
            sent_after(3)
            free_first[:3] = lax.optimization_barrier(free_first[:3])
            beside_first[0] = beside(0, free_first[:2])
            arrived, beside_first[0], free_first[2], *free_second[:2] = lax.optimization_barrier(
                (arrived, beside_first[0], free_first[2], *free_second[:2])
            )
        previous, before = arrived, leaving
        if hop < peers - 2:
            leaving = call(hop_kernel, 12, 2, whole, whole_map, whole_source, arrived)
    leaving, onward = call(
        last_hop_kernel,
        12,
        2,
        (whole, whole),
        jnp.reshape(place % 2, (1,)),
        whole_map,
        whole_source,
        previous,
        before,
        in_specs=[pl.BlockSpec(memory_space=pltpu.SMEM)] + [near] * 4,
        out_specs=(near, near),
    )

    def both(pairs):
        return [(a * peers + i, b * peers + j) for a, b in pairs for i, j in wire_up]

    arrived = lax.ppermute(leaving, "slab", swaps((peers - 2) % 2))
    carried_second = lax.ppermute(onward, ("energy", "slab"), both(second_pairs))
    sent_on(3)
    beside_second[0] = beside(0, free_second[:2])
    beside_first[1] = beside(1, free_first[2:])
    arrived, beside_first[1], beside_second[0], free_second[2] = lax.optimization_barrier(
        (arrived, beside_first[1], beside_second[0], free_second[2])
    )
    carried = jnp.where(place % 2 == 1, arrived, previous)
    carried_first = lax.ppermute(carried, "energy", first_pairs)
    greens, _ = call(
        functools.partial(own_greens_kernel, count),
        24,
        4 * count,
        (blocks, whole),
        free,
        coupling,
        sums,
        carried,
        grid=(count,),
        in_specs=[block, block, pl.BlockSpec(sums.shape, lambda s: (0, 0)), one_state],
        out_specs=(block, one_state),
    )
    carried_second, greens, free_second[3], field, perm = lax.optimization_barrier(
        (carried_second, greens, free_second[3], potential_old, permittivity)
    )

    twin_ends = twin_ends.reshape(2, 2, cells, 1, depth)
    ends_before = jnp.where(odd == 1, twin_ends[:, 1], other_ends[:, :, rows - 1 :])
    ends_after = jnp.where(odd == 1, other_ends[:, :, :1], twin_ends[:, 0])
    edge = jnp.zeros((2, cells, rows, 1), jnp.float32)
    halos = ((wire_before, wire_after), (ends_before, ends_after), (edge, edge))
    potential_new = relaxed(field, perm, charge, halos)

    beside_second[1] = beside(1, free_second[2:])
    greens_second = []
    for part in beside_second:
        made, carried_second = greens_of(16, *part, carried_second)
        greens_second.append(made)
    carried_first, greens_second, potential_new = lax.optimization_barrier(
        (carried_first, greens_second, potential_new)
    )

    outputs = []
    for index, part in enumerate(beside_first):
        here, there, carried_first = call(
            mixing_kernel,
            20,
            2 * half,
            (shape(half, 2, width, width), shape(half, 2, width, width), whole),
            pick,
            *part,
            carried_first,
            greens,
            greens_second[index],
            weights,
            grid=(half,),
            in_specs=[
                pl.BlockSpec(memory_space=pltpu.SMEM),
                block,
                block,
                one_state,
                own_block[index],
                block,
                pl.BlockSpec((4, width, width), lambda s: (0, 0, 0)),
            ],
            out_specs=(block, block, one_state),
        )
        if outputs:
            outputs[0], there = lax.optimization_barrier((outputs[0], there))
        outputs.append(here + lax.ppermute(there, "energy", twin_pairs))
    return potential_new, jnp.concatenate(outputs, axis=0)[None]


def solution(mesh):
    in_specs = (
        P("slab", "energy", None),
        P("slab", "energy", None),
        P("slab", "energy", None),
        P("slab", None),
        P("energy", "slab", None, None, None),
        P("slab", None, None, None),
        P(),
        P(),
        P(),
    )
    out_specs = (P("slab", "energy", None), P("energy", "slab", None, None, None))
    return jax.shard_map(
        per_device, mesh=mesh, in_specs=in_specs, out_specs=out_specs, check_vma=False
    )
```

```python
import functools
import math
import jax
import jax.numpy as jnp
from jax import lax
from jax.experimental import pallas as pl
from jax.experimental.pallas import tpu as pltpu
from jax.sharding import PartitionSpec as P

MIB = 1024 * 1024


def halves(value):
    high = value.astype(jnp.bfloat16)
    low = (value - high.astype(jnp.float32)).astype(jnp.bfloat16)
    return high, low


def parts_of(block):
    real, imag = block
    return [halves(real), halves(imag), halves(0.5 * real + 0.5 * imag)]


def left_form(block):
    return [jnp.concatenate([high, high, low], axis=1) for high, low in parts_of(block)]


def right_form(block, axis=0):
    return [jnp.concatenate([high, low, high], axis=axis) for high, low in parts_of(block)]


def three_products(left, right, flipped):
    dims = (((1,), (1 if flipped else 0,)), ((), ()))
    by_real, by_imag, by_mean = (
        lax.dot_general(a, b, dimension_numbers=dims, preferred_element_type=jnp.float32)
        for a, b in zip(left, right)
    )
    return by_real - by_imag, 4.0 * (by_mean - 0.25 * by_real - 0.25 * by_imag)


def product(former, latter):
    return three_products(left_form(former), right_form(latter), False)


def sandwich(link, inner):
    half_way = three_products(left_form(link), right_form(inner), False)
    return three_products(left_form(half_way), right_form(link, 1), True)


def added(first, second):
    return first[0] + second[0], first[1] + second[1]


def pair_of(ref, *where):
    return ref[(*where, 0)], ref[(*where, 1)]


def put(ref, value, *where):
    ref[(*where, 0)] = value[0]
    ref[(*where, 1)] = value[1]


def call(kernel, room, products, out_shapes, *operands, **more):
    flops = products * 9 * 2 * max(x.shape[-1] for x in operands) ** 3
    moved = sum(4 * math.prod(x.shape) for x in jax.tree.leaves((operands, out_shapes)))
    cost = pl.CostEstimate(flops=flops, bytes_accessed=moved, transcendentals=0)
    return pl.pallas_call(
        kernel,
        out_shape=out_shapes,
        cost_estimate=cost,
        compiler_params=pltpu.CompilerParams(vmem_limit_bytes=room * MIB),
        **more,
    )(*operands)


def shape(*dims):
    return jax.ShapeDtypeStruct(dims, jnp.float32)


def gather_kernel(rows, peers, mine, field, perm, charge, before, after, owner, free, *refs):
    out, ends, *parts, held, here, gone = refs
    loads, stores = [], []
    for index in range(len(parts)):
        slab = free.at[index + 1 : index + 2]
        loads.append(
            pltpu.make_async_copy(slab, held.at[index : index + 1], here.at[index])
        )
        loads[-1].start()
    total, depth = charge.shape
    count, orbitals = owner.shape
    height = total // count
    cross = rows * peers
    row_ids = lax.broadcasted_iota(jnp.int32, (total, depth), 0) % rows
    lane_ids = lax.broadcasted_iota(jnp.int32, (total, depth), 1)

    def neighbours(inner, first, last):
        down = jnp.concatenate([first, inner[:-rows]], axis=0)
        up = jnp.concatenate([inner[rows:], last], axis=0)
        left = jnp.where(lane_ids == 0, 0.0, pltpu.roll(inner, 1, axis=1))
        right = jnp.where(lane_ids == depth - 1, 0.0, pltpu.roll(inner, depth - 1, axis=1))
        low = jnp.where(row_ids == 0, 0.0, pltpu.roll(inner, 1, axis=0))
        high = jnp.where(row_ids == rows - 1, 0.0, pltpu.roll(inner, total - 1, axis=0))
        return (down + up) + (left + right) + (low + high)

    first, last = (before[0], before[1]), (after[0], after[1])
    field_now, perm_now = field[...], perm[...]
    both = perm_now * field_now
    own = [
        charge[...],
        perm_now,
        neighbours(field_now, first[0], last[0]),
        neighbours(both, first[0] * first[1], last[0] * last[1]),
        neighbours(perm_now, first[1], last[1]),
    ]
    beside = [jnp.zeros_like(both), jnp.zeros_like(both), field_now, both, perm_now]
    kinds = len(own)
    places = lax.broadcasted_iota(jnp.int32, (2 * height, orbitals), 0)
    depths = lax.broadcasted_iota(jnp.int32, (depth, orbitals), 0)
    first_row = mine[0] * rows
    step = 0
    for slab in range(count):
        if slab == count // 2:
            for index, part in enumerate(parts):
                loads[index].wait()
                stores.append(
                    pltpu.make_async_copy(held.at[index : index + 1], part, gone.at[index])
                )
                stores[-1].start()
        cells = owner[slab : slab + 1, :]
        lane, line = cells % depth, cells // depth
        across, along = line % cross - first_row, line // cross * rows
        key = jnp.where(across == rows, height + along + rows - 1, -1)
        key = jnp.where(across == -1, height + along, key)
        key = jnp.where((across >= 0) & (across < rows), along + across, key)
        cut = slice(slab * height, (slab + 1) * height)
        table = jnp.concatenate(
            [
                jnp.concatenate([t[cut] for t in own], axis=1),
                jnp.concatenate([t[cut] for t in beside], axis=1),
            ],
            axis=0,
        ).T
        high, rest = halves(table)
        middle = rest.astype(jnp.float32)
        lowest = ((table - high.astype(jnp.float32)) - middle).astype(jnp.bfloat16)
        hit = jnp.where(places == key, 1.0, 0.0).astype(jnp.bfloat16)
        found = jnp.dot(
            jnp.concatenate([high, rest, lowest], axis=1),
            jnp.concatenate([hit, hit, hit], axis=0),
            preferred_element_type=jnp.float32,
        )
        for kind in range(kinds):
            part = found[kind * depth : (kind + 1) * depth]
            value = jnp.sum(jnp.where(depths == lane, part, 0.0), axis=0, keepdims=True)
            for piece in range(orbitals // depth):
                row = sums_row(kind, slab, count, orbitals // depth) + piece
                out[row : row + 1, :] = value[:, piece * depth : (piece + 1) * depth]
    start = 0
    for array in (field, perm):
        for end in (0, rows - 1):
            ends[start : start + total // rows, :] = array[
                pl.ds(end, total // rows, stride=rows), :
            ]
            start += total // rows
    for store in stores:
        store.wait()


def sums_row(kind, slab, count, pieces):
    return (kind * count + slab) * pieces


def potential_of(sums, slab, count, orbitals):
    pieces = orbitals // sums.shape[1]

    def value(kind):
        first = sums_row(kind, slab, count, pieces)
        return jnp.concatenate([sums[pl.ds(first + p, 1), :] for p in range(pieces)], axis=1)

    charge, perm, fields, both, perms = (value(kind) for kind in range(5))
    return (charge + 0.5 * (perm * fields + both)) / (3.0 * perm + 0.5 * perms)


def source_of(block, potential):
    scaled = (block[0] * potential, block[1] * potential)
    return added(block, product(scaled, block))


def own_kernel(free, coupling, sums, whole_map, whole_source):
    count = free.shape[0]
    links, state = [], None
    for slab in range(count):
        block = pair_of(free, slab)
        links.append(product(block, pair_of(coupling, slab)))
        source = source_of(block, potential_of(sums, slab, count, free.shape[-1]))
        state = source if state is None else added(sandwich(links[slab], state), source)
    put(whole_source, state)
    while len(links) > 1:
        paired = [product(b, a) for a, b in zip(links[0::2], links[1::2])]
        links = paired + links[len(paired) * 2 :]
    put(whole_map, links[0])


def hop_kernel(whole_map, whole_source, carried, out):
    put(out, added(sandwich(pair_of(whole_map), pair_of(carried)), pair_of(whole_source)))


def last_hop_kernel(odd, whole_map, whole_source, carried, before, out, onward):
    now = added(sandwich(pair_of(whole_map), pair_of(carried)), pair_of(whole_source))
    put(out, now)
    put(onward, [jnp.where(odd[0] != 0, before[part], now[part]) for part in range(2)])


def beside_kernel(start, count, parts, *refs):
    frees, (coupling, sums, link, source) = refs[:parts], refs[parts:]
    slab = 0
    for free in frees:
        for place in range(free.shape[0]):
            block = pair_of(free, place)
            put(link, product(block, pair_of(coupling, slab)), slab)
            row = potential_of(sums, start + slab, count, free.shape[-1])
            put(source, source_of(block, row), slab)
            slab += 1


def greens_kernel(link, source, carried, greens, state):
    @pl.when(pl.program_id(0) == 0)
    def _():
        state[...] = carried[...]

    now = added(sandwich(pair_of(link, 0), pair_of(state)), pair_of(source, 0))
    put(state, now)
    put(greens, now, 0)


def own_greens_kernel(count, free, coupling, sums, carried, greens, state):
    @pl.when(pl.program_id(0) == 0)
    def _():
        state[...] = carried[...]

    block = pair_of(free, 0)
    link = product(block, pair_of(coupling, 0))
    row = potential_of(sums, pl.program_id(0), count, free.shape[-1])
    now = added(sandwich(link, pair_of(state)), source_of(block, row))
    put(state, now)
    put(greens, now, 0)


def mixing_kernel(pick, link, source, carried, own, second, weights, here, there, state):
    @pl.when(pl.program_id(0) == 0)
    def _():
        state[...] = carried[...]

    first = added(sandwich(pair_of(link, 0), pair_of(state)), pair_of(source, 0))
    put(state, first)
    for part in range(2):
        second_now = jnp.where(pick[1] != 0, second[0, part], 0.0)
        here[0, part] = weights[0] * first[part] + weights[1] * second_now
        picked = jnp.where(pick[0] == 0, first[part], second_now)
        there[0, part] = weights[2] * own[0, part] + weights[3] * picked


def relaxed(field, perm, charge, halos):
    numerator = charge
    denominator = jnp.zeros_like(charge)
    for dim in range(3):
        length = charge.shape[dim]
        before, after = halos[dim]
        for side in range(2):
            sides = []
            for which, array in enumerate((field, perm)):
                if side == 0:
                    kept = lax.slice_in_dim(array, 1, length, axis=dim)
                    parts = [kept, after[which]]
                else:
                    kept = lax.slice_in_dim(array, 0, length - 1, axis=dim)
                    parts = [before[which], kept]
                sides.append(jnp.concatenate(parts, axis=dim))
            face = 0.5 * (perm + sides[1])
            numerator = numerator + face * sides[0]
            denominator = denominator + face
    return numerator / denominator


def end_planes(array, dim):
    length = array.shape[dim]
    return (
        lax.slice_in_dim(array, 0, 1, axis=dim),
        lax.slice_in_dim(array, length - 1, length, axis=dim),
    )


def exchanged(sums, ends, early):
    peers = lax.axis_size("energy")
    assert peers >= 4 and peers & (peers - 1) == 0
    masks = [2, 1] + [1 << k for k in range(2, peers.bit_length() - 1)]
    rows, twin_ends = sums.shape[0], None
    first = None
    sums, early = lax.optimization_barrier((sums, early))
    for mask in masks:
        given = jnp.concatenate([sums, ends]) if mask == 1 else sums
        arrived = lax.ppermute(given, "energy", [(e, e ^ mask) for e in range(peers)])
        if mask == 1:
            twin_ends = arrived[rows:]
        sums = sums + arrived[:rows]
        first = arrived if first is None else first
    return sums, twin_ends, first, early


def per_device(
    potential_old,
    charge,
    permittivity,
    owner_cell,
    green_free,
    coupling,
    shifts,
    occupation,
    mode_tiles,
):
    energies, peers = lax.axis_size("energy"), lax.axis_size("slab")
    mine = lax.axis_index("energy")
    free = green_free[0]
    count, _, width, _ = free.shape
    whole = shape(2, width, width)
    blocks = shape(count, 2, width, width)

    everyone = range(energies)
    relayed = energies == 8
    if relayed:
        first_pairs = [(e, e ^ 2) for e in everyone]
        second_pairs = [(2, 4), (3, 5), (4, 2), (5, 3)]
        relay_pairs = [(e, e ^ 4) for e in everyone]
        turned = (mine // 2) % 2
        has_second = jnp.where((mine >= 2) & (mine < 6), 1, 0)
    else:
        first_pairs = [(e, e - 2) for e in everyone if e >= 2]
        second_pairs = [(e, e + 2) for e in everyone if e + 2 < energies]
        relay_pairs = second_pairs
        turned = jnp.zeros_like(mine)
        has_second = jnp.ones_like(mine)
    twin_pairs = [(e, e ^ 1) for e in everyone]

    half = count // 2
    one_slab = shape(1, 2, width, width)
    first_cut = free[:1]
    free_first = [lax.ppermute(first_cut, "energy", first_pairs)]

    place = lax.axis_index("slab")
    wire_up = [(i, i + 1) for i in range(peers - 1)]

    def swaps(start):
        pairs = [(i, i + 1) for i in range(start, peers - 1, 2)]
        return pairs + [(j, i) for i, j in pairs]

    first_cut, stacked = lax.optimization_barrier(
        (first_cut, jnp.stack([potential_old, permittivity]))
    )
    lower, upper = end_planes(stacked, 1)
    even = place % 2 == 0
    arrived = lax.ppermute(jnp.where(even, upper, lower), "slab", swaps(0))
    crossed = lax.ppermute(jnp.where(even, lower, upper), "slab", swaps(1))
    wire_before = jnp.where(even, crossed, arrived)
    wire_after = jnp.where(even, arrived, crossed)

    cells, rows, depth = charge.shape
    beyond = [(e, e + 1) for e in range(1, energies - 1, 2)]
    other_ends = lax.ppermute(stacked, "energy", beyond + [(b, a) for a, b in beyond])
    far, near = pl.BlockSpec(memory_space=pl.ANY), pl.BlockSpec(memory_space=pltpu.VMEM)
    sums, ends, *cuts = call(
        functools.partial(gather_kernel, rows, energies),
        56,
        1,
        (
            shape(5 * count * (width // depth), depth),
            shape(4 * cells, depth),
            *[one_slab] * (count - 1),
        ),
        jnp.reshape(mine, (1,)),
        *(array.reshape(-1, depth) for array in (potential_old, permittivity, charge)),
        wire_before.reshape(2, rows, depth),
        wire_after.reshape(2, rows, depth),
        owner_cell,
        free,
        in_specs=[pl.BlockSpec(memory_space=pltpu.SMEM)] + [near] * 6 + [far],
        out_specs=(near, near, *[far] * (count - 1)),
        scratch_shapes=[
            pltpu.VMEM((count - 1, 2, width, width), jnp.float32),
            pltpu.SemaphoreType.DMA((count - 1,)),
            pltpu.SemaphoreType.DMA((count - 1,)),
        ],
    )
    cuts = [first_cut, *cuts]
    sums, twin_ends, crossed, (arrived, other_ends) = exchanged(
        sums, ends, (free_first[0], other_ends)
    )

    crossed, cuts[1] = lax.optimization_barrier((crossed, cuts[1]))
    sums, arrived = lax.optimization_barrier((sums, arrived))
    free_first = [arrived, lax.ppermute(cuts[1], "energy", first_pairs)]
    free_second = []

    def sent_on(part):
        given = free_first[part] if relayed else cuts[part]
        free_second.append(lax.ppermute(given, "energy", relay_pairs))

    def sent_after(part):
        free_first[part - 1], cut = lax.optimization_barrier((free_first[part - 1], cuts[part]))
        free_first.append(lax.ppermute(cut, "energy", first_pairs))

    sent_on(0)
    whole_map, whole_source = call(
        own_kernel,
        32,
        5 * count - 3,
        (whole, whole),
        free,
        coupling,
        sums,
    )

    whole_source, mode_tiles = lax.optimization_barrier((whole_source, mode_tiles))
    odd = mine % 2
    distance = jnp.array([2, 2, 1, 1], jnp.int32)
    lowered = jnp.stack([turned, 1 - turned, 1 - odd, odd]).astype(jnp.float32)
    factors = (shifts[None, :] == distance[:, None]) * (occupation[None, :] + lowered[:, None])
    weights = jnp.sum(factors[:, :, None, None] * mode_tiles[None], axis=1)
    pick = jnp.stack([turned ^ odd, has_second]).astype(jnp.int32)

    block = pl.BlockSpec((1, 2, width, width), lambda s: (s, 0, 0, 0))
    one_state = pl.BlockSpec((2, width, width), lambda s: (0, 0, 0))
    own_block = [
        pl.BlockSpec((1, 2, width, width), lambda s, first=i * half: (first + s, 0, 0, 0))
        for i in range(2)
    ]

    def beside(index, parts):
        made = shape(half, 2, width, width)
        whole_spec = pl.BlockSpec((half, 2, width, width), lambda s: (0, 0, 0, 0))
        return call(
            functools.partial(beside_kernel, index * half, count, len(parts)),
            24,
            2 * half,
            (made, made),
            *parts,
            coupling,
            sums,
            grid=(1,),
            in_specs=[pl.BlockSpec(part.shape, lambda s: (0, 0, 0, 0)) for part in parts]
            + [
                pl.BlockSpec((half, 2, width, width), lambda s: (index, 0, 0, 0)),
                pl.BlockSpec(sums.shape, lambda s: (0, 0)),
            ],
            out_specs=(whole_spec, whole_spec),
        )

    def greens_of(room, link, source, carried):
        return call(
            greens_kernel,
            room,
            2 * link.shape[0],
            (shape(*link.shape), whole),
            link,
            source,
            carried,
            grid=(link.shape[0],),
            in_specs=[block, block, one_state],
            out_specs=(block, one_state),
        )

    assert peers % 2 == 0
    leaving, previous, before = whole_source, None, None
    beside_first, beside_second = [None, None], [None, None]
    for hop in range(1, peers - 1):
        arrived = lax.ppermute(leaving, "slab", swaps((hop - 1) % 2))
        if hop == 1:
            sent_on(1)
            sent_after(2)
            arrived, weights, free_first[1] = lax.optimization_barrier(
                (arrived, weights, free_first[1])
            )
        if hop == 2:
            sent_on(2)
            sent_after(3)
            free_first[:3] = lax.optimization_barrier(free_first[:3])
            beside_first[0] = beside(0, free_first[:2])
            arrived, beside_first[0], free_first[2], *free_second[:2] = lax.optimization_barrier(
                (arrived, beside_first[0], free_first[2], *free_second[:2])
            )
        previous, before = arrived, leaving
        if hop < peers - 2:
            leaving = call(hop_kernel, 12, 2, whole, whole_map, whole_source, arrived)
    leaving, onward = call(
        last_hop_kernel,
        12,
        2,
        (whole, whole),
        jnp.reshape(place % 2, (1,)),
        whole_map,
        whole_source,
        previous,
        before,
        in_specs=[pl.BlockSpec(memory_space=pltpu.SMEM)] + [near] * 4,
        out_specs=(near, near),
    )

    def both(pairs):
        return [(a * peers + i, b * peers + j) for a, b in pairs for i, j in wire_up]

    arrived = lax.ppermute(leaving, "slab", swaps((peers - 2) % 2))
    sent_on(3)
    beside_second[0] = beside(0, free_second[:2])
    beside_first[1] = beside(1, free_first[2:])
    onward, beside_first[1] = lax.optimization_barrier((onward, beside_first[1]))
    carried_second = lax.ppermute(onward, ("energy", "slab"), both(second_pairs))
    arrived, beside_first[1], beside_second[0], free_second[2] = lax.optimization_barrier(
        (arrived, beside_first[1], beside_second[0], free_second[2])
    )
    carried = jnp.where(place % 2 == 1, arrived, previous)
    carried_first = lax.ppermute(carried, "energy", first_pairs)
    greens, _ = call(
        functools.partial(own_greens_kernel, count),
        24,
        4 * count,
        (blocks, whole),
        free,
        coupling,
        sums,
        carried,
        grid=(count,),
        in_specs=[block, block, pl.BlockSpec(sums.shape, lambda s: (0, 0)), one_state],
        out_specs=(block, one_state),
    )
    carried_second, greens, free_second[3], field, perm = lax.optimization_barrier(
        (carried_second, greens, free_second[3], potential_old, permittivity)
    )

    twin_ends = twin_ends.reshape(2, 2, cells, 1, depth)
    ends_before = jnp.where(odd == 1, twin_ends[:, 1], other_ends[:, :, rows - 1 :])
    ends_after = jnp.where(odd == 1, other_ends[:, :, :1], twin_ends[:, 0])
    edge = jnp.zeros((2, cells, rows, 1), jnp.float32)
    halos = ((wire_before, wire_after), (ends_before, ends_after), (edge, edge))
    potential_new = relaxed(field, perm, charge, halos)

    beside_second[1] = beside(1, free_second[2:])
    greens_second = []
    for part in beside_second:
        made, carried_second = greens_of(16, *part, carried_second)
        greens_second.append(made)
    carried_first, greens_second, potential_new = lax.optimization_barrier(
        (carried_first, greens_second, potential_new)
    )

    outputs = []
    for index, part in enumerate(beside_first):
        here, there, carried_first = call(
            mixing_kernel,
            20,
            2 * half,
            (shape(half, 2, width, width), shape(half, 2, width, width), whole),
            pick,
            *part,
            carried_first,
            greens,
            greens_second[index],
            weights,
            grid=(half,),
            in_specs=[
                pl.BlockSpec(memory_space=pltpu.SMEM),
                block,
                block,
                one_state,
                own_block[index],
                block,
                pl.BlockSpec((4, width, width), lambda s: (0, 0, 0)),
            ],
            out_specs=(block, block, one_state),
        )
        if outputs:
            outputs[0], there = lax.optimization_barrier((outputs[0], there))
        outputs.append(here + lax.ppermute(there, "energy", twin_pairs))
    return potential_new, jnp.concatenate(outputs, axis=0)[None]


def solution(mesh):
    in_specs = (
        P("slab", "energy", None),
        P("slab", "energy", None),
        P("slab", "energy", None),
        P("slab", None),
        P("energy", "slab", None, None, None),
        P("slab", None, None, None),
        P(),
        P(),
        P(),
    )
    out_specs = (P("slab", "energy", None), P("energy", "slab", None, None, None))
    return jax.shard_map(
        per_device, mesh=mesh, in_specs=in_specs, out_specs=out_specs, check_vma=False
    )
```

```python
import functools
import math
import jax
import jax.numpy as jnp
from jax import lax
from jax.experimental import pallas as pl
from jax.experimental.pallas import tpu as pltpu
from jax.sharding import PartitionSpec as P

MIB = 1024 * 1024


def halves(value):
    high = value.astype(jnp.bfloat16)
    low = (value - high.astype(jnp.float32)).astype(jnp.bfloat16)
    return high, low


def parts_of(block):
    real, imag = block
    return [halves(real), halves(imag), halves(0.5 * real + 0.5 * imag)]


def left_form(block):
    return [jnp.concatenate([high, high, low], axis=1) for high, low in parts_of(block)]


def right_form(block, axis=0):
    return [jnp.concatenate([high, low, high], axis=axis) for high, low in parts_of(block)]


def three_products(left, right, flipped):
    dims = (((1,), (1 if flipped else 0,)), ((), ()))
    by_real, by_imag, by_mean = (
        lax.dot_general(a, b, dimension_numbers=dims, preferred_element_type=jnp.float32)
        for a, b in zip(left, right)
    )
    return by_real - by_imag, 4.0 * (by_mean - 0.25 * by_real - 0.25 * by_imag)


def product(former, latter):
    return three_products(left_form(former), right_form(latter), False)


def sandwich(link, inner):
    half_way = three_products(left_form(link), right_form(inner), False)
    return three_products(left_form(half_way), right_form(link, 1), True)


def added(first, second):
    return first[0] + second[0], first[1] + second[1]


def pair_of(ref, *where):
    return ref[(*where, 0)], ref[(*where, 1)]


def put(ref, value, *where):
    ref[(*where, 0)] = value[0]
    ref[(*where, 1)] = value[1]


def call(kernel, room, products, out_shapes, *operands, **more):
    flops = products * 9 * 2 * max(x.shape[-1] for x in operands) ** 3
    moved = sum(4 * math.prod(x.shape) for x in jax.tree.leaves((operands, out_shapes)))
    cost = pl.CostEstimate(flops=flops, bytes_accessed=moved, transcendentals=0)
    return pl.pallas_call(
        kernel,
        out_shape=out_shapes,
        cost_estimate=cost,
        compiler_params=pltpu.CompilerParams(vmem_limit_bytes=room * MIB),
        **more,
    )(*operands)


def shape(*dims):
    return jax.ShapeDtypeStruct(dims, jnp.float32)


def gather_kernel(rows, peers, mine, field, perm, charge, before, after, owner, free, *refs):
    out, ends, *parts, held, here, gone = refs
    loads, stores = [], []
    for index in range(len(parts)):
        slab = free.at[index + 1 : index + 2]
        loads.append(
            pltpu.make_async_copy(slab, held.at[index : index + 1], here.at[index])
        )
        loads[-1].start()
    total, depth = charge.shape
    count, orbitals = owner.shape
    height = total // count
    cross = rows * peers
    row_ids = lax.broadcasted_iota(jnp.int32, (total, depth), 0) % rows
    lane_ids = lax.broadcasted_iota(jnp.int32, (total, depth), 1)

    def neighbours(inner, first, last):
        down = jnp.concatenate([first, inner[:-rows]], axis=0)
        up = jnp.concatenate([inner[rows:], last], axis=0)
        left = jnp.where(lane_ids == 0, 0.0, pltpu.roll(inner, 1, axis=1))
        right = jnp.where(lane_ids == depth - 1, 0.0, pltpu.roll(inner, depth - 1, axis=1))
        low = jnp.where(row_ids == 0, 0.0, pltpu.roll(inner, 1, axis=0))
        high = jnp.where(row_ids == rows - 1, 0.0, pltpu.roll(inner, total - 1, axis=0))
        return (down + up) + (left + right) + (low + high)

    first, last = (before[0], before[1]), (after[0], after[1])
    field_now, perm_now = field[...], perm[...]
    both = perm_now * field_now
    own = [
        charge[...],
        perm_now,
        neighbours(field_now, first[0], last[0]),
        neighbours(both, first[0] * first[1], last[0] * last[1]),
        neighbours(perm_now, first[1], last[1]),
    ]
    beside = [jnp.zeros_like(both), jnp.zeros_like(both), field_now, both, perm_now]
    kinds = len(own)
    places = lax.broadcasted_iota(jnp.int32, (2 * height, orbitals), 0)
    depths = lax.broadcasted_iota(jnp.int32, (depth, orbitals), 0)
    first_row = mine[0] * rows
    step = 0
    for slab in range(count):
        if slab == count // 2:
            for index, part in enumerate(parts):
                loads[index].wait()
                stores.append(
                    pltpu.make_async_copy(held.at[index : index + 1], part, gone.at[index])
                )
                stores[-1].start()
        cells = owner[slab : slab + 1, :]
        lane, line = cells % depth, cells // depth
        across, along = line % cross - first_row, line // cross * rows
        key = jnp.where(across == rows, height + along + rows - 1, -1)
        key = jnp.where(across == -1, height + along, key)
        key = jnp.where((across >= 0) & (across < rows), along + across, key)
        cut = slice(slab * height, (slab + 1) * height)
        table = jnp.concatenate(
            [
                jnp.concatenate([t[cut] for t in own], axis=1),
                jnp.concatenate([t[cut] for t in beside], axis=1),
            ],
            axis=0,
        ).T
        high, rest = halves(table)
        middle = rest.astype(jnp.float32)
        lowest = ((table - high.astype(jnp.float32)) - middle).astype(jnp.bfloat16)
        hit = jnp.where(places == key, 1.0, 0.0).astype(jnp.bfloat16)
        found = jnp.dot(
            jnp.concatenate([high, rest, lowest], axis=1),
            jnp.concatenate([hit, hit, hit], axis=0),
            preferred_element_type=jnp.float32,
        )
        for kind in range(kinds):
            part = found[kind * depth : (kind + 1) * depth]
            value = jnp.sum(jnp.where(depths == lane, part, 0.0), axis=0, keepdims=True)
            for piece in range(orbitals // depth):
                row = sums_row(kind, slab, count, orbitals // depth) + piece
                out[row : row + 1, :] = value[:, piece * depth : (piece + 1) * depth]
    start = 0
    for array in (field, perm):
        for end in (0, rows - 1):
            ends[start : start + total // rows, :] = array[
                pl.ds(end, total // rows, stride=rows), :
            ]
            start += total // rows
    for store in stores:
        store.wait()


def sums_row(kind, slab, count, pieces):
    return (kind * count + slab) * pieces


def potential_of(sums, slab, count, orbitals):
    pieces = orbitals // sums.shape[1]

    def value(kind):
        first = sums_row(kind, slab, count, pieces)
        return jnp.concatenate([sums[pl.ds(first + p, 1), :] for p in range(pieces)], axis=1)

    charge, perm, fields, both, perms = (value(kind) for kind in range(5))
    return (charge + 0.5 * (perm * fields + both)) / (3.0 * perm + 0.5 * perms)


def source_of(block, potential):
    scaled = (block[0] * potential, block[1] * potential)
    return added(block, product(scaled, block))


def own_kernel(free, coupling, sums, whole_map, whole_source):
    count = free.shape[0]
    links, state = [], None
    for slab in range(count):
        block = pair_of(free, slab)
        links.append(product(block, pair_of(coupling, slab)))
        source = source_of(block, potential_of(sums, slab, count, free.shape[-1]))
        state = source if state is None else added(sandwich(links[slab], state), source)
    put(whole_source, state)
    while len(links) > 1:
        paired = [product(b, a) for a, b in zip(links[0::2], links[1::2])]
        links = paired + links[len(paired) * 2 :]
    put(whole_map, links[0])


def hop_kernel(whole_map, whole_source, carried, out):
    put(out, added(sandwich(pair_of(whole_map), pair_of(carried)), pair_of(whole_source)))


def last_hop_kernel(odd, whole_map, whole_source, carried, before, out, onward):
    now = added(sandwich(pair_of(whole_map), pair_of(carried)), pair_of(whole_source))
    put(out, now)
    put(onward, [jnp.where(odd[0] != 0, before[part], now[part]) for part in range(2)])


def beside_kernel(start, count, parts, *refs):
    frees, (coupling, sums, link, source) = refs[:parts], refs[parts:]
    slab = 0
    for free in frees:
        for place in range(free.shape[0]):
            block = pair_of(free, place)
            put(link, product(block, pair_of(coupling, slab)), slab)
            row = potential_of(sums, start + slab, count, free.shape[-1])
            put(source, source_of(block, row), slab)
            slab += 1


def greens_kernel(link, source, carried, greens, state):
    @pl.when(pl.program_id(0) == 0)
    def _():
        state[...] = carried[...]

    now = added(sandwich(pair_of(link, 0), pair_of(state)), pair_of(source, 0))
    put(state, now)
    put(greens, now, 0)


def own_greens_kernel(count, free, coupling, sums, carried, greens, state):
    @pl.when(pl.program_id(0) == 0)
    def _():
        state[...] = carried[...]

    block = pair_of(free, 0)
    link = product(block, pair_of(coupling, 0))
    row = potential_of(sums, pl.program_id(0), count, free.shape[-1])
    now = added(sandwich(link, pair_of(state)), source_of(block, row))
    put(state, now)
    put(greens, now, 0)


def mixing_kernel(pick, link, source, carried, own, second, weights, here, there, state):
    @pl.when(pl.program_id(0) == 0)
    def _():
        state[...] = carried[...]

    first = added(sandwich(pair_of(link, 0), pair_of(state)), pair_of(source, 0))
    put(state, first)
    for part in range(2):
        second_now = jnp.where(pick[1] != 0, second[0, part], 0.0)
        here[0, part] = weights[0] * first[part] + weights[1] * second_now
        picked = jnp.where(pick[0] == 0, first[part], second_now)
        there[0, part] = weights[2] * own[0, part] + weights[3] * picked


def relaxed(field, perm, charge, halos):
    numerator = charge
    denominator = jnp.zeros_like(charge)
    for dim in range(3):
        length = charge.shape[dim]
        before, after = halos[dim]
        for side in range(2):
            sides = []
            for which, array in enumerate((field, perm)):
                if side == 0:
                    kept = lax.slice_in_dim(array, 1, length, axis=dim)
                    parts = [kept, after[which]]
                else:
                    kept = lax.slice_in_dim(array, 0, length - 1, axis=dim)
                    parts = [before[which], kept]
                sides.append(jnp.concatenate(parts, axis=dim))
            face = 0.5 * (perm + sides[1])
            numerator = numerator + face * sides[0]
            denominator = denominator + face
    return numerator / denominator


def end_planes(array, dim):
    length = array.shape[dim]
    return (
        lax.slice_in_dim(array, 0, 1, axis=dim),
        lax.slice_in_dim(array, length - 1, length, axis=dim),
    )


def exchanged(sums, ends, early):
    peers = lax.axis_size("energy")
    assert peers >= 4 and peers & (peers - 1) == 0
    masks = [2, 1] + [1 << k for k in range(2, peers.bit_length() - 1)]
    rows, twin_ends = sums.shape[0], None
    first = None
    sums, early = lax.optimization_barrier((sums, early))
    payload = jnp.concatenate([sums, ends])
    for mask in masks:
        given = payload if mask == 1 else payload[:rows]
        arrived = lax.ppermute(given, "energy", [(e, e ^ mask) for e in range(peers)])
        if mask == 1:
            twin_ends = arrived[rows:]
        added_rows = ((0, payload.shape[0] - rows), (0, 0))
        payload = payload + jnp.pad(arrived[:rows], added_rows)
        first = arrived if first is None else first
    return payload[:rows], twin_ends, first, early


def per_device(
    potential_old,
    charge,
    permittivity,
    owner_cell,
    green_free,
    coupling,
    shifts,
    occupation,
    mode_tiles,
):
    energies, peers = lax.axis_size("energy"), lax.axis_size("slab")
    mine = lax.axis_index("energy")
    free = green_free[0]
    count, _, width, _ = free.shape
    whole = shape(2, width, width)
    blocks = shape(count, 2, width, width)

    everyone = range(energies)
    relayed = energies == 8
    if relayed:
        first_pairs = [(e, e ^ 2) for e in everyone]
        second_pairs = [(2, 4), (3, 5), (4, 2), (5, 3)]
        relay_pairs = [(e, e ^ 4) for e in everyone]
        turned = (mine // 2) % 2
        has_second = jnp.where((mine >= 2) & (mine < 6), 1, 0)
    else:
        first_pairs = [(e, e - 2) for e in everyone if e >= 2]
        second_pairs = [(e, e + 2) for e in everyone if e + 2 < energies]
        relay_pairs = second_pairs
        turned = jnp.zeros_like(mine)
        has_second = jnp.ones_like(mine)
    twin_pairs = [(e, e ^ 1) for e in everyone]

    half = count // 2
    one_slab = shape(1, 2, width, width)
    first_cut = free[:1]
    free_first = [lax.ppermute(first_cut, "energy", first_pairs)]

    place = lax.axis_index("slab")
    wire_up = [(i, i + 1) for i in range(peers - 1)]

    def swaps(start):
        pairs = [(i, i + 1) for i in range(start, peers - 1, 2)]
        return pairs + [(j, i) for i, j in pairs]

    first_cut, stacked = lax.optimization_barrier(
        (first_cut, jnp.stack([potential_old, permittivity]))
    )
    lower, upper = end_planes(stacked, 1)
    even = place % 2 == 0
    arrived = lax.ppermute(jnp.where(even, upper, lower), "slab", swaps(0))
    crossed = lax.ppermute(jnp.where(even, lower, upper), "slab", swaps(1))
    wire_before = jnp.where(even, crossed, arrived)
    wire_after = jnp.where(even, arrived, crossed)

    cells, rows, depth = charge.shape
    beyond = [(e, e + 1) for e in range(1, energies - 1, 2)]
    other_ends = lax.ppermute(stacked, "energy", beyond + [(b, a) for a, b in beyond])
    far, near = pl.BlockSpec(memory_space=pl.ANY), pl.BlockSpec(memory_space=pltpu.VMEM)
    sums, ends, *cuts = call(
        functools.partial(gather_kernel, rows, energies),
        56,
        1,
        (
            shape(5 * count * (width // depth), depth),
            shape(4 * cells, depth),
            *[one_slab] * (count - 1),
        ),
        jnp.reshape(mine, (1,)),
        *(array.reshape(-1, depth) for array in (potential_old, permittivity, charge)),
        wire_before.reshape(2, rows, depth),
        wire_after.reshape(2, rows, depth),
        owner_cell,
        free,
        in_specs=[pl.BlockSpec(memory_space=pltpu.SMEM)] + [near] * 6 + [far],
        out_specs=(near, near, *[far] * (count - 1)),
        scratch_shapes=[
            pltpu.VMEM((count - 1, 2, width, width), jnp.float32),
            pltpu.SemaphoreType.DMA((count - 1,)),
            pltpu.SemaphoreType.DMA((count - 1,)),
        ],
    )
    cuts = [first_cut, *cuts]
    sums, twin_ends, crossed, (arrived, other_ends) = exchanged(
        sums, ends, (free_first[0], other_ends)
    )

    crossed, cuts[1] = lax.optimization_barrier((crossed, cuts[1]))
    sums, arrived = lax.optimization_barrier((sums, arrived))
    free_first = [arrived, lax.ppermute(cuts[1], "energy", first_pairs)]
    free_second = []

    def sent_on(part):
        given = free_first[part] if relayed else cuts[part]
        free_second.append(lax.ppermute(given, "energy", relay_pairs))

    def sent_after(part):
        free_first[part - 1], cut = lax.optimization_barrier((free_first[part - 1], cuts[part]))
        free_first.append(lax.ppermute(cut, "energy", first_pairs))

    sent_on(0)
    whole_map, whole_source = call(
        own_kernel,
        32,
        5 * count - 3,
        (whole, whole),
        free,
        coupling,
        sums,
    )

    whole_source, mode_tiles = lax.optimization_barrier((whole_source, mode_tiles))
    odd = mine % 2
    distance = jnp.array([2, 2, 1, 1], jnp.int32)
    lowered = jnp.stack([turned, 1 - turned, 1 - odd, odd]).astype(jnp.float32)
    factors = (shifts[None, :] == distance[:, None]) * (occupation[None, :] + lowered[:, None])
    weights = jnp.sum(factors[:, :, None, None] * mode_tiles[None], axis=1)
    pick = jnp.stack([turned ^ odd, has_second]).astype(jnp.int32)

    block = pl.BlockSpec((1, 2, width, width), lambda s: (s, 0, 0, 0))
    one_state = pl.BlockSpec((2, width, width), lambda s: (0, 0, 0))
    own_block = [
        pl.BlockSpec((1, 2, width, width), lambda s, first=i * half: (first + s, 0, 0, 0))
        for i in range(2)
    ]

    def beside(index, parts):
        made = shape(half, 2, width, width)
        whole_spec = pl.BlockSpec((half, 2, width, width), lambda s: (0, 0, 0, 0))
        return call(
            functools.partial(beside_kernel, index * half, count, len(parts)),
            24,
            2 * half,
            (made, made),
            *parts,
            coupling,
            sums,
            grid=(1,),
            in_specs=[pl.BlockSpec(part.shape, lambda s: (0, 0, 0, 0)) for part in parts]
            + [
                pl.BlockSpec((half, 2, width, width), lambda s: (index, 0, 0, 0)),
                pl.BlockSpec(sums.shape, lambda s: (0, 0)),
            ],
            out_specs=(whole_spec, whole_spec),
        )

    def greens_of(room, link, source, carried):
        return call(
            greens_kernel,
            room,
            2 * link.shape[0],
            (shape(*link.shape), whole),
            link,
            source,
            carried,
            grid=(link.shape[0],),
            in_specs=[block, block, one_state],
            out_specs=(block, one_state),
        )

    assert peers % 2 == 0
    leaving, previous, before = whole_source, None, None
    beside_first, beside_second = [None, None], [None, None]
    for hop in range(1, peers - 1):
        arrived = lax.ppermute(leaving, "slab", swaps((hop - 1) % 2))
        if hop == 1:
            sent_on(1)
            sent_after(2)
            arrived, weights, free_first[1] = lax.optimization_barrier(
                (arrived, weights, free_first[1])
            )
        if hop == 2:
            sent_on(2)
            sent_after(3)
            free_first[:3] = lax.optimization_barrier(free_first[:3])
            beside_first[0] = beside(0, free_first[:2])
            arrived, beside_first[0], free_first[2], *free_second[:2] = lax.optimization_barrier(
                (arrived, beside_first[0], free_first[2], *free_second[:2])
            )
        previous, before = arrived, leaving
        if hop < peers - 2:
            leaving = call(hop_kernel, 12, 2, whole, whole_map, whole_source, arrived)
    leaving, onward = call(
        last_hop_kernel,
        12,
        2,
        (whole, whole),
        jnp.reshape(place % 2, (1,)),
        whole_map,
        whole_source,
        previous,
        before,
        in_specs=[pl.BlockSpec(memory_space=pltpu.SMEM)] + [near] * 4,
        out_specs=(near, near),
    )

    def both(pairs):
        return [(a * peers + i, b * peers + j) for a, b in pairs for i, j in wire_up]

    arrived = lax.ppermute(leaving, "slab", swaps((peers - 2) % 2))
    sent_on(3)
    beside_second[0] = beside(0, free_second[:2])
    beside_first[1] = beside(1, free_first[2:])
    onward, beside_first[1] = lax.optimization_barrier((onward, beside_first[1]))
    carried_second = lax.ppermute(onward, ("energy", "slab"), both(second_pairs))
    arrived, beside_first[1], beside_second[0], free_second[2] = lax.optimization_barrier(
        (arrived, beside_first[1], beside_second[0], free_second[2])
    )
    carried = jnp.where(place % 2 == 1, arrived, previous)
    carried_first = lax.ppermute(carried, "energy", first_pairs)
    greens, _ = call(
        functools.partial(own_greens_kernel, count),
        24,
        4 * count,
        (blocks, whole),
        free,
        coupling,
        sums,
        carried,
        grid=(count,),
        in_specs=[block, block, pl.BlockSpec(sums.shape, lambda s: (0, 0)), one_state],
        out_specs=(block, one_state),
    )
    carried_second, greens, free_second[3], field, perm = lax.optimization_barrier(
        (carried_second, greens, free_second[3], potential_old, permittivity)
    )

    twin_ends = twin_ends.reshape(2, 2, cells, 1, depth)
    ends_before = jnp.where(odd == 1, twin_ends[:, 1], other_ends[:, :, rows - 1 :])
    ends_after = jnp.where(odd == 1, other_ends[:, :, :1], twin_ends[:, 0])
    edge = jnp.zeros((2, cells, rows, 1), jnp.float32)
    halos = ((wire_before, wire_after), (ends_before, ends_after), (edge, edge))
    potential_new = relaxed(field, perm, charge, halos)

    beside_second[1] = beside(1, free_second[2:])
    greens_second = []
    for part in beside_second:
        made, carried_second = greens_of(16, *part, carried_second)
        greens_second.append(made)
    carried_first, greens_second, potential_new = lax.optimization_barrier(
        (carried_first, greens_second, potential_new)
    )

    outputs = []
    for index, part in enumerate(beside_first):
        here, there, carried_first = call(
            mixing_kernel,
            20,
            2 * half,
            (shape(half, 2, width, width), shape(half, 2, width, width), whole),
            pick,
            *part,
            carried_first,
            greens,
            greens_second[index],
            weights,
            grid=(half,),
            in_specs=[
                pl.BlockSpec(memory_space=pltpu.SMEM),
                block,
                block,
                one_state,
                own_block[index],
                block,
                pl.BlockSpec((4, width, width), lambda s: (0, 0, 0)),
            ],
            out_specs=(block, block, one_state),
        )
        if outputs:
            outputs[0], there = lax.optimization_barrier((outputs[0], there))
        outputs.append(here + lax.ppermute(there, "energy", twin_pairs))
    return potential_new, jnp.concatenate(outputs, axis=0)[None]


def solution(mesh):
    in_specs = (
        P("slab", "energy", None),
        P("slab", "energy", None),
        P("slab", "energy", None),
        P("slab", None),
        P("energy", "slab", None, None, None),
        P("slab", None, None, None),
        P(),
        P(),
        P(),
    )
    out_specs = (P("slab", "energy", None), P("energy", "slab", None, None, None))
    return jax.shard_map(
        per_device, mesh=mesh, in_specs=in_specs, out_specs=out_specs, check_vma=False
    )
```
